32 devices in a mesh: dp: 2 (over x), fsdp: 16 (over z, y, core).
Axes of the slice: x: 2, y: 2, z: 4, core: 2. Of those that a mesh axis runs over, the one named last changes fastest.
Arguments:
- pixels: bfloat16 [23552, 512], P(('dp', 'fsdp')), may hold values from -6 to 6
- embedding: bfloat16 [96, 2048], P(('dp', 'fsdp')), may hold values from -6 to 6
- text_states: bfloat16 [96, 77, 4096], P(('dp', 'fsdp')), may hold values from -6 to 6
- text_mask: int32 [96, 77], P(('dp', 'fsdp')), may hold values 0 or 1
- occupancy: int32 [32, 3], P(('dp', 'fsdp')), may hold values 0 or 1
- cotangent: bfloat16 [23552, 1024], P(('dp', 'fsdp')), may hold values from -6 to 6
- in_gain: bfloat16 [512], P('fsdp'), may hold values from 0.5 to 1.5
- in_shift: bfloat16 [512], P('fsdp'), may hold values from -3 to 3
- conv_first: bfloat16 [4608, 1024], P('fsdp'), may hold values from -0.09375 to 0.09375
- first_bias: bfloat16 [1024], P('fsdp'), may hold values from -2 to 2
- emb_weight: bfloat16 [2048, 2048], P('fsdp'), may hold values from -0.0625 to 0.0625
- emb_bias: bfloat16 [2048], P('fsdp'), may hold values from -2 to 2
- mid_gain: bfloat16 [1024], P('fsdp'), may hold values from 0.5 to 1.5
- mid_shift: bfloat16 [1024], P('fsdp'), may hold values from -3 to 3
- conv_second: bfloat16 [9216, 1024], P('fsdp'), may hold values from -0.0625 to 0.0625
- second_bias: bfloat16 [1024], P('fsdp'), may hold values from -2 to 2
- skip_weight: bfloat16 [512, 1024], P('fsdp'), may hold values from -0.25 to 0.25
- skip_bias: bfloat16 [1024], P('fsdp'), may hold values from -2 to 2
- attn_gain: bfloat16 [1024], P('fsdp'), may hold values from 0.5 to 1.5
- attn_shift: bfloat16 [1024], P('fsdp'), may hold values from -3 to 3
- attend_weight: bfloat16 [1024, 1536], P('fsdp'), may hold values from -0.1875 to 0.1875
- text_weight: bfloat16 [4096, 1024], P('fsdp'), may hold values from -0.09375 to 0.09375
- out_weight: bfloat16 [512, 1024], P('fsdp'), may hold values from -1.5 to 1.5
- out_bias: bfloat16 [1024], P('fsdp'), may hold values from -2 to 2
Outputs:
- block_output: bfloat16 [23552, 1024], P(('dp', 'fsdp'))
- grad_pixels: float32 [23552, 512], P(('dp', 'fsdp'))
- grad_in_gain: float32 [512], P('fsdp')
- grad_in_shift: float32 [512], P('fsdp')
- grad_conv_first: float32 [4608, 1024], P('fsdp')
- grad_first_bias: float32 [1024], P('fsdp')
- grad_emb_weight: float32 [2048, 2048], P('fsdp')
- grad_emb_bias: float32 [2048], P('fsdp')
- grad_mid_gain: float32 [1024], P('fsdp')
- grad_mid_shift: float32 [1024], P('fsdp')
- grad_conv_second: float32 [9216, 1024], P('fsdp')
- grad_second_bias: float32 [1024], P('fsdp')
- grad_skip_weight: float32 [512, 1024], P('fsdp')
- grad_skip_bias: float32 [1024], P('fsdp')
- grad_attn_gain: float32 [1024], P('fsdp')
- grad_attn_shift: float32 [1024], P('fsdp')
- grad_attend_weight: float32 [1024, 1536], P('fsdp')
- grad_text_weight: float32 [4096, 1024], P('fsdp')
- grad_out_weight: float32 [512, 1024], P('fsdp')
- grad_out_bias: float32 [1024], P('fsdp')
The draws below stay inside these ranges and needn't reach their ends.
All inputs are finite; a program needn't handle non-finite values. No bound on the sum of `text_mask` or of `occupancy` on one device may be relied on, other than what follows from the above.
Results may differ from the reference program's by a relative error of at most 0.02.
Values may be sent and summed in bfloat16 or wider, within the bound.
A program may use at most 320 MiB of HBM per device.

```python
import jax
import jax.numpy as jnp
from jax import lax

C_IN = 512
C = 1024
EMB = 2048
HEADS = 8
HEAD = 64
TEXT_DIM = 4096
TEXT_LEN = 77
GROUPS = 32
UNIT = 4
INNER = 512
PIX = 736
SLOTS = 96
ROWS = 23552
DEVICES = 32


def plant(result, key, low, largest):
    extent = result.shape
    index_at = [jax.random.randint(jax.random.fold_in(key, axis), (), 0, extent[axis]) for axis in range(len(extent))]
    result = result.at[tuple(index_at)].set(low)
    longest = extent.index(max(extent))
    index_at[longest] = (index_at[longest] + 1) % extent[longest]
    return result.at[tuple(index_at)].set(largest)


def shard_levels(own_key, shape, cuts, least, high):
    loudness, own = 1.0, jax.random.fold_in(own_key, 6)
    for dim, parts in cuts:
        steps = jnp.exp(jax.random.uniform(jax.random.fold_in(own, dim), (parts,), jnp.float32, least / len(cuts), high / len(cuts)))
        loudness = loudness * jnp.repeat(steps, shape[dim] // parts).reshape([-1 if axis == dim else 1 for axis in range(len(shape))])
    return loudness


def bell_draw(stream_key, shape, scale, most, cuts=(), kind=jnp.bfloat16):
    level = shard_levels(stream_key, shape, cuts, -0.22, 0.18) if cuts else 1.0
    array = jax.random.normal(stream_key, shape, jnp.float32) * scale * level
    return jnp.minimum(jnp.maximum(array, -most), most).astype(kind)


def setup_inputs(seed: int = 0) -> dict:
    splits = jax.random.split(jax.random.key(seed), 25)
    pixels = bell_draw(splits[0], (ROWS, C_IN), 1.0, 6.0, ((0, 32),))
    embedding = bell_draw(splits[1], (SLOTS, EMB), 1.0, 6.0, ((0, 32),))
    text_states = bell_draw(splits[2], (SLOTS, TEXT_LEN, TEXT_DIM), 1.0, 6.0, ((0, 32),))
    text_mask = plant((jax.random.randint(splits[3], (SLOTS, TEXT_LEN), 0, 4) < 3).astype(jnp.int32), jax.random.fold_in(splits[3], 1), 0, 1)
    occupancy = plant((jax.random.randint(splits[4], (DEVICES, 3), 0, 4) < 3).astype(jnp.int32), jax.random.fold_in(splits[4], 1), 0, 1)
    cotangent = bell_draw(splits[5], (ROWS, C), 1.0, 6.0, ((0, 32),))
    in_gain = jnp.clip(0.5 + 1.0 * jax.random.uniform(splits[6], (C_IN,), jnp.float32) ** shard_levels(splits[6], (C_IN,), ((0, 16),), -0.2, 0.2), 0.5, 1.5).astype(jnp.bfloat16)
    in_shift = bell_draw(splits[7], (C_IN,), 0.5, 3.0, ((0, 16),))
    conv_first = bell_draw(splits[8], (9 * C_IN, C), (9 * C_IN) ** -0.5, 0.09375, ((0, 16),))
    first_bias = bell_draw(splits[9], (C,), 0.3, 2.0, ((0, 16),))
    emb_weight = bell_draw(splits[10], (EMB, 2 * C), (4 * EMB) ** -0.5, 0.0625, ((0, 16),))
    emb_bias = bell_draw(splits[11], (2 * C,), 0.3, 2.0, ((0, 16),))
    mid_gain = jnp.clip(0.5 + 1.0 * jax.random.uniform(splits[12], (C,), jnp.float32) ** shard_levels(splits[12], (C,), ((0, 16),), -0.2, 0.2), 0.5, 1.5).astype(jnp.bfloat16)
    mid_shift = bell_draw(splits[13], (C,), 0.5, 3.0, ((0, 16),))
    conv_second = bell_draw(splits[14], (9 * C, C), (9 * C) ** -0.5, 0.0625, ((0, 16),))
    second_bias = bell_draw(splits[15], (C,), 0.3, 2.0, ((0, 16),))
    skip_weight = bell_draw(splits[16], (C_IN, C), C_IN ** -0.5, 0.25, ((0, 16),))
    skip_bias = bell_draw(splits[17], (C,), 0.3, 2.0, ((0, 16),))
    attn_gain = jnp.clip(0.5 + 1.0 * jax.random.uniform(splits[18], (C,), jnp.float32) ** shard_levels(splits[18], (C,), ((0, 16),), -0.2, 0.2), 0.5, 1.5).astype(jnp.bfloat16)
    attn_shift = bell_draw(splits[19], (C,), 0.5, 3.0, ((0, 16),))
    attend_weight = bell_draw(splits[20], (C, 3 * INNER), C ** -0.5, 0.1875, ((0, 16),))
    text_weight = bell_draw(splits[21], (TEXT_DIM, 2 * INNER), TEXT_DIM ** -0.5, 0.09375, ((0, 16),))
    out_weight = bell_draw(splits[22], (INNER, C), (INNER // 32) ** -0.5, 1.5, ((0, 16),))
    out_bias = bell_draw(splits[23], (C,), 0.3, 2.0, ((0, 16),))
    return dict(pixels=pixels, embedding=embedding, text_states=text_states, text_mask=text_mask, occupancy=occupancy, cotangent=cotangent, in_gain=in_gain, in_shift=in_shift, conv_first=conv_first, first_bias=first_bias, emb_weight=emb_weight, emb_bias=emb_bias, mid_gain=mid_gain, mid_shift=mid_shift, conv_second=conv_second, second_bias=second_bias, skip_weight=skip_weight, skip_bias=skip_bias, attn_gain=attn_gain, attn_shift=attn_shift, attend_weight=attend_weight, text_weight=text_weight, out_weight=out_weight, out_bias=out_bias)


@jax.custom_vjp
def low(v):
    return lax.optimization_barrier(v.astype(jnp.bfloat16)).astype(jnp.float32)

@jax.custom_vjp
def low_back(v):
    return v

def low_keep(v):
    return (low(v), None)

def low_pass(kept, grad):
    return (grad,)

def back_keep(v):
    return (v, None)

def back_low(kept, grad):
    return (low(grad),)
low.defvjp(low_keep, low_pass)
low_back.defvjp(back_keep, back_low)

def matmul_high(first_operand, second_operand):
    return jnp.dot(first_operand, second_operand, preferred_element_type=jnp.float32, precision=lax.Precision.HIGHEST)

def group_norm(entries, norm_gain, norm_shift):
    pixel_count, channels = entries.shape
    grouped = entries.reshape(pixel_count, GROUPS, channels // GROUPS)
    center = lax.optimization_barrier(jnp.mean(grouped, axis=(0, 2), keepdims=True))
    spread = lax.optimization_barrier(jnp.mean(jnp.square(grouped - center), axis=(0, 2), keepdims=True))
    scaled = ((grouped - center) * lax.rsqrt(spread + 1e-05)).reshape(pixel_count, channels)
    return scaled * norm_gain + norm_shift

def patches(flat_rows, height, breadth):
    channels = flat_rows.shape[-1]
    picture = flat_rows.reshape(height, breadth, channels)
    padded = jnp.pad(picture, ((1, 1), (1, 1), (0, 0)))
    windows = [padded[step_down:step_down + height, step_across:step_across + breadth] for step_down in range(3) for step_across in range(3)]
    return jnp.concatenate(windows, axis=-1).reshape(height * breadth, 9 * channels)

def picture_forward(weight_set, pixel_rows, emb_row, text_rows, text_keep, present, height, breadth):
    in_gain, in_shift, conv_first, first_bias, emb_weight, emb_bias, mid_gain, mid_shift, conv_second, second_bias, skip_weight, skip_bias, attn_gain, attn_shift, attend_weight, text_weight, out_weight, out_bias = weight_set
    channels = conv_first.shape[1]
    inner_width = out_weight.shape[0]
    pixel_count = height * breadth
    first_act = low(jax.nn.silu(group_norm(pixel_rows, in_gain, in_shift)))
    first_conv = low_back(matmul_high(patches(first_act, height, breadth), conv_first)) + first_bias
    emb_act = low(jax.nn.silu(emb_row))[None, :]
    modulation = low_back(matmul_high(emb_act, emb_weight))[0] + emb_bias
    middle = group_norm(first_conv, mid_gain, mid_shift) * (1.0 + modulation[:channels]) + modulation[channels:]
    second_act = low(jax.nn.silu(middle))
    second_conv = low_back(matmul_high(patches(second_act, height, breadth), conv_second)) + second_bias
    skip_part = low_back(matmul_high(low(pixel_rows), skip_weight)) + skip_bias
    residual = skip_part + second_conv
    normed = low(group_norm(residual, attn_gain, attn_shift))
    triple = low(low_back(matmul_high(normed, attend_weight)))
    text_pair = low(low_back(matmul_high(low(text_rows), text_weight)))
    queries = triple[:, :inner_width].reshape(pixel_count, HEADS, HEAD)
    key_rows = jnp.concatenate([triple[:, inner_width:2 * inner_width], text_pair[:, :inner_width]], 0)
    key_rows = key_rows.reshape(-1, HEADS, HEAD)
    value_rows = jnp.concatenate([triple[:, 2 * inner_width:], text_pair[:, inner_width:]], 0)
    value_rows = value_rows.reshape(-1, HEADS, HEAD)
    key_keep = jnp.concatenate([jnp.ones((pixel_count,), jnp.bool_), text_keep > 0])
    raw_scores = jnp.einsum('qhd,khd->hqk', queries, key_rows, preferred_element_type=jnp.float32, precision=lax.Precision.HIGHEST)
    scores = low_back(raw_scores) * HEAD ** (-0.5)
    scores = jnp.where(key_keep[None, None, :], scores, -1000000000.0)
    attn_probs = jax.nn.softmax(scores, axis=-1)
    attended = jnp.einsum('hqk,khd->qhd', low(attn_probs), value_rows, preferred_element_type=jnp.float32, precision=lax.Precision.HIGHEST).reshape(pixel_count, inner_width)
    output_part = low_back(matmul_high(low(low_back(attended)), out_weight)) + out_bias
    return present * (residual + output_part)

def reference(pixels, embedding, text_states, text_mask, occupancy, cotangent, in_gain, in_shift, conv_first, first_bias, emb_weight, emb_bias, mid_gain, mid_shift, conv_second, second_bias, skip_weight, skip_bias, attn_gain, attn_shift, attend_weight, text_weight, out_weight, out_bias):
    weights = tuple((member.astype(jnp.float32) for member in (in_gain, in_shift, conv_first, first_bias, emb_weight, emb_bias, mid_gain, mid_shift, conv_second, second_bias, skip_weight, skip_bias, attn_gain, attn_shift, attend_weight, text_weight, out_weight, out_bias)))
    shapes = ((4 * UNIT, 4 * UNIT), (3 * UNIT, 5 * UNIT), (5 * UNIT, 3 * UNIT))
    pixel_stack = pixels.astype(jnp.float32).reshape(DEVICES, PIX, C_IN)
    emb_stack = embedding.astype(jnp.float32).reshape(DEVICES, 3, EMB)
    text_stack = text_states.astype(jnp.float32).reshape(DEVICES, 3, TEXT_LEN, TEXT_DIM)
    keep_stack = text_mask.reshape(DEVICES, 3, TEXT_LEN)
    present_stack = occupancy.astype(jnp.float32)

    def device_forward(weight_set, pixel_block, emb_block, text_block, keep_block, present_block):
        outputs = []
        offset = 0
        for bucket in range(3):
            height, breadth = shapes[bucket]
            outputs.append(picture_forward(weight_set, pixel_block[offset:offset + height * breadth], emb_block[bucket], text_block[bucket], keep_block[bucket], present_block[bucket], height, breadth))
            offset += height * breadth
        return jnp.concatenate(outputs, 0)
    stepper = jax.checkpoint(device_forward)

    def whole_forward(weight_set, pixel_all):

        def apply_one(sliced):
            return stepper(weight_set, *sliced)
        return lax.map(apply_one, (pixel_all, emb_stack, text_stack, keep_stack, present_stack))
    output, pullback = jax.vjp(whole_forward, weights, pixel_stack)
    grad_weights, grad_stack = pullback(cotangent.astype(jnp.float32).reshape(DEVICES, PIX, C))
    block_output = output.reshape(DEVICES * PIX, C).astype(jnp.bfloat16)
    grad_pixels = grad_stack.reshape(DEVICES * PIX, C_IN)
    return (block_output, grad_pixels, grad_weights[0], grad_weights[1], grad_weights[2], grad_weights[3], grad_weights[4], grad_weights[5], grad_weights[6], grad_weights[7], grad_weights[8], grad_weights[9], grad_weights[10], grad_weights[11], grad_weights[12], grad_weights[13], grad_weights[14], grad_weights[15], grad_weights[16], grad_weights[17])
```

```python
import functools

import jax
import jax.numpy as jnp
from jax import lax
from jax.experimental import pallas as pl
from jax.experimental.pallas import tpu as pltpu
from jax.sharding import PartitionSpec as P

MESH = pl.DeviceIdType.MESH
BF16=jnp.bfloat16
DEPTH = 4


class Where:
    def __init__(self, replicas, parts):
        self.replicas, self.parts = replicas, parts
        self.span = parts // (2 * DEPTH)
        self.group = lax.axis_index("dp")
        self.place = lax.axis_index("fsdp")
        self.core = lax.rem(self.place, 2)
        self.y = lax.rem(self.place // 2, self.span)
        self.z = self.place // (2 * self.span)
        self.side = lax.rem(self.group, 2)

    def index(self, z, y, core):
        return (z * self.span + y) * 2 + core

    def device(self, z=None, y=None, core=None, flip=False):
        z = self.z if z is None else z
        y = self.y if y is None else y
        core = self.core if core is None else core
        group = self.group + 1 - 2 * self.side if flip else self.group
        return (group, self.index(z, y, core))

    def barrier(self):
        sem = pltpu.get_barrier_semaphore()
        greet = lambda device: pl.semaphore_signal(sem, inc=1, device_id=device, device_id_type=MESH)
        greet(self.device(flip=True))
        def one(i, carry):
            greet((self.group, lax.rem(self.place + i, self.parts)))
            return carry
        lax.fori_loop(1, self.parts, one, 0)
        pl.semaphore_wait(sem, self.parts)


def gather_kernel(replicas, parts, rows, lead, own, note, emb, full, mod, notes, part, sums, n_send, n_recv, m_send, m_recv, z_send, z_recv, y_send, y_recv, s_send, s_recv, x_send, x_recv, c_send, c_recv, own_sem):
    me = Where(replicas, parts)
    span = me.span
    total, width = own.shape
    chunks = total // rows
    half = width // 2
    side = me.side
    thin = 128
    z_cols = pl.ds(pl.multiple_of(side * thin, thin), width - thin)
    a_cols = pl.ds(pl.multiple_of(side * half, half), half)
    thin_cols = pl.ds(pl.multiple_of((1 - side) * (width - thin), thin), thin)
    thin_out = pl.ds(pl.multiple_of(side * (width - thin), thin), thin)
    b_cols = pl.ds(pl.multiple_of((1 - side) * half, half), half)

    me.barrier()
    local = pltpu.make_async_copy(own, full.at[me.place], own_sem)
    local.start()

    def at(k):
        return pl.ds(pl.multiple_of(k * rows, 16), rows)

    def copy(src, dst, send, recv, device):
        return pltpu.make_async_remote_copy(src_ref=src, dst_ref=dst, send_sem=send, recv_sem=recv, device_id=device, device_id_type=MESH)

    def piece(k, z, y, cols, core=None):
        return full.at[me.index(z, y, me.core if core is None else core), at(k), cols]

    def z_copy(k, z, step, mine):
        src = own.at[at(k), z_cols] if mine else piece(k, z, me.y, z_cols)
        return copy(src, piece(k, z, me.y, z_cols), z_send.at[k, z, (step + 1) // 2], z_recv.at[k, z], me.device(z=me.z + step))

    def y_copy(k, z, turn, mine):
        src = own.at[at(k), a_cols] if mine else piece(k, z, me.y, a_cols)
        return copy(src, piece(k, z, me.y, a_cols), y_send.at[k, z, turn - 1], y_recv.at[k, z, turn - 1], me.device(y=lax.rem(me.y + turn, span)))

    def thin_copy(k, z):
        return copy(piece(k, z, me.y, thin_out), piece(k, z, me.y, thin_out), s_send.at[k, z], s_recv.at[k, z], me.device(flip=True))

    def x_copy(k, z, turn):
        y = lax.rem(me.y + turn, span)
        return copy(piece(k, z, y, a_cols), piece(k, z, y, a_cols), x_send.at[k, z, turn - 1], x_recv.at[k, z, turn - 1], me.device(flip=True))

    def core_copy(k, z, y, cols, mine=False):
        src = own.at[at(k), cols] if mine else piece(k, z, y, cols)
        return copy(src, piece(k, z, y, cols), c_send.at[k], c_recv.at[k], me.device(core=1 - me.core))

    everything = pl.ds(0, width)
    below = lambda s: (me.z - s >= 0, me.z - s)
    above = lambda s: (me.z + s < DEPTH, me.z + s)

    def start_own(k):
        @pl.when(me.z < DEPTH - 1)
        def _():
            z_copy(k, me.z, 1, True).start()
        @pl.when(me.z > 0)
        def _():
            z_copy(k, me.z, -1, True).start()
        for turn in range(1, span):
            y_copy(k, me.z, turn, True).start()
        core_copy(k, me.z, me.y, everything, True).start()

    def along_z(k, s):
        for (ok, z), step in ((below(s), 1), (above(s), -1)):
            @pl.when(ok)
            def _():
                z_copy(k, z, step, False).wait_recv()
                if s < DEPTH - 1:
                    more = me.z < DEPTH - 1 if step > 0 else me.z > 0
                    @pl.when(more)
                    def _():
                        z_copy(k, z, step, False).start()
                for turn in range(1, span):
                    y_copy(k, z, turn, False).start()
                thin_copy(k, z).start()
                core_copy(k, z, me.y, z_cols).start()

    def across(k, s):
        for ok, z in ((below(s), above(s)) if s else (below(0),)):
            @pl.when(ok)
            def _():
                for turn in range(1, span):
                    y_copy(k, z, turn, False).wait_recv()
                    x_copy(k, z, span - turn).start()
                    core_copy(k, z, lax.rem(me.y + span - turn, span), a_cols).start()

    def beside(k, s):
        for ok, z in ((below(s), above(s)) if s else (below(0),)):
            @pl.when(ok)
            def _():
                for turn in range(1, span):
                    x_copy(k, z, turn).wait_recv()
                    core_copy(k, z, lax.rem(me.y + turn, span), b_cols).start()

    def beside_thin(k, s):
        for ok, z in (below(s), above(s)):
            @pl.when(ok)
            def _():
                thin_copy(k, z).wait_recv()
                core_copy(k, z, me.y, thin_cols).start()

    for k in range(min(lead, chunks)):
        start_own(k)

    last = 2 * (DEPTH - 1) + 3

    def slot(t, carry):
        def stage(delay, work):
            k = t - delay
            @pl.when(jnp.logical_and(k >= 0, k < chunks))
            def _():
                work(k)
        @pl.when(t + lead < chunks)
        def _():
            start_own(t + lead)
        for s in range(1, DEPTH):
            stage(s - 1, functools.partial(along_z, s=s))
        for s in range(DEPTH):
            stage(s + 0, functools.partial(across, s=s))
        for s in range(1, DEPTH):
            stage(s + 0, functools.partial(beside_thin, s=s))
        for s in range(DEPTH):
            stage(s + 1, functools.partial(beside, s=s))
        return carry

    def to_all(make):
        def one(i, carry):
            make(lax.rem(me.place + i, parts)).start()
            return carry
        lax.fori_loop(1, parts, one, 0)

    def wait_all(ref, send, recv):
        others = ref.at[pl.ds(0, parts - 1)]
        every = copy(others, others, send, recv, me.device(core=1 - me.core))
        every.wait_send()
        every.wait_recv()

    to_all(lambda far: copy(note.at[far], notes.at[me.place], n_send, n_recv, (me.group, far)))
    notes[me.place] = note[me.place]
    lax.fori_loop(0, 2, slot, 0)
    wait_all(notes, n_send, n_recv)
    rows_in = notes.shape[1]
    step = 512
    for at_col in range(0, emb.shape[1], step):
        cols = slice(at_col, at_col + step)
        product = jnp.dot(notes[...].reshape(parts * rows_in, 128), emb[:, cols], preferred_element_type=jnp.float32)
        part[:, :, cols] = product.reshape(parts, rows_in, step)[:, :8]
    to_all(lambda far: copy(part.at[far], sums.at[me.place], m_send, m_recv, (me.group, far)))
    sums[me.place] = part[me.place]
    lax.fori_loop(2, chunks + DEPTH, slot, 0)
    local.wait()
    wait_all(sums, m_send, m_recv)
    mod[...] = jnp.sum(sums[...], axis=0)

    def finish(k, carry):
        for step, edge in ((1, me.z < DEPTH - 1), (-1, me.z > 0)):
            for s in range(DEPTH - 1):
                ok, z = below(s) if step > 0 else above(s)
                @pl.when(jnp.logical_and(ok, edge))
                def _():
                    z_copy(k, z, step, False).wait_send()
        for z in range(DEPTH):
            for turn in range(1, span):
                y_copy(k, z, turn, False).wait_send()
                x_copy(k, z, turn).wait_send()
            @pl.when(z != me.z)
            def _():
                thin_copy(k, z).wait_send()
        lane = full.at[pl.ds(0, parts // 2), at(k)]
        whole = copy(lane, lane, c_send.at[k], c_recv.at[k], me.device(core=1 - me.core))
        whole.wait_send()
        whole.wait_recv()
        return carry

    lax.fori_loop(0, chunks, finish, 0)


def gather_all(own, note, emb, replicas, parts, rows=80, lead=3):
    wide = emb.shape[1]
    total, width = own.shape
    chunks = total // rows
    span = parts // (2 * DEPTH)
    dma = lambda *shape: pltpu.SemaphoreType.DMA(shape)
    return pl.pallas_call(
        functools.partial(gather_kernel, replicas, parts, rows, lead),
        out_shape=[
            jax.ShapeDtypeStruct((parts, total, width), own.dtype),
            jax.ShapeDtypeStruct((8, wide), jnp.float32),
            jax.ShapeDtypeStruct(note.shape, note.dtype),
        ],
        in_specs=[pl.BlockSpec(memory_space=pl.ANY)] + [pl.BlockSpec(memory_space=pltpu.VMEM)] * 2,
        out_specs=[pl.BlockSpec(memory_space=pl.ANY)] + [pl.BlockSpec(memory_space=pltpu.VMEM)] * 2,
        scratch_shapes=[
            pltpu.VMEM((parts, 8, wide), jnp.float32),
            pltpu.VMEM((parts, 8, wide), jnp.float32),
            dma(), dma(), dma(), dma(),
            dma(chunks, DEPTH, 2), dma(chunks, DEPTH),
            dma(chunks, DEPTH, span - 1), dma(chunks, DEPTH, span - 1),
            dma(chunks, DEPTH), dma(chunks, DEPTH),
            dma(chunks, DEPTH, span - 1), dma(chunks, DEPTH, span - 1),
            dma(chunks), dma(chunks), pltpu.SemaphoreType.DMA,
        ],
        compiler_params=pltpu.CompilerParams(collective_id=0, has_side_effects=True, vmem_limit_bytes=40 << 20),
        name="gather_all",
    )(own, note, emb)


F32=jnp.float32


class Seat(Where):
    def bit(self, b):
        step = 1 << b
        group = self.group + step - 2 * step * lax.rem(self.group // step, 2)
        return (group, self.place)

    def meet(self, bits, everyone):
        sem = pltpu.get_barrier_semaphore()
        greet = lambda device: pl.semaphore_signal(sem, inc=1, device_id=device, device_id_type=MESH)
        if everyone:
            count = self.replicas * self.parts
            def one(i, carry):
                far = lax.rem(self.group * self.parts + self.place + i, count)
                greet((far // self.parts, lax.rem(far, self.parts)))
                return carry
            lax.fori_loop(1, count, one, 0)
            pl.semaphore_wait(sem, count - 1)
            return


def reduce_kernel(replicas, parts, rows, spans, lead, ring, nrc, lag, ngrad, *refs):
    grads, note, out, notes = refs[:ngrad], refs[ngrad], refs[ngrad + 1], refs[ngrad + 2]
    (hold, rc, xr, yr, zu, zd, fr, tb, l_sem, c_send, c_recv, x_send, x_recv, y_send, y_recv,
     u_send, u_recv, d_send, d_recv, f_send, f_recv, n_send, n_recv, free) = refs[ngrad + 3:]
    me = Seat(replicas, parts)
    span = me.span
    width = out.shape[1]
    chunks = out.shape[0] // rows
    side = me.side
    bits = replicas.bit_length() - 1
    apart, joint = 3 * width // 8, 5 * width // 8

    me.meet(bits, True)

    def copy(src, dst, send, recv, device):
        return pltpu.make_async_remote_copy(src_ref=src, dst_ref=dst, send_sem=send, recv_sem=recv, device_id=device, device_id_type=MESH)

    count = replicas * parts
    mine = me.group * parts + me.place

    def note_copy(far):
        return copy(note.at[lax.rem(far, parts)], notes.at[mine], n_send, n_recv, (far // parts, lax.rem(far, parts)))

    def send_note(i, carry):
        note_copy(lax.rem(mine + i, count)).start()
        return carry

    lax.fori_loop(1, count, send_note, 0)
    own_note = pltpu.make_async_copy(note.at[me.place], notes.at[mine], l_sem.at[ring])
    own_note.start()

    def core_copy(k, src):
        return copy(src, rc.at[lax.rem(k, nrc)], c_send.at[k], c_recv.at[lax.rem(k, nrc)], me.device(core=1 - me.core))

    def begin(k):
        @pl.when(k >= nrc)
        def _():
            pl.semaphore_wait(free, 1)
        for grad, (lo, hi) in zip(grads, spans):
            @pl.when(jnp.logical_and(k >= lo, k < hi))
            def _():
                at = pl.ds(pl.multiple_of((k - lo) * rows, 16), rows)
                slot = lax.rem(k, ring)
                pltpu.make_async_copy(grad.at[:, :, me.core, at, :], hold.at[slot], l_sem.at[slot]).start()
                core_copy(k, grad.at[:, :, 1 - me.core, at, :]).start()

    def x_copy(k, turn):
        slot = lax.rem(k, ring)
        cols = pl.ds(pl.multiple_of((1 - side) * joint, 128), apart)
        return copy(hold.at[slot, :, lax.rem(me.y + turn, span), :, cols], xr.at[k, turn - 1], x_send.at[k, turn - 1], x_recv.at[k, turn - 1], me.bit(0))

    def y_copy(k, turn):
        slot = lax.rem(k, ring)
        cols = pl.ds(pl.multiple_of(side * apart, 128), joint)
        return copy(hold.at[slot, :, lax.rem(me.y + turn, span), :, cols], yr.at[k, turn - 1], y_send.at[k, turn - 1], y_recv.at[k, turn - 1], me.device(y=lax.rem(me.y + turn, span)))

    def up_copy(k, z):
        slot = lax.rem(k, ring)
        return copy(hold.at[slot, z + 1 : DEPTH, me.y], zu.at[k, 0 : DEPTH - 1 - z], u_send.at[k], u_recv.at[k], me.device(z=me.z + 1))

    def down_copy(k, z):
        slot = lax.rem(k, ring)
        return copy(hold.at[slot, 0:z, me.y], zd.at[k, 0:z], d_send.at[k], d_recv.at[k], me.device(z=me.z - 1))

    def f_copy(k, b):
        slot = lax.rem(k, ring)
        src = hold.at[slot, me.z, me.y] if b == 0 else tb.at[b - 1, k]
        return copy(src, fr.at[b, k], f_send.at[b, k], f_recv.at[b, k], me.bit(b))

    def fold_core(k):
        slot = lax.rem(k, ring)
        here = hold.at[slot]
        pltpu.make_async_copy(here, here, l_sem.at[slot]).wait()
        core_copy(k, rc.at[lax.rem(k, nrc)]).wait_recv()
        hold[slot] = hold[slot] + rc[lax.rem(k, nrc)]
        @pl.when(k + nrc < chunks)
        def _():
            pl.semaphore_signal(free, inc=1, device_id=me.device(core=1 - me.core), device_id_type=MESH)
        for turn in range(1, span):
            x_copy(k, turn).start()

    def fold_x(k):
        slot = lax.rem(k, ring)
        for turn in range(1, span):
            x_copy(k, turn).wait_recv()
            y = lax.rem(me.y + turn, span)
            for s in range(2):
                @pl.when(side == s)
                def _():
                    cols = slice(0, apart) if s == 0 else slice(joint, width)
                    hold[slot, :, y, :, cols] = hold[slot, :, y, :, cols] + xr[k, turn - 1]
            y_copy(k, turn).start()

    def fold_y(k):
        slot = lax.rem(k, ring)
        for turn in range(1, span):
            y_copy(k, turn).wait_recv()
            for s in range(2):
                @pl.when(side == s)
                def _():
                    cols = slice(0, joint) if s == 0 else slice(apart, width)
                    hold[slot, :, me.y, :, cols] = hold[slot, :, me.y, :, cols] + yr[k, turn - 1]

    def hop(k, h):
        slot = lax.rem(k, ring)
        @pl.when(me.z == h)
        def _():
            if h > 0:
                up_copy(k, h - 1).wait_recv()
                hold[slot, h:, me.y] = hold[slot, h:, me.y] + zu[k, 0 : DEPTH - h]
            if h < DEPTH - 1:
                up_copy(k, h).start()
        z = DEPTH - 1 - h
        @pl.when(me.z == z)
        def _():
            if h > 0:
                down_copy(k, z + 1).wait_recv()
                hold[slot, : z + 1, me.y] = hold[slot, : z + 1, me.y] + zd[k, 0 : z + 1]
            if h < DEPTH - 1:
                down_copy(k, z).start()

    def finish(k, b):
        slot = lax.rem(k, ring)
        f_copy(k, b).wait_recv()
        before = hold[slot, me.z, me.y] if b == 0 else tb[b - 1, k]
        total = before.astype(F32) + fr[b, k].astype(F32)
        if b == bits - 1:
            out[pl.ds(pl.multiple_of(k * rows, 16), rows), :] = total
        else:
            tb[b, k] = total.astype(BF16)
            f_copy(k, b + 1).start()

    def retire(k):
        core_copy(k, rc.at[0]).wait_send()
        for turn in range(1, span):
            x_copy(k, turn).wait_send()
            y_copy(k, turn).wait_send()
        for z in range(DEPTH):
            @pl.when(me.z == z)
            def _():
                if z < DEPTH - 1:
                    up_copy(k, z).wait_send()
                if z > 0:
                    down_copy(k, z).wait_send()
        for b in range(bits):
            f_copy(k, b).wait_send()

    for k in range(lead):
        begin(jnp.int32(k))

    first_f = (2 + DEPTH) * lag

    def slot_work(t, carry):
        def stage(delay, work):
            k = t - delay
            @pl.when(jnp.logical_and(k >= 0, k < chunks))
            def _():
                work(k)
        for h in range(DEPTH - 1, 0, -1):
            stage((2 + h) * lag, functools.partial(hop, h=h))
        stage((1 + DEPTH) * lag, lambda k: f_copy(k, 0).start())
        def pair(k):
            fold_y(k)
            hop(k, 0)
        stage(2 * lag, pair)
        stage(lag, fold_x)
        stage(0, fold_core)
        for b in range(bits):
            stage(first_f + b * lag, functools.partial(finish, b=b))
        stage(first_f + bits * lag, retire)
        @pl.when(t + lead < chunks)
        def _():
            begin(t + lead)
        return carry

    lax.fori_loop(0, chunks + first_f + bits * lag + 1, slot_work, 0)
    own_note.wait()
    others = notes.at[pl.ds(0, count - 1)]
    every = copy(others, others, n_send, n_recv, me.device(core=1 - me.core))
    every.wait_send()
    every.wait_recv()


def reduce_all(grads, note, replicas, parts, rows, lead=2, nrc=3, lag=2):
    span = parts // (2 * DEPTH)
    width = grads[0].shape[1]
    spans, at = [], 0
    views = []
    for grad in grads:
        size = grad.shape[0] // parts
        spans.append((at // rows, (at + size) // rows))
        at += size
        views.append(grad.reshape(DEPTH, span, 2, size, width))
    total = at
    chunks = total // rows
    bits = replicas.bit_length() - 1
    ring = lead + (2 + DEPTH + bits) * lag + 2
    dma = lambda *shape: pltpu.SemaphoreType.DMA(shape)
    vm = lambda *shape: pltpu.VMEM(shape, BF16)
    return pl.pallas_call(
        functools.partial(reduce_kernel, replicas, parts, rows, spans, lead, ring, nrc, lag, len(grads)),
        out_shape=[jax.ShapeDtypeStruct((total, width), F32), jax.ShapeDtypeStruct((replicas * parts,) + note.shape[1:], note.dtype)],
        in_specs=[pl.BlockSpec(memory_space=pl.ANY)] * (len(grads) + 1),
        out_specs=[pl.BlockSpec(memory_space=pltpu.VMEM), pl.BlockSpec(memory_space=pl.ANY)],
        scratch_shapes=[
            vm(ring, DEPTH, span, rows, width),
            vm(nrc, DEPTH, span, rows, width),
            vm(chunks, span - 1, DEPTH, rows, 3 * width // 8),
            vm(chunks, span - 1, DEPTH, rows, 5 * width // 8),
            vm(chunks, DEPTH - 1, rows, width),
            vm(chunks, DEPTH - 1, rows, width),
            vm(bits, chunks, rows, width),
            vm(max(bits - 1, 1), chunks if bits > 1 else 1, rows, width),
            dma(ring + 1),
            dma(chunks), dma(nrc),
            dma(chunks, span - 1), dma(chunks, span - 1),
            dma(chunks, span - 1), dma(chunks, span - 1),
            dma(chunks), dma(chunks), dma(chunks), dma(chunks),
            dma(bits, chunks), dma(bits, chunks),
            pltpu.SemaphoreType.DMA, pltpu.SemaphoreType.DMA,
            pltpu.SemaphoreType.REGULAR,
        ],
        compiler_params=pltpu.CompilerParams(collective_id=1, has_side_effects=True, vmem_limit_bytes=60 << 20),
        name="reduce_all",
    )(*views, note)


HEADS = 8
HEAD = 64
GROUPS = 32
UNIT = 4
SHAPES = ((4 * UNIT, 4 * UNIT), (3 * UNIT, 5 * UNIT), (5 * UNIT, 3 * UNIT))
SIZES = tuple(height * breadth for height, breadth in SHAPES)
STARTS = (0, SIZES[0], SIZES[0] + SIZES[1])


def dot(left, right, dims=((1,), (0,))):
    return lax.dot_general(left, right, (dims, ((), ())), preferred_element_type=F32)


def images(rows):
    return [rows[start : start + size] for start, size in zip(STARTS, SIZES)]


def group_mean(column_sums, count):
    channels = column_sums.shape[-1]
    width = channels // GROUPS
    totals = jnp.sum(column_sums.reshape(GROUPS, width), axis=1, keepdims=True) / (count * width)
    return jnp.broadcast_to(totals, (GROUPS, width)).reshape(1, channels)


def normalise(rows):
    count = rows.shape[0]
    centered = rows - group_mean(jnp.sum(rows, axis=0), count)
    spread = group_mean(jnp.sum(jnp.square(centered), axis=0), count)
    inverse = lax.rsqrt(spread + 1e-05)
    return centered * inverse, inverse


def norm_back(grad, hat, inverse, factor):
    count = grad.shape[0]
    plain = jnp.sum(grad, axis=0)
    crossed = jnp.sum(grad * hat, axis=0)
    mean_plain = group_mean(plain * factor, count)
    mean_crossed = group_mean(crossed * factor, count)
    return inverse * (grad * factor[None, :] - mean_plain - hat * mean_crossed), plain, crossed


def silu_slope(value):
    gate = jax.nn.sigmoid(value)
    return gate * (1.0 + value * (1.0 - gate))


def patches(rows, flip=False):
    channels = rows.shape[-1]
    parts = []
    for (height, breadth), picture in zip(SHAPES, images(rows)):
        padded = jnp.pad(picture.reshape(height, breadth, channels), ((1, 1), (1, 1), (0, 0)))
        windows = [
            padded[down : down + height, across : across + breadth]
            for down in range(3)
            for across in range(3)
        ]
        if flip:
            windows = windows[::-1]
        parts.append(jnp.concatenate(windows, axis=-1).reshape(height * breadth, 9 * channels))
    return jnp.concatenate(parts, 0)


TEXT_PAD = 128


def attention_kernel(q_ref, k_ref, v_ref, tk_ref, tv_ref, mask_ref, go_ref, o_ref, dq_ref, dk_ref, dv_ref, dtk_ref, dtv_ref):
    lane = lax.broadcasted_iota(jnp.int32, (1, 2 * HEAD), 1)
    for image in range(3):
        rows = pl.ds(STARTS[image], SIZES[image])
        size = SIZES[image]
        q, k, v, go = q_ref[rows, :], k_ref[rows, :], v_ref[rows, :], go_ref[rows, :]
        tk, tv = tk_ref[image], tv_ref[image]
        mask = mask_ref[image : image + 1, :]
        results = []
        for head in range(2):
            mine = (lane >= HEAD) if head else (lane < HEAD)
            qh = jnp.where(mine, q, jnp.zeros_like(q))
            gh = jnp.where(mine, go, jnp.zeros_like(go))
            scale = HEAD ** -0.5
            nt = ((1,), (1,))
            tn = ((0,), (0,))
            sp = dot(qh, k, nt) * scale
            st = dot(qh, tk, nt) * scale
            st = jnp.where(mask == 1, st, jnp.where(mask == 0, -1000000000.0, -jnp.inf))
            peak = jnp.maximum(
                jnp.max(sp, axis=1, keepdims=True), jnp.max(st, axis=1, keepdims=True)
            )
            ep, et = jnp.exp(sp - peak), jnp.exp(st - peak)
            total = jnp.sum(ep, axis=1, keepdims=True) + jnp.sum(et, axis=1, keepdims=True)
            inv = 1.0 / total
            pp, pt = ep * inv, et * inv
            ppl, ptl = pp.astype(BF16), pt.astype(BF16)
            out = dot(ppl, v) + dot(ptl, tv)
            dv = dot(ppl, go, tn)
            dtv = dot(ptl, go, tn)
            dpp = dot(gh, v, nt)
            dpt = dot(gh, tv, nt)
            inner = jnp.sum(dpp * pp, axis=1, keepdims=True) + jnp.sum(
                dpt * pt, axis=1, keepdims=True
            )
            dsp = (pp * (dpp - inner) * scale).astype(BF16)
            dst = (pt * (dpt - inner) * scale).astype(BF16)
            dq = dot(dsp, k) + dot(dst, tk)
            dk = dot(dsp, q, tn)
            dtk = dot(dst, q, tn)
            results.append((out, dq, dk, dv, dtk, dtv))
        first, second = results
        low = lane < HEAD
        merged = [jnp.where(low, a, b).astype(BF16) for a, b in zip(first, second)]
        o_ref[rows, :] = merged[0]
        dq_ref[rows, :] = merged[1]
        dk_ref[rows, :] = merged[2]
        dv_ref[rows, :] = merged[3]
        dtk_ref[image] = merged[4]
        dtv_ref[image] = merged[5]


def attention(triple, text_pair, mask, grad_attended):
    rows, inner = triple.shape[0], triple.shape[1] // 3
    pairs = inner // (2 * HEAD)
    col = lambda shift: pl.BlockSpec((rows, 2 * HEAD), lambda h: (0, h + shift * pairs))
    txt = lambda shift: pl.BlockSpec((3, TEXT_PAD, 2 * HEAD), lambda h: (0, 0, h + shift * pairs))
    wide = jax.ShapeDtypeStruct((rows, inner), BF16)
    wide_text = jax.ShapeDtypeStruct((3, TEXT_PAD, inner), BF16)
    return pl.pallas_call(
        attention_kernel,
        grid=(pairs,),
        in_specs=[
            col(0),
            col(1),
            col(2),
            txt(0),
            txt(1),
            pl.BlockSpec((3, TEXT_PAD), lambda h: (0, 0)),
            col(0),
        ],
        out_specs=[col(0)] * 4 + [txt(0)] * 2,
        out_shape=[wide] * 4 + [wide_text] * 2,
        compiler_params=pltpu.CompilerParams(vmem_limit_bytes=40 << 20),
    )(triple, triple, triple, text_pair, text_pair, mask, grad_attended)


def body(
    pixels,
    embedding,
    text_states,
    text_mask,
    occupancy,
    cotangent,
    in_gain,
    in_shift,
    conv_first,
    first_bias,
    emb_weight,
    emb_bias,
    mid_gain,
    mid_shift,
    conv_second,
    second_bias,
    skip_weight,
    skip_bias,
    attn_gain,
    attn_shift,
    attend_weight,
    text_weight,
    out_weight,
    out_bias,
):
    place = lax.axis_index("fsdp")
    group = lax.axis_index("dp")
    parts = lax.axis_size("fsdp")
    replicas = lax.axis_size("dp")
    depth = emb_weight.shape[0]
    images_here = embedding.shape[0]
    emb_act = jax.nn.silu(embedding.astype(F32)).astype(BF16)
    emb_cut = emb_act.reshape(images_here, parts, depth).transpose(1, 0, 2)
    emb_cut = jnp.pad(emb_cut, ((0, 0), (0, 0), (0, 128 - depth)))

    vectors = (in_gain, in_shift, first_bias, emb_bias, mid_gain, mid_shift, second_bias, skip_bias, attn_gain, attn_shift, out_bias)
    flat = jnp.concatenate(vectors)
    room = 16 - images_here
    flat = jnp.pad(flat, (0, room * 128 - flat.shape[0])).reshape(1, room, 128)
    note = jnp.concatenate([emb_cut, jnp.broadcast_to(flat, (parts, room, 128))], 1)
    small = jnp.concatenate([skip_weight, out_weight, attend_weight.reshape(-1, skip_weight.shape[1])], 0)
    own = jnp.concatenate([conv_first, conv_second, text_weight, small], 0)
    full, modulation, notes = gather_all(own, note, jnp.pad(emb_weight, ((0, 128 - depth), (0, 0))), replicas, parts)
    packed = notes[:, images_here:].reshape(parts, -1).astype(F32)
    whole = []
    at = 0
    for vector in vectors:
        whole.append(packed[:, at : at + vector.shape[0]].reshape(-1))
        at += vector.shape[0]
    (in_gain, in_shift, first_bias, emb_bias, mid_gain, mid_shift, second_bias, skip_bias, attn_gain, attn_shift, out_bias) = whole
    modulation = modulation[:images_here] + emb_bias

    cuts = []
    at = 0
    for part in (conv_first, conv_second, text_weight, skip_weight, out_weight):
        size = part.shape[0]
        cuts.append(full[:, at : at + size].reshape(parts * size, -1))
        at += size
    attend_width = attend_weight.shape[1]
    attend_weight = full[:, at:].reshape(-1, attend_width)
    conv_first, conv_second, text_weight, skip_weight, out_weight = cuts
    channels = conv_first.shape[1]
    inner = out_weight.shape[0]
    scale, shift = modulation[:, :channels], modulation[:, channels:]

    pixel_hat = [normalise(part.astype(F32)) for part in images(pixels)]
    first_pre = [hat * in_gain + in_shift for hat, _ in pixel_hat]
    first_act = jnp.concatenate([jax.nn.silu(part) for part in first_pre], 0).astype(BF16)
    first_patches = patches(first_act)
    first_conv = dot(first_patches, conv_first) + first_bias
    mid_hat = [normalise(part) for part in images(first_conv)]
    mid_pre = [
        (hat * mid_gain + mid_shift) * (1.0 + scale[i]) + shift[i]
        for i, (hat, _) in enumerate(mid_hat)
    ]
    second_act = jnp.concatenate([jax.nn.silu(part) for part in mid_pre], 0).astype(BF16)
    second_patches = patches(second_act)
    residual = dot(pixels, skip_weight) + dot(second_patches, conv_second) + (skip_bias + second_bias)
    attn_hat = [normalise(part) for part in images(residual)]
    normed = jnp.concatenate([hat * attn_gain + attn_shift for hat, _ in attn_hat], 0).astype(BF16)
    triple = dot(normed, attend_weight).astype(BF16)
    text_len = text_states.shape[1]
    text_rows = text_states.reshape(3 * text_len, -1)
    text_pair = dot(text_rows, text_weight).astype(BF16).reshape(3, text_len, -1)
    text_pair = jnp.pad(text_pair, ((0, 0), (0, TEXT_PAD - text_len), (0, 0)))
    mask = jnp.pad(
        (text_mask > 0).astype(jnp.int32), ((0, 0), (0, TEXT_PAD - text_len)), constant_values=2
    )
    present = jnp.concatenate(
        [jnp.broadcast_to(occupancy[0, i].astype(F32), (SIZES[i], 1)) for i in range(3)], 0
    )
    grad_out = cotangent.astype(F32) * present
    grad_low = grad_out.astype(BF16)
    grad_attended = dot(grad_low, out_weight, ((1,), (1,))).astype(BF16)
    attended, dq, dk, dv, dtk, dtv = attention(triple, text_pair, mask, grad_attended)
    block_output = (present * (residual + (dot(attended, out_weight) + out_bias))).astype(BF16)

    tn = ((0,), (0,))
    nt = ((1,), (1,))
    grad_out_bias = jnp.sum(grad_out, axis=0)
    grad_out_weight = dot(attended, grad_low, tn)
    grad_triple = jnp.concatenate([dq, dk, dv], 1)
    grad_text = jnp.concatenate([dtk, dtv], 2)[:, :text_len].reshape(3 * text_len, -1)
    grad_attend_weight = dot(normed, grad_triple, tn)
    grad_text_weight = dot(text_rows, grad_text, tn)
    grad_normed = dot(grad_triple, attend_weight, nt)
    backs = [
        norm_back(part, hat, inverse, attn_gain)
        for part, (hat, inverse) in zip(images(grad_normed), attn_hat)
    ]
    grad_attn_shift = sum(back[1] for back in backs)
    grad_attn_gain = sum(back[2] for back in backs)
    grad_residual = jnp.concatenate([back[0] for back in backs], 0) + grad_out
    grad_second_bias = jnp.sum(grad_residual, axis=0)
    res_low = grad_residual.astype(BF16)
    grad_skip_weight = dot(pixels, res_low, tn)
    grad_conv_second = dot(second_patches, res_low, tn)
    res_patches = patches(res_low, flip=True).reshape(-1, 9, channels)
    grad_second_act = lax.dot_general(
        res_patches,
        conv_second.reshape(9, channels, channels),
        (((1, 2), (0, 2)), ((), ())),
        preferred_element_type=F32,
    )
    backs = []
    grad_mod = []
    for i, part in enumerate(images(grad_second_act)):
        hat, inverse = mid_hat[i]
        grad_pre = part * silu_slope(mid_pre[i])
        factor = 1.0 + scale[i]
        rows, plain, crossed = norm_back(grad_pre, hat, inverse, factor * mid_gain)
        grad_mod.append(jnp.concatenate([crossed * mid_gain + plain * mid_shift, plain]))
        backs.append((rows, plain * factor, crossed * factor))
    grad_mid_shift = sum(back[1] for back in backs)
    grad_mid_gain = sum(back[2] for back in backs)
    grad_first_conv = jnp.concatenate([back[0] for back in backs], 0)
    grad_first_bias = jnp.sum(grad_first_conv, axis=0)
    conv_low = grad_first_conv.astype(BF16)
    grad_conv_first = dot(first_patches, conv_low, tn)
    first_width = pixels.shape[1]
    conv_patches = patches(conv_low, flip=True).reshape(-1, 9, channels)
    grad_first_act = lax.dot_general(
        conv_patches,
        conv_first.reshape(9, first_width, channels),
        (((1, 2), (0, 2)), ((), ())),
        preferred_element_type=F32,
    )
    backs = [
        norm_back(part * silu_slope(pre), hat, inverse, in_gain)
        for part, pre, (hat, inverse) in zip(images(grad_first_act), first_pre, pixel_hat)
    ]
    grad_in_shift = sum(back[1] for back in backs)
    grad_in_gain = sum(back[2] for back in backs)
    grad_pixels = jnp.concatenate([back[0] for back in backs], 0) + dot(res_low, skip_weight, nt)

    small = (grad_in_gain, grad_in_shift, grad_first_bias, grad_mid_gain, grad_mid_shift, grad_second_bias, grad_attn_gain, grad_attn_shift, grad_out_bias)
    cut = jnp.concatenate([vector.reshape(parts, -1) for vector in small], 1)
    mod_rows = jnp.stack(grad_mod).reshape(1, -1, 128)
    mod_count = mod_rows.shape[1]
    room = 64 - mod_count - images_here
    cut = jnp.pad(cut, ((0, 0), (0, room * 128 - cut.shape[1]))).reshape(parts, room, 128)
    note = jnp.concatenate(
        [jnp.broadcast_to(mod_rows, (parts,) + mod_rows.shape[1:]).astype(BF16), emb_cut, cut.astype(BF16)], 1
    )
    pack = lambda part: part.reshape(parts, -1, channels)
    grad_small = jnp.concatenate(
        [pack(grad_skip_weight), pack(grad_out_weight), pack(grad_attend_weight)], 1
    ).astype(BF16).reshape(-1, channels)
    owned, notes = reduce_all(
        [grad_conv_first.astype(BF16), grad_conv_second.astype(BF16), grad_text_weight.astype(BF16), grad_small],
        note, replicas, parts, 512 // parts,
    )
    at = 0
    cuts = []
    for size in (conv_first.shape[0], conv_second.shape[0], text_weight.shape[0], skip_weight.shape[0], out_weight.shape[0]):
        cuts.append(owned[at : at + size // parts])
        at += size // parts
    grad_conv_first, grad_conv_second, grad_text_weight, grad_skip_weight, grad_out_weight = cuts
    grad_attend_weight = owned[at:].reshape(-1, attend_width)
    mod_rows = notes[:, :mod_count].reshape(-1, 2 * channels)
    all_act = notes[:, mod_count : mod_count + images_here, :depth].reshape(-1, depth)
    grad_emb_weight = dot(all_act, mod_rows, tn)
    grad_emb_bias = jnp.sum(mod_rows.astype(F32), axis=0)
    grad_emb_bias = lax.dynamic_slice_in_dim(grad_emb_bias, place * depth, depth, 0)
    packed = jnp.sum(notes[:, mod_count + images_here :].astype(F32), axis=0).reshape(-1)
    owned = []
    at = 0
    for vector in small:
        size = vector.shape[0] // parts
        owned.append(packed[at : at + size])
        at += size
    (grad_in_gain, grad_in_shift, grad_first_bias, grad_mid_gain, grad_mid_shift, grad_second_bias, grad_attn_gain, grad_attn_shift, grad_out_bias) = owned

    return (
        block_output,
        grad_pixels,
        grad_in_gain,
        grad_in_shift,
        grad_conv_first,
        grad_first_bias,
        grad_emb_weight,
        grad_emb_bias,
        grad_mid_gain,
        grad_mid_shift,
        grad_conv_second,
        grad_second_bias,
        grad_skip_weight,
        grad_second_bias,
        grad_attn_gain,
        grad_attn_shift,
        grad_attend_weight,
        grad_text_weight,
        grad_out_weight,
        grad_out_bias,
    )


def solution(mesh):
    rows = P(("dp", "fsdp"), None)
    vector = P("fsdp")
    matrix = P("fsdp", None)
    weights = (vector, vector, matrix, vector, matrix, vector, vector, vector, matrix, vector, matrix, vector, vector, vector, matrix, matrix, matrix, vector)
    return jax.shard_map(
        body,
        mesh=mesh,
        in_specs=(rows, rows, P(("dp", "fsdp"), None, None), rows, rows, rows) + weights,
        out_specs=(rows, rows) + weights,
        check_vma=False,
    )
```

```python
import functools

import jax
import jax.numpy as jnp
from jax import lax
from jax.experimental import pallas as pl
from jax.experimental.pallas import tpu as pltpu
from jax.sharding import PartitionSpec as P

BF16 = jnp.bfloat16
F32 = jnp.float32
HEADS = 8
HEAD = 64
GROUPS = 32
UNIT = 4
SHAPES = ((4 * UNIT, 4 * UNIT), (3 * UNIT, 5 * UNIT), (5 * UNIT, 3 * UNIT))
SIZES = tuple(height * breadth for height, breadth in SHAPES)
STARTS = (0, SIZES[0], SIZES[0] + SIZES[1])
PIX = sum(SIZES)
EDGE = 32
BASES = tuple(EDGE + start + i * EDGE for i, start in enumerate(STARTS))
PADDED = PIX + 4 * EDGE
BLOCK = 1152
TEXT_PAD = 128
TEXT_ROWS = 80
SUB = 16
NT = (((1,), (1,)), ((), ()))
TN = (((0,), (0,)), ((), ()))
V_IN_GAIN, V_IN_SHIFT, V_FIRST, V_EMB, V_MID_GAIN, V_MID_SHIFT, V_SECOND, V_SKIP, V_ATTN_GAIN, V_ATTN_SHIFT, V_OUT = range(11)


def dot(left, right, dims=((1,), (0,))):
    return lax.dot_general(left, right, (dims, ((), ())), preferred_element_type=F32)


def group_mean(sums, count):
    channels = sums.shape[1]
    width = channels // GROUPS
    lane = lax.broadcasted_iota(jnp.int32, sums.shape, 1)
    step = 1
    while step < width:
        odd = lax.rem(lane // step, 2) == 1
        sums = sums + jnp.where(odd, pltpu.roll(sums, step, 1), pltpu.roll(sums, channels - step, 1))
        step *= 2
    return sums / (count * width)


def rows_of(image, i):
    return pl.ds(pl.multiple_of(STARTS[image] + i * SUB, SUB), SUB)


def over_rows(image, work, start):
    return lax.fori_loop(0, SIZES[image] // SUB, lambda i, carry: work(i, rows_of(image, i), carry), start)


def column_sum(image, channels, value):
    def add(i, rows, carry):
        v = value(rows)
        return carry + (v[:8] + v[8:])
    total = over_rows(image, add, jnp.zeros((8, channels), F32))
    return jnp.broadcast_to(jnp.sum(total, axis=0, keepdims=True), (8, channels))


def norm_figures(image, channels, value):
    count = SIZES[image]
    center = group_mean(column_sum(image, channels, value), count)[:1]
    spread = group_mean(column_sum(image, channels, lambda rows: jnp.square(value(rows) - center)), count)[:1]
    return center, lax.rsqrt(spread + 1e-05)


def store_padded(pad, image, i, act):
    breadth = SHAPES[image][1]
    at = pl.ds(pl.multiple_of(BASES[image] + i * SUB, SUB), SUB)
    column = lax.rem(i * SUB + lax.broadcasted_iota(jnp.int32, (SUB, 1), 0), breadth)
    pad[0, at, :] = jnp.where(column == breadth - 1, 0.0, act).astype(BF16)
    pad[1, at, :] = act.astype(BF16)
    pad[2, at, :] = jnp.where(column == 0, 0.0, act).astype(BF16)


def zero_edges(pad):
    zeros = jnp.zeros((EDGE, pad.shape[2]), BF16)
    for side in range(3):
        for at in [base - EDGE for base in BASES] + [PADDED - EDGE]:
            pad[side, at : at + EDGE, :] = zeros


def shifted(pad, tap, image, cols, flip=False):
    down, across = divmod(8 - tap if flip else tap, 3)
    start = BASES[image] + (down - 1) * SHAPES[image][1] + across - 1
    return pad[across, start : start + SIZES[image], cols]


def gather_block(pad, q, out):
    channels = pad.shape[2]
    for tap in range(9):
        low, high = max(q * BLOCK, tap * channels), min((q + 1) * BLOCK, (tap + 1) * channels)
        if low < high:
            for image in range(3):
                out[STARTS[image] : STARTS[image] + SIZES[image], low - q * BLOCK : high - q * BLOCK] = shifted(
                    pad, tap, image, slice(low - tap * channels, high - tap * channels)
                )


class Rows:
    def __init__(self, parts, pix_channels, channels, text_dim, inner):
        self.parts = parts
        sizes = (9 * pix_channels // parts, 9 * channels // parts, pix_channels // parts, inner // parts, channels // parts, channels // parts // 2, text_dim // parts)
        starts = [0]
        for size in sizes:
            starts.append(starts[-1] + size)
        self.first, self.second, self.skip, self.out, self.attend, self.attend_more, self.text = zip(starts, sizes)
        self.total = starts[-1]

    def load(self, full, which, q, rows, buf, sem):
        start, size = which
        each = rows // size
        for i in range(each):
            pltpu.make_async_copy(full.at[q * each + i, pl.ds(start, size)], buf.at[pl.ds(i * size, size)], sem).start()

    def load_attend(self, full, buf, sem):
        start, size = self.attend
        more, half = self.attend_more
        def one(f, carry):
            at = pl.multiple_of(f * size, SUB)
            pltpu.make_async_copy(full.at[f, pl.ds(start, size)], buf.at[pl.ds(at, size), pl.ds(0, 1024)], sem).start()
            for i in range(2):
                pltpu.make_async_copy(
                    full.at[f, pl.ds(more, half), pl.ds(512 * i, 512)],
                    buf.at[pl.ds(pl.multiple_of(at + i * half, SUB), half), pl.ds(1024, 512)],
                    sem,
                ).start()
            return carry
        lax.fori_loop(0, self.parts, one, 0)


def waited(ref, sem):
    pltpu.make_async_copy(ref, ref, sem).wait()


class Forward:
    def __init__(self, rows, full, pixels, text, g_low, vec, mod, outs, scratch):
        self.rows, self.full, self.pixels, self.text, self.g_low, self.vec, self.mod = rows, full, pixels, text, g_low, vec, mod
        (self.o_a1, self.o_a2, self.o_mid_hat, self.o_residual, self.o_hat, self.o_normed, self.triple, self.text_pair, self.grad_attended, self.inverses) = outs
        (self.a1, self.a2, self.patch, self.weight, self.acc0, self.acc1, self.normed, self.w_attend, self.w_skip, self.w_out, self.w_sem, self.s_sem, self.o_sem) = scratch

    def out_copy(self, i, src, dst):
        return pltpu.make_async_copy(src, dst, self.o_sem.at[i])

    def row(self, r, channels=1024):
        return self.vec[r : r + 1, :channels]

    def zero(self):
        zero_edges(self.a1)
        zero_edges(self.a2)

    def first_norm(self, image):
        pixels, channels = self.pixels, self.pixels.shape[1]
        value = lambda rows: pixels[rows, :].astype(F32)
        center, inverse = norm_figures(image, channels, value)
        gain, shift = self.row(V_IN_GAIN, channels) * inverse, self.row(V_IN_SHIFT, channels)
        self.inverses[image : image + 1, :channels] = inverse
        self.inverses[16 + image : 17 + image, :channels] = center
        def act(i, rows, carry):
            store_padded(self.a1, image, i, jax.nn.silu((value(rows) - center) * gain + shift))
            return carry
        over_rows(image, act, 0)
        if image == 2:
            self.out_copy(0, self.a1, self.o_a1).start()

    def load_first(self, q):
        self.rows.load(self.full, self.rows.first, q, BLOCK, self.weight.at[lax.rem(q, 2)], self.w_sem.at[lax.rem(q, 2)])

    def load_second(self, q):
        self.rows.load(self.full, self.rows.second, q, BLOCK, self.weight.at[lax.rem(q, 2)], self.w_sem.at[lax.rem(q, 2)])

    def load_text(self, q):
        self.rows.load(self.full, self.rows.text, q, 1024, self.weight.at[lax.rem(q, 2)], self.w_sem.at[lax.rem(q, 2)])

    def conv_step(self, q, pad, acc, load, count, start):
        @pl.when(q + 1 < count)
        def _():
            load(q + 1)
        for known in range(count):
            @pl.when(q == known)
            def _():
                gather_block(pad, known, self.patch)
        par = lax.rem(q, 2)
        waited(self.weight.at[par], self.w_sem.at[par])
        @pl.when(q == 0)
        def _():
            start()
        for col in (0, 512):
            cols = slice(col, col + 512)
            acc[:, cols] = acc[:, cols] + dot(self.patch[...], self.weight[par, :, cols])

    def first_conv(self, q):
        def start():
            self.acc0[...] = jnp.zeros_like(self.acc0)
        self.conv_step(q, self.a1, self.acc0, self.load_first, 9 * self.pixels.shape[1] // BLOCK, start)

    def mid_norm(self, image):
        acc, channels = self.acc0, self.acc0.shape[1]
        bias = self.row(V_FIRST)
        def shift_up(i, rows, carry):
            acc[rows, :] = acc[rows, :] + bias
            return carry
        over_rows(image, shift_up, 0)
        center, inverse = norm_figures(image, channels, lambda rows: acc[rows, :])
        self.inverses[3 + image : 4 + image, :] = inverse
        scale, shift = 1.0 + self.mod[image : image + 1, :channels], self.mod[image : image + 1, channels:]
        gain, lift = self.row(V_MID_GAIN) * scale, self.row(V_MID_SHIFT) * scale + shift
        def act(i, rows, carry):
            hat = (acc[rows, :] - center) * inverse
            acc[rows, :] = hat
            store_padded(self.a2, image, i, jax.nn.silu(hat * gain + lift))
            return carry
        over_rows(image, act, 0)
        if image == 2:
            self.out_copy(1, self.a2, self.o_a2).start()
            self.out_copy(2, self.acc0, self.o_mid_hat).start()

    def load_small(self):
        rows = self.rows
        def one(f, carry):
            for i, ((start, size), buf) in enumerate(((rows.skip, self.w_skip), (rows.out, self.w_out))):
                pltpu.make_async_copy(self.full.at[f, pl.ds(start, size)], buf.at[pl.ds(pl.multiple_of(f * size, SUB), size)], self.s_sem.at[i]).start()
            return carry
        lax.fori_loop(0, rows.parts, one, 0)
        rows.load_attend(self.full, self.w_attend, self.s_sem.at[2])

    def skip_product(self):
        for i, buf in enumerate((self.w_skip, self.w_out, self.w_attend)):
            waited(buf, self.s_sem.at[i])
        self.acc1[...] = self.acc1[...] + dot(self.pixels[...], self.w_skip[...])

    def attended_grad(self):
        self.grad_attended[...] = lax.dot_general(self.g_low[...], self.w_out[...], NT, preferred_element_type=F32).astype(BF16)

    def second_conv(self, q):
        def start():
            self.acc1[...] = jnp.zeros_like(self.acc1)
        self.conv_step(q, self.a2, self.acc1, self.load_second, 9 * self.acc1.shape[1] // BLOCK, start)

    def last_norm(self, image):
        acc, hats, channels = self.acc1, self.acc0, self.acc1.shape[1]
        if image == 0:
            self.out_copy(2, self.acc0, self.o_mid_hat).wait()
        bias = self.row(V_SECOND) + self.row(V_SKIP)
        def shift_up(i, rows, carry):
            acc[rows, :] = acc[rows, :] + bias
            return carry
        over_rows(image, shift_up, 0)
        center, inverse = norm_figures(image, channels, lambda rows: acc[rows, :])
        self.inverses[6 + image : 7 + image, :] = inverse
        gain, shift = self.row(V_ATTN_GAIN), self.row(V_ATTN_SHIFT)
        def act(i, rows, carry):
            hat = (acc[rows, :] - center) * inverse
            hats[rows, :] = hat
            self.normed[rows, :] = (hat * gain + shift).astype(BF16)
            return carry
        over_rows(image, act, 0)
        if image == 2:
            self.out_copy(3, self.acc1, self.o_residual).start()
            self.out_copy(4, self.acc0, self.o_hat).start()
            self.out_copy(5, self.normed, self.o_normed).start()

    def project(self, i):
        cols = slice(512 * i, 512 * (i + 1))
        self.triple[:, cols] = dot(self.normed[...], self.w_attend[:, cols]).astype(BF16)

    def text_step(self, q, total):
        if q + 1 < 4:
            self.load_text(q + 1)
        par = q % 2
        waited(self.weight.at[par, pl.ds(0, 1024)], self.w_sem.at[par])
        part = dot(self.text[:, 1024 * q : 1024 * (q + 1)], self.weight[par, :1024, :])
        if q:
            part = total[...] + part
        if q < 3:
            total[...] = part
        else:
            self.text_pair[...] = jnp.zeros_like(self.text_pair)
            for image in range(3):
                self.text_pair[image, :TEXT_ROWS, :] = part[TEXT_ROWS * image : TEXT_ROWS * (image + 1)].astype(BF16)

    def finish(self):
        self.out_copy(0, self.a1, self.o_a1).wait()
        self.out_copy(1, self.a2, self.o_a2).wait()
        self.out_copy(3, self.acc1, self.o_residual).wait()
        self.out_copy(4, self.acc0, self.o_hat).wait()
        self.out_copy(5, self.normed, self.o_normed).wait()


MESH = pl.DeviceIdType.MESH
DEPTH = 4


class Where:
    def __init__(self, replicas, parts):
        self.replicas, self.parts = replicas, parts
        self.span = parts // (2 * DEPTH)
        self.group = lax.axis_index("dp")
        self.place = lax.axis_index("fsdp")
        self.core = lax.rem(self.place, 2)
        self.y = lax.rem(self.place // 2, self.span)
        self.z = self.place // (2 * self.span)
        self.side = lax.rem(self.group, 2)

    def index(self, z, y, core):
        return (z * self.span + y) * 2 + core

    def device(self, z=None, y=None, core=None, flip=False):
        z = self.z if z is None else z
        y = self.y if y is None else y
        core = self.core if core is None else core
        group = self.group + 1 - 2 * self.side if flip else self.group
        return (group, self.index(z, y, core))

    def barrier(self):
        sem = pltpu.get_barrier_semaphore()
        greet = lambda device: pl.semaphore_signal(sem, inc=1, device_id=device, device_id_type=MESH)
        greet(self.device(flip=True))
        def one(i, carry):
            greet((self.group, lax.rem(self.place + i, self.parts)))
            return carry
        lax.fori_loop(1, self.parts, one, 0)
        pl.semaphore_wait(sem, self.parts)


def forward_kernel(replicas, parts, rows, lead, inner, images, *refs):
    own, note, emb, pixels, text, g_low = refs[:6]
    full, mod, vec, notes = refs[6:10]
    outs = refs[10:20]
    part, sums, text_total = refs[20:23]
    scratch = refs[23:36]
    (n_send, n_recv, m_send, m_recv, z_send, z_recv, y_send, y_recv, s_send, s_recv, x_send, x_recv, c_send, c_recv, own_sem) = refs[36:]
    me = Where(replicas, parts)
    span = me.span
    total, width = own.shape
    chunks = total // rows
    half = width // 2
    side = me.side
    thin = 128
    z_cols = pl.ds(pl.multiple_of(side * thin, thin), width - thin)
    a_cols = pl.ds(pl.multiple_of(side * half, half), half)
    thin_cols = pl.ds(pl.multiple_of((1 - side) * (width - thin), thin), thin)
    thin_out = pl.ds(pl.multiple_of(side * (width - thin), thin), thin)
    b_cols = pl.ds(pl.multiple_of((1 - side) * half, half), half)

    me.barrier()
    local = pltpu.make_async_copy(own, full.at[me.place], own_sem)
    local.start()

    def at(k):
        return pl.ds(pl.multiple_of(k * rows, 16), rows)

    def copy(src, dst, send, recv, device):
        return pltpu.make_async_remote_copy(src_ref=src, dst_ref=dst, send_sem=send, recv_sem=recv, device_id=device, device_id_type=MESH)

    def piece(k, z, y, cols, core=None):
        return full.at[me.index(z, y, me.core if core is None else core), at(k), cols]

    def z_copy(k, z, step, mine):
        src = own.at[at(k), z_cols] if mine else piece(k, z, me.y, z_cols)
        return copy(src, piece(k, z, me.y, z_cols), z_send.at[k, z, (step + 1) // 2], z_recv.at[k, z], me.device(z=me.z + step))

    def y_copy(k, z, turn, mine):
        src = own.at[at(k), a_cols] if mine else piece(k, z, me.y, a_cols)
        return copy(src, piece(k, z, me.y, a_cols), y_send.at[k, z, turn - 1], y_recv.at[k, z, turn - 1], me.device(y=lax.rem(me.y + turn, span)))

    def thin_copy(k, z):
        return copy(piece(k, z, me.y, thin_out), piece(k, z, me.y, thin_out), s_send.at[k, z], s_recv.at[k, z], me.device(flip=True))

    def x_copy(k, z, turn):
        y = lax.rem(me.y + turn, span)
        return copy(piece(k, z, y, a_cols), piece(k, z, y, a_cols), x_send.at[k, z, turn - 1], x_recv.at[k, z, turn - 1], me.device(flip=True))

    def core_copy(k, z, y, cols, mine=False):
        src = own.at[at(k), cols] if mine else piece(k, z, y, cols)
        return copy(src, piece(k, z, y, cols), c_send.at[k], c_recv.at[k], me.device(core=1 - me.core))

    everything = pl.ds(0, width)
    below = lambda s: (me.z - s >= 0, me.z - s)
    above = lambda s: (me.z + s < DEPTH, me.z + s)

    def start_own(k):
        @pl.when(me.z < DEPTH - 1)
        def _():
            z_copy(k, me.z, 1, True).start()
        @pl.when(me.z > 0)
        def _():
            z_copy(k, me.z, -1, True).start()
        for turn in range(1, span):
            y_copy(k, me.z, turn, True).start()
        core_copy(k, me.z, me.y, everything, True).start()

    def along_z(k, s):
        for (ok, z), step in ((below(s), 1), (above(s), -1)):
            @pl.when(ok)
            def _():
                z_copy(k, z, step, False).wait_recv()
                if s < DEPTH - 1:
                    more = me.z < DEPTH - 1 if step > 0 else me.z > 0
                    @pl.when(more)
                    def _():
                        z_copy(k, z, step, False).start()
                for turn in range(1, span):
                    y_copy(k, z, turn, False).start()
                thin_copy(k, z).start()
                core_copy(k, z, me.y, z_cols).start()

    def across(k, s):
        for ok, z in ((below(s), above(s)) if s else (below(0),)):
            @pl.when(ok)
            def _():
                for turn in range(1, span):
                    y_copy(k, z, turn, False).wait_recv()
                    x_copy(k, z, span - turn).start()
                    core_copy(k, z, lax.rem(me.y + span - turn, span), a_cols).start()

    def beside(k, s):
        for ok, z in ((below(s), above(s)) if s else (below(0),)):
            @pl.when(ok)
            def _():
                for turn in range(1, span):
                    x_copy(k, z, turn).wait_recv()
                    core_copy(k, z, lax.rem(me.y + turn, span), b_cols).start()

    def beside_thin(k, s):
        for ok, z in (below(s), above(s)):
            @pl.when(ok)
            def _():
                thin_copy(k, z).wait_recv()
                core_copy(k, z, me.y, thin_cols).start()

    def lane(k, wait):
        half = full.at[pl.ds(0, parts // 2), at(k)]
        whole = copy(half, half, c_send.at[k], c_recv.at[k], me.device(core=1 - me.core))
        whole.wait_recv() if wait else whole.wait_send()

    lane_in = functools.partial(lane, wait=True)

    table = Rows(parts, pixels.shape[1], width, text.shape[1], inner)
    forward = Forward(table, full, pixels, text, g_low, vec, mod, outs, scratch)
    ready = DEPTH + 1
    have = lambda which: (sum(which) - 1) // rows + ready
    t1 = max(have(table.first), 5)
    t2 = max(have(table.second), t1 + 4)
    t3 = max(have(table.attend_more), t2 + 2)
    t4 = max(t2 + 4, t3 + 1)
    t5 = max(have(table.text), t4 + 1)
    slots = max(chunks + ready, t5 + 1)

    def steps(t):
        def once(when, *work):
            @pl.when(t == when)
            def _():
                for one in work:
                    one()
        def many(when, until, each, work):
            @pl.when(jnp.logical_and(t >= when, t < until))
            def _():
                for i in range(each):
                    work((t - when) * each + i)
        once(0, forward.zero)
        for image in range(3):
            once(2 + image, functools.partial(forward.first_norm, image))
        once(5, modulate)
        once(t1, lambda: forward.load_first(jnp.int32(0)))
        many(t1, t1 + 2, 2, forward.first_conv)
        for image in range(3):
            once(t1 + 2 + image // 2, functools.partial(forward.mid_norm, image))
        once(t2, lambda: forward.load_second(jnp.int32(0)))
        many(t2, t2 + 4, 2, forward.second_conv)
        once(t3, forward.load_small)
        once(t4, forward.skip_product, forward.attended_grad)
        for image in range(3):
            once(t4 + image // 2, functools.partial(forward.last_norm, image))

    for k in range(min(lead, chunks)):
        start_own(k)

    last = 2 * (DEPTH - 1) + 3

    def slot(t, carry):
        def stage(delay, work):
            k = t - delay
            @pl.when(jnp.logical_and(k >= 0, k < chunks))
            def _():
                work(k)
        @pl.when(t + lead < chunks)
        def _():
            start_own(t + lead)
        for s in range(1, DEPTH):
            stage(s - 1, functools.partial(along_z, s=s))
        for s in range(DEPTH):
            stage(s + 0, functools.partial(across, s=s))
        for s in range(1, DEPTH):
            stage(s + 0, functools.partial(beside_thin, s=s))
        for s in range(DEPTH):
            stage(s + 1, functools.partial(beside, s=s))
        stage(ready, lane_in)
        steps(t)
        return carry

    def to_all(make):
        def one(i, carry):
            make(lax.rem(me.place + i, parts)).start()
            return carry
        lax.fori_loop(1, parts, one, 0)

    def wait_all(ref, send, recv):
        others = ref.at[pl.ds(0, parts - 1)]
        every = copy(others, others, send, recv, me.device(core=1 - me.core))
        every.wait_send()
        every.wait_recv()

    def modulate():
        wait_all(sums, m_send, m_recv)
        mod[...] = jnp.sum(sums[...], axis=0) + vec[V_EMB : V_EMB + 1, :]

    to_all(lambda far: copy(note.at[far], notes.at[me.place], n_send, n_recv, (me.group, far)))
    notes[me.place] = note[me.place]
    lax.fori_loop(0, 2, slot, 0)
    wait_all(notes, n_send, n_recv)
    vec[...] = jnp.zeros_like(vec)
    for row in range(V_OUT + 1):
        size = {V_IN_GAIN: pixels.shape[1], V_IN_SHIFT: pixels.shape[1], V_EMB: emb.shape[1]}.get(row, width)
        each = 128 * parts // size
        for block in range(size // 128):
            value = notes[block * each, images + row : images + row + 1, :].astype(jnp.float32)
            for i in range(1, each):
                value = value + notes[block * each + i, images + row : images + row + 1, :].astype(jnp.float32)
            vec[row : row + 1, block * 128 : (block + 1) * 128] = value
    rows_in = notes.shape[1]
    step = 512
    for at_col in range(0, emb.shape[1], step):
        cols = slice(at_col, at_col + step)
        product = jnp.dot(notes[...].reshape(parts * rows_in, 128), emb[:, cols], preferred_element_type=jnp.float32)
        part[:, :, cols] = product.reshape(parts, rows_in, step)[:, :8]
    to_all(lambda far: copy(part.at[far], sums.at[me.place], m_send, m_recv, (me.group, far)))
    sums[me.place] = part[me.place]
    local.wait()
    lax.fori_loop(2, slots, slot, 0)
    forward.load_text(jnp.int32(0))
    for i in range(3):
        forward.project(i)
    for q in range(4):
        forward.text_step(q, text_total)

    def finish(k, carry):
        for step, edge in ((1, me.z < DEPTH - 1), (-1, me.z > 0)):
            for s in range(DEPTH - 1):
                ok, z = below(s) if step > 0 else above(s)
                @pl.when(jnp.logical_and(ok, edge))
                def _():
                    z_copy(k, z, step, False).wait_send()
        for z in range(DEPTH):
            for turn in range(1, span):
                y_copy(k, z, turn, False).wait_send()
                x_copy(k, z, turn).wait_send()
            @pl.when(z != me.z)
            def _():
                thin_copy(k, z).wait_send()
        lane(k, False)
        return carry

    lax.fori_loop(0, chunks, finish, 0)
    forward.finish()


def forward_all(own, note, emb, pixels, text, g_low, images, inner, replicas, parts, rows=80, lead=3):
    total, width = own.shape
    chunks = total // rows
    span = parts // (2 * DEPTH)
    pix, pix_width = pixels.shape
    dma = lambda *shape: pltpu.SemaphoreType.DMA(shape)
    bf = lambda *shape: jax.ShapeDtypeStruct(shape, BF16)
    fl = lambda *shape: jax.ShapeDtypeStruct(shape, F32)
    hbm, vmem = pl.BlockSpec(memory_space=pl.ANY), pl.BlockSpec(memory_space=pltpu.VMEM)
    return pl.pallas_call(
        functools.partial(forward_kernel, replicas, parts, rows, lead, inner, images),
        out_shape=[
            bf(parts, total, width), fl(8, emb.shape[1]), fl(16, emb.shape[1]), bf(*note.shape),
            bf(3, PADDED, pix_width), bf(3, PADDED, width), fl(pix, width), fl(pix, width), fl(pix, width), bf(pix, width),
            bf(pix, 3 * inner), bf(3, TEXT_PAD, 2 * inner), bf(pix, inner), fl(24, width),
        ],
        in_specs=[hbm] + [vmem] * 5,
        out_specs=[hbm, vmem, vmem, vmem] + [hbm] * 6 + [vmem] * 4,
        scratch_shapes=[
            pltpu.VMEM((parts, 8, emb.shape[1]), F32),
            pltpu.VMEM((parts, 8, emb.shape[1]), F32),
            pltpu.VMEM((text.shape[0], width), F32),
            pltpu.VMEM((3, PADDED, pix_width), BF16), pltpu.VMEM((3, PADDED, width), BF16),
            pltpu.VMEM((pix, BLOCK), BF16), pltpu.VMEM((2, BLOCK, width), BF16),
            pltpu.VMEM((pix, width), F32), pltpu.VMEM((pix, width), F32), pltpu.VMEM((pix, width), BF16),
            pltpu.VMEM((width, 3 * inner), BF16), pltpu.VMEM((pix_width, width), BF16), pltpu.VMEM((inner, width), BF16),
            dma(2), dma(3), dma(6),
            dma(), dma(), dma(), dma(),
            dma(chunks, DEPTH, 2), dma(chunks, DEPTH),
            dma(chunks, DEPTH, span - 1), dma(chunks, DEPTH, span - 1),
            dma(chunks, DEPTH), dma(chunks, DEPTH),
            dma(chunks, DEPTH, span - 1), dma(chunks, DEPTH, span - 1),
            dma(chunks), dma(chunks), dma(),
        ],
        compiler_params=pltpu.CompilerParams(collective_id=0, has_side_effects=True, vmem_limit_bytes=60 << 20),
        name="forward_all",
    )(own, note, emb, pixels, text, g_low)


class Seat(Where):
    def bit(self, b):
        step = 1 << b
        group = self.group + step - 2 * step * lax.rem(self.group // step, 2)
        return (group, self.place)

    def meet(self, bits, everyone):
        sem = pltpu.get_barrier_semaphore()
        greet = lambda device: pl.semaphore_signal(sem, inc=1, device_id=device, device_id_type=MESH)
        if everyone:
            count = self.replicas * self.parts
            def one(i, carry):
                far = lax.rem(self.group * self.parts + self.place + i, count)
                greet((far // self.parts, lax.rem(far, self.parts)))
                return carry
            lax.fori_loop(1, count, one, 0)
            pl.semaphore_wait(sem, count - 1)
            return


def reduce_kernel(replicas, parts, rows, spans, lead, ring, nrc, lag, ngrad, *refs):
    grads, note, out, notes = refs[:ngrad], refs[ngrad], refs[ngrad + 1], refs[ngrad + 2]
    (hold, rc, xr, yr, zu, zd, fr, tb, l_sem, c_send, c_recv, x_send, x_recv, y_send, y_recv,
     u_send, u_recv, d_send, d_recv, f_send, f_recv, n_send, n_recv, free) = refs[ngrad + 3:]
    me = Seat(replicas, parts)
    span = me.span
    width = out.shape[1]
    chunks = out.shape[0] // rows
    side = me.side
    bits = replicas.bit_length() - 1
    apart, joint = 3 * width // 8, 5 * width // 8

    me.meet(bits, True)

    def copy(src, dst, send, recv, device):
        return pltpu.make_async_remote_copy(src_ref=src, dst_ref=dst, send_sem=send, recv_sem=recv, device_id=device, device_id_type=MESH)

    count = replicas * parts
    mine = me.group * parts + me.place

    def note_copy(far):
        return copy(note.at[lax.rem(far, parts)], notes.at[mine], n_send, n_recv, (far // parts, lax.rem(far, parts)))

    def send_note(i, carry):
        note_copy(lax.rem(mine + i, count)).start()
        return carry

    lax.fori_loop(1, count, send_note, 0)
    own_note = pltpu.make_async_copy(note.at[me.place], notes.at[mine], l_sem.at[ring])
    own_note.start()

    def core_copy(k, src):
        return copy(src, rc.at[lax.rem(k, nrc)], c_send.at[k], c_recv.at[lax.rem(k, nrc)], me.device(core=1 - me.core))

    def begin(k):
        @pl.when(k >= nrc)
        def _():
            pl.semaphore_wait(free, 1)
        for grad, (lo, hi) in zip(grads, spans):
            @pl.when(jnp.logical_and(k >= lo, k < hi))
            def _():
                at = pl.ds(pl.multiple_of((k - lo) * rows, 16), rows)
                slot = lax.rem(k, ring)
                pltpu.make_async_copy(grad.at[:, :, me.core, at, :], hold.at[slot], l_sem.at[slot]).start()
                core_copy(k, grad.at[:, :, 1 - me.core, at, :]).start()

    def x_copy(k, turn):
        slot = lax.rem(k, ring)
        cols = pl.ds(pl.multiple_of((1 - side) * joint, 128), apart)
        return copy(hold.at[slot, :, lax.rem(me.y + turn, span), :, cols], xr.at[k, turn - 1], x_send.at[k, turn - 1], x_recv.at[k, turn - 1], me.bit(0))

    def y_copy(k, turn):
        slot = lax.rem(k, ring)
        cols = pl.ds(pl.multiple_of(side * apart, 128), joint)
        return copy(hold.at[slot, :, lax.rem(me.y + turn, span), :, cols], yr.at[k, turn - 1], y_send.at[k, turn - 1], y_recv.at[k, turn - 1], me.device(y=lax.rem(me.y + turn, span)))

    def up_copy(k, z):
        slot = lax.rem(k, ring)
        return copy(hold.at[slot, z + 1 : DEPTH, me.y], zu.at[k, 0 : DEPTH - 1 - z], u_send.at[k], u_recv.at[k], me.device(z=me.z + 1))

    def down_copy(k, z):
        slot = lax.rem(k, ring)
        return copy(hold.at[slot, 0:z, me.y], zd.at[k, 0:z], d_send.at[k], d_recv.at[k], me.device(z=me.z - 1))

    def f_copy(k, b):
        slot = lax.rem(k, ring)
        src = hold.at[slot, me.z, me.y] if b == 0 else tb.at[b - 1, k]
        return copy(src, fr.at[b, k], f_send.at[b, k], f_recv.at[b, k], me.bit(b))

    def fold_core(k):
        slot = lax.rem(k, ring)
        here = hold.at[slot]
        pltpu.make_async_copy(here, here, l_sem.at[slot]).wait()
        core_copy(k, rc.at[lax.rem(k, nrc)]).wait_recv()
        hold[slot] = hold[slot] + rc[lax.rem(k, nrc)]
        @pl.when(k + nrc < chunks)
        def _():
            pl.semaphore_signal(free, inc=1, device_id=me.device(core=1 - me.core), device_id_type=MESH)
        for turn in range(1, span):
            x_copy(k, turn).start()

    def fold_x(k):
        slot = lax.rem(k, ring)
        for turn in range(1, span):
            x_copy(k, turn).wait_recv()
            y = lax.rem(me.y + turn, span)
            for s in range(2):
                @pl.when(side == s)
                def _():
                    cols = slice(0, apart) if s == 0 else slice(joint, width)
                    hold[slot, :, y, :, cols] = hold[slot, :, y, :, cols] + xr[k, turn - 1]
            y_copy(k, turn).start()

    def fold_y(k):
        slot = lax.rem(k, ring)
        for turn in range(1, span):
            y_copy(k, turn).wait_recv()
            for s in range(2):
                @pl.when(side == s)
                def _():
                    cols = slice(0, joint) if s == 0 else slice(apart, width)
                    hold[slot, :, me.y, :, cols] = hold[slot, :, me.y, :, cols] + yr[k, turn - 1]

    def hop(k, h):
        slot = lax.rem(k, ring)
        @pl.when(me.z == h)
        def _():
            if h > 0:
                up_copy(k, h - 1).wait_recv()
                hold[slot, h:, me.y] = hold[slot, h:, me.y] + zu[k, 0 : DEPTH - h]
            if h < DEPTH - 1:
                up_copy(k, h).start()
        z = DEPTH - 1 - h
        @pl.when(me.z == z)
        def _():
            if h > 0:
                down_copy(k, z + 1).wait_recv()
                hold[slot, : z + 1, me.y] = hold[slot, : z + 1, me.y] + zd[k, 0 : z + 1]
            if h < DEPTH - 1:
                down_copy(k, z).start()

    def finish(k, b):
        slot = lax.rem(k, ring)
        f_copy(k, b).wait_recv()
        before = hold[slot, me.z, me.y] if b == 0 else tb[b - 1, k]
        total = before.astype(F32) + fr[b, k].astype(F32)
        if b == bits - 1:
            out[pl.ds(pl.multiple_of(k * rows, 16), rows), :] = total
        else:
            tb[b, k] = total.astype(BF16)
            f_copy(k, b + 1).start()

    def retire(k):
        core_copy(k, rc.at[0]).wait_send()
        for turn in range(1, span):
            x_copy(k, turn).wait_send()
            y_copy(k, turn).wait_send()
        for z in range(DEPTH):
            @pl.when(me.z == z)
            def _():
                if z < DEPTH - 1:
                    up_copy(k, z).wait_send()
                if z > 0:
                    down_copy(k, z).wait_send()
        for b in range(bits):
            f_copy(k, b).wait_send()

    for k in range(lead):
        begin(jnp.int32(k))

    first_f = (2 + DEPTH) * lag

    def slot_work(t, carry):
        def stage(delay, work):
            k = t - delay
            @pl.when(jnp.logical_and(k >= 0, k < chunks))
            def _():
                work(k)
        for h in range(DEPTH - 1, 0, -1):
            stage((2 + h) * lag, functools.partial(hop, h=h))
        stage((1 + DEPTH) * lag, lambda k: f_copy(k, 0).start())
        def pair(k):
            fold_y(k)
            hop(k, 0)
        stage(2 * lag, pair)
        stage(lag, fold_x)
        stage(0, fold_core)
        for b in range(bits):
            stage(first_f + b * lag, functools.partial(finish, b=b))
        stage(first_f + bits * lag, retire)
        @pl.when(t + lead < chunks)
        def _():
            begin(t + lead)
        return carry

    lax.fori_loop(0, chunks + first_f + bits * lag + 1, slot_work, 0)
    own_note.wait()
    others = notes.at[pl.ds(0, count - 1)]
    every = copy(others, others, n_send, n_recv, me.device(core=1 - me.core))
    every.wait_send()
    every.wait_recv()


def reduce_all(grads, note, replicas, parts, rows, lead=2, nrc=3, lag=2):
    span = parts // (2 * DEPTH)
    width = grads[0].shape[1]
    spans, at = [], 0
    views = []
    for grad in grads:
        size = grad.shape[0] // parts
        spans.append((at // rows, (at + size) // rows))
        at += size
        views.append(grad.reshape(DEPTH, span, 2, size, width))
    total = at
    chunks = total // rows
    bits = replicas.bit_length() - 1
    ring = lead + (2 + DEPTH + bits) * lag + 2
    dma = lambda *shape: pltpu.SemaphoreType.DMA(shape)
    vm = lambda *shape: pltpu.VMEM(shape, BF16)
    return pl.pallas_call(
        functools.partial(reduce_kernel, replicas, parts, rows, spans, lead, ring, nrc, lag, len(grads)),
        out_shape=[jax.ShapeDtypeStruct((total, width), F32), jax.ShapeDtypeStruct((replicas * parts,) + note.shape[1:], note.dtype)],
        in_specs=[pl.BlockSpec(memory_space=pl.ANY)] * (len(grads) + 1),
        out_specs=[pl.BlockSpec(memory_space=pltpu.VMEM), pl.BlockSpec(memory_space=pl.ANY)],
        scratch_shapes=[
            vm(ring, DEPTH, span, rows, width),
            vm(nrc, DEPTH, span, rows, width),
            vm(chunks, span - 1, DEPTH, rows, 3 * width // 8),
            vm(chunks, span - 1, DEPTH, rows, 5 * width // 8),
            vm(chunks, DEPTH - 1, rows, width),
            vm(chunks, DEPTH - 1, rows, width),
            vm(bits, chunks, rows, width),
            vm(max(bits - 1, 1), chunks if bits > 1 else 1, rows, width),
            dma(ring + 1),
            dma(chunks), dma(nrc),
            dma(chunks, span - 1), dma(chunks, span - 1),
            dma(chunks, span - 1), dma(chunks, span - 1),
            dma(chunks), dma(chunks), dma(chunks), dma(chunks),
            dma(bits, chunks), dma(bits, chunks),
            pltpu.SemaphoreType.DMA, pltpu.SemaphoreType.DMA,
            pltpu.SemaphoreType.REGULAR,
        ],
        compiler_params=pltpu.CompilerParams(collective_id=1, has_side_effects=True, vmem_limit_bytes=60 << 20),
        name="reduce_all",
    )(*views, note)


def images(rows):
    return [rows[start : start + size] for start, size in zip(STARTS, SIZES)]


def flat_group_mean(column_sums, count):
    channels = column_sums.shape[-1]
    width = channels // GROUPS
    totals = jnp.sum(column_sums.reshape(GROUPS, width), axis=1, keepdims=True) / (count * width)
    return jnp.broadcast_to(totals, (GROUPS, width)).reshape(1, channels)


def normalise(rows):
    count = rows.shape[0]
    centered = rows - flat_group_mean(jnp.sum(rows, axis=0), count)
    spread = flat_group_mean(jnp.sum(jnp.square(centered), axis=0), count)
    inverse = lax.rsqrt(spread + 1e-05)
    return centered * inverse, inverse


def norm_back(grad, hat, inverse, factor):
    count = grad.shape[0]
    plain = jnp.sum(grad, axis=0)
    crossed = jnp.sum(grad * hat, axis=0)
    mean_plain = flat_group_mean(plain * factor, count)
    mean_crossed = flat_group_mean(crossed * factor, count)
    return inverse * (grad * factor[None, :] - mean_plain - hat * mean_crossed), plain, crossed


def silu_slope(value):
    gate = jax.nn.sigmoid(value)
    return gate * (1.0 + value * (1.0 - gate))


def patches(rows, flip=False):
    channels = rows.shape[-1]
    parts = []
    for (height, breadth), picture in zip(SHAPES, images(rows)):
        padded = jnp.pad(picture.reshape(height, breadth, channels), ((1, 1), (1, 1), (0, 0)))
        windows = [
            padded[down : down + height, across : across + breadth]
            for down in range(3)
            for across in range(3)
        ]
        if flip:
            windows = windows[::-1]
        parts.append(jnp.concatenate(windows, axis=-1).reshape(height * breadth, 9 * channels))
    return jnp.concatenate(parts, 0)


def attention_kernel(q_ref, k_ref, v_ref, tk_ref, tv_ref, mask_ref, go_ref, o_ref, dq_ref, dk_ref, dv_ref, dtk_ref, dtv_ref):
    lane = lax.broadcasted_iota(jnp.int32, (1, 2 * HEAD), 1)
    for image in range(3):
        rows = pl.ds(STARTS[image], SIZES[image])
        size = SIZES[image]
        q, k, v, go = q_ref[rows, :], k_ref[rows, :], v_ref[rows, :], go_ref[rows, :]
        tk, tv = tk_ref[image], tv_ref[image]
        mask = mask_ref[image : image + 1, :]
        results = []
        for head in range(2):
            mine = (lane >= HEAD) if head else (lane < HEAD)
            qh = jnp.where(mine, q, jnp.zeros_like(q))
            gh = jnp.where(mine, go, jnp.zeros_like(go))
            scale = HEAD ** -0.5
            nt = ((1,), (1,))
            tn = ((0,), (0,))
            sp = dot(qh, k, nt) * scale
            st = dot(qh, tk, nt) * scale
            st = jnp.where(mask == 1, st, jnp.where(mask == 0, -1000000000.0, -jnp.inf))
            peak = jnp.maximum(
                jnp.max(sp, axis=1, keepdims=True), jnp.max(st, axis=1, keepdims=True)
            )
            ep, et = jnp.exp(sp - peak), jnp.exp(st - peak)
            total = jnp.sum(ep, axis=1, keepdims=True) + jnp.sum(et, axis=1, keepdims=True)
            inv = 1.0 / total
            pp, pt = ep * inv, et * inv
            ppl, ptl = pp.astype(BF16), pt.astype(BF16)
            out = dot(ppl, v) + dot(ptl, tv)
            dv = dot(ppl, go, tn)
            dtv = dot(ptl, go, tn)
            dpp = dot(gh, v, nt)
            dpt = dot(gh, tv, nt)
            inner = jnp.sum(dpp * pp, axis=1, keepdims=True) + jnp.sum(
                dpt * pt, axis=1, keepdims=True
            )
            dsp = (pp * (dpp - inner) * scale).astype(BF16)
            dst = (pt * (dpt - inner) * scale).astype(BF16)
            dq = dot(dsp, k) + dot(dst, tk)
            dk = dot(dsp, q, tn)
            dtk = dot(dst, q, tn)
            results.append((out, dq, dk, dv, dtk, dtv))
        first, second = results
        low = lane < HEAD
        merged = [jnp.where(low, a, b).astype(BF16) for a, b in zip(first, second)]
        o_ref[rows, :] = merged[0]
        dq_ref[rows, :] = merged[1]
        dk_ref[rows, :] = merged[2]
        dv_ref[rows, :] = merged[3]
        dtk_ref[image] = merged[4]
        dtv_ref[image] = merged[5]


def attention(triple, text_pair, mask, grad_attended):
    rows, inner = triple.shape[0], triple.shape[1] // 3
    pairs = inner // (2 * HEAD)
    col = lambda shift: pl.BlockSpec((rows, 2 * HEAD), lambda h: (0, h + shift * pairs))
    txt = lambda shift: pl.BlockSpec((3, TEXT_PAD, 2 * HEAD), lambda h: (0, 0, h + shift * pairs))
    wide = jax.ShapeDtypeStruct((rows, inner), BF16)
    wide_text = jax.ShapeDtypeStruct((3, TEXT_PAD, inner), BF16)
    return pl.pallas_call(
        attention_kernel,
        grid=(pairs,),
        in_specs=[
            col(0),
            col(1),
            col(2),
            txt(0),
            txt(1),
            pl.BlockSpec((3, TEXT_PAD), lambda h: (0, 0)),
            col(0),
        ],
        out_specs=[col(0)] * 4 + [txt(0)] * 2,
        out_shape=[wide] * 4 + [wide_text] * 2,
        compiler_params=pltpu.CompilerParams(vmem_limit_bytes=40 << 20),
    )(triple, triple, triple, text_pair, text_pair, mask, grad_attended)


def fold_attend(part, width):
    more = part[..., width:]
    half = part.shape[-2] // 2
    return [part[..., :width], jnp.concatenate([more[..., :half, :], more[..., half:, :]], -1)]


def unfold_attend(part, columns):
    blocks, rows, width = part.shape
    size = rows * 2 // 3
    more = part[:, size:]
    half = columns - width
    return jnp.concatenate([part[:, :size], jnp.concatenate([more[..., :half], more[..., half:]], 1)], -1).reshape(blocks * size, columns)


def body(
    pixels,
    embedding,
    text_states,
    text_mask,
    occupancy,
    cotangent,
    in_gain,
    in_shift,
    conv_first,
    first_bias,
    emb_weight,
    emb_bias,
    mid_gain,
    mid_shift,
    conv_second,
    second_bias,
    skip_weight,
    skip_bias,
    attn_gain,
    attn_shift,
    attend_weight,
    text_weight,
    out_weight,
    out_bias,
):
    place = lax.axis_index("fsdp")
    group = lax.axis_index("dp")
    parts = lax.axis_size("fsdp")
    replicas = lax.axis_size("dp")
    depth = emb_weight.shape[0]
    images_here = embedding.shape[0]
    emb_act = jax.nn.silu(embedding.astype(F32)).astype(BF16)
    emb_cut = emb_act.reshape(images_here, parts, depth).transpose(1, 0, 2)
    emb_cut = jnp.pad(emb_cut, ((0, 0), (0, 0), (0, 128 - depth)))

    vectors = (in_gain, in_shift, first_bias, emb_bias, mid_gain, mid_shift, second_bias, skip_bias, attn_gain, attn_shift, out_bias)
    lane = lax.broadcasted_iota(jnp.int32, (1, 128), 1)
    lines = []
    for vector in vectors:
        size = vector.shape[0]
        wide = jnp.tile(vector, 128 // size).reshape(1, 128)
        lines.append(jnp.where(lane // size == lax.rem(place, 128 // size), wide, jnp.zeros_like(wide)))
    room = 16 - images_here - len(lines)
    flat = jnp.concatenate(lines + [jnp.zeros((room, 128), BF16)] if room else lines, 0)[None]
    note = jnp.concatenate([emb_cut, jnp.broadcast_to(flat, (parts,) + flat.shape[1:])], 1)
    channels = skip_weight.shape[1]
    inner = out_weight.shape[0] * parts
    own = jnp.concatenate([conv_first, conv_second, skip_weight, out_weight] + fold_attend(attend_weight, channels) + [text_weight], 0)
    present = jnp.concatenate(
        [jnp.broadcast_to(occupancy[0, i].astype(F32), (SIZES[i], 1)) for i in range(3)], 0
    )
    grad_out = cotangent.astype(F32) * present
    grad_low = grad_out.astype(BF16)
    text_len = text_states.shape[1]
    text_rows = jnp.pad(text_states, ((0, 0), (0, TEXT_ROWS - text_len), (0, 0))).reshape(3 * TEXT_ROWS, -1)
    (full, modulation, vec, _, act1, act2, mid_hats, residual, hats, normed, triple, text_pair, grad_attended, inverses) = forward_all(
        own, note, jnp.pad(emb_weight, ((0, 128 - depth), (0, 0))), pixels, text_rows, grad_low, images_here, inner, replicas, parts)
    scale, shift = modulation[:images_here, :channels], modulation[:images_here, channels:]
    in_gain, in_shift = vec[V_IN_GAIN, : pixels.shape[1]], vec[V_IN_SHIFT, : pixels.shape[1]]
    mid_gain, mid_shift, attn_gain, out_bias = (vec[row, :channels] for row in (V_MID_GAIN, V_MID_SHIFT, V_ATTN_GAIN, V_OUT))
    table = Rows(parts, pixels.shape[1], channels, text_states.shape[2], inner)
    cut = lambda which: full[:, which[0] : sum(which)].reshape(parts * which[1], -1)
    conv_first, conv_second, skip_weight, out_weight = (cut(which) for which in (table.first, table.second, table.skip, table.out))
    attend_weight = unfold_attend(full[:, table.attend[0] : sum(table.attend_more)], 3 * inner)

    middles = lambda act: jnp.concatenate([act[1, base : base + size] for base, size in zip(BASES, SIZES)], 0)
    first_act, second_act = middles(act1), middles(act2)
    pixel_hat = [
        ((part.astype(F32) - inverses[16 + i, : pixels.shape[1]]) * inverses[i, : pixels.shape[1]], inverses[i, : pixels.shape[1]])
        for i, part in enumerate(images(pixels))
    ]
    first_pre = [hat * in_gain + in_shift for hat, _ in pixel_hat]
    first_patches = patches(first_act)
    mid_hat = [(part, inverses[3 + i]) for i, part in enumerate(images(mid_hats))]
    mid_pre = [
        (hat * mid_gain + mid_shift) * (1.0 + scale[i]) + shift[i]
        for i, (hat, _) in enumerate(mid_hat)
    ]
    second_patches = patches(second_act)
    attn_hat = [(part, inverses[6 + i]) for i, part in enumerate(images(hats))]
    mask = jnp.pad(
        (text_mask > 0).astype(jnp.int32), ((0, 0), (0, TEXT_PAD - text_len)), constant_values=2
    )
    attended, dq, dk, dv, dtk, dtv = attention(triple, text_pair, mask, grad_attended)
    text_rows = text_states.reshape(3 * text_len, -1)
    block_output = (present * (residual + (dot(attended, out_weight) + out_bias))).astype(BF16)

    tn = ((0,), (0,))
    nt = ((1,), (1,))
    grad_out_bias = jnp.sum(grad_out, axis=0)
    grad_out_weight = dot(attended, grad_low, tn)
    grad_triple = jnp.concatenate([dq, dk, dv], 1)
    grad_text = jnp.concatenate([dtk, dtv], 2)[:, :text_len].reshape(3 * text_len, -1)
    grad_attend_weight = dot(normed, grad_triple, tn)
    grad_text_weight = dot(text_rows, grad_text, tn)
    grad_normed = dot(grad_triple, attend_weight, nt)
    backs = [
        norm_back(part, hat, inverse, attn_gain)
        for part, (hat, inverse) in zip(images(grad_normed), attn_hat)
    ]
    grad_attn_shift = sum(back[1] for back in backs)
    grad_attn_gain = sum(back[2] for back in backs)
    grad_residual = jnp.concatenate([back[0] for back in backs], 0) + grad_out
    grad_second_bias = jnp.sum(grad_residual, axis=0)
    res_low = grad_residual.astype(BF16)
    grad_skip_weight = dot(pixels, res_low, tn)
    grad_conv_second = dot(second_patches, res_low, tn)
    res_patches = patches(res_low, flip=True).reshape(-1, 9, channels)
    grad_second_act = lax.dot_general(
        res_patches,
        conv_second.reshape(9, channels, channels),
        (((1, 2), (0, 2)), ((), ())),
        preferred_element_type=F32,
    )
    backs = []
    grad_mod = []
    for i, part in enumerate(images(grad_second_act)):
        hat, inverse = mid_hat[i]
        grad_pre = part * silu_slope(mid_pre[i])
        factor = 1.0 + scale[i]
        rows, plain, crossed = norm_back(grad_pre, hat, inverse, factor * mid_gain)
        grad_mod.append(jnp.concatenate([crossed * mid_gain + plain * mid_shift, plain]))
        backs.append((rows, plain * factor, crossed * factor))
    grad_mid_shift = sum(back[1] for back in backs)
    grad_mid_gain = sum(back[2] for back in backs)
    grad_first_conv = jnp.concatenate([back[0] for back in backs], 0)
    grad_first_bias = jnp.sum(grad_first_conv, axis=0)
    conv_low = grad_first_conv.astype(BF16)
    grad_conv_first = dot(first_patches, conv_low, tn)
    first_width = pixels.shape[1]
    conv_patches = patches(conv_low, flip=True).reshape(-1, 9, channels)
    grad_first_act = lax.dot_general(
        conv_patches,
        conv_first.reshape(9, first_width, channels),
        (((1, 2), (0, 2)), ((), ())),
        preferred_element_type=F32,
    )
    backs = [
        norm_back(part * silu_slope(pre), hat, inverse, in_gain)
        for part, pre, (hat, inverse) in zip(images(grad_first_act), first_pre, pixel_hat)
    ]
    grad_in_shift = sum(back[1] for back in backs)
    grad_in_gain = sum(back[2] for back in backs)
    grad_pixels = jnp.concatenate([back[0] for back in backs], 0) + dot(res_low, skip_weight, nt)

    small = (grad_in_gain, grad_in_shift, grad_first_bias, grad_mid_gain, grad_mid_shift, grad_second_bias, grad_attn_gain, grad_attn_shift, grad_out_bias)
    cut = jnp.concatenate([vector.reshape(parts, -1) for vector in small], 1)
    mod_rows = jnp.stack(grad_mod).reshape(1, -1, 128)
    mod_count = mod_rows.shape[1]
    room = 64 - mod_count - images_here
    cut = jnp.pad(cut, ((0, 0), (0, room * 128 - cut.shape[1]))).reshape(parts, room, 128)
    note = jnp.concatenate(
        [jnp.broadcast_to(mod_rows, (parts,) + mod_rows.shape[1:]).astype(BF16), emb_cut, cut.astype(BF16)], 1
    )
    pack = lambda part: part.astype(BF16).reshape(parts, -1, part.shape[-1])
    grad_small = jnp.concatenate(
        [pack(grad_skip_weight), pack(grad_out_weight)] + fold_attend(pack(grad_attend_weight), channels), 1
    ).reshape(-1, channels)
    owned, notes = reduce_all(
        [grad_conv_first.astype(BF16), grad_conv_second.astype(BF16), grad_text_weight.astype(BF16), grad_small],
        note, replicas, parts, 512 // parts,
    )
    at = 0
    cuts = []
    for size in (conv_first.shape[0], conv_second.shape[0], text_weight.shape[0] * parts, skip_weight.shape[0], out_weight.shape[0]):
        cuts.append(owned[at : at + size // parts])
        at += size // parts
    grad_conv_first, grad_conv_second, grad_text_weight, grad_skip_weight, grad_out_weight = cuts
    grad_attend_weight = unfold_attend(owned[None, at:], 3 * inner)
    mod_rows = notes[:, :mod_count].reshape(-1, 2 * channels)
    all_act = notes[:, mod_count : mod_count + images_here, :depth].reshape(-1, depth)
    grad_emb_weight = dot(all_act, mod_rows, tn)
    grad_emb_bias = jnp.sum(mod_rows.astype(F32), axis=0)
    grad_emb_bias = lax.dynamic_slice_in_dim(grad_emb_bias, place * depth, depth, 0)
    packed = jnp.sum(notes[:, mod_count + images_here :].astype(F32), axis=0).reshape(-1)
    owned = []
    at = 0
    for vector in small:
        size = vector.shape[0] // parts
        owned.append(packed[at : at + size])
        at += size
    (grad_in_gain, grad_in_shift, grad_first_bias, grad_mid_gain, grad_mid_shift, grad_second_bias, grad_attn_gain, grad_attn_shift, grad_out_bias) = owned

    return (
        block_output,
        grad_pixels,
        grad_in_gain,
        grad_in_shift,
        grad_conv_first,
        grad_first_bias,
        grad_emb_weight,
        grad_emb_bias,
        grad_mid_gain,
        grad_mid_shift,
        grad_conv_second,
        grad_second_bias,
        grad_skip_weight,
        grad_second_bias,
        grad_attn_gain,
        grad_attn_shift,
        grad_attend_weight,
        grad_text_weight,
        grad_out_weight,
        grad_out_bias,
    )


def solution(mesh):
    rows = P(("dp", "fsdp"), None)
    vector = P("fsdp")
    matrix = P("fsdp", None)
    weights = (vector, vector, matrix, vector, matrix, vector, vector, vector, matrix, vector, matrix, vector, vector, vector, matrix, matrix, matrix, vector)
    return jax.shard_map(
        body,
        mesh=mesh,
        in_specs=(rows, rows, P(("dp", "fsdp"), None, None), rows, rows, rows) + weights,
        out_specs=(rows, rows) + weights,
        check_vma=False,
    )
```

```python
import functools

import jax
import jax.numpy as jnp
from jax import lax
from jax.experimental import pallas as pl
from jax.experimental.pallas import tpu as pltpu
from jax.sharding import PartitionSpec as P

BF16 = jnp.bfloat16
F32 = jnp.float32
HEADS = 8
HEAD = 64
GROUPS = 32
UNIT = 4
SHAPES = ((4 * UNIT, 4 * UNIT), (3 * UNIT, 5 * UNIT), (5 * UNIT, 3 * UNIT))
SIZES = tuple(height * breadth for height, breadth in SHAPES)
STARTS = (0, SIZES[0], SIZES[0] + SIZES[1])
PIX = sum(SIZES)
EDGE = 32
BASES = tuple(EDGE + start + i * EDGE for i, start in enumerate(STARTS))
PADDED = PIX + 4 * EDGE
BLOCK = 1152
TEXT_PAD = 128
TEXT_ROWS = 80
SUB = 16
NT = (((1,), (1,)), ((), ()))
TN = (((0,), (0,)), ((), ()))
V_IN_GAIN, V_IN_SHIFT, V_FIRST, V_EMB, V_MID_GAIN, V_MID_SHIFT, V_SECOND, V_SKIP, V_ATTN_GAIN, V_ATTN_SHIFT, V_OUT = range(11)


def dot(left, right, dims=((1,), (0,))):
    return lax.dot_general(left, right, (dims, ((), ())), preferred_element_type=F32)


def group_mean(sums, count):
    channels = sums.shape[1]
    width = channels // GROUPS
    lane = lax.broadcasted_iota(jnp.int32, sums.shape, 1)
    step = 1
    while step < width:
        odd = lax.rem(lane // step, 2) == 1
        sums = sums + jnp.where(odd, pltpu.roll(sums, step, 1), pltpu.roll(sums, channels - step, 1))
        step *= 2
    return sums / (count * width)


def rows_of(image, i):
    return pl.ds(pl.multiple_of(STARTS[image] + i * SUB, SUB), SUB)


def over_rows(image, work, start):
    return lax.fori_loop(0, SIZES[image] // SUB, lambda i, carry: work(i, rows_of(image, i), carry), start)


def column_sum(image, channels, value):
    def add(i, rows, carry):
        v = value(rows)
        return carry + (v[:8] + v[8:])
    total = over_rows(image, add, jnp.zeros((8, channels), F32))
    return jnp.broadcast_to(jnp.sum(total, axis=0, keepdims=True), (8, channels))


def norm_figures(image, channels, value):
    count = SIZES[image]
    center = group_mean(column_sum(image, channels, value), count)[:1]
    spread = group_mean(column_sum(image, channels, lambda rows: jnp.square(value(rows) - center)), count)[:1]
    return center, lax.rsqrt(spread + 1e-05)


def store_padded(pad, image, i, act):
    breadth = SHAPES[image][1]
    at = pl.ds(pl.multiple_of(BASES[image] + i * SUB, SUB), SUB)
    column = lax.rem(i * SUB + lax.broadcasted_iota(jnp.int32, (SUB, 1), 0), breadth)
    pad[0, at, :] = jnp.where(column == breadth - 1, 0.0, act).astype(BF16)
    pad[1, at, :] = act.astype(BF16)
    pad[2, at, :] = jnp.where(column == 0, 0.0, act).astype(BF16)


def zero_edges(pad):
    zeros = jnp.zeros((EDGE, pad.shape[2]), BF16)
    for side in range(3):
        for at in [base - EDGE for base in BASES] + [PADDED - EDGE]:
            pad[side, at : at + EDGE, :] = zeros


def shifted(pad, tap, image, cols, flip=False):
    down, across = divmod(8 - tap if flip else tap, 3)
    start = BASES[image] + (down - 1) * SHAPES[image][1] + across - 1
    return pad[across, start : start + SIZES[image], cols]


def gather_block(pad, q, out):
    channels = pad.shape[2]
    for tap in range(9):
        low, high = max(q * BLOCK, tap * channels), min((q + 1) * BLOCK, (tap + 1) * channels)
        if low < high:
            for image in range(3):
                out[STARTS[image] : STARTS[image] + SIZES[image], low - q * BLOCK : high - q * BLOCK] = shifted(
                    pad, tap, image, slice(low - tap * channels, high - tap * channels)
                )


class Rows:
    def __init__(self, parts, pix_channels, channels, text_dim, inner):
        self.parts = parts
        sizes = (9 * pix_channels // parts, 9 * channels // parts, pix_channels // parts, inner // parts, channels // parts, channels // parts // 2, text_dim // parts)
        starts = [0]
        for size in sizes:
            starts.append(starts[-1] + size)
        self.first, self.second, self.skip, self.out, self.attend, self.attend_more, self.text = zip(starts, sizes)
        self.total = starts[-1]

    def load(self, full, which, q, rows, buf, sem):
        start, size = which
        each = rows // size
        for i in range(each):
            pltpu.make_async_copy(full.at[q * each + i, pl.ds(start, size)], buf.at[pl.ds(i * size, size)], sem).start()

    def load_attend(self, full, buf, sem):
        start, size = self.attend
        more, half = self.attend_more
        def one(f, carry):
            at = pl.multiple_of(f * size, SUB)
            pltpu.make_async_copy(full.at[f, pl.ds(start, size)], buf.at[pl.ds(at, size), pl.ds(0, 1024)], sem).start()
            for i in range(2):
                pltpu.make_async_copy(
                    full.at[f, pl.ds(more, half), pl.ds(512 * i, 512)],
                    buf.at[pl.ds(pl.multiple_of(at + i * half, SUB), half), pl.ds(1024, 512)],
                    sem,
                ).start()
            return carry
        lax.fori_loop(0, self.parts, one, 0)


def waited(ref, sem):
    pltpu.make_async_copy(ref, ref, sem).wait()


class Forward:
    def __init__(self, rows, full, pixels, text, g_low, vec, mod, outs, scratch):
        self.rows, self.full, self.pixels, self.text, self.g_low, self.vec, self.mod = rows, full, pixels, text, g_low, vec, mod
        (self.o_a1, self.o_a2, self.o_mid_hat, self.o_residual, self.o_hat, self.o_normed, self.triple, self.text_pair, self.grad_attended, self.inverses) = outs
        (self.a1, self.a2, self.patch, self.weight, self.acc0, self.acc1, self.normed, self.w_attend, self.w_skip, self.w_out, self.w_sem, self.s_sem, self.o_sem) = scratch

    def out_copy(self, i, src, dst):
        return pltpu.make_async_copy(src, dst, self.o_sem.at[i])

    def row(self, r, channels=1024):
        return self.vec[r : r + 1, :channels]

    def zero(self):
        zero_edges(self.a1)
        zero_edges(self.a2)

    def first_norm(self, image):
        pixels, channels = self.pixels, self.pixels.shape[1]
        value = lambda rows: pixels[rows, :].astype(F32)
        center, inverse = norm_figures(image, channels, value)
        gain, shift = self.row(V_IN_GAIN, channels) * inverse, self.row(V_IN_SHIFT, channels)
        self.inverses[image : image + 1, :channels] = inverse
        self.inverses[16 + image : 17 + image, :channels] = center
        def act(i, rows, carry):
            store_padded(self.a1, image, i, jax.nn.silu((value(rows) - center) * gain + shift))
            return carry
        over_rows(image, act, 0)
        if image == 2:
            self.out_copy(0, self.a1, self.o_a1).start()

    def load_first(self, q):
        self.rows.load(self.full, self.rows.first, q, BLOCK, self.weight.at[lax.rem(q, 2)], self.w_sem.at[lax.rem(q, 2)])

    def load_second(self, q):
        self.rows.load(self.full, self.rows.second, q, BLOCK, self.weight.at[lax.rem(q, 2)], self.w_sem.at[lax.rem(q, 2)])

    def load_text(self, q):
        self.rows.load(self.full, self.rows.text, q, 1024, self.weight.at[lax.rem(q, 2)], self.w_sem.at[lax.rem(q, 2)])

    def conv_step(self, q, pad, acc, load, count, start):
        @pl.when(q + 1 < count)
        def _():
            load(q + 1)
        for known in range(count):
            @pl.when(q == known)
            def _():
                gather_block(pad, known, self.patch)
        par = lax.rem(q, 2)
        waited(self.weight.at[par], self.w_sem.at[par])
        @pl.when(q == 0)
        def _():
            start()
        for col in (0, 512):
            cols = slice(col, col + 512)
            acc[:, cols] = acc[:, cols] + dot(self.patch[...], self.weight[par, :, cols])

    def first_conv(self, q):
        def start():
            self.acc0[...] = jnp.zeros_like(self.acc0)
        self.conv_step(q, self.a1, self.acc0, self.load_first, 9 * self.pixels.shape[1] // BLOCK, start)

    def mid_norm(self, image):
        acc, channels = self.acc0, self.acc0.shape[1]
        bias = self.row(V_FIRST)
        def shift_up(i, rows, carry):
            acc[rows, :] = acc[rows, :] + bias
            return carry
        over_rows(image, shift_up, 0)
        center, inverse = norm_figures(image, channels, lambda rows: acc[rows, :])
        self.inverses[3 + image : 4 + image, :] = inverse
        scale, shift = 1.0 + self.mod[image : image + 1, :channels], self.mod[image : image + 1, channels:]
        gain, lift = self.row(V_MID_GAIN) * scale, self.row(V_MID_SHIFT) * scale + shift
        def act(i, rows, carry):
            hat = (acc[rows, :] - center) * inverse
            acc[rows, :] = hat
            store_padded(self.a2, image, i, jax.nn.silu(hat * gain + lift))
            return carry
        over_rows(image, act, 0)
        if image == 2:
            self.out_copy(1, self.a2, self.o_a2).start()
            self.out_copy(2, self.acc0, self.o_mid_hat).start()

    def load_small(self):
        rows = self.rows
        def one(f, carry):
            for i, ((start, size), buf) in enumerate(((rows.skip, self.w_skip), (rows.out, self.w_out))):
                pltpu.make_async_copy(self.full.at[f, pl.ds(start, size)], buf.at[pl.ds(pl.multiple_of(f * size, SUB), size)], self.s_sem.at[i]).start()
            return carry
        lax.fori_loop(0, rows.parts, one, 0)
        rows.load_attend(self.full, self.w_attend, self.s_sem.at[2])

    def skip_product(self):
        for i, buf in enumerate((self.w_skip, self.w_out, self.w_attend)):
            waited(buf, self.s_sem.at[i])
        self.acc1[...] = self.acc1[...] + dot(self.pixels[...], self.w_skip[...])

    def attended_grad(self):
        self.grad_attended[...] = lax.dot_general(self.g_low[...], self.w_out[...], NT, preferred_element_type=F32).astype(BF16)

    def second_conv(self, q):
        def start():
            self.acc1[...] = jnp.zeros_like(self.acc1)
        self.conv_step(q, self.a2, self.acc1, self.load_second, 9 * self.acc1.shape[1] // BLOCK, start)

    def last_norm(self, image):
        acc, hats, channels = self.acc1, self.acc0, self.acc1.shape[1]
        if image == 0:
            self.out_copy(2, self.acc0, self.o_mid_hat).wait()
        bias = self.row(V_SECOND) + self.row(V_SKIP)
        def shift_up(i, rows, carry):
            acc[rows, :] = acc[rows, :] + bias
            return carry
        over_rows(image, shift_up, 0)
        center, inverse = norm_figures(image, channels, lambda rows: acc[rows, :])
        self.inverses[6 + image : 7 + image, :] = inverse
        gain, shift = self.row(V_ATTN_GAIN), self.row(V_ATTN_SHIFT)
        def act(i, rows, carry):
            hat = (acc[rows, :] - center) * inverse
            hats[rows, :] = hat
            self.normed[rows, :] = (hat * gain + shift).astype(BF16)
            return carry
        over_rows(image, act, 0)
        if image == 2:
            self.out_copy(3, self.acc1, self.o_residual).start()
            self.out_copy(4, self.acc0, self.o_hat).start()
            self.out_copy(5, self.normed, self.o_normed).start()

    def project(self, i):
        cols = slice(512 * i, 512 * (i + 1))
        self.triple[:, cols] = dot(self.normed[...], self.w_attend[:, cols]).astype(BF16)

    def text_step(self, q, total):
        if q + 1 < 4:
            self.load_text(q + 1)
        par = q % 2
        waited(self.weight.at[par, pl.ds(0, 1024)], self.w_sem.at[par])
        part = dot(self.text[:, 1024 * q : 1024 * (q + 1)], self.weight[par, :1024, :])
        if q:
            part = total[...] + part
        if q < 3:
            total[...] = part
        else:
            self.text_pair[...] = jnp.zeros_like(self.text_pair)
            for image in range(3):
                self.text_pair[image, :TEXT_ROWS, :] = part[TEXT_ROWS * image : TEXT_ROWS * (image + 1)].astype(BF16)

    def finish(self):
        self.out_copy(0, self.a1, self.o_a1).wait()
        self.out_copy(1, self.a2, self.o_a2).wait()
        self.out_copy(3, self.acc1, self.o_residual).wait()
        self.out_copy(4, self.acc0, self.o_hat).wait()
        self.out_copy(5, self.normed, self.o_normed).wait()


MESH = pl.DeviceIdType.MESH
DEPTH = 4


class Where:
    def __init__(self, replicas, parts):
        self.replicas, self.parts = replicas, parts
        self.span = parts // (2 * DEPTH)
        self.group = lax.axis_index("dp")
        self.place = lax.axis_index("fsdp")
        self.core = lax.rem(self.place, 2)
        self.y = lax.rem(self.place // 2, self.span)
        self.z = self.place // (2 * self.span)
        self.side = lax.rem(self.group, 2)

    def index(self, z, y, core):
        return (z * self.span + y) * 2 + core

    def device(self, z=None, y=None, core=None, flip=False):
        z = self.z if z is None else z
        y = self.y if y is None else y
        core = self.core if core is None else core
        group = self.group + 1 - 2 * self.side if flip else self.group
        return (group, self.index(z, y, core))

    def barrier(self):
        sem = pltpu.get_barrier_semaphore()
        greet = lambda device: pl.semaphore_signal(sem, inc=1, device_id=device, device_id_type=MESH)
        greet(self.device(flip=True))
        def one(i, carry):
            greet((self.group, lax.rem(self.place + i, self.parts)))
            return carry
        lax.fori_loop(1, self.parts, one, 0)
        pl.semaphore_wait(sem, self.parts)


def forward_kernel(replicas, parts, rows, lead, inner, images, *refs):
    own, note, emb, pixels, text, g_low = refs[:6]
    full, mod, vec, notes = refs[6:10]
    outs = refs[10:20]
    part, sums, text_total = refs[20:23]
    scratch = refs[23:36]
    (n_send, n_recv, m_send, m_recv, z_send, z_recv, y_send, y_recv, s_send, s_recv, x_send, x_recv, c_send, c_recv, own_sem) = refs[36:]
    me = Where(replicas, parts)
    span = me.span
    total, width = own.shape
    chunks = total // rows
    half = width // 2
    side = me.side
    thin = 128
    z_cols = pl.ds(pl.multiple_of(side * thin, thin), width - thin)
    a_cols = pl.ds(pl.multiple_of(side * half, half), half)
    thin_cols = pl.ds(pl.multiple_of((1 - side) * (width - thin), thin), thin)
    thin_out = pl.ds(pl.multiple_of(side * (width - thin), thin), thin)
    b_cols = pl.ds(pl.multiple_of((1 - side) * half, half), half)

    me.barrier()
    local = pltpu.make_async_copy(own, full.at[me.place], own_sem)
    local.start()

    def at(k):
        return pl.ds(pl.multiple_of(k * rows, 16), rows)

    def copy(src, dst, send, recv, device):
        return pltpu.make_async_remote_copy(src_ref=src, dst_ref=dst, send_sem=send, recv_sem=recv, device_id=device, device_id_type=MESH)

    def piece(k, z, y, cols, core=None):
        return full.at[me.index(z, y, me.core if core is None else core), at(k), cols]

    def z_copy(k, z, step, mine):
        src = own.at[at(k), z_cols] if mine else piece(k, z, me.y, z_cols)
        return copy(src, piece(k, z, me.y, z_cols), z_send.at[k, z, (step + 1) // 2], z_recv.at[k, z], me.device(z=me.z + step))

    def y_copy(k, z, turn, mine):
        src = own.at[at(k), a_cols] if mine else piece(k, z, me.y, a_cols)
        return copy(src, piece(k, z, me.y, a_cols), y_send.at[k, z, turn - 1], y_recv.at[k, z, turn - 1], me.device(y=lax.rem(me.y + turn, span)))

    def thin_copy(k, z):
        return copy(piece(k, z, me.y, thin_out), piece(k, z, me.y, thin_out), s_send.at[k, z], s_recv.at[k, z], me.device(flip=True))

    def x_copy(k, z, turn):
        y = lax.rem(me.y + turn, span)
        return copy(piece(k, z, y, a_cols), piece(k, z, y, a_cols), x_send.at[k, z, turn - 1], x_recv.at[k, z, turn - 1], me.device(flip=True))

    def core_copy(k, z, y, cols, mine=False):
        src = own.at[at(k), cols] if mine else piece(k, z, y, cols)
        return copy(src, piece(k, z, y, cols), c_send.at[k], c_recv.at[k], me.device(core=1 - me.core))

    everything = pl.ds(0, width)
    below = lambda s: (me.z - s >= 0, me.z - s)
    above = lambda s: (me.z + s < DEPTH, me.z + s)

    def start_own(k):
        @pl.when(me.z < DEPTH - 1)
        def _():
            z_copy(k, me.z, 1, True).start()
        @pl.when(me.z > 0)
        def _():
            z_copy(k, me.z, -1, True).start()
        for turn in range(1, span):
            y_copy(k, me.z, turn, True).start()
        core_copy(k, me.z, me.y, everything, True).start()

    def along_z(k, s):
        for (ok, z), step in ((below(s), 1), (above(s), -1)):
            @pl.when(ok)
            def _():
                z_copy(k, z, step, False).wait_recv()
                if s < DEPTH - 1:
                    more = me.z < DEPTH - 1 if step > 0 else me.z > 0
                    @pl.when(more)
                    def _():
                        z_copy(k, z, step, False).start()
                for turn in range(1, span):
                    y_copy(k, z, turn, False).start()
                thin_copy(k, z).start()
                core_copy(k, z, me.y, z_cols).start()

    def across(k, s):
        for ok, z in ((below(s), above(s)) if s else (below(0),)):
            @pl.when(ok)
            def _():
                for turn in range(1, span):
                    y_copy(k, z, turn, False).wait_recv()
                    x_copy(k, z, span - turn).start()
                    core_copy(k, z, lax.rem(me.y + span - turn, span), a_cols).start()

    def beside(k, s):
        for ok, z in ((below(s), above(s)) if s else (below(0),)):
            @pl.when(ok)
            def _():
                for turn in range(1, span):
                    x_copy(k, z, turn).wait_recv()
                    core_copy(k, z, lax.rem(me.y + turn, span), b_cols).start()

    def beside_thin(k, s):
        for ok, z in (below(s), above(s)):
            @pl.when(ok)
            def _():
                thin_copy(k, z).wait_recv()
                core_copy(k, z, me.y, thin_cols).start()

    def lane(k, wait):
        half = full.at[pl.ds(0, parts // 2), at(k)]
        whole = copy(half, half, c_send.at[k], c_recv.at[k], me.device(core=1 - me.core))
        whole.wait_recv() if wait else whole.wait_send()

    lane_in = functools.partial(lane, wait=True)

    table = Rows(parts, pixels.shape[1], width, text.shape[1], inner)
    forward = Forward(table, full, pixels, text, g_low, vec, mod, outs, scratch)
    ready = DEPTH + 1
    have = lambda which: (sum(which) - 1) // rows + ready
    t1 = max(have(table.first), 5)
    t2 = max(have(table.second), t1 + 4)
    t3 = max(have(table.attend_more), t2 + 2)
    t4 = max(t2 + 4, t3 + 1)
    t5 = max(have(table.text), t4 + 1)
    slots = max(chunks + ready, t5 + 1)

    def steps(t):
        def once(when, *work):
            @pl.when(t == when)
            def _():
                for one in work:
                    one()
        def many(when, until, each, work):
            @pl.when(jnp.logical_and(t >= when, t < until))
            def _():
                for i in range(each):
                    work((t - when) * each + i)
        once(0, forward.zero)
        for image in range(3):
            once(2 + image, functools.partial(forward.first_norm, image))
        once(5, modulate)
        once(t1, lambda: forward.load_first(jnp.int32(0)))
        many(t1, t1 + 2, 2, forward.first_conv)
        for image in range(3):
            once(t1 + 2 + image // 2, functools.partial(forward.mid_norm, image))
        once(t2, lambda: forward.load_second(jnp.int32(0)))
        many(t2, t2 + 4, 2, forward.second_conv)
        once(t3, forward.load_small)
        once(t4, forward.skip_product, forward.attended_grad)
        for image in range(3):
            once(t4 + image // 2, functools.partial(forward.last_norm, image))

    for k in range(min(lead, chunks)):
        start_own(k)

    last = 2 * (DEPTH - 1) + 3

    def slot(t, carry):
        def stage(delay, work):
            k = t - delay
            @pl.when(jnp.logical_and(k >= 0, k < chunks))
            def _():
                work(k)
        @pl.when(t + lead < chunks)
        def _():
            start_own(t + lead)
        for s in range(1, DEPTH):
            stage(s - 1, functools.partial(along_z, s=s))
        for s in range(DEPTH):
            stage(s + 0, functools.partial(across, s=s))
        for s in range(1, DEPTH):
            stage(s + 0, functools.partial(beside_thin, s=s))
        for s in range(DEPTH):
            stage(s + 1, functools.partial(beside, s=s))
        stage(ready, lane_in)
        steps(t)
        return carry

    def to_all(make):
        def one(i, carry):
            make(lax.rem(me.place + i, parts)).start()
            return carry
        lax.fori_loop(1, parts, one, 0)

    def wait_all(ref, send, recv):
        others = ref.at[pl.ds(0, parts - 1)]
        every = copy(others, others, send, recv, me.device(core=1 - me.core))
        every.wait_send()
        every.wait_recv()

    def modulate():
        wait_all(sums, m_send, m_recv)
        mod[...] = jnp.sum(sums[...], axis=0) + vec[V_EMB : V_EMB + 1, :]

    to_all(lambda far: copy(note.at[far], notes.at[me.place], n_send, n_recv, (me.group, far)))
    notes[me.place] = note[me.place]
    lax.fori_loop(0, 2, slot, 0)
    wait_all(notes, n_send, n_recv)
    vec[...] = jnp.zeros_like(vec)
    for row in range(V_OUT + 1):
        size = {V_IN_GAIN: pixels.shape[1], V_IN_SHIFT: pixels.shape[1], V_EMB: emb.shape[1]}.get(row, width)
        each = 128 * parts // size
        for block in range(size // 128):
            value = notes[block * each, images + row : images + row + 1, :].astype(jnp.float32)
            for i in range(1, each):
                value = value + notes[block * each + i, images + row : images + row + 1, :].astype(jnp.float32)
            vec[row : row + 1, block * 128 : (block + 1) * 128] = value
    rows_in = notes.shape[1]
    step = 512
    for at_col in range(0, emb.shape[1], step):
        cols = slice(at_col, at_col + step)
        product = jnp.dot(notes[...].reshape(parts * rows_in, 128), emb[:, cols], preferred_element_type=jnp.float32)
        part[:, :, cols] = product.reshape(parts, rows_in, step)[:, :8]
    to_all(lambda far: copy(part.at[far], sums.at[me.place], m_send, m_recv, (me.group, far)))
    sums[me.place] = part[me.place]
    local.wait()
    lax.fori_loop(2, slots, slot, 0)
    forward.load_text(jnp.int32(0))
    for i in range(3):
        forward.project(i)
    for q in range(4):
        forward.text_step(q, text_total)

    def finish(k, carry):
        for step, edge in ((1, me.z < DEPTH - 1), (-1, me.z > 0)):
            for s in range(DEPTH - 1):
                ok, z = below(s) if step > 0 else above(s)
                @pl.when(jnp.logical_and(ok, edge))
                def _():
                    z_copy(k, z, step, False).wait_send()
        for z in range(DEPTH):
            for turn in range(1, span):
                y_copy(k, z, turn, False).wait_send()
                x_copy(k, z, turn).wait_send()
            @pl.when(z != me.z)
            def _():
                thin_copy(k, z).wait_send()
        lane(k, False)
        return carry

    lax.fori_loop(0, chunks, finish, 0)
    forward.finish()


def forward_all(own, note, emb, pixels, text, g_low, images, inner, replicas, parts, rows=80, lead=3):
    total, width = own.shape
    chunks = total // rows
    span = parts // (2 * DEPTH)
    pix, pix_width = pixels.shape
    dma = lambda *shape: pltpu.SemaphoreType.DMA(shape)
    bf = lambda *shape: jax.ShapeDtypeStruct(shape, BF16)
    fl = lambda *shape: jax.ShapeDtypeStruct(shape, F32)
    hbm, vmem = pl.BlockSpec(memory_space=pl.ANY), pl.BlockSpec(memory_space=pltpu.VMEM)
    return pl.pallas_call(
        functools.partial(forward_kernel, replicas, parts, rows, lead, inner, images),
        out_shape=[
            bf(parts, total, width), fl(8, emb.shape[1]), fl(16, emb.shape[1]), bf(*note.shape),
            bf(3, PADDED, pix_width), bf(3, PADDED, width), fl(pix, width), fl(pix, width), fl(pix, width), bf(pix, width),
            bf(pix, 3 * inner), bf(3, TEXT_PAD, 2 * inner), bf(pix, inner), fl(24, width),
        ],
        in_specs=[hbm] + [vmem] * 5,
        out_specs=[hbm, vmem, vmem, vmem] + [hbm] * 6 + [vmem] * 4,
        scratch_shapes=[
            pltpu.VMEM((parts, 8, emb.shape[1]), F32),
            pltpu.VMEM((parts, 8, emb.shape[1]), F32),
            pltpu.VMEM((text.shape[0], width), F32),
            pltpu.VMEM((3, PADDED, pix_width), BF16), pltpu.VMEM((3, PADDED, width), BF16),
            pltpu.VMEM((pix, BLOCK), BF16), pltpu.VMEM((2, BLOCK, width), BF16),
            pltpu.VMEM((pix, width), F32), pltpu.VMEM((pix, width), F32), pltpu.VMEM((pix, width), BF16),
            pltpu.VMEM((width, 3 * inner), BF16), pltpu.VMEM((pix_width, width), BF16), pltpu.VMEM((inner, width), BF16),
            dma(2), dma(3), dma(6),
            dma(), dma(), dma(), dma(),
            dma(chunks, DEPTH, 2), dma(chunks, DEPTH),
            dma(chunks, DEPTH, span - 1), dma(chunks, DEPTH, span - 1),
            dma(chunks, DEPTH), dma(chunks, DEPTH),
            dma(chunks, DEPTH, span - 1), dma(chunks, DEPTH, span - 1),
            dma(chunks), dma(chunks), dma(),
        ],
        compiler_params=pltpu.CompilerParams(collective_id=0, has_side_effects=True, vmem_limit_bytes=60 << 20),
        name="forward_all",
    )(own, note, emb, pixels, text, g_low)


class Seat(Where):
    def bit(self, b):
        step = 1 << b
        group = self.group + step - 2 * step * lax.rem(self.group // step, 2)
        return (group, self.place)

    def meet(self):
        sem = pltpu.get_barrier_semaphore()
        count = self.replicas * self.parts
        def one(i, carry):
            far = lax.rem(self.group * self.parts + self.place + i, count)
            pl.semaphore_signal(sem, inc=1, device_id=(far // self.parts, lax.rem(far, self.parts)), device_id_type=MESH)
            return carry
        lax.fori_loop(1, count, one, 0)
        pl.semaphore_wait(sem, count - 1)


def norm_pull(image, factor, inverse, grad, hat, plain, crossed, put):
    count = SIZES[image]
    mean_plain = group_mean(plain * factor, count)[:1]
    mean_crossed = group_mean(crossed * factor, count)[:1]
    def one(i, rows, carry):
        value = inverse * (grad(rows) * factor - mean_plain - hat(rows) * mean_crossed)
        put(i, rows, value)
        return carry + (value[:8] + value[8:])
    total = over_rows(image, one, jnp.zeros(plain.shape, F32))
    return jnp.sum(total, axis=0, keepdims=True)


def two_sums(image, channels, pair):
    def add(i, rows, carry):
        a, b = pair(i, rows)
        return carry[0] + (a[:8] + a[8:]), carry[1] + (b[:8] + b[8:])
    zero = jnp.zeros((8, channels), F32)
    sums = over_rows(image, add, (zero, zero))
    return [jnp.broadcast_to(jnp.sum(part, axis=0, keepdims=True), (8, channels)) for part in sums]


def silu_pull(value):
    gate = jax.nn.sigmoid(value)
    return gate * (1.0 + value * (1.0 - gate))


G_IN_GAIN, G_IN_SHIFT, G_FIRST, G_MID_GAIN, G_MID_SHIFT, G_SECOND, G_ATTN_GAIN, G_ATTN_SHIFT, G_OUT = range(9)


class Backward:
    def __init__(self, rows, full, r_low, pixels, vec, mod, inverses, a1, a2, mid_hat, outs, scratch):
        self.rows, self.full, self.r_low, self.pixels, self.vec, self.mod, self.inverses = rows, full, r_low, pixels, vec, mod, inverses
        self.h_a1, self.h_a2, self.h_mid = a1, a2, mid_hat
        self.g_first, self.g_second, self.g_skip, self.grad_pixels = outs
        (self.a1, self.pad, self.hat, self.acc, self.acc1, self.c_low, self.patch, self.weight, self.stage, self.w_skip,
         self.vecs, self.mods, self.in_sem, self.w_sem, self.o_sem) = scratch

    def row(self, r, channels=1024):
        return self.vec[r : r + 1, :channels]

    def add_row(self, r, value):
        width = value.shape[1]
        self.vecs[r : r + 1, :width] = self.vecs[r : r + 1, :width] + value[:1]

    def fetch(self):
        for i, (src, dst) in enumerate(((self.h_a2, self.pad), (self.h_a1, self.a1), (self.h_mid, self.hat))):
            pltpu.make_async_copy(src, dst, self.in_sem.at[i]).start()
        start, size = self.rows.skip
        def one(f, carry):
            pltpu.make_async_copy(self.full.at[f, pl.ds(start, size)], self.w_skip.at[pl.ds(pl.multiple_of(f * size, SUB), size)], self.in_sem.at[3]).start()
            return carry
        lax.fori_loop(0, self.rows.parts, one, 0)

    def arrived(self, i):
        waited((self.pad, self.a1, self.hat, self.w_skip)[i], self.in_sem.at[i])

    def put_out(self, dst, first, count):
        span, size = dst.shape[1], dst.shape[3]
        for i in range(count):
            f = first + i
            pltpu.make_async_copy(
                self.stage.at[pl.ds(i * size, size)],
                dst.at[f // (2 * span), lax.rem(f // 2, span), lax.rem(f, 2)],
                self.o_sem,
            ).start()

    def weight_grad(self, q, pad, count, grad, dst):
        for known in range(count):
            @pl.when(q == known)
            def _():
                gather_block(pad, known, self.patch)
        @pl.when(q > 0)
        def _():
            self.stored()
        for col in range(0, 1024, 256):
            cols = slice(col, col + 256)
            self.stage[:, cols] = lax.dot_general(self.patch[...], grad[:, cols], TN, preferred_element_type=F32).astype(BF16)
        each = BLOCK // dst.shape[3]
        self.put_out(dst, q * each, each)

    def second_weight(self, q):
        self.weight_grad(q, self.pad, 9 * self.pad.shape[2] // BLOCK, self.r_low, self.g_second)

    def first_weight(self, q):
        self.weight_grad(q, self.a1, 9 * self.a1.shape[2] // BLOCK, self.c_low, self.g_first)

    def stored(self, size=BLOCK):
        waited(self.stage.at[pl.ds(0, size)], self.o_sem)

    def skip_weight(self):
        size = self.pixels.shape[1]
        for col in range(0, 1024, 512):
            cols = slice(col, col + 512)
            self.stage[:size, cols] = lax.dot_general(self.pixels[...], self.r_low[:, cols], TN, preferred_element_type=F32).astype(BF16)
        self.put_out(self.g_skip, jnp.int32(0), self.rows.parts)
        self.stored(size)

    def pad_residual(self):
        zero_edges(self.pad)
        for image in range(3):
            def one(i, rows, carry):
                store_padded(self.pad, image, i, self.r_low[rows, :].astype(F32))
                return carry
            over_rows(image, one, 0)

    def load_tap(self, which, height, tap):
        start, size = which
        for known in range(9):
            @pl.when(tap == known)
            def _():
                at = known * height
                while at < (known + 1) * height:
                    shard, inside = divmod(at, size)
                    count = min(size - inside, (known + 1) * height - at)
                    pltpu.make_async_copy(
                        self.full.at[shard, pl.ds(start + inside, count)],
                        self.weight.at[known % 2, pl.ds(at - known * height, count)],
                        self.w_sem.at[known % 2],
                    ).start()
                    at += count

    def pull_step(self, tap, which, height, acc):
        @pl.when(tap + 1 < 9)
        def _():
            self.load_tap(which, height, tap + 1)
        @pl.when(tap == 0)
        def _():
            acc[...] = jnp.zeros_like(acc)
        for known in range(9):
            @pl.when(tap == known)
            def _():
                for image in range(3):
                    self.patch[STARTS[image] : STARTS[image] + SIZES[image], :1024] = shifted(self.pad, known, image, slice(0, 1024), True)
        par = lax.rem(tap, 2)
        waited(self.weight.at[par, pl.ds(0, height)], self.w_sem.at[par])
        for col in range(0, height, 512):
            cols = slice(col, col + 512)
            acc[:, cols] = acc[:, cols] + lax.dot_general(self.patch[:, :1024], self.weight[par, cols, :], NT, preferred_element_type=F32)

    def load_second(self):
        self.load_tap(self.rows.second, 1024, jnp.int32(0))

    def second_pull(self, tap):
        self.pull_step(tap, self.rows.second, 1024, self.acc)

    def load_first(self):
        self.load_tap(self.rows.first, self.pixels.shape[1], jnp.int32(0))

    def first_pull(self, tap):
        self.pull_step(tap, self.rows.first, self.pixels.shape[1], self.acc1)

    def mid_pull(self, image):
        acc, hat, channels = self.acc, self.hat, 1024
        if image == 0:
            self.vecs[...] = jnp.zeros_like(self.vecs)
            self.mods[...] = jnp.zeros_like(self.mods)
            zero_edges(self.pad)
        scale, shift = 1.0 + self.mod[image : image + 1, :channels], self.mod[image : image + 1, channels:]
        gain, bias = self.row(V_MID_GAIN), self.row(V_MID_SHIFT)
        factor, lift = gain * scale, bias * scale + shift
        def pair(i, rows):
            h = hat[rows, :]
            grad = acc[rows, :] * silu_pull(h * factor + lift)
            acc[rows, :] = grad
            return grad, grad * h
        plain, crossed = two_sums(image, channels, pair)
        def put(i, rows, value):
            store_padded(self.pad, image, i, value)
            self.c_low[rows, :] = value.astype(BF16)
        inverse = self.inverses[3 + image : 4 + image, :]
        total = norm_pull(image, factor, inverse, lambda rows: acc[rows, :], lambda rows: hat[rows, :], plain, crossed, put)
        self.add_row(G_FIRST, total)
        self.add_row(G_MID_GAIN, crossed * scale)
        self.add_row(G_MID_SHIFT, plain * scale)
        self.mods[image : image + 1, :channels] = (crossed * gain + plain * bias)[:1]
        self.mods[image : image + 1, channels:] = plain[:1]

    def first_norm_pull(self, image):
        acc, pixels = self.acc1, self.pixels
        channels = pixels.shape[1]
        inverse, center = self.inverses[image : image + 1, :channels], self.inverses[16 + image : 17 + image, :channels]
        gain, bias = self.row(V_IN_GAIN, channels), self.row(V_IN_SHIFT, channels)
        hat = lambda rows: (pixels[rows, :].astype(F32) - center) * inverse
        def pair(i, rows):
            h = hat(rows)
            grad = acc[rows, :] * silu_pull(h * gain + bias)
            acc[rows, :] = grad
            return grad, grad * h
        plain, crossed = two_sums(image, channels, pair)
        def put(i, rows, value):
            self.grad_pixels[rows, :] = self.grad_pixels[rows, :] + value
        norm_pull(image, gain, inverse, lambda rows: acc[rows, :], hat, plain, crossed, put)
        self.add_row(G_IN_GAIN, crossed)
        self.add_row(G_IN_SHIFT, plain)

    def skip_pull(self):
        self.grad_pixels[...] = lax.dot_general(self.r_low[...], self.w_skip[...], NT, preferred_element_type=F32)


def reduce_kernel(replicas, parts, rows, spans, lead, ring, nrc, rb, lag, inner, text_dim, images, known, *refs):
    early = refs[:known]
    full, r_low, pixels, vec, mod, inverses, a1, a2, mid_hat, emb_note, more = refs[known : known + 11]
    out, notes, g_first, g_second, g_skip, grad_pixels = refs[known + 11 : known + 17]
    rest = refs[known + 17 :]
    (hold, rc, xr, yr, zu, zd, fr, tb, shared, target, shared32, target32) = rest[:12]
    scratch = rest[12:27]
    (l_sem, c_send, c_recv, x_send, x_recv, y_send, y_recv,
     u_send, u_recv, d_send, d_recv, f_send, f_recv, n_send, n_recv, free, x_free, y_free, u_free, d_free) = rest[27:]
    me = Seat(replicas, parts)
    span = me.span
    width = out.shape[1]
    chunks = out.shape[0] // rows
    side = me.side
    bits = replicas.bit_length() - 1
    apart, joint = 3 * width // 8, 5 * width // 8
    table = Rows(parts, pixels.shape[1], width, text_dim, inner)
    back = Backward(table, full, r_low, pixels, vec, mod, inverses, a1, a2, mid_hat, (g_first, g_second, g_skip, grad_pixels), scratch)
    grads = list(early) + [g_second, g_skip, g_first]

    me.meet()
    back.fetch()

    def copy(src, dst, send, recv, device):
        return pltpu.make_async_remote_copy(src_ref=src, dst_ref=dst, send_sem=send, recv_sem=recv, device_id=device, device_id_type=MESH)

    def give(sem, device):
        pl.semaphore_signal(sem, inc=1, device_id=device, device_id_type=MESH)

    def take(sem, k, size):
        @pl.when(k >= size)
        def _():
            pl.semaphore_wait(sem, 1)

    def core_copy(k, src):
        return copy(src, rc.at[lax.rem(k, nrc)], c_send.at[k], c_recv.at[lax.rem(k, nrc)], me.device(core=1 - me.core))

    def begin(k):
        take(free, k, nrc)
        for grad, (lo, hi) in zip(grads, spans):
            @pl.when(jnp.logical_and(k >= lo, k < hi))
            def _():
                at = pl.ds(pl.multiple_of((k - lo) * rows, 16), rows)
                slot = lax.rem(k, ring)
                pltpu.make_async_copy(grad.at[:, :, me.core, at, :], hold.at[slot], l_sem.at[slot]).start()
                core_copy(k, grad.at[:, :, 1 - me.core, at, :]).start()

    def x_copy(k, turn):
        slot = lax.rem(k, ring)
        cols = pl.ds(pl.multiple_of((1 - side) * joint, 128), apart)
        return copy(hold.at[slot, :, lax.rem(me.y + turn, span), :, cols], xr.at[lax.rem(k, rb), turn - 1], x_send.at[k, turn - 1], x_recv.at[k, turn - 1], me.bit(0))

    def y_copy(k, turn):
        slot = lax.rem(k, ring)
        cols = pl.ds(pl.multiple_of(side * apart, 128), joint)
        return copy(hold.at[slot, :, lax.rem(me.y + turn, span), :, cols], yr.at[lax.rem(k, rb), turn - 1], y_send.at[k, turn - 1], y_recv.at[k, turn - 1], me.device(y=lax.rem(me.y + turn, span)))

    def up_copy(k, z):
        slot = lax.rem(k, ring)
        return copy(hold.at[slot, z + 1 : DEPTH, me.y], zu.at[lax.rem(k, rb), 0 : DEPTH - 1 - z], u_send.at[k], u_recv.at[k], me.device(z=me.z + 1))

    def down_copy(k, z):
        slot = lax.rem(k, ring)
        return copy(hold.at[slot, 0:z, me.y], zd.at[lax.rem(k, rb), 0:z], d_send.at[k], d_recv.at[k], me.device(z=me.z - 1))

    def f_copy(k, b):
        slot = lax.rem(k, ring)
        src = hold.at[slot, me.z, me.y] if b == 0 else tb.at[b - 1, k]
        return copy(src, fr.at[b, k], f_send.at[b, k], f_recv.at[b, k], me.bit(b))

    def fold_core(k):
        slot = lax.rem(k, ring)
        waited(hold.at[slot], l_sem.at[slot])
        core_copy(k, rc.at[lax.rem(k, nrc)]).wait_recv()
        hold[slot] = hold[slot] + rc[lax.rem(k, nrc)]
        @pl.when(k + nrc < chunks)
        def _():
            give(free, me.device(core=1 - me.core))
        for turn in range(1, span):
            take(x_free.at[turn - 1], k, rb)
            x_copy(k, turn).start()

    def fold_x(k):
        slot = lax.rem(k, ring)
        for turn in range(1, span):
            x_copy(k, turn).wait_recv()
            y = lax.rem(me.y + turn, span)
            for s in range(2):
                @pl.when(side == s)
                def _():
                    cols = slice(0, apart) if s == 0 else slice(joint, width)
                    hold[slot, :, y, :, cols] = hold[slot, :, y, :, cols] + xr[lax.rem(k, rb), turn - 1]
            @pl.when(k + rb < chunks)
            def _():
                give(x_free.at[turn - 1], me.bit(0))
            take(y_free.at[turn - 1], k, rb)
            y_copy(k, turn).start()

    def fold_y(k):
        slot = lax.rem(k, ring)
        for turn in range(1, span):
            y_copy(k, turn).wait_recv()
            for s in range(2):
                @pl.when(side == s)
                def _():
                    cols = slice(0, joint) if s == 0 else slice(apart, width)
                    hold[slot, :, me.y, :, cols] = hold[slot, :, me.y, :, cols] + yr[lax.rem(k, rb), turn - 1]
            @pl.when(k + rb < chunks)
            def _():
                give(y_free.at[turn - 1], me.device(y=lax.rem(me.y + span - turn, span)))

    def hop(k, h):
        slot = lax.rem(k, ring)
        @pl.when(me.z == h)
        def _():
            if h > 0:
                up_copy(k, h - 1).wait_recv()
                hold[slot, h:, me.y] = hold[slot, h:, me.y] + zu[lax.rem(k, rb), 0 : DEPTH - h]
                @pl.when(k + rb < chunks)
                def _():
                    give(u_free, me.device(z=me.z - 1))
            if h < DEPTH - 1:
                take(u_free, k, rb)
                up_copy(k, h).start()
        z = DEPTH - 1 - h
        @pl.when(me.z == z)
        def _():
            if h > 0:
                down_copy(k, z + 1).wait_recv()
                hold[slot, : z + 1, me.y] = hold[slot, : z + 1, me.y] + zd[lax.rem(k, rb), 0 : z + 1]
                @pl.when(k + rb < chunks)
                def _():
                    give(d_free, me.device(z=me.z + 1))
            if h < DEPTH - 1:
                take(d_free, k, rb)
                down_copy(k, z).start()

    def finish(k, b):
        slot = lax.rem(k, ring)
        f_copy(k, b).wait_recv()
        before = hold[slot, me.z, me.y] if b == 0 else tb[b - 1, k]
        total = before.astype(F32) + fr[b, k].astype(F32)
        if b == bits - 1:
            out[pl.ds(pl.multiple_of(k * rows, 16), rows), :] = total
        else:
            tb[b, k] = total.astype(BF16)
            f_copy(k, b + 1).start()

    def retire(k):
        core_copy(k, rc.at[0]).wait_send()
        for turn in range(1, span):
            x_copy(k, turn).wait_send()
            y_copy(k, turn).wait_send()
        for z in range(DEPTH):
            @pl.when(me.z == z)
            def _():
                if z < DEPTH - 1:
                    up_copy(k, z).wait_send()
                if z > 0:
                    down_copy(k, z).wait_send()
        for b in range(bits):
            f_copy(k, b).wait_send()

    count = replicas * parts
    mine = me.group * parts + me.place
    tall = shared.shape[0]

    def note_copies(far):
        device = (far // parts, lax.rem(far, parts))
        return (
            copy(shared, notes.at[mine, pl.ds(0, tall)], n_send, n_recv, device),
            copy(target.at[lax.rem(far, parts)], notes.at[mine, pl.ds(tall, 16)], n_send, n_recv, device),
        )

    def tell():
        back.vecs[:, :] = back.vecs[:, :] + more[...]
        target32[...] = emb_note[...]
        each = 2 * width // 128
        for image in range(images):
            for j in range(each):
                shared32[image * each + j : image * each + j + 1, :] = back.mods[image : image + 1, j * 128 : (j + 1) * 128]
        shared[...] = shared32[...].astype(BF16)
        for row in range(G_OUT + 1):
            size = (pixels.shape[1] if row in (G_IN_GAIN, G_IN_SHIFT) else width) // parts
            for f in range(parts):
                block = f * size // 128
                target32[f, images + row : images + row + 1, :] = back.vecs[row : row + 1, block * 128 : (block + 1) * 128]
        target[...] = target32[...].astype(BF16)
        def send(i, carry):
            for one in note_copies(lax.rem(mine + i, count)):
                one.start()
            return carry
        lax.fori_loop(1, count, send, 0)
        locals_ = (
            pltpu.make_async_copy(shared, notes.at[mine, pl.ds(0, tall)], l_sem.at[ring]),
            pltpu.make_async_copy(target.at[me.place], notes.at[mine, pl.ds(tall, 16)], l_sem.at[ring + 1]),
        )
        for one in locals_:
            one.start()
        for one in locals_:
            one.wait()

    lo_second, lo_skip, lo_first = (spans[known + i][0] - lead for i in range(3))
    n2, n1 = 9 * width // BLOCK, 9 * pixels.shape[1] // BLOCK
    s0 = n2 + 1
    s1 = s0 + 9
    s2 = s1 + 3
    s3 = s2 + n1 + 1
    s4 = s3 + 5
    assert s0 <= lo_second and s2 + n1 < lo_first
    last = max(chunks + (2 + DEPTH + bits) * lag + 1, s4 + 5)

    def steps(t):
        def once(when, *work):
            @pl.when(t == when)
            def _():
                for one in work:
                    one()
        def many(when, until, each, limit, work):
            @pl.when(jnp.logical_and(t >= when, t < until))
            def _():
                for i in range(each):
                    at = (t - when) * each + i
                    if limit % each:
                        pl.when(at < limit)(lambda: work(at))
                    else:
                        work(at)
        once(0, lambda: back.arrived(0))
        many(0, n2, 1, n2, back.second_weight)
        once(n2, back.stored, back.skip_weight, back.pad_residual, back.load_second)
        many(s0, s1, 1, 9, back.second_pull)
        once(s1, lambda: back.arrived(1), lambda: back.arrived(2), lambda: back.arrived(3))
        for image in range(3):
            once(s1 + image, functools.partial(back.mid_pull, image))
        many(s2, s2 + n1, 1, n1, back.first_weight)
        once(s2 + n1, back.stored, back.load_first)
        many(s3, s4, 2, 9, back.first_pull)
        once(s4, back.skip_pull)
        for image in range(3):
            once(s4 + 1 + image, functools.partial(back.first_norm_pull, image))
        once(s4 + 4, tell)

    for k in range(lead):
        begin(jnp.int32(k))

    first_f = (2 + DEPTH) * lag

    def slot_work(t, carry):
        def stage(delay, work):
            k = t - delay
            @pl.when(jnp.logical_and(k >= 0, k < chunks))
            def _():
                work(k)
        for h in range(DEPTH - 1, 0, -1):
            stage((2 + h) * lag, functools.partial(hop, h=h))
        stage((1 + DEPTH) * lag, lambda k: f_copy(k, 0).start())
        def pair(k):
            fold_y(k)
            hop(k, 0)
        stage(2 * lag, pair)
        stage(lag, fold_x)
        stage(0, fold_core)
        for b in range(bits):
            stage(first_f + b * lag, functools.partial(finish, b=b))
        stage(first_f + bits * lag, retire)
        @pl.when(t + lead < chunks)
        def _():
            begin(t + lead)
        steps(t)
        return carry

    lax.fori_loop(0, last, slot_work, 0)
    others = notes.at[pl.ds(0, count - 1)]
    every = copy(others, others, n_send, n_recv, me.device(core=1 - me.core))
    every.wait_send()
    every.wait_recv()


def reduce_all(early, full, r_low, pixels, vec, mod, inverses, a1, a2, mid_hat, emb_note, more, inner, text_dim, images, replicas, parts, rows, lead=2, nrc=3, lag=2, rb=8):
    span = parts // (2 * DEPTH)
    pix, width = r_low.shape
    pix_width = pixels.shape[1]
    spans, at = [], 0
    views = []
    for size in [grad.shape[0] // parts for grad in early] + [9 * width // parts, pix_width // parts, 9 * pix_width // parts]:
        spans.append((at // rows, (at + size) // rows))
        at += size
    for grad in early:
        views.append(grad.reshape(DEPTH, span, 2, grad.shape[0] // parts, width))
    total = at
    chunks = total // rows
    bits = replicas.bit_length() - 1
    ring = lead + (2 + DEPTH + bits) * lag + 2
    dma = lambda *shape: pltpu.SemaphoreType.DMA(shape)
    reg = lambda *shape: pltpu.SemaphoreType.REGULAR(shape)
    vm = lambda *shape: pltpu.VMEM(shape, BF16)
    vf = lambda *shape: pltpu.VMEM(shape, F32)
    bf = lambda *shape: jax.ShapeDtypeStruct(shape, BF16)
    fl = lambda *shape: jax.ShapeDtypeStruct(shape, F32)
    hbm, vmem = pl.BlockSpec(memory_space=pl.ANY), pl.BlockSpec(memory_space=pltpu.VMEM)
    tall = images * 2 * width // 128
    return pl.pallas_call(
        functools.partial(reduce_kernel, replicas, parts, rows, spans, lead, ring, nrc, rb, lag, inner, text_dim, images, len(early)),
        out_shape=[
            fl(total, width), bf(replicas * parts, tall + 16, 128),
            *(bf(DEPTH, span, 2, size // parts, width) for size in (9 * pix_width, 9 * width, pix_width)), fl(pix, pix_width),
        ],
        in_specs=[hbm] * (len(early) + 1) + [vmem] * 5 + [hbm] * 3 + [vmem] * 2,
        out_specs=[vmem, hbm, hbm, hbm, hbm, vmem],
        scratch_shapes=[
            vm(ring, DEPTH, span, rows, width),
            vm(nrc, DEPTH, span, rows, width),
            vm(rb, span - 1, DEPTH, rows, 3 * width // 8),
            vm(rb, span - 1, DEPTH, rows, 5 * width // 8),
            vm(rb, DEPTH - 1, rows, width),
            vm(rb, DEPTH - 1, rows, width),
            vm(bits, chunks, rows, width),
            vm(max(bits - 1, 1), chunks if bits > 1 else 1, rows, width),
            vm(tall, 128), vm(parts, 16, 128), vf(tall, 128), vf(parts, 16, 128),
            vm(3, PADDED, pix_width), vm(3, PADDED, width), vf(pix, width), vf(pix, width), vf(pix, pix_width), vm(pix, width),
            vm(pix, BLOCK), vm(2, 1024, width), vm(BLOCK, width), vm(pix_width, width), vf(16, width), vf(8, 2 * width),
            dma(4), dma(2), dma(),
            dma(ring + 2),
            dma(chunks), dma(nrc),
            dma(chunks, span - 1), dma(chunks, span - 1),
            dma(chunks, span - 1), dma(chunks, span - 1),
            dma(chunks), dma(chunks), dma(chunks), dma(chunks),
            dma(bits, chunks), dma(bits, chunks),
            pltpu.SemaphoreType.DMA, pltpu.SemaphoreType.DMA,
            pltpu.SemaphoreType.REGULAR, reg(span - 1), reg(span - 1), pltpu.SemaphoreType.REGULAR, pltpu.SemaphoreType.REGULAR,
        ],
        compiler_params=pltpu.CompilerParams(collective_id=1, has_side_effects=True, vmem_limit_bytes=62 << 20),
        name="reduce_all",
    )(*views, full, r_low, pixels, vec, mod, inverses, a1, a2, mid_hat, emb_note, more)


def middle_kernel(parts, inner, text_dim, triple, text_pair, mask, grad_attended, g_low, normed, hats, residual, text, pres, vec, inverses, full,
                  block_output, r_low, g_out, g_attend, g_more, g_text, more, attended, grad_triple, grad_text, rows_grad, w_attend, w_out, stage, sems, o_sem):
    width = g_low.shape[1]
    table = Rows(parts, 512, width, text_dim, inner)
    start, size = table.out
    def one(f, carry):
        pltpu.make_async_copy(full.at[f, pl.ds(start, size)], w_out.at[pl.ds(pl.multiple_of(f * size, SUB), size)], sems.at[0]).start()
        return carry
    lax.fori_loop(0, parts, one, 0)
    table.load_attend(full, w_attend, sems.at[1])

    lane = lax.broadcasted_iota(jnp.int32, (1, 2 * HEAD), 1)
    nt, tn = ((1,), (1,)), ((0,), (0,))
    scale = HEAD ** -0.5

    def heads(pair, carry):
        at = lambda shift: pl.ds(pl.multiple_of(pair * 2 * HEAD + shift * inner, 128), 2 * HEAD)
        for image in range(3):
            rows = pl.ds(STARTS[image], SIZES[image])
            q, k, v, go = triple[rows, at(0)], triple[rows, at(1)], triple[rows, at(2)], grad_attended[rows, at(0)]
            tk, tv = text_pair[image, :, at(0)], text_pair[image, :, at(1)]
            keep = mask[image : image + 1, :]
            results = []
            for head in range(2):
                own = (lane >= HEAD) if head else (lane < HEAD)
                qh = jnp.where(own, q, jnp.zeros_like(q))
                gh = jnp.where(own, go, jnp.zeros_like(go))
                sp = dot(qh, k, nt) * scale
                st = dot(qh, tk, nt) * scale
                st = jnp.where(keep == 1, st, jnp.where(keep == 0, -1000000000.0, -jnp.inf))
                peak = jnp.maximum(jnp.max(sp, axis=1, keepdims=True), jnp.max(st, axis=1, keepdims=True))
                ep, et = jnp.exp(sp - peak), jnp.exp(st - peak)
                inv = 1.0 / (jnp.sum(ep, axis=1, keepdims=True) + jnp.sum(et, axis=1, keepdims=True))
                pp, pt = ep * inv, et * inv
                ppl, ptl = pp.astype(BF16), pt.astype(BF16)
                out = dot(ppl, v) + dot(ptl, tv)
                dv = dot(ppl, go, tn)
                dtv = dot(ptl, go, tn)
                dpp, dpt = dot(gh, v, nt), dot(gh, tv, nt)
                mean = jnp.sum(dpp * pp, axis=1, keepdims=True) + jnp.sum(dpt * pt, axis=1, keepdims=True)
                dsp = (pp * (dpp - mean) * scale).astype(BF16)
                dst = (pt * (dpt - mean) * scale).astype(BF16)
                results.append((out, dot(dsp, k) + dot(dst, tk), dot(dsp, q, tn), dv, dot(dst, q, tn), dtv))
            merged = [jnp.where(lane < HEAD, a, b).astype(BF16) for a, b in zip(*results)]
            attended[rows, at(0)] = merged[0]
            for i in range(3):
                grad_triple[rows, at(i)] = merged[1 + i]
            text_rows = pl.ds(image * TEXT_ROWS, TEXT_ROWS)
            for i in range(2):
                grad_text[text_rows, at(i)] = merged[4 + i][:TEXT_ROWS]
        return carry

    lax.fori_loop(0, inner // (2 * HEAD), heads, 0)

    def text_block(q, carry):
        @pl.when(q > 0)
        def _():
            waited(stage, o_sem)
        for col in range(0, width, 512):
            cols = slice(col, col + 512)
            stage[:, cols] = lax.dot_general(text[:, pl.ds(pl.multiple_of(q * 1024, 128), 1024)], grad_text[:, cols], TN, preferred_element_type=F32).astype(BF16)
        pltpu.make_async_copy(stage, g_text.at[pl.ds(pl.multiple_of(q * 1024, 128), 1024)], o_sem).start()
        return carry

    lax.fori_loop(0, text_dim // 1024, text_block, 0)

    waited(w_out, sems.at[0])
    bias = vec[V_OUT : V_OUT + 1, :width]
    for image in range(3):
        rows = pl.ds(STARTS[image], SIZES[image])
        block_output[rows, :] = (
            pres[image : image + 1, :] * (residual[rows, :] + (dot(attended[rows, :], w_out[...]) + bias))
        ).astype(BF16)
    for col in range(0, width, 512):
        cols = slice(col, col + 512)
        g_out[:, cols] = lax.dot_general(attended[...], g_low[:, cols], TN, preferred_element_type=F32).astype(BF16)
        g_attend[:, cols] = lax.dot_general(normed[...], grad_triple[:, cols], TN, preferred_element_type=F32).astype(BF16)
    last = lax.dot_general(normed[...], grad_triple[:, width:], TN, preferred_element_type=F32).astype(BF16)
    half = width // parts // 2
    for f in range(parts):
        for i in range(2):
            g_more[f * half : (f + 1) * half, 512 * i : 512 * (i + 1)] = last[(2 * f + i) * half : (2 * f + i + 1) * half]
    waited(w_attend, sems.at[1])
    for col in range(0, width, 512):
        cols = slice(col, col + 512)
        rows_grad[:, cols] = lax.dot_general(grad_triple[...], w_attend[cols, :], NT, preferred_element_type=F32)

    more[...] = jnp.zeros_like(more)
    gain = vec[V_ATTN_GAIN : V_ATTN_GAIN + 1, :width]
    for image in range(3):
        def pair(i, rows):
            grad = rows_grad[rows, :]
            return grad, grad * hats[rows, :]
        plain, crossed = two_sums(image, width, pair)
        def put(i, rows, value):
            rows_grad[rows, :] = value + g_low[rows, :].astype(F32)
        norm_pull(image, gain, inverses[6 + image : 7 + image, :], lambda rows: rows_grad[rows, :], lambda rows: hats[rows, :], plain, crossed, put)
        def ends(i, rows):
            value = rows_grad[rows, :]
            r_low[rows, :] = value.astype(BF16)
            return value, g_low[rows, :].astype(F32)
        total, outer = two_sums(image, width, ends)
        for row, value in ((G_ATTN_GAIN, crossed), (G_ATTN_SHIFT, plain), (G_SECOND, total), (G_OUT, outer)):
            more[row : row + 1, :] = more[row : row + 1, :] + value[:1]
    waited(stage, o_sem)


def middle(triple, text_pair, mask, grad_attended, g_low, normed, hats, residual, text, pres, vec, inverses, full, parts, inner, text_dim):
    pix, width = g_low.shape
    bf = lambda *shape: jax.ShapeDtypeStruct(shape, BF16)
    vm = lambda *shape: pltpu.VMEM(shape, BF16)
    hbm, vmem = pl.BlockSpec(memory_space=pl.ANY), pl.BlockSpec(memory_space=pltpu.VMEM)
    return pl.pallas_call(
        functools.partial(middle_kernel, parts, inner, text_dim),
        out_shape=[bf(pix, width), bf(pix, width), bf(inner, width), bf(width, width), bf(width // 2, width), bf(text_dim, width), jax.ShapeDtypeStruct((16, width), F32)],
        in_specs=[vmem] * 12 + [hbm],
        out_specs=[vmem] * 5 + [hbm, vmem],
        scratch_shapes=[
            vm(pix, inner), vm(pix, 3 * inner), vm(text.shape[0], 2 * inner), pltpu.VMEM((pix, width), F32),
            vm(width, 3 * inner), vm(inner, width), vm(1024, width),
            pltpu.SemaphoreType.DMA((2,)), pltpu.SemaphoreType.DMA(()),
        ],
        compiler_params=pltpu.CompilerParams(vmem_limit_bytes=60 << 20),
        name="middle",
    )(triple, text_pair, mask, grad_attended, g_low, normed, hats, residual, text, pres, vec, inverses, full)


def fold_attend(part, width):
    more = part[..., width:]
    half = part.shape[-2] // 2
    return [part[..., :width], jnp.concatenate([more[..., :half, :], more[..., half:, :]], -1)]


def unfold_attend(part, columns):
    blocks, rows, width = part.shape
    size = rows * 2 // 3
    more = part[:, size:]
    half = columns - width
    return jnp.concatenate([part[:, :size], jnp.concatenate([more[..., :half], more[..., half:]], 1)], -1).reshape(blocks * size, columns)


def body(
    pixels,
    embedding,
    text_states,
    text_mask,
    occupancy,
    cotangent,
    in_gain,
    in_shift,
    conv_first,
    first_bias,
    emb_weight,
    emb_bias,
    mid_gain,
    mid_shift,
    conv_second,
    second_bias,
    skip_weight,
    skip_bias,
    attn_gain,
    attn_shift,
    attend_weight,
    text_weight,
    out_weight,
    out_bias,
):
    place = lax.axis_index("fsdp")
    group = lax.axis_index("dp")
    parts = lax.axis_size("fsdp")
    replicas = lax.axis_size("dp")
    depth = emb_weight.shape[0]
    images_here = embedding.shape[0]
    emb_act = jax.nn.silu(embedding.astype(F32)).astype(BF16)
    emb_cut = emb_act.reshape(images_here, parts, depth).transpose(1, 0, 2)
    emb_cut = jnp.pad(emb_cut, ((0, 0), (0, 0), (0, 128 - depth)))

    vectors = (in_gain, in_shift, first_bias, emb_bias, mid_gain, mid_shift, second_bias, skip_bias, attn_gain, attn_shift, out_bias)
    lane = lax.broadcasted_iota(jnp.int32, (1, 128), 1)
    lines = []
    for vector in vectors:
        size = vector.shape[0]
        wide = jnp.tile(vector, 128 // size).reshape(1, 128)
        lines.append(jnp.where(lane // size == lax.rem(place, 128 // size), wide, jnp.zeros_like(wide)))
    room = 16 - images_here - len(lines)
    flat = jnp.concatenate(lines + [jnp.zeros((room, 128), BF16)] if room else lines, 0)[None]
    note = jnp.concatenate([emb_cut, jnp.broadcast_to(flat, (parts,) + flat.shape[1:])], 1)
    channels = skip_weight.shape[1]
    inner = out_weight.shape[0] * parts
    own = jnp.concatenate([conv_first, conv_second, skip_weight, out_weight] + fold_attend(attend_weight, channels) + [text_weight], 0)
    present = jnp.concatenate(
        [jnp.broadcast_to(occupancy[0, i].astype(F32), (SIZES[i], 1)) for i in range(3)], 0
    )
    grad_out = cotangent.astype(F32) * present
    grad_low = grad_out.astype(BF16)
    text_len = text_states.shape[1]
    text_rows = jnp.pad(text_states, ((0, 0), (0, TEXT_ROWS - text_len), (0, 0))).reshape(3 * TEXT_ROWS, -1)
    (full, modulation, vec, _, act1, act2, mid_hats, residual, hats, normed, triple, text_pair, grad_attended, inverses) = forward_all(
        own, note, jnp.pad(emb_weight, ((0, 128 - depth), (0, 0))), pixels, text_rows, grad_low, images_here, inner, replicas, parts)
    scale, shift = modulation[:images_here, :channels], modulation[:images_here, channels:]
    mask = jnp.pad(
        (text_mask > 0).astype(jnp.int32), ((0, 0), (0, TEXT_PAD - text_len)), constant_values=2
    )
    pres = jnp.broadcast_to(occupancy[0].astype(F32)[:, None], (images_here, channels))
    block_output, r_low, g_out, g_attend, g_more, g_text, more = middle(
        triple, text_pair, mask, grad_attended, grad_low, normed, hats, residual, text_rows, pres, vec, inverses, full, parts, inner, text_states.shape[2]
    )
    emb_note = jnp.pad(emb_cut.astype(F32), ((0, 0), (0, 16 - images_here), (0, 0)))
    owned, notes, _, _, _, grad_pixels = reduce_all(
        [g_text, g_out, g_attend, g_more], full, r_low, pixels, vec, modulation, inverses, act1, act2, mid_hats, emb_note, more,
        inner, text_states.shape[2], images_here, replicas, parts, 512 // parts,
    )
    cuts = []
    at = 0
    for size in (text_weight.shape[0], out_weight.shape[0], 3 * attend_weight.shape[0] // 2, conv_second.shape[0], skip_weight.shape[0], conv_first.shape[0]):
        cuts.append(owned[at : at + size])
        at += size
    grad_text_weight, grad_out_weight, grad_attend_weight, grad_conv_second, grad_skip_weight, grad_conv_first = cuts
    grad_attend_weight = unfold_attend(grad_attend_weight[None], 3 * inner)
    mod_count = notes.shape[1] - 16
    mod_rows = notes[:, :mod_count].reshape(-1, 2 * channels)
    all_act = notes[:, mod_count : mod_count + images_here, :depth].reshape(-1, depth)
    grad_emb_weight = dot(all_act, mod_rows, ((0,), (0,)))
    grad_emb_bias = jnp.sum(mod_rows.astype(F32), axis=0)
    grad_emb_bias = lax.dynamic_slice_in_dim(grad_emb_bias, place * depth, depth, 0)
    packed = jnp.sum(notes[:, mod_count + images_here :].astype(F32), axis=0)

    def small(row):
        size = (pixels.shape[1] if row in (G_IN_GAIN, G_IN_SHIFT) else channels) // parts
        return lax.dynamic_slice_in_dim(packed[row], lax.rem(place, 128 // size) * size, size, 0)

    grad_second_bias = small(G_SECOND)
    return (
        block_output,
        grad_pixels,
        small(G_IN_GAIN),
        small(G_IN_SHIFT),
        grad_conv_first,
        small(G_FIRST),
        grad_emb_weight,
        grad_emb_bias,
        small(G_MID_GAIN),
        small(G_MID_SHIFT),
        grad_conv_second,
        grad_second_bias,
        grad_skip_weight,
        grad_second_bias,
        small(G_ATTN_GAIN),
        small(G_ATTN_SHIFT),
        grad_attend_weight,
        grad_text_weight,
        grad_out_weight,
        small(G_OUT),
    )


def solution(mesh):
    rows = P(("dp", "fsdp"), None)
    vector = P("fsdp")
    matrix = P("fsdp", None)
    weights = (vector, vector, matrix, vector, matrix, vector, vector, vector, matrix, vector, matrix, vector, vector, vector, matrix, matrix, matrix, vector)
    return jax.shard_map(
        body,
        mesh=mesh,
        in_specs=(rows, rows, P(("dp", "fsdp"), None, None), rows, rows, rows) + weights,
        out_specs=(rows, rows) + weights,
        check_vma=False,
    )
```

```python
import functools

import jax
import jax.numpy as jnp
from jax import lax
from jax.experimental import pallas as pl
from jax.experimental.pallas import tpu as pltpu
from jax.sharding import PartitionSpec as P

BF16 = jnp.bfloat16
F32 = jnp.float32
HEADS = 8
HEAD = 64
GROUPS = 32
UNIT = 4
SHAPES = ((4 * UNIT, 4 * UNIT), (3 * UNIT, 5 * UNIT), (5 * UNIT, 3 * UNIT))
SIZES = tuple(height * breadth for height, breadth in SHAPES)
STARTS = (0, SIZES[0], SIZES[0] + SIZES[1])
PIX = sum(SIZES)
EDGE = 32
BASES = tuple(EDGE + start + i * EDGE for i, start in enumerate(STARTS))
PADDED = PIX + 4 * EDGE
BLOCK = 1152
KEYS = 384
TEXT_ROWS = 80
SUB = 16
NT = (((1,), (1,)), ((), ()))
TN = (((0,), (0,)), ((), ()))
V_IN_GAIN, V_IN_SHIFT, V_EMB, V_FIRST, V_MID_GAIN, V_MID_SHIFT, V_SECOND, V_SKIP, V_ATTN_GAIN, V_ATTN_SHIFT, V_OUT = range(11)


def dot(left, right, dims=((1,), (0,))):
    return lax.dot_general(left, right, (dims, ((), ())), preferred_element_type=F32)


def group_mean(sums, count):
    channels = sums.shape[1]
    width = channels // GROUPS
    lane = lax.broadcasted_iota(jnp.int32, sums.shape, 1)
    step = 1
    while step < width:
        odd = lax.rem(lane // step, 2) == 1
        sums = sums + jnp.where(odd, pltpu.roll(sums, step, 1), pltpu.roll(sums, channels - step, 1))
        step *= 2
    return sums / (count * width)


def rows_of(image, i):
    return pl.ds(pl.multiple_of(STARTS[image] + i * SUB, SUB), SUB)


def over_rows(image, work, start):
    return lax.fori_loop(0, SIZES[image] // SUB, lambda i, carry: work(i, rows_of(image, i), carry), start)


def column_sum(image, channels, value):
    def add(i, rows, carry):
        v = value(rows)
        return carry + (v[:8] + v[8:])
    total = over_rows(image, add, jnp.zeros((8, channels), F32))
    return jnp.broadcast_to(jnp.sum(total, axis=0, keepdims=True), (8, channels))


def norm_figures(image, channels, value):
    count = SIZES[image]
    center = group_mean(column_sum(image, channels, value), count)[:1]
    spread = group_mean(column_sum(image, channels, lambda rows: jnp.square(value(rows) - center)), count)[:1]
    return center, lax.rsqrt(spread + 1e-05)


def store_padded(pad, image, i, act):
    breadth = SHAPES[image][1]
    at = pl.ds(pl.multiple_of(BASES[image] + i * SUB, SUB), SUB)
    column = lax.rem(i * SUB + lax.broadcasted_iota(jnp.int32, (SUB, 1), 0), breadth)
    pad[0, at, :] = jnp.where(column == breadth - 1, 0.0, act).astype(BF16)
    pad[1, at, :] = act.astype(BF16)
    pad[2, at, :] = jnp.where(column == 0, 0.0, act).astype(BF16)


def zero_edges(pad):
    zeros = jnp.zeros((EDGE, pad.shape[2]), BF16)
    for side in range(3):
        for at in [base - EDGE for base in BASES] + [PADDED - EDGE]:
            pad[side, at : at + EDGE, :] = zeros


def shifted(pad, tap, image, cols, flip=False):
    down, across = divmod(8 - tap if flip else tap, 3)
    start = BASES[image] + (down - 1) * SHAPES[image][1] + across - 1
    return pad[across, start : start + SIZES[image], cols]


def gather_block(pad, q, out):
    channels = pad.shape[2]
    for tap in range(9):
        low, high = max(q * BLOCK, tap * channels), min((q + 1) * BLOCK, (tap + 1) * channels)
        if low < high:
            for image in range(3):
                out[STARTS[image] : STARTS[image] + SIZES[image], low - q * BLOCK : high - q * BLOCK] = shifted(
                    pad, tap, image, slice(low - tap * channels, high - tap * channels)
                )


class Rows:
    def __init__(self, parts, pix_channels, channels, text_dim, inner):
        self.parts = parts
        sizes = (9 * pix_channels // parts, 9 * channels // parts, pix_channels // parts, inner // parts, channels // parts, channels // parts // 2, text_dim // parts)
        starts = [0]
        for size in sizes:
            starts.append(starts[-1] + size)
        self.first, self.second, self.skip, self.out, self.attend, self.attend_more, self.text = zip(starts, sizes)
        self.total = starts[-1]

    def load(self, full, which, q, rows, buf, sem):
        start, size = which
        each = rows // size
        for i in range(each):
            pltpu.make_async_copy(full.at[q * each + i, pl.ds(start, size)], buf.at[pl.ds(i * size, size)], sem).start()

    def load_attend(self, full, buf, sem):
        start, size = self.attend
        more, half = self.attend_more
        def one(f, carry):
            at = pl.multiple_of(f * size, SUB)
            pltpu.make_async_copy(full.at[f, pl.ds(start, size)], buf.at[pl.ds(at, size), pl.ds(0, 1024)], sem).start()
            for i in range(2):
                pltpu.make_async_copy(
                    full.at[f, pl.ds(more, half), pl.ds(512 * i, 512)],
                    buf.at[pl.ds(pl.multiple_of(at + i * half, SUB), half), pl.ds(1024, 512)],
                    sem,
                ).start()
            return carry
        lax.fori_loop(0, self.parts, one, 0)


def outgoing(cotangent, present, image):
    rows = pl.ds(STARTS[image], SIZES[image])
    return (cotangent[rows, :].astype(F32) * present[0, image].astype(F32)).astype(BF16)


def waited(ref, sem):
    pltpu.make_async_copy(ref, ref, sem).wait()


class Forward:
    def __init__(self, rows, full, pixels, text_in, cotangent, present, vec, mod, outs, scratch):
        self.rows, self.full, self.pixels, self.text_in, self.cotangent, self.present, self.vec, self.mod = rows, full, pixels, text_in, cotangent, present, vec, mod
        (self.o_a1, self.o_a2, self.o_mid_hat, self.o_residual, self.o_hat, self.o_normed, self.triple, self.text_pair, self.grad_attended, self.inverses, self.o_text) = outs
        (self.a1, self.a2, self.patch, self.weight, self.acc0, self.acc1, self.normed, self.w_attend, self.w_skip, self.w_out, self.text, self.w_sem, self.s_sem, self.o_sem) = scratch

    def out_copy(self, i, src, dst):
        return pltpu.make_async_copy(src, dst, self.o_sem.at[i])

    def row(self, r, channels=1024):
        return self.vec[r : r + 1, :channels]

    def zero(self):
        zero_edges(self.a1)
        zero_edges(self.a2)
        count = self.text_in.shape[1]
        for image in range(3):
            at = image * TEXT_ROWS
            self.text[at + TEXT_ROWS - SUB : at + TEXT_ROWS, :] = jnp.zeros((SUB, self.text.shape[1]), BF16)
            self.text[at : at + count, :] = self.text_in[image]
        self.out_copy(6, self.text, self.o_text).start()

    def first_norm(self, image):
        pixels, channels = self.pixels, self.pixels.shape[1]
        value = lambda rows: pixels[rows, :].astype(F32)
        center, inverse = norm_figures(image, channels, value)
        gain, shift = self.row(V_IN_GAIN, channels) * inverse, self.row(V_IN_SHIFT, channels)
        self.inverses[image : image + 1, :channels] = inverse
        self.inverses[16 + image : 17 + image, :channels] = center
        def act(i, rows, carry):
            store_padded(self.a1, image, i, jax.nn.silu((value(rows) - center) * gain + shift))
            return carry
        over_rows(image, act, 0)
        if image == 2:
            self.out_copy(0, self.a1, self.o_a1).start()

    def load_first(self, q):
        self.rows.load(self.full, self.rows.first, q, BLOCK, self.weight.at[lax.rem(q, 2)], self.w_sem.at[lax.rem(q, 2)])

    def load_second(self, q):
        self.rows.load(self.full, self.rows.second, q, BLOCK, self.weight.at[lax.rem(q, 2)], self.w_sem.at[lax.rem(q, 2)])

    def load_text(self, q):
        self.rows.load(self.full, self.rows.text, q, 1024, self.weight.at[lax.rem(q, 2)], self.w_sem.at[lax.rem(q, 2)])

    def conv_step(self, q, pad, acc, load, count, start):
        @pl.when(q + 1 < count)
        def _():
            load(q + 1)
        for known in range(count):
            @pl.when(q == known)
            def _():
                gather_block(pad, known, self.patch)
        par = lax.rem(q, 2)
        waited(self.weight.at[par], self.w_sem.at[par])
        @pl.when(q == 0)
        def _():
            start()
        for col in (0, 512):
            cols = slice(col, col + 512)
            acc[:, cols] = acc[:, cols] + dot(self.patch[...], self.weight[par, :, cols])

    def first_conv(self, q):
        def start():
            self.acc0[...] = jnp.zeros_like(self.acc0)
        self.conv_step(q, self.a1, self.acc0, self.load_first, 9 * self.pixels.shape[1] // BLOCK, start)

    def mid_norm(self, image):
        acc, channels = self.acc0, self.acc0.shape[1]
        bias = self.row(V_FIRST)
        def shift_up(i, rows, carry):
            acc[rows, :] = acc[rows, :] + bias
            return carry
        over_rows(image, shift_up, 0)
        center, inverse = norm_figures(image, channels, lambda rows: acc[rows, :])
        self.inverses[3 + image : 4 + image, :] = inverse
        scale, shift = 1.0 + self.mod[image : image + 1, :channels], self.mod[image : image + 1, channels:]
        gain, lift = self.row(V_MID_GAIN) * scale, self.row(V_MID_SHIFT) * scale + shift
        def act(i, rows, carry):
            hat = (acc[rows, :] - center) * inverse
            acc[rows, :] = hat
            store_padded(self.a2, image, i, jax.nn.silu(hat * gain + lift))
            return carry
        over_rows(image, act, 0)
        if image == 2:
            self.out_copy(1, self.a2, self.o_a2).start()
            self.out_copy(2, self.acc0, self.o_mid_hat).start()

    def load_small(self):
        rows = self.rows
        def one(f, carry):
            for i, ((start, size), buf) in enumerate(((rows.skip, self.w_skip), (rows.out, self.w_out))):
                pltpu.make_async_copy(self.full.at[f, pl.ds(start, size)], buf.at[pl.ds(pl.multiple_of(f * size, SUB), size)], self.s_sem.at[i]).start()
            return carry
        lax.fori_loop(0, rows.parts, one, 0)
        rows.load_attend(self.full, self.w_attend, self.s_sem.at[2])

    def skip_product(self):
        for i, buf in enumerate((self.w_skip, self.w_out, self.w_attend)):
            waited(buf, self.s_sem.at[i])
        self.acc1[...] = self.acc1[...] + dot(self.pixels[...], self.w_skip[...])

    def attended_grad(self):
        for image in range(3):
            rows = pl.ds(STARTS[image], SIZES[image])
            grad = outgoing(self.cotangent, self.present, image)
            self.grad_attended[rows, :] = lax.dot_general(grad, self.w_out[...], NT, preferred_element_type=F32).astype(BF16)

    def second_conv(self, q):
        def start():
            self.acc1[...] = jnp.zeros_like(self.acc1)
        self.conv_step(q, self.a2, self.acc1, self.load_second, 9 * self.acc1.shape[1] // BLOCK, start)

    def last_norm(self, image):
        acc, hats, channels = self.acc1, self.acc0, self.acc1.shape[1]
        if image == 0:
            self.out_copy(2, self.acc0, self.o_mid_hat).wait()
        bias = self.row(V_SECOND) + self.row(V_SKIP)
        def shift_up(i, rows, carry):
            acc[rows, :] = acc[rows, :] + bias
            return carry
        over_rows(image, shift_up, 0)
        center, inverse = norm_figures(image, channels, lambda rows: acc[rows, :])
        self.inverses[6 + image : 7 + image, :] = inverse
        gain, shift = self.row(V_ATTN_GAIN), self.row(V_ATTN_SHIFT)
        def act(i, rows, carry):
            hat = (acc[rows, :] - center) * inverse
            hats[rows, :] = hat
            self.normed[rows, :] = (hat * gain + shift).astype(BF16)
            return carry
        over_rows(image, act, 0)
        if image == 2:
            self.out_copy(3, self.acc1, self.o_residual).start()
            self.out_copy(4, self.acc0, self.o_hat).start()
            self.out_copy(5, self.normed, self.o_normed).start()

    def project(self, i):
        cols = slice(512 * i, 512 * (i + 1))
        self.triple[:, cols] = dot(self.normed[...], self.w_attend[:, cols]).astype(BF16)

    def text_step(self, q, total):
        if q + 1 < 4:
            self.load_text(q + 1)
        par = q % 2
        waited(self.weight.at[par, pl.ds(0, 1024)], self.w_sem.at[par])
        part = dot(self.text[:, 1024 * q : 1024 * (q + 1)], self.weight[par, :1024, :])
        if q:
            part = total[...] + part
        if q < 3:
            total[...] = part
        else:
            self.text_pair[...] = part.astype(BF16)

    def finish(self):
        self.out_copy(0, self.a1, self.o_a1).wait()
        self.out_copy(1, self.a2, self.o_a2).wait()
        self.out_copy(3, self.acc1, self.o_residual).wait()
        self.out_copy(4, self.acc0, self.o_hat).wait()
        self.out_copy(5, self.normed, self.o_normed).wait()
        self.out_copy(6, self.text, self.o_text).wait()


MESH = pl.DeviceIdType.MESH
DEPTH = 4


STEPS = True
UNP = 3
SLACK = 0


class Where:
    def __init__(self, replicas, parts):
        self.replicas, self.parts = replicas, parts
        self.span = parts // (2 * DEPTH)
        self.group = lax.axis_index("dp")
        self.place = lax.axis_index("fsdp")
        self.core = lax.rem(self.place, 2)
        self.y = lax.rem(self.place // 2, self.span)
        self.z = self.place // (2 * self.span)
        self.side = lax.rem(self.group, 2)

    def index(self, z, y, core):
        return (z * self.span + y) * 2 + core

    def device(self, z=None, y=None, core=None, flip=False):
        z = self.z if z is None else z
        y = self.y if y is None else y
        core = self.core if core is None else core
        group = self.group + 1 - 2 * self.side if flip else self.group
        return (group, self.index(z, y, core))

    def barrier(self):
        sem = pltpu.get_barrier_semaphore()
        greet = lambda device: pl.semaphore_signal(sem, inc=1, device_id=device, device_id_type=MESH)
        greet(self.device(flip=True))
        def one(i, carry):
            greet((self.group, lax.rem(self.place + i, self.parts)))
            return carry
        lax.fori_loop(1, self.parts, one, 0)
        pl.semaphore_wait(sem, self.parts)


def forward_kernel(replicas, parts, rows, lead, lag, inner, images, *refs):
    own, note, emb, pixels, text, cotangent, present = refs[:7]
    full, mod, vec, notes = refs[7:11]
    outs = refs[11:22]
    part, sums, text_total = refs[22:25]
    scratch = refs[25:39]
    (n_send, n_recv, m_send, m_recv, z_send, z_recv, y_send, y_recv, s_send, s_recv, x_send, x_recv, c_send, c_recv, own_sem) = refs[39:]
    me = Where(replicas, parts)
    span = me.span
    total, width = own.shape
    chunks = total // rows
    joint, apart = 5 * width // 8, 3 * width // 8
    side = me.side
    thin = width // 4
    z_cols = pl.ds(pl.multiple_of(side * thin, thin), width - thin)
    a_cols = pl.ds(pl.multiple_of(side * apart, 128), joint)
    thin_cols = pl.ds(pl.multiple_of((1 - side) * (width - thin), thin), thin)
    thin_out = pl.ds(pl.multiple_of(side * (width - thin), thin), thin)
    b_cols = pl.ds(pl.multiple_of((1 - side) * joint, 128), apart)
    b_out = pl.ds(pl.multiple_of(side * joint, 128), apart)

    me.barrier()
    local = pltpu.make_async_copy(own, full.at[me.place], own_sem)
    local.start()

    def at(k):
        return pl.ds(pl.multiple_of(k * rows, 16), rows)

    def copy(src, dst, send, recv, device):
        return pltpu.make_async_remote_copy(src_ref=src, dst_ref=dst, send_sem=send, recv_sem=recv, device_id=device, device_id_type=MESH)

    def piece(k, z, y, cols, core=None):
        return full.at[me.index(z, y, me.core if core is None else core), at(k), cols]

    def z_copy(k, z, step, mine):
        src = own.at[at(k), z_cols] if mine else piece(k, z, me.y, z_cols)
        return copy(src, piece(k, z, me.y, z_cols), z_send.at[k, z, (step + 1) // 2], z_recv.at[k, z], me.device(z=me.z + step))

    def y_copy(k, z, turn, mine):
        src = own.at[at(k), a_cols] if mine else piece(k, z, me.y, a_cols)
        return copy(src, piece(k, z, me.y, a_cols), y_send.at[k, z, turn - 1], y_recv.at[k, z, turn - 1], me.device(y=lax.rem(me.y + turn, span)))

    def thin_copy(k, z):
        return copy(piece(k, z, me.y, thin_out), piece(k, z, me.y, thin_out), s_send.at[k, z], s_recv.at[k, z], me.device(flip=True))

    def x_copy(k, z, turn):
        y = lax.rem(me.y + turn, span)
        return copy(piece(k, z, y, b_out), piece(k, z, y, b_out), x_send.at[k, z, turn - 1], x_recv.at[k, z, turn - 1], me.device(flip=True))

    def core_copy(k, z, y, cols, mine=False):
        src = own.at[at(k), cols] if mine else piece(k, z, y, cols)
        return copy(src, piece(k, z, y, cols), c_send.at[k], c_recv.at[k], me.device(core=1 - me.core))

    everything = pl.ds(0, width)
    below = lambda s: (me.z - s >= 0, me.z - s)
    above = lambda s: (me.z + s < DEPTH, me.z + s)

    def start_own(k):
        @pl.when(me.z < DEPTH - 1)
        def _():
            z_copy(k, me.z, 1, True).start()
        @pl.when(me.z > 0)
        def _():
            z_copy(k, me.z, -1, True).start()
        for turn in range(1, span):
            y_copy(k, me.z, turn, True).start()
        core_copy(k, me.z, me.y, everything, True).start()

    def along_z(k, s):
        for (ok, z), step in ((below(s), 1), (above(s), -1)):
            @pl.when(ok)
            def _():
                z_copy(k, z, step, False).wait_recv()
                if s < DEPTH - 1:
                    more = me.z < DEPTH - 1 if step > 0 else me.z > 0
                    @pl.when(more)
                    def _():
                        z_copy(k, z, step, False).start()
                for turn in range(1, span):
                    y_copy(k, z, turn, False).start()
                thin_copy(k, z).start()
                core_copy(k, z, me.y, z_cols).start()

    def across(k, s):
        for ok, z in ((below(s), above(s)) if s else (below(0),)):
            @pl.when(ok)
            def _():
                for turn in range(1, span):
                    y_copy(k, z, turn, False).wait_recv()
                    x_copy(k, z, span - turn).start()
                    core_copy(k, z, lax.rem(me.y + span - turn, span), a_cols).start()

    def beside(k, s):
        for ok, z in ((below(s), above(s)) if s else (below(0),)):
            @pl.when(ok)
            def _():
                for turn in range(1, span):
                    x_copy(k, z, turn).wait_recv()
                    core_copy(k, z, lax.rem(me.y + turn, span), b_cols).start()

    def beside_thin(k, s):
        for ok, z in (below(s), above(s)):
            @pl.when(ok)
            def _():
                thin_copy(k, z).wait_recv()
                core_copy(k, z, me.y, thin_cols).start()

    def lane(k, wait):
        half = full.at[pl.ds(0, parts // 2), at(k)]
        whole = copy(half, half, c_send.at[k], c_recv.at[k], me.device(core=1 - me.core))
        whole.wait_recv() if wait else whole.wait_send()

    lane_in = functools.partial(lane, wait=True)

    def to_all(make):
        def one(i, carry):
            make(lax.rem(me.place + i, parts)).start()
            return carry
        lax.fori_loop(1, parts, one, 0)

    def wait_all(ref, send, recv):
        others = ref.at[pl.ds(0, parts - 1)]
        every = copy(others, others, send, recv, me.device(core=1 - me.core))
        every.wait_send()
        every.wait_recv()

    def modulate():
        wait_all(sums, m_send, m_recv)
        total = jnp.sum(sums[...], axis=0)
        blocks = emb.shape[1] // 128
        for j in range(blocks):
            for image in range(images):
                row = image * blocks + j
                mod[image : image + 1, j * 128 : (j + 1) * 128] = total[row : row + 1, :] + vec[V_EMB : V_EMB + 1, j * 128 : (j + 1) * 128]

    def unpack():
        wait_all(notes, n_send, n_recv)
        vec[...] = jnp.zeros_like(vec)
        for row in range(V_OUT + 1):
            size = {V_IN_GAIN: pixels.shape[1], V_IN_SHIFT: pixels.shape[1], V_EMB: emb.shape[1]}.get(row, width)
            each = 128 * parts // size
            for block in range(size // 128):
                value = notes[block * each, images + row : images + row + 1, :].astype(jnp.float32)
                for i in range(1, each):
                    value = value + notes[block * each + i, images + row : images + row + 1, :].astype(jnp.float32)
                vec[row : row + 1, block * 128 : (block + 1) * 128] = value
        rows_in = notes.shape[1]
        blocks = emb.shape[1] // 128
        for j in range(blocks):
            product = jnp.dot(notes[...].reshape(parts * rows_in, 128), emb[:, j * 128 : (j + 1) * 128], preferred_element_type=jnp.float32)
            product = product.reshape(parts, rows_in, 128)
            for image in range(images):
                part[:, image * blocks + j, :] = product[:, image, :]
        to_all(lambda far: copy(part.at[far], sums.at[me.place], m_send, m_recv, (me.group, far)))
        sums[me.place] = part[me.place]

    to_all(lambda far: copy(note.at[far], notes.at[me.place], n_send, n_recv, (me.group, far)))
    notes[me.place] = note[me.place]

    table = Rows(parts, pixels.shape[1], width, text.shape[2], inner)
    forward = Forward(table, full, pixels, text, cotangent, present, vec, mod, outs, scratch)
    ready = (DEPTH + 1) * lag + SLACK
    have = lambda which: (sum(which) - 1) // rows + ready
    t1 = max(have(table.first), 7)
    t2 = max(have(table.second), t1 + 4)
    t3 = max(have(table.attend_more), t2 + 2)
    t4 = max(t2 + 4, t3 + 1)
    t5 = max(have(table.text), t4 + 1)
    slots = max(chunks + ready, t5 + 1)

    def steps(t):
        if not STEPS:
            pl.when(t == 8)(local.wait)
            pl.when(t == UNP)(unpack)
            return
        def once(when, *work):
            @pl.when(t == when)
            def _():
                for one in work:
                    one()
        def many(when, until, each, work):
            @pl.when(jnp.logical_and(t >= when, t < until))
            def _():
                for i in range(each):
                    work((t - when) * each + i)
        once(0, forward.zero)
        once(t1, local.wait)
        once(3, unpack)
        for image in range(3):
            once(4 + image, functools.partial(forward.first_norm, image))
        once(t1, lambda: forward.load_first(jnp.int32(0)))
        many(t1, t1 + 2, 2, forward.first_conv)
        once(t1 + 1, modulate)
        for image in range(3):
            once(t1 + 2 + image // 2, functools.partial(forward.mid_norm, image))
        once(t2, lambda: forward.load_second(jnp.int32(0)))
        many(t2, t2 + 4, 2, forward.second_conv)
        once(t3, forward.load_small)
        once(t4, forward.skip_product, forward.attended_grad)
        for image in range(3):
            once(t4 + image // 2, functools.partial(forward.last_norm, image))

    for k in range(min(lead, chunks)):
        start_own(k)

    last = 2 * (DEPTH - 1) + 3

    def slot(t, carry):
        def stage(delay, work):
            k = t - delay
            @pl.when(jnp.logical_and(k >= 0, k < chunks))
            def _():
                work(k)
        @pl.when(t + lead < chunks)
        def _():
            start_own(t + lead)
        for s in range(1, DEPTH):
            stage((s - 1) * lag, functools.partial(along_z, s=s))
        for s in range(DEPTH):
            stage(s * lag, functools.partial(across, s=s))
        for s in range(1, DEPTH):
            stage(s * lag, functools.partial(beside_thin, s=s))
        for s in range(DEPTH):
            stage((s + 1) * lag, functools.partial(beside, s=s))
        stage(ready, lane_in)
        steps(t)
        return carry

    lax.fori_loop(0, slots, slot, 0)
    if STEPS:
        forward.load_text(jnp.int32(0))
        for i in range(3):
            forward.project(i)
        for q in range(4):
            forward.text_step(q, text_total)
    else:
        modulate()

    def finish(k, carry):
        for step, edge in ((1, me.z < DEPTH - 1), (-1, me.z > 0)):
            for s in range(DEPTH - 1):
                ok, z = below(s) if step > 0 else above(s)
                @pl.when(jnp.logical_and(ok, edge))
                def _():
                    z_copy(k, z, step, False).wait_send()
        for z in range(DEPTH):
            for turn in range(1, span):
                y_copy(k, z, turn, False).wait_send()
                x_copy(k, z, turn).wait_send()
            @pl.when(z != me.z)
            def _():
                thin_copy(k, z).wait_send()
        lane(k, False)
        return carry

    lax.fori_loop(0, chunks, finish, 0)
    if STEPS:
        forward.finish()


def forward_all(own, note, emb, pixels, text, cotangent, present, images, inner, replicas, parts, rows=80, lead=3, lag=1):
    total, width = own.shape
    chunks = total // rows
    span = parts // (2 * DEPTH)
    pix, pix_width = pixels.shape
    dma = lambda *shape: pltpu.SemaphoreType.DMA(shape)
    bf = lambda *shape: jax.ShapeDtypeStruct(shape, BF16)
    fl = lambda *shape: jax.ShapeDtypeStruct(shape, F32)
    hbm, vmem = pl.BlockSpec(memory_space=pl.ANY), pl.BlockSpec(memory_space=pltpu.VMEM)
    return pl.pallas_call(
        functools.partial(forward_kernel, replicas, parts, rows, lead, lag, inner, images),
        out_shape=[
            bf(parts, total, width), fl(8, emb.shape[1]), fl(16, emb.shape[1]), bf(*note.shape),
            bf(3, PADDED, pix_width), bf(3, PADDED, width), fl(pix, width), fl(pix, width), fl(pix, width), bf(pix, width),
            bf(pix, 3 * inner), bf(3 * TEXT_ROWS, 2 * inner), bf(pix, inner), fl(24, width), bf(3 * TEXT_ROWS, text.shape[2]),
        ],
        in_specs=[hbm] + [vmem] * 5 + [pl.BlockSpec(memory_space=pltpu.SMEM)],
        out_specs=[hbm, vmem, vmem, vmem] + [hbm] * 6 + [vmem] * 4 + [hbm],
        scratch_shapes=[
            pltpu.VMEM((parts, images * emb.shape[1] // 128, 128), F32),
            pltpu.VMEM((parts, images * emb.shape[1] // 128, 128), F32),
            pltpu.VMEM((3 * TEXT_ROWS, width), F32),
            pltpu.VMEM((3, PADDED, pix_width), BF16), pltpu.VMEM((3, PADDED, width), BF16),
            pltpu.VMEM((pix, BLOCK), BF16), pltpu.VMEM((2, BLOCK, width), BF16),
            pltpu.VMEM((pix, width), F32), pltpu.VMEM((pix, width), F32), pltpu.VMEM((pix, width), BF16),
            pltpu.VMEM((width, 3 * inner), BF16), pltpu.VMEM((pix_width, width), BF16), pltpu.VMEM((inner, width), BF16), pltpu.VMEM((3 * TEXT_ROWS, text.shape[2]), BF16),
            dma(2), dma(3), dma(7),
            dma(), dma(), dma(), dma(),
            dma(chunks, DEPTH, 2), dma(chunks, DEPTH),
            dma(chunks, DEPTH, span - 1), dma(chunks, DEPTH, span - 1),
            dma(chunks, DEPTH), dma(chunks, DEPTH),
            dma(chunks, DEPTH, span - 1), dma(chunks, DEPTH, span - 1),
            dma(chunks), dma(chunks), dma(),
        ],
        compiler_params=pltpu.CompilerParams(collective_id=0, has_side_effects=True, vmem_limit_bytes=60 << 20),
        name="forward_all",
    )(own, note, emb, pixels, text, cotangent, present)


class Seat(Where):
    def bit(self, b):
        step = 1 << b
        group = self.group + step - 2 * step * lax.rem(self.group // step, 2)
        return (group, self.place)

    def meet(self):
        sem = pltpu.get_barrier_semaphore()
        count = self.replicas * self.parts
        def one(i, carry):
            far = lax.rem(self.group * self.parts + self.place + i, count)
            pl.semaphore_signal(sem, inc=1, device_id=(far // self.parts, lax.rem(far, self.parts)), device_id_type=MESH)
            return carry
        lax.fori_loop(1, count, one, 0)
        pl.semaphore_wait(sem, count - 1)


def norm_pull(image, factor, inverse, grad, hat, plain, crossed, put):
    count = SIZES[image]
    mean_plain = group_mean(plain * factor, count)[:1]
    mean_crossed = group_mean(crossed * factor, count)[:1]
    def one(i, rows, carry):
        value = inverse * (grad(rows) * factor - mean_plain - hat(rows) * mean_crossed)
        put(i, rows, value)
        return carry + (value[:8] + value[8:])
    total = over_rows(image, one, jnp.zeros(plain.shape, F32))
    return jnp.sum(total, axis=0, keepdims=True)


def two_sums(image, channels, pair):
    def add(i, rows, carry):
        a, b = pair(i, rows)
        return carry[0] + (a[:8] + a[8:]), carry[1] + (b[:8] + b[8:])
    zero = jnp.zeros((8, channels), F32)
    sums = over_rows(image, add, (zero, zero))
    return [jnp.broadcast_to(jnp.sum(part, axis=0, keepdims=True), (8, channels)) for part in sums]


def silu_pull(value):
    gate = jax.nn.sigmoid(value)
    return gate * (1.0 + value * (1.0 - gate))


G_IN_GAIN, G_IN_SHIFT, G_FIRST, G_MID_GAIN, G_MID_SHIFT, G_SECOND, G_ATTN_GAIN, G_ATTN_SHIFT, G_OUT = range(9)


class Backward:
    def __init__(self, rows, full, r_low, pixels, vec, mod, inverses, a1, a2, mid_hat, outs, scratch):
        self.rows, self.full, self.r_low, self.pixels, self.vec, self.mod, self.inverses = rows, full, r_low, pixels, vec, mod, inverses
        self.h_a1, self.h_a2, self.h_mid = a1, a2, mid_hat
        self.g_first, self.g_second, self.g_skip, self.grad_pixels = outs
        (self.a1, self.pad, self.hat, self.acc, self.acc1, self.c_low, self.patch, self.weight, self.stage, self.w_skip,
         self.vecs, self.mods, self.in_sem, self.w_sem, self.o_sem) = scratch

    def row(self, r, channels=1024):
        return self.vec[r : r + 1, :channels]

    def add_row(self, r, value):
        width = value.shape[1]
        self.vecs[r : r + 1, :width] = self.vecs[r : r + 1, :width] + value[:1]

    def fetch(self):
        for i, (src, dst) in enumerate(((self.h_a2, self.pad), (self.h_a1, self.a1), (self.h_mid, self.hat))):
            pltpu.make_async_copy(src, dst, self.in_sem.at[i]).start()
        start, size = self.rows.skip
        def one(f, carry):
            pltpu.make_async_copy(self.full.at[f, pl.ds(start, size)], self.w_skip.at[pl.ds(pl.multiple_of(f * size, SUB), size)], self.in_sem.at[3]).start()
            return carry
        lax.fori_loop(0, self.rows.parts, one, 0)

    def arrived(self, i):
        waited((self.pad, self.a1, self.hat, self.w_skip)[i], self.in_sem.at[i])

    def put_out(self, dst, first, count):
        span, size = dst.shape[1], dst.shape[3]
        for i in range(count):
            f = first + i
            pltpu.make_async_copy(
                self.stage.at[pl.ds(i * size, size)],
                dst.at[f // (2 * span), lax.rem(f // 2, span), lax.rem(f, 2)],
                self.o_sem,
            ).start()

    def weight_grad(self, q, pad, count, grad, dst):
        for known in range(count):
            @pl.when(q == known)
            def _():
                gather_block(pad, known, self.patch)
        @pl.when(q > 0)
        def _():
            self.stored()
        for col in range(0, 1024, 256):
            cols = slice(col, col + 256)
            self.stage[:, cols] = lax.dot_general(self.patch[...], grad[:, cols], TN, preferred_element_type=F32).astype(BF16)
        each = BLOCK // dst.shape[3]
        self.put_out(dst, q * each, each)

    def second_weight(self, q):
        self.weight_grad(q, self.pad, 9 * self.pad.shape[2] // BLOCK, self.r_low, self.g_second)

    def first_weight(self, q):
        self.weight_grad(q, self.a1, 9 * self.a1.shape[2] // BLOCK, self.c_low, self.g_first)

    def stored(self, size=BLOCK):
        waited(self.stage.at[pl.ds(0, size)], self.o_sem)

    def skip_weight(self):
        size = self.pixels.shape[1]
        for col in range(0, 1024, 512):
            cols = slice(col, col + 512)
            self.stage[:size, cols] = lax.dot_general(self.pixels[...], self.r_low[:, cols], TN, preferred_element_type=F32).astype(BF16)
        self.put_out(self.g_skip, jnp.int32(0), self.rows.parts)
        self.stored(size)

    def pad_residual(self):
        zero_edges(self.pad)
        for image in range(3):
            def one(i, rows, carry):
                store_padded(self.pad, image, i, self.r_low[rows, :].astype(F32))
                return carry
            over_rows(image, one, 0)

    def load_tap(self, which, height, tap):
        start, size = which
        for known in range(9):
            @pl.when(tap == known)
            def _():
                at = known * height
                while at < (known + 1) * height:
                    shard, inside = divmod(at, size)
                    count = min(size - inside, (known + 1) * height - at)
                    pltpu.make_async_copy(
                        self.full.at[shard, pl.ds(start + inside, count)],
                        self.weight.at[known % 2, pl.ds(at - known * height, count)],
                        self.w_sem.at[known % 2],
                    ).start()
                    at += count

    def pull_step(self, tap, which, height, acc):
        @pl.when(tap + 1 < 9)
        def _():
            self.load_tap(which, height, tap + 1)
        @pl.when(tap == 0)
        def _():
            acc[...] = jnp.zeros_like(acc)
        for known in range(9):
            @pl.when(tap == known)
            def _():
                for image in range(3):
                    self.patch[STARTS[image] : STARTS[image] + SIZES[image], :1024] = shifted(self.pad, known, image, slice(0, 1024), True)
        par = lax.rem(tap, 2)
        waited(self.weight.at[par, pl.ds(0, height)], self.w_sem.at[par])
        for col in range(0, height, 512):
            cols = slice(col, col + 512)
            acc[:, cols] = acc[:, cols] + lax.dot_general(self.patch[:, :1024], self.weight[par, cols, :], NT, preferred_element_type=F32)

    def load_second(self):
        self.load_tap(self.rows.second, 1024, jnp.int32(0))

    def second_pull(self, tap):
        self.pull_step(tap, self.rows.second, 1024, self.acc)

    def load_first(self):
        self.load_tap(self.rows.first, self.pixels.shape[1], jnp.int32(0))

    def first_pull(self, tap):
        self.pull_step(tap, self.rows.first, self.pixels.shape[1], self.acc1)

    def mid_pull(self, image):
        acc, hat, channels = self.acc, self.hat, 1024
        if image == 0:
            self.vecs[...] = jnp.zeros_like(self.vecs)
            self.mods[...] = jnp.zeros_like(self.mods)
            zero_edges(self.pad)
        scale, shift = 1.0 + self.mod[image : image + 1, :channels], self.mod[image : image + 1, channels:]
        gain, bias = self.row(V_MID_GAIN), self.row(V_MID_SHIFT)
        factor, lift = gain * scale, bias * scale + shift
        def pair(i, rows):
            h = hat[rows, :]
            grad = acc[rows, :] * silu_pull(h * factor + lift)
            acc[rows, :] = grad
            return grad, grad * h
        plain, crossed = two_sums(image, channels, pair)
        def put(i, rows, value):
            store_padded(self.pad, image, i, value)
            self.c_low[rows, :] = value.astype(BF16)
        inverse = self.inverses[3 + image : 4 + image, :]
        total = norm_pull(image, factor, inverse, lambda rows: acc[rows, :], lambda rows: hat[rows, :], plain, crossed, put)
        self.add_row(G_FIRST, total)
        self.add_row(G_MID_GAIN, crossed * scale)
        self.add_row(G_MID_SHIFT, plain * scale)
        self.mods[image : image + 1, :channels] = (crossed * gain + plain * bias)[:1]
        self.mods[image : image + 1, channels:] = plain[:1]

    def first_norm_pull(self, image):
        acc, pixels = self.acc1, self.pixels
        channels = pixels.shape[1]
        inverse, center = self.inverses[image : image + 1, :channels], self.inverses[16 + image : 17 + image, :channels]
        gain, bias = self.row(V_IN_GAIN, channels), self.row(V_IN_SHIFT, channels)
        hat = lambda rows: (pixels[rows, :].astype(F32) - center) * inverse
        def pair(i, rows):
            h = hat(rows)
            grad = acc[rows, :] * silu_pull(h * gain + bias)
            acc[rows, :] = grad
            return grad, grad * h
        plain, crossed = two_sums(image, channels, pair)
        def put(i, rows, value):
            self.grad_pixels[rows, :] = self.grad_pixels[rows, :] + value
        norm_pull(image, gain, inverse, lambda rows: acc[rows, :], hat, plain, crossed, put)
        self.add_row(G_IN_GAIN, crossed)
        self.add_row(G_IN_SHIFT, plain)

    def skip_pull(self):
        self.grad_pixels[...] = lax.dot_general(self.r_low[...], self.w_skip[...], NT, preferred_element_type=F32)


def reduce_kernel(replicas, parts, rows, spans, lead, ring, nrc, rb, lag, inner, text_dim, images, known, *refs):
    early = refs[:known]
    full, r_low, pixels, vec, mod, inverses, a1, a2, mid_hat, emb_note, more = refs[known : known + 11]
    kinds = len(spans)
    refs = refs[known + 11 :]
    outs, refs = refs[:kinds], refs[kinds:]
    notes, g_first, g_second, g_skip, grad_pixels, g_narrow, g_wide = refs[:7]
    rest = refs[7:]
    (hold, rc, xr, yr, tr, zu, zd, fr, tb, shared, target, shared32, target32) = rest[:13]
    scratch = rest[13:28]
    (l_sem, c_send, c_recv, x_send, x_recv, y_send, y_recv,
     u_send, u_recv, d_send, d_recv, f_send, f_recv, n_send, n_recv, t_send, t_recv, free, x_free, y_free, u_free, d_free) = rest[28:]
    me = Seat(replicas, parts)
    span = me.span
    width = r_low.shape[1]
    chunks = spans[-1][1]
    side = me.side
    bits = replicas.bit_length() - 1
    apart, joint = 3 * width // 8, 5 * width // 8
    thin = 128
    main = width - thin
    z_cols = pl.ds(pl.multiple_of(side * thin, thin), main)
    thin_cols = pl.ds(pl.multiple_of((1 - side) * main, thin), thin)
    thin_in = pl.ds(pl.multiple_of(side * main, thin), thin)
    x_in = pl.ds(pl.multiple_of(side * joint, 128), apart)
    y_cols = pl.ds(pl.multiple_of(side * apart, 128), joint)
    table = Rows(parts, pixels.shape[1], width, text_dim, inner)
    back = Backward(table, full, r_low, pixels, vec, mod, inverses, a1, a2, mid_hat, (g_first, g_second, g_skip, grad_pixels), scratch)
    grads = list(early) + [g_second, g_skip, g_first]

    me.meet()
    back.fetch()

    def copy(src, dst, send, recv, device):
        return pltpu.make_async_remote_copy(src_ref=src, dst_ref=dst, send_sem=send, recv_sem=recv, device_id=device, device_id_type=MESH)

    def give(sem, device):
        pl.semaphore_signal(sem, inc=1, device_id=device, device_id_type=MESH)

    def take(sem, k, size):
        @pl.when(k >= size)
        def _():
            pl.semaphore_wait(sem, 1)

    def core_copy(k, src):
        return copy(src, rc.at[lax.rem(k, nrc)], c_send.at[k], c_recv.at[lax.rem(k, nrc)], me.device(core=1 - me.core))

    def begin(k):
        take(free, k, nrc)
        for grad, (lo, hi) in zip(grads, spans):
            @pl.when(jnp.logical_and(k >= lo, k < hi))
            def _():
                at = pl.ds(pl.multiple_of((k - lo) * rows, 16), rows)
                slot = lax.rem(k, ring)
                pltpu.make_async_copy(grad.at[:, :, me.core, at, :], hold.at[slot], l_sem.at[slot]).start()
                core_copy(k, grad.at[:, :, 1 - me.core, at, :]).start()

    def x_copy(k, turn):
        slot = lax.rem(k, ring)
        cols = pl.ds(pl.multiple_of((1 - side) * joint, 128), apart)
        return copy(hold.at[slot, :, lax.rem(me.y + turn, span), :, cols], xr.at[lax.rem(k, rb), turn - 1], x_send.at[k, turn - 1], x_recv.at[k, turn - 1], me.bit(0))

    def y_copy(k, turn):
        slot = lax.rem(k, ring)
        return copy(hold.at[slot, :, lax.rem(me.y + turn, span), :, y_cols], yr.at[lax.rem(k, rb), turn - 1], y_send.at[k, turn - 1], y_recv.at[k, turn - 1], me.device(y=lax.rem(me.y + turn, span)))

    def t_copy(k):
        slot = lax.rem(k, ring)
        return copy(hold.at[slot, :, me.y, :, thin_cols], tr.at[lax.rem(k, rb)], t_send.at[k], t_recv.at[k], me.bit(0))

    def up_copy(k, z):
        slot = lax.rem(k, ring)
        return copy(hold.at[slot, z + 1 : DEPTH, me.y, :, z_cols], zu.at[lax.rem(k, rb), 0 : DEPTH - 1 - z], u_send.at[k], u_recv.at[k], me.device(z=me.z + 1))

    def down_copy(k, z):
        slot = lax.rem(k, ring)
        return copy(hold.at[slot, 0:z, me.y, :, z_cols], zd.at[lax.rem(k, rb), 0:z], d_send.at[k], d_recv.at[k], me.device(z=me.z - 1))

    def f_copy(k, b):
        slot = lax.rem(k, ring)
        src = hold.at[slot, me.z, me.y, :, z_cols] if b == 0 else tb.at[b - 1, k]
        dst = fr.at[b, k, :, pl.ds(0, main)] if b == 0 else fr.at[b, k]
        return copy(src, dst, f_send.at[b, k], f_recv.at[b, k], me.bit(b))

    def fold_core(k):
        slot = lax.rem(k, ring)
        waited(hold.at[slot], l_sem.at[slot])
        core_copy(k, rc.at[lax.rem(k, nrc)]).wait_recv()
        hold[slot] = hold[slot] + rc[lax.rem(k, nrc)]
        @pl.when(k + nrc < chunks)
        def _():
            give(free, me.device(core=1 - me.core))
        for turn in range(1, span):
            take(x_free.at[turn - 1], k, rb)
            x_copy(k, turn).start()
        t_copy(k).start()

    def fold_x(k):
        slot = lax.rem(k, ring)
        t_copy(k).wait_recv()
        hold[slot, :, me.y, :, thin_in] = hold[slot, :, me.y, :, thin_in] + tr[lax.rem(k, rb)]
        for turn in range(1, span):
            x_copy(k, turn).wait_recv()
            y = lax.rem(me.y + turn, span)
            hold[slot, :, y, :, x_in] = hold[slot, :, y, :, x_in] + xr[lax.rem(k, rb), turn - 1]
            @pl.when(k + rb < chunks)
            def _():
                give(x_free.at[turn - 1], me.bit(0))
            take(y_free.at[turn - 1], k, rb)
            y_copy(k, turn).start()

    def fold_y(k):
        slot = lax.rem(k, ring)
        for turn in range(1, span):
            y_copy(k, turn).wait_recv()
            hold[slot, :, me.y, :, y_cols] = hold[slot, :, me.y, :, y_cols] + yr[lax.rem(k, rb), turn - 1]
            @pl.when(k + rb < chunks)
            def _():
                give(y_free.at[turn - 1], me.device(y=lax.rem(me.y + span - turn, span)))

    def hop(k, h):
        slot = lax.rem(k, ring)
        @pl.when(me.z == h)
        def _():
            if h > 0:
                up_copy(k, h - 1).wait_recv()
                hold[slot, h:, me.y, :, z_cols] = hold[slot, h:, me.y, :, z_cols] + zu[lax.rem(k, rb), 0 : DEPTH - h]
                @pl.when(k + rb < chunks)
                def _():
                    give(u_free, me.device(z=me.z - 1))
            if h < DEPTH - 1:
                take(u_free, k, rb)
                up_copy(k, h).start()
        z = DEPTH - 1 - h
        @pl.when(me.z == z)
        def _():
            if h > 0:
                down_copy(k, z + 1).wait_recv()
                hold[slot, : z + 1, me.y, :, z_cols] = hold[slot, : z + 1, me.y, :, z_cols] + zd[lax.rem(k, rb), 0 : z + 1]
                @pl.when(k + rb < chunks)
                def _():
                    give(d_free, me.device(z=me.z + 1))
            if h < DEPTH - 1:
                take(d_free, k, rb)
                down_copy(k, z).start()

    def finish(k, b):
        slot = lax.rem(k, ring)
        f_copy(k, b).wait_recv()
        if b == 0:
            came = jnp.concatenate([fr[b, k, :, :main].astype(F32), jnp.zeros((rows, thin), F32)], 1)
            before = hold[slot, me.z, me.y].astype(F32)
            column = lax.broadcasted_iota(jnp.int32, before.shape, 1)
            came = pltpu.roll(came, thin * (1 - side), 1)
            ours = jnp.logical_and(column >= thin * side, column < main + thin * side)
            theirs = jnp.logical_and(column >= thin * (1 - side), column < main + thin * (1 - side))
            total = jnp.where(ours, before, 0.0) + jnp.where(theirs, came, 0.0)
        else:
            total = tb[b - 1, k].astype(F32) + fr[b, k].astype(F32)
        if b == bits - 1:
            for out, (lo, hi) in zip(outs, spans):
                @pl.when(jnp.logical_and(k >= lo, k < hi))
                def _():
                    out[pl.ds(pl.multiple_of((k - lo) * rows, 16), rows), :] = total
        else:
            tb[b, k] = total.astype(BF16)
            f_copy(k, b + 1).start()

    def retire(k):
        core_copy(k, rc.at[0]).wait_send()
        t_copy(k).wait_send()
        for turn in range(1, span):
            x_copy(k, turn).wait_send()
            y_copy(k, turn).wait_send()
        for z in range(DEPTH):
            @pl.when(me.z == z)
            def _():
                if z < DEPTH - 1:
                    up_copy(k, z).wait_send()
                if z > 0:
                    down_copy(k, z).wait_send()
        for b in range(bits):
            f_copy(k, b).wait_send()

    count = replicas * parts
    mine = me.group * parts + me.place
    tall = shared.shape[0]

    def note_copies(far):
        device = (far // parts, lax.rem(far, parts))
        return (
            copy(shared, notes.at[mine, pl.ds(0, tall)], n_send, n_recv, device),
            copy(target.at[lax.rem(far, parts)], notes.at[mine, pl.ds(tall, 16)], n_send, n_recv, device),
        )

    def tell():
        back.vecs[:, :] = back.vecs[:, :] + more[...]
        target32[...] = emb_note[...].astype(F32)
        each = 2 * width // 128
        for image in range(images):
            for j in range(each):
                shared32[image * each + j : image * each + j + 1, :] = back.mods[image : image + 1, j * 128 : (j + 1) * 128]
        shared[...] = shared32[...].astype(BF16)
        for row in range(G_OUT + 1):
            size = (pixels.shape[1] if row in (G_IN_GAIN, G_IN_SHIFT) else width) // parts
            for f in range(parts):
                block = f * size // 128
                target32[f, images + row : images + row + 1, :] = back.vecs[row : row + 1, block * 128 : (block + 1) * 128]
        target[...] = target32[...].astype(BF16)
        def send(i, carry):
            for one in note_copies(lax.rem(mine + i, count)):
                one.start()
            return carry
        lax.fori_loop(1, count, send, 0)
        notes[mine, :tall, :] = shared[...]
        notes[mine, tall:, :] = target[me.place]
    lo_second, lo_skip, lo_first = (spans[known + i][0] - lead for i in range(3))
    n2, n1 = 9 * width // BLOCK, 9 * pixels.shape[1] // BLOCK
    s0 = n2 + 1
    s1 = s0 + 9
    s2 = s1 + 3
    s3 = s2 + n1 + 1
    s4 = s3 + 5
    assert s0 <= lo_second and s2 + n1 < lo_first
    last = max(chunks + (2 + DEPTH + bits) * lag + 1, s4 + 5)

    def steps(t):
        if not STEPS:
            return
        def once(when, *work):
            @pl.when(t == when)
            def _():
                for one in work:
                    one()
        def many(when, until, each, limit, work):
            @pl.when(jnp.logical_and(t >= when, t < until))
            def _():
                for i in range(each):
                    at = (t - when) * each + i
                    if limit % each:
                        pl.when(at < limit)(lambda: work(at))
                    else:
                        work(at)
        once(0, lambda: back.arrived(0))
        many(0, n2, 1, n2, back.second_weight)
        once(n2, back.stored, back.skip_weight, back.pad_residual, back.load_second)
        many(s0, s1, 1, 9, back.second_pull)
        once(s1, lambda: back.arrived(1), lambda: back.arrived(2), lambda: back.arrived(3))
        for image in range(3):
            once(s1 + image, functools.partial(back.mid_pull, image))
        many(s2, s2 + n1, 1, n1, back.first_weight)
        once(s2 + n1, back.stored, back.load_first)
        many(s3, s4, 2, 9, back.first_pull)
        once(s4, back.skip_pull)
        for image in range(3):
            once(s4 + 1 + image, functools.partial(back.first_norm_pull, image))
        once(s4 + 4, tell)

    for k in range(lead):
        begin(jnp.int32(k))

    first_f = (2 + DEPTH) * lag

    def slot_work(t, carry):
        def stage(delay, work):
            k = t - delay
            @pl.when(jnp.logical_and(k >= 0, k < chunks))
            def _():
                work(k)
        for h in range(DEPTH - 1, 0, -1):
            stage((2 + h) * lag, functools.partial(hop, h=h))
        stage((1 + DEPTH) * lag, lambda k: f_copy(k, 0).start())
        def pair(k):
            fold_y(k)
            hop(k, 0)
        stage(2 * lag, pair)
        stage(lag, fold_x)
        stage(0, fold_core)
        for b in range(bits):
            stage(first_f + b * lag, functools.partial(finish, b=b))
        stage(first_f + bits * lag, retire)
        @pl.when(t + lead < chunks)
        def _():
            begin(t + lead)
        steps(t)
        return carry

    lax.fori_loop(0, last, slot_work, 0)
    others = notes.at[pl.ds(0, count - 1)]
    every = copy(others, others, n_send, n_recv, me.device(core=1 - me.core))
    every.wait_send()
    every.wait_recv()
    total = jnp.sum(notes[:, tall:, :].astype(F32), axis=0)
    for dst, first, last in ((g_narrow, G_IN_GAIN, G_IN_SHIFT), (g_wide, G_FIRST, G_OUT)):
        size = dst.shape[2]
        turn = lax.rem(128 - lax.rem(me.place * size, 128), 128)
        mine_only = pltpu.roll(total, turn, 1)
        for row in range(first, last + 1):
            dst[row - first] = mine_only[images + row : images + row + 1, :size]


def reduce_all(early, full, r_low, pixels, vec, mod, inverses, a1, a2, mid_hat, emb_note, more, inner, text_dim, images, replicas, parts, rows, lead=2, nrc=3, lag=2, rb=8):
    span = parts // (2 * DEPTH)
    pix, width = r_low.shape
    pix_width = pixels.shape[1]
    spans, at = [], 0
    views = []
    for size in [grad.shape[0] // parts for grad in early] + [9 * width // parts, pix_width // parts, 9 * pix_width // parts]:
        spans.append((at // rows, (at + size) // rows))
        at += size
    for grad in early:
        views.append(grad.reshape(DEPTH, span, 2, grad.shape[0] // parts, width))
    total = at
    chunks = total // rows
    bits = replicas.bit_length() - 1
    ring = lead + (2 + DEPTH + bits) * lag + 2
    dma = lambda *shape: pltpu.SemaphoreType.DMA(shape)
    reg = lambda *shape: pltpu.SemaphoreType.REGULAR(shape)
    vm = lambda *shape: pltpu.VMEM(shape, BF16)
    vf = lambda *shape: pltpu.VMEM(shape, F32)
    bf = lambda *shape: jax.ShapeDtypeStruct(shape, BF16)
    fl = lambda *shape: jax.ShapeDtypeStruct(shape, F32)
    hbm, vmem = pl.BlockSpec(memory_space=pl.ANY), pl.BlockSpec(memory_space=pltpu.VMEM)
    tall = images * 2 * width // 128
    return pl.pallas_call(
        functools.partial(reduce_kernel, replicas, parts, rows, spans, lead, ring, nrc, rb, lag, inner, text_dim, images, len(early)),
        out_shape=[
            *(fl((hi - lo) * rows, width) for lo, hi in spans), bf(replicas * parts, tall + 16, 128),
            *(bf(DEPTH, span, 2, size // parts, width) for size in (9 * pix_width, 9 * width, pix_width)), fl(pix, pix_width),
            fl(2, 1, pix_width // parts), fl(7, 1, width // parts),
        ],
        in_specs=[hbm] * (len(early) + 1) + [vmem] * 5 + [hbm] * 3 + [vmem] * 2,
        out_specs=[vmem] * (len(spans) + 1) + [hbm] * 3 + [vmem] * 3,
        scratch_shapes=[
            vm(ring, DEPTH, span, rows, width),
            vm(nrc, DEPTH, span, rows, width),
            vm(rb, span - 1, DEPTH, rows, 3 * width // 8),
            vm(rb, span - 1, DEPTH, rows, 5 * width // 8),
            vm(rb, DEPTH, rows, 128),
            vm(rb, DEPTH - 1, rows, width - 128),
            vm(rb, DEPTH - 1, rows, width - 128),
            vm(bits, chunks, rows, width),
            vm(max(bits - 1, 1), chunks if bits > 1 else 1, rows, width),
            vm(tall, 128), vm(parts, 16, 128), vf(tall, 128), vf(parts, 16, 128),
            vm(3, PADDED, pix_width), vm(3, PADDED, width), vf(pix, width), vf(pix, width), vf(pix, pix_width), vm(pix, width),
            vm(pix, BLOCK), vm(2, 1024, width), vm(BLOCK, width), vm(pix_width, width), vf(16, width), vf(8, 2 * width),
            dma(4), dma(2), dma(),
            dma(ring),
            dma(chunks), dma(nrc),
            dma(chunks, span - 1), dma(chunks, span - 1),
            dma(chunks, span - 1), dma(chunks, span - 1),
            dma(chunks), dma(chunks), dma(chunks), dma(chunks),
            dma(bits, chunks), dma(bits, chunks),
            pltpu.SemaphoreType.DMA, pltpu.SemaphoreType.DMA, dma(chunks), dma(chunks),
            pltpu.SemaphoreType.REGULAR, reg(span - 1), reg(span - 1), pltpu.SemaphoreType.REGULAR, pltpu.SemaphoreType.REGULAR,
        ],
        compiler_params=pltpu.CompilerParams(collective_id=1, has_side_effects=True, vmem_limit_bytes=62 << 20),
        name="reduce_all",
    )(*views, full, r_low, pixels, vec, mod, inverses, a1, a2, mid_hat, emb_note, more)


def middle_kernel(parts, inner, text_dim, triple, text_pair, keep, grad_attended, cotangent, normed, hats, residual, text, vec, inverses, present, full,
                  block_output, r_low, g_out, g_attend, g_more, g_text, more, attended, grad_triple, grad_text, rows_grad, w_attend, w_out, stage,
                  g_low, queries, outs, keys, values, sems, o_sem):
    width = cotangent.shape[1]
    table = Rows(parts, 512, width, text_dim, inner)
    start, size = table.out
    def one(f, carry):
        pltpu.make_async_copy(full.at[f, pl.ds(start, size)], w_out.at[pl.ds(pl.multiple_of(f * size, SUB), size)], sems.at[0]).start()
        return carry
    lax.fori_loop(0, parts, one, 0)
    table.load_attend(full, w_attend, sems.at[1])

    for image in range(3):
        g_low[pl.ds(STARTS[image], SIZES[image]), :] = outgoing(cotangent, present, image)

    lane = lax.broadcasted_iota(jnp.int32, (1, 2 * HEAD), 1)
    scale = HEAD ** -0.5
    room = min(SIZES) + TEXT_ROWS
    for buf in (keys, values):
        buf[room:, :] = jnp.zeros((KEYS - room, 2 * HEAD), BF16)

    def heads(pair, carry):
        at = lambda shift: pl.ds(pl.multiple_of(pair * 2 * HEAD + shift * inner, 128), 2 * HEAD)
        for image in range(3):
            size = SIZES[image]
            rows = pl.ds(STARTS[image], size)
            text_rows = pl.ds(image * TEXT_ROWS, TEXT_ROWS)
            for buf, part in ((queries, triple[rows, at(0)] * jnp.asarray(scale, BF16)), (outs, grad_attended[rows, at(0)])):
                buf[:size, :] = jnp.where(lane < HEAD, part, jnp.zeros_like(part))
                buf[size : 2 * size, :] = jnp.where(lane < HEAD, jnp.zeros_like(part), part)
            for i, buf in enumerate((keys, values)):
                buf[:size, :] = triple[rows, at(1 + i)]
                buf[size : size + TEXT_ROWS, :] = text_pair[text_rows, at(i)]
            q, go = queries[: 2 * size, :], outs[: 2 * size, :]
            seen = keep[image : image + 1, :]
            s = lax.dot_general(q, keys[...], NT, preferred_element_type=F32)
            s = jnp.where(seen == 1, s, jnp.where(seen == 0, -1000000000.0, -jnp.inf))
            e = jnp.exp(s - jnp.max(s, axis=1, keepdims=True))
            p = e * (1.0 / jnp.sum(e, axis=1, keepdims=True))
            low = p.astype(BF16)
            out = dot(low, values[...])
            dv = lax.dot_general(low, go, TN, preferred_element_type=F32)
            dp = lax.dot_general(go, values[...], NT, preferred_element_type=F32)
            ds = (p * (dp - jnp.sum(dp * p, axis=1, keepdims=True))).astype(BF16)
            dq = dot(ds, keys[...]) * scale
            dk = lax.dot_general(ds, q, TN, preferred_element_type=F32)
            merge = lambda part: jnp.where(lane < HEAD, part[:size], part[size:]).astype(BF16)
            attended[rows, at(0)] = merge(out)
            grad_triple[rows, at(0)] = merge(dq)
            grad_triple[rows, at(1)] = dk[:size].astype(BF16)
            grad_triple[rows, at(2)] = dv[:size].astype(BF16)
            grad_text[text_rows, at(0)] = dk[size : size + TEXT_ROWS].astype(BF16)
            grad_text[text_rows, at(1)] = dv[size : size + TEXT_ROWS].astype(BF16)
        return carry

    lax.fori_loop(0, inner // (2 * HEAD), heads, 0)

    def text_block(q, carry):
        @pl.when(q > 0)
        def _():
            waited(stage, o_sem)
        for col in range(0, width, 512):
            cols = slice(col, col + 512)
            stage[:, cols] = lax.dot_general(text[:, pl.ds(pl.multiple_of(q * 1024, 128), 1024)], grad_text[:, cols], TN, preferred_element_type=F32).astype(BF16)
        pltpu.make_async_copy(stage, g_text.at[pl.ds(pl.multiple_of(q * 1024, 128), 1024)], o_sem).start()
        return carry

    lax.fori_loop(0, text_dim // 1024, text_block, 0)

    waited(w_out, sems.at[0])
    bias = vec[V_OUT : V_OUT + 1, :width]
    for image in range(3):
        rows = pl.ds(STARTS[image], SIZES[image])
        block_output[rows, :] = (
            present[0, image].astype(F32) * (residual[rows, :] + (dot(attended[rows, :], w_out[...]) + bias))
        ).astype(BF16)
    for col in range(0, width, 512):
        cols = slice(col, col + 512)
        g_out[:, cols] = lax.dot_general(attended[...], g_low[:, cols], TN, preferred_element_type=F32).astype(BF16)
        g_attend[:, cols] = lax.dot_general(normed[...], grad_triple[:, cols], TN, preferred_element_type=F32).astype(BF16)
    last = lax.dot_general(normed[...], grad_triple[:, width:], TN, preferred_element_type=F32).astype(BF16)
    half = width // parts // 2
    for f in range(parts):
        for i in range(2):
            g_more[f * half : (f + 1) * half, 512 * i : 512 * (i + 1)] = last[(2 * f + i) * half : (2 * f + i + 1) * half]
    waited(w_attend, sems.at[1])
    for col in range(0, width, 512):
        cols = slice(col, col + 512)
        rows_grad[:, cols] = lax.dot_general(grad_triple[...], w_attend[cols, :], NT, preferred_element_type=F32)

    more[...] = jnp.zeros_like(more)
    gain = vec[V_ATTN_GAIN : V_ATTN_GAIN + 1, :width]
    for image in range(3):
        def pair(i, rows):
            grad = rows_grad[rows, :]
            return grad, grad * hats[rows, :]
        plain, crossed = two_sums(image, width, pair)
        def put(i, rows, value):
            rows_grad[rows, :] = value + g_low[rows, :].astype(F32)
        norm_pull(image, gain, inverses[6 + image : 7 + image, :], lambda rows: rows_grad[rows, :], lambda rows: hats[rows, :], plain, crossed, put)
        def ends(i, rows):
            value = rows_grad[rows, :]
            r_low[rows, :] = value.astype(BF16)
            return value, g_low[rows, :].astype(F32)
        total, outer = two_sums(image, width, ends)
        for row, value in ((G_ATTN_GAIN, crossed), (G_ATTN_SHIFT, plain), (G_SECOND, total), (G_OUT, outer)):
            more[row : row + 1, :] = more[row : row + 1, :] + value[:1]
    waited(stage, o_sem)


def middle(triple, text_pair, keep, grad_attended, cotangent, normed, hats, residual, text, vec, inverses, present, full, parts, inner, text_dim):
    pix, width = cotangent.shape
    bf = lambda *shape: jax.ShapeDtypeStruct(shape, BF16)
    vm = lambda *shape: pltpu.VMEM(shape, BF16)
    hbm, vmem = pl.BlockSpec(memory_space=pl.ANY), pl.BlockSpec(memory_space=pltpu.VMEM)
    return pl.pallas_call(
        functools.partial(middle_kernel, parts, inner, text_dim),
        out_shape=[bf(pix, width), bf(pix, width), bf(inner, width), bf(width, width), bf(width // 2, width), bf(text_dim, width), jax.ShapeDtypeStruct((16, width), F32)],
        in_specs=[vmem] * 11 + [pl.BlockSpec(memory_space=pltpu.SMEM), hbm],
        out_specs=[vmem] * 5 + [hbm, vmem],
        scratch_shapes=[
            vm(pix, inner), vm(pix, 3 * inner), vm(text.shape[0], 2 * inner), pltpu.VMEM((pix, width), F32),
            vm(width, 3 * inner), vm(inner, width), vm(1024, width), vm(pix, width),
            vm(2 * max(SIZES), 2 * HEAD), vm(2 * max(SIZES), 2 * HEAD), vm(KEYS, 2 * HEAD), vm(KEYS, 2 * HEAD),
            pltpu.SemaphoreType.DMA((2,)), pltpu.SemaphoreType.DMA(()),
        ],
        compiler_params=pltpu.CompilerParams(vmem_limit_bytes=60 << 20),
        name="middle",
    )(triple, text_pair, keep, grad_attended, cotangent, normed, hats, residual, text, vec, inverses, present, full)


def fold_attend(part, width):
    more = part[..., width:]
    half = part.shape[-2] // 2
    return [part[..., :width], jnp.concatenate([more[..., :half, :], more[..., half:, :]], -1)]


def unfold_attend(wide, more):
    half = more.shape[1] // 2
    return jnp.concatenate([wide, jnp.concatenate([more[:, :half], more[:, half:]], 0)], 1)


def body(
    pixels,
    embedding,
    text_states,
    text_mask,
    occupancy,
    cotangent,
    in_gain,
    in_shift,
    conv_first,
    first_bias,
    emb_weight,
    emb_bias,
    mid_gain,
    mid_shift,
    conv_second,
    second_bias,
    skip_weight,
    skip_bias,
    attn_gain,
    attn_shift,
    attend_weight,
    text_weight,
    out_weight,
    out_bias,
):
    place = lax.axis_index("fsdp")
    group = lax.axis_index("dp")
    parts = lax.axis_size("fsdp")
    replicas = lax.axis_size("dp")
    depth = emb_weight.shape[0]
    images_here = embedding.shape[0]
    emb_act = jax.nn.silu(embedding.astype(F32)).astype(BF16)
    emb_cut = emb_act.reshape(images_here, parts, depth).transpose(1, 0, 2)
    emb_cut = jnp.pad(emb_cut, ((0, 0), (0, 0), (0, 128 - depth)))

    lane = lax.broadcasted_iota(jnp.int32, (1, 128), 1)

    def placed(vectors):
        size = vectors[0].shape[0]
        wide = jnp.concatenate([jnp.stack(vectors)] * (128 // size), 1)
        return jnp.where(lane // size == lax.rem(place, 128 // size), wide, jnp.zeros_like(wide))

    lines = [placed((in_gain, in_shift)), placed((emb_bias,)), placed((first_bias, mid_gain, mid_shift, second_bias, skip_bias, attn_gain, attn_shift, out_bias))]
    room = 16 - images_here - sum(line.shape[0] for line in lines)
    flat = jnp.concatenate(lines + [jnp.zeros((room, 128), BF16)] if room else lines, 0)[None]
    note = jnp.concatenate([emb_cut, jnp.broadcast_to(flat, (parts,) + flat.shape[1:])], 1)
    channels = skip_weight.shape[1]
    inner = out_weight.shape[0] * parts
    own = jnp.concatenate([conv_first, conv_second, skip_weight, out_weight] + fold_attend(attend_weight, channels) + [text_weight], 0)
    text_len = text_states.shape[1]
    (full, modulation, vec, _, act1, act2, mid_hats, residual, hats, normed, triple, text_pair, grad_attended, inverses, text_rows) = forward_all(
        own, note, jnp.pad(emb_weight, ((0, 128 - depth), (0, 0))), pixels, text_states, cotangent, occupancy, images_here, inner, replicas, parts)
    keep = (text_mask > 0).astype(jnp.int32)
    keep = jnp.stack([
        jnp.pad(jnp.pad(keep[i], (size, 0), constant_values=1), (0, KEYS - size - text_len), constant_values=2)
        for i, size in enumerate(SIZES)
    ])
    block_output, r_low, g_out, g_attend, g_more, g_text, more = middle(
        triple, text_pair, keep, grad_attended, cotangent, normed, hats, residual, text_rows, vec, inverses, occupancy, full, parts, inner, text_states.shape[2]
    )
    (grad_text_weight, grad_out_weight, attend, attend_more, grad_conv_second, grad_skip_weight, grad_conv_first,
     notes, _, _, _, grad_pixels, narrow, wide) = reduce_all(
        [g_text, g_out, g_attend, g_more], full, r_low, pixels, vec, modulation, inverses, act1, act2, mid_hats, note, more,
        inner, text_states.shape[2], images_here, replicas, parts, 512 // parts,
    )
    grad_attend_weight = unfold_attend(attend, attend_more)
    mod_count = notes.shape[1] - 16
    mod_rows = notes[:, :mod_count].reshape(-1, 2 * channels)
    all_act = notes[:, mod_count : mod_count + images_here, :depth].reshape(-1, depth)
    grad_emb_weight = dot(all_act, mod_rows, ((0,), (0,)))
    grad_emb_bias = jnp.sum(mod_rows.astype(F32), axis=0)
    grad_emb_bias = lax.dynamic_slice_in_dim(grad_emb_bias, place * depth, depth, 0)
    small = lambda row: (narrow[row] if row < G_FIRST else wide[row - G_FIRST]).reshape(-1)
    grad_second_bias = small(G_SECOND)
    return (
        block_output,
        grad_pixels,
        small(G_IN_GAIN),
        small(G_IN_SHIFT),
        grad_conv_first,
        small(G_FIRST),
        grad_emb_weight,
        grad_emb_bias,
        small(G_MID_GAIN),
        small(G_MID_SHIFT),
        grad_conv_second,
        grad_second_bias,
        grad_skip_weight,
        grad_second_bias,
        small(G_ATTN_GAIN),
        small(G_ATTN_SHIFT),
        grad_attend_weight,
        grad_text_weight,
        grad_out_weight,
        small(G_OUT),
    )


def solution(mesh):
    rows = P(("dp", "fsdp"), None)
    vector = P("fsdp")
    matrix = P("fsdp", None)
    weights = (vector, vector, matrix, vector, matrix, vector, vector, vector, matrix, vector, matrix, vector, vector, vector, matrix, matrix, matrix, vector)
    return jax.shard_map(
        body,
        mesh=mesh,
        in_specs=(rows, rows, P(("dp", "fsdp"), None, None), rows, rows, rows) + weights,
        out_specs=(rows, rows) + weights,
        check_vma=False,
    )
```

```python
import functools

import jax
import jax.numpy as jnp
from jax import lax
from jax.experimental import pallas as pl
from jax.experimental.pallas import tpu as pltpu
from jax.sharding import PartitionSpec as P

BF16 = jnp.bfloat16
F32 = jnp.float32
HEADS = 8
HEAD = 64
GROUPS = 32
UNIT = 4
SHAPES = ((4 * UNIT, 4 * UNIT), (3 * UNIT, 5 * UNIT), (5 * UNIT, 3 * UNIT))
SIZES = tuple(height * breadth for height, breadth in SHAPES)
STARTS = (0, SIZES[0], SIZES[0] + SIZES[1])
PIX = sum(SIZES)
EDGE = 32
BASES = tuple(EDGE + start + i * EDGE for i, start in enumerate(STARTS))
PADDED = PIX + 4 * EDGE
BLOCK = 1152
KEYS = 384
TEXT_ROWS = 80
SUB = 16
NT = (((1,), (1,)), ((), ()))
TN = (((0,), (0,)), ((), ()))
V_IN_GAIN, V_IN_SHIFT, V_EMB, V_FIRST, V_MID_GAIN, V_MID_SHIFT, V_SECOND, V_SKIP, V_ATTN_GAIN, V_ATTN_SHIFT, V_OUT = range(11)


def dot(left, right, dims=((1,), (0,))):
    return lax.dot_general(left, right, (dims, ((), ())), preferred_element_type=F32)


def group_mean(sums, count):
    channels = sums.shape[1]
    width = channels // GROUPS
    lane = lax.broadcasted_iota(jnp.int32, sums.shape, 1)
    step = 1
    while step < width:
        odd = lax.rem(lane // step, 2) == 1
        sums = sums + jnp.where(odd, pltpu.roll(sums, step, 1), pltpu.roll(sums, channels - step, 1))
        step *= 2
    return sums / (count * width)


def rows_of(image, i):
    return pl.ds(pl.multiple_of(STARTS[image] + i * SUB, SUB), SUB)


def over_rows(image, work, start):
    return lax.fori_loop(0, SIZES[image] // SUB, lambda i, carry: work(i, rows_of(image, i), carry), start)


def column_sum(image, channels, value):
    def add(i, rows, carry):
        v = value(rows)
        return carry + (v[:8] + v[8:])
    total = over_rows(image, add, jnp.zeros((8, channels), F32))
    return jnp.broadcast_to(jnp.sum(total, axis=0, keepdims=True), (8, channels))


def norm_figures(image, channels, value):
    count = SIZES[image]
    center = group_mean(column_sum(image, channels, value), count)[:1]
    spread = group_mean(column_sum(image, channels, lambda rows: jnp.square(value(rows) - center)), count)[:1]
    return center, lax.rsqrt(spread + 1e-05)


def store_padded(pad, image, i, act):
    breadth = SHAPES[image][1]
    at = pl.ds(pl.multiple_of(BASES[image] + i * SUB, SUB), SUB)
    column = lax.rem(i * SUB + lax.broadcasted_iota(jnp.int32, (SUB, 1), 0), breadth)
    pad[0, at, :] = jnp.where(column == breadth - 1, 0.0, act).astype(BF16)
    pad[1, at, :] = act.astype(BF16)
    pad[2, at, :] = jnp.where(column == 0, 0.0, act).astype(BF16)


def zero_edges(pad):
    zeros = jnp.zeros((EDGE, pad.shape[2]), BF16)
    for side in range(3):
        for at in [base - EDGE for base in BASES] + [PADDED - EDGE]:
            pad[side, at : at + EDGE, :] = zeros


def shifted(pad, tap, image, cols, flip=False):
    down, across = divmod(8 - tap if flip else tap, 3)
    start = BASES[image] + (down - 1) * SHAPES[image][1] + across - 1
    return pad[across, start : start + SIZES[image], cols]


def gather_blocks(pad, blocks, out):
    per_tap = pad.shape[2] // 128
    for i, block in enumerate(blocks):
        tap, col = divmod(block, per_tap)
        for image in range(3):
            out[STARTS[image] : STARTS[image] + SIZES[image], i * 128 : (i + 1) * 128] = shifted(
                pad, tap, image, slice(col * 128, (col + 1) * 128)
            )


def shard_of(full, f, *where):
    return full.at[(f // 2, f % 2 if isinstance(f, int) else lax.rem(f, 2)) + where]


class Rows:
    def __init__(self, parts, pix_channels, channels, text_dim, inner):
        self.parts = parts
        sizes = (9 * pix_channels // parts, 9 * channels // parts, pix_channels // parts, inner // parts, channels // parts, channels // parts // 2, text_dim // parts)
        starts = [0]
        for size in sizes:
            starts.append(starts[-1] + size)
        self.first, self.second, self.skip, self.out, self.attend, self.attend_more, self.text = zip(starts, sizes)
        self.total = starts[-1]

    def arrivals(self, which):
        size = which[1]
        blocks = []
        for block in range(size * self.parts // 128):
            pieces, at = [], block * 128
            while at < (block + 1) * 128:
                shard, inside = divmod(at, size)
                count = min(size - inside, (block + 1) * 128 - at)
                pieces.append((shard, inside, count))
                at += count
            blocks.append((max(inside + count for _, inside, count in pieces), block, pieces))
        blocks.sort()
        each = BLOCK // 128
        steps = [blocks[i : i + each] for i in range(0, len(blocks), each)]
        return [([(block, pieces) for _, block, pieces in step], step[-1][0]) for step in steps]

    def load_step(self, full, which, step, buf, sem):
        at = 0
        for _, pieces in step:
            for shard, inside, count in pieces:
                pltpu.make_async_copy(shard_of(full, shard, pl.ds(which[0] + inside, count)), buf.at[pl.ds(at, count)], sem).start()
                at += count

    def pack(self, weights, own, sems):
        first, second, skip, out, attend, text = weights
        half = self.attend_more[1]
        wide = own.shape[1]
        jobs = [(ref, which) for ref, which in ((first, self.first), (second, self.second), (skip, self.skip), (out, self.out), (text, self.text))]
        jobs.append((attend.at[:, pl.ds(0, wide)], self.attend))
        for i, (ref, (start, size)) in enumerate(jobs):
            pltpu.make_async_copy(ref, own.at[pl.ds(start, size)], sems.at[i]).start()
        for i in range(2):
            pltpu.make_async_copy(
                attend.at[pl.ds(i * half, half), pl.ds(wide, wide // 2)],
                own.at[pl.ds(self.attend_more[0], half), pl.ds(i * wide // 2, wide // 2)],
                sems.at[6 + i],
            ).start()

    def packed(self, own, sems):
        wide = own.shape[1]
        for i, (start, size) in enumerate((self.first, self.second, self.skip, self.out, self.text, self.attend)):
            waited(own.at[pl.ds(start, size)], sems.at[i])
        for i in range(2):
            waited(own.at[pl.ds(self.attend_more[0], self.attend_more[1]), pl.ds(i * wide // 2, wide // 2)], sems.at[6 + i])

    def load(self, full, which, q, rows, buf, sem):
        start, size = which
        each = rows // size
        for i in range(each):
            pltpu.make_async_copy(shard_of(full, q * each + i, pl.ds(start, size)), buf.at[pl.ds(i * size, size)], sem).start()

    def load_attend(self, full, buf, sem):
        start, size = self.attend
        more, half = self.attend_more
        def one(f, carry):
            at = pl.multiple_of(f * size, SUB)
            pltpu.make_async_copy(shard_of(full, f, pl.ds(start, size)), buf.at[pl.ds(at, size), pl.ds(0, 1024)], sem).start()
            for i in range(2):
                pltpu.make_async_copy(
                    shard_of(full, f, pl.ds(more, half), pl.ds(512 * i, 512)),
                    buf.at[pl.ds(pl.multiple_of(at + i * half, SUB), half), pl.ds(1024, 512)],
                    sem,
                ).start()
            return carry
        lax.fori_loop(0, self.parts, one, 0)


def outgoing(cotangent, present, image):
    rows = pl.ds(STARTS[image], SIZES[image])
    return (cotangent[rows, :].astype(F32) * present[0, image].astype(F32)).astype(BF16)


def waited(ref, sem):
    pltpu.make_async_copy(ref, ref, sem).wait()


class Forward:
    def __init__(self, rows, full, pixels, text_in, cotangent, present, vec, mod, outs, scratch):
        self.rows, self.full, self.pixels, self.text_in, self.cotangent, self.present, self.vec, self.mod = rows, full, pixels, text_in, cotangent, present, vec, mod
        (self.o_a1, self.o_a2, self.o_mid_hat, self.o_residual, self.o_hat, self.o_normed, self.triple, self.text_pair, self.grad_attended, self.inverses, self.o_text) = outs
        (self.a1, self.a2, self.patch, self.weight, self.acc0, self.acc1, self.normed, self.w_attend, self.w_skip, self.w_out, self.text, self.w_sem, self.s_sem, self.o_sem) = scratch

    def out_copy(self, i, src, dst):
        return pltpu.make_async_copy(src, dst, self.o_sem.at[i])

    def row(self, r, channels=1024):
        return self.vec[r : r + 1, :channels]

    def zero(self):
        zero_edges(self.a1)
        zero_edges(self.a2)
        count = self.text_in.shape[1]
        for image in range(3):
            at = image * TEXT_ROWS
            self.text[at + TEXT_ROWS - SUB : at + TEXT_ROWS, :] = jnp.zeros((SUB, self.text.shape[1]), BF16)
            self.text[at : at + count, :] = self.text_in[image]
        self.out_copy(6, self.text, self.o_text).start()

    def first_norm(self, image):
        pixels, channels = self.pixels, self.pixels.shape[1]
        value = lambda rows: pixels[rows, :].astype(F32)
        center, inverse = norm_figures(image, channels, value)
        gain, shift = self.row(V_IN_GAIN, channels) * inverse, self.row(V_IN_SHIFT, channels)
        self.inverses[image : image + 1, :channels] = inverse
        self.inverses[16 + image : 17 + image, :channels] = center
        def act(i, rows, carry):
            store_padded(self.a1, image, i, jax.nn.silu((value(rows) - center) * gain + shift))
            return carry
        over_rows(image, act, 0)
        if image == 2:
            self.out_copy(0, self.a1, self.o_a1).start()

    def load_text(self, q):
        self.rows.load(self.full, self.rows.text, q, 1024, self.weight.at[lax.rem(q, 2)], self.w_sem.at[lax.rem(q, 2)])

    def conv_step(self, q, pad, acc, which, steps, early):
        def load(known):
            self.rows.load_step(self.full, which, steps[known][0], self.weight.at[known % 2], self.w_sem.at[known % 2])
        for known in range(len(steps)):
            ahead = known + 1 < len(steps) and early[known + 1]
            @pl.when(q == known)
            def _():
                if not early[known]:
                    load(known)
                if ahead:
                    load(known + 1)
                gather_blocks(pad, [block for block, _ in steps[known][0]], self.patch)
        par = lax.rem(q, 2)
        waited(self.weight.at[par], self.w_sem.at[par])
        @pl.when(q == 0)
        def _():
            acc[...] = jnp.zeros_like(acc)
        for col in (0, 512):
            cols = slice(col, col + 512)
            acc[:, cols] = acc[:, cols] + dot(self.patch[...], self.weight[par, :, cols])

    def mid_norm(self, image):
        acc, channels = self.acc0, self.acc0.shape[1]
        bias = self.row(V_FIRST)
        def shift_up(i, rows, carry):
            acc[rows, :] = acc[rows, :] + bias
            return carry
        over_rows(image, shift_up, 0)
        center, inverse = norm_figures(image, channels, lambda rows: acc[rows, :])
        self.inverses[3 + image : 4 + image, :] = inverse
        scale, shift = 1.0 + self.mod[image : image + 1, :channels], self.mod[image : image + 1, channels:]
        gain, lift = self.row(V_MID_GAIN) * scale, self.row(V_MID_SHIFT) * scale + shift
        def act(i, rows, carry):
            hat = (acc[rows, :] - center) * inverse
            acc[rows, :] = hat
            store_padded(self.a2, image, i, jax.nn.silu(hat * gain + lift))
            return carry
        over_rows(image, act, 0)
        if image == 2:
            self.out_copy(1, self.a2, self.o_a2).start()
            self.out_copy(2, self.acc0, self.o_mid_hat).start()

    def load_small(self):
        rows = self.rows
        def one(f, carry):
            for i, ((start, size), buf) in enumerate(((rows.skip, self.w_skip), (rows.out, self.w_out))):
                pltpu.make_async_copy(shard_of(self.full, f, pl.ds(start, size)), buf.at[pl.ds(pl.multiple_of(f * size, SUB), size)], self.s_sem.at[i]).start()
            return carry
        lax.fori_loop(0, rows.parts, one, 0)
        rows.load_attend(self.full, self.w_attend, self.s_sem.at[2])

    def skip_product(self):
        for i, buf in enumerate((self.w_skip, self.w_out, self.w_attend)):
            waited(buf, self.s_sem.at[i])
        self.acc1[...] = self.acc1[...] + dot(self.pixels[...], self.w_skip[...])

    def attended_grad(self):
        for image in range(3):
            rows = pl.ds(STARTS[image], SIZES[image])
            grad = outgoing(self.cotangent, self.present, image)
            self.grad_attended[rows, :] = lax.dot_general(grad, self.w_out[...], NT, preferred_element_type=F32).astype(BF16)

    def last_norm(self, image):
        acc, hats, channels = self.acc1, self.acc0, self.acc1.shape[1]
        if image == 0:
            self.out_copy(2, self.acc0, self.o_mid_hat).wait()
        bias = self.row(V_SECOND) + self.row(V_SKIP)
        def shift_up(i, rows, carry):
            acc[rows, :] = acc[rows, :] + bias
            return carry
        over_rows(image, shift_up, 0)
        center, inverse = norm_figures(image, channels, lambda rows: acc[rows, :])
        self.inverses[6 + image : 7 + image, :] = inverse
        gain, shift = self.row(V_ATTN_GAIN), self.row(V_ATTN_SHIFT)
        def act(i, rows, carry):
            hat = (acc[rows, :] - center) * inverse
            hats[rows, :] = hat
            self.normed[rows, :] = (hat * gain + shift).astype(BF16)
            return carry
        over_rows(image, act, 0)
        if image == 2:
            self.out_copy(3, self.acc1, self.o_residual).start()
            self.out_copy(4, self.acc0, self.o_hat).start()
            self.out_copy(5, self.normed, self.o_normed).start()

    def project(self, i):
        cols = slice(512 * i, 512 * (i + 1))
        self.triple[:, cols] = dot(self.normed[...], self.w_attend[:, cols]).astype(BF16)

    def text_step(self, q, total):
        if q + 1 < 4:
            self.load_text(q + 1)
        par = q % 2
        waited(self.weight.at[par, pl.ds(0, 1024)], self.w_sem.at[par])
        part = dot(self.text[:, 1024 * q : 1024 * (q + 1)], self.weight[par, :1024, :])
        if q:
            part = total[...] + part
        if q < 3:
            total[...] = part
        else:
            self.text_pair[...] = part.astype(BF16)

    def finish(self):
        self.out_copy(0, self.a1, self.o_a1).wait()
        self.out_copy(1, self.a2, self.o_a2).wait()
        self.out_copy(3, self.acc1, self.o_residual).wait()
        self.out_copy(4, self.acc0, self.o_hat).wait()
        self.out_copy(5, self.normed, self.o_normed).wait()
        self.out_copy(6, self.text, self.o_text).wait()


MESH = pl.DeviceIdType.MESH
DEPTH = 4


STEPS = True
UNP = 3
BUDGET = 7.5
SHOW = False


class Where:
    def __init__(self, replicas, parts):
        self.replicas, self.parts = replicas, parts
        self.span = parts // (2 * DEPTH)
        self.group = lax.axis_index("dp")
        self.place = lax.axis_index("fsdp")
        self.core = lax.rem(self.place, 2)
        self.y = lax.rem(self.place // 2, self.span)
        self.z = self.place // (2 * self.span)
        self.side = lax.rem(self.group, 2)

    def index(self, z, y, core):
        return (z * self.span + y) * 2 + core

    def device(self, z=None, y=None, core=None, flip=False):
        z = self.z if z is None else z
        y = self.y if y is None else y
        core = self.core if core is None else core
        group = self.group + 1 - 2 * self.side if flip else self.group
        return (group, self.index(z, y, core))

    def barrier(self):
        sem = pltpu.get_barrier_semaphore()
        greet = lambda device: pl.semaphore_signal(sem, inc=1, device_id=device, device_id_type=MESH)
        greet(self.device(flip=True))
        def one(i, carry):
            greet((self.group, lax.rem(self.place + i, self.parts)))
            return carry
        lax.fori_loop(1, self.parts, one, 0)
        pl.semaphore_wait(sem, self.parts)


def forward_kernel(replicas, parts, rows, lead, lag, inner, images, *refs):
    weights, refs = refs[:6], refs[6:]
    note, emb, pixels, text, cotangent, present = refs[:6]
    full, mod, vec, notes = refs[6:10]
    outs = refs[10:21]
    own, part, sums, text_total = refs[21:25]
    scratch = refs[25:39]
    (n_send, n_recv, m_send, m_recv, z_send, z_recv, y_send, y_recv, s_send, s_recv, x_send, x_recv, c_send, c_recv, own_sem) = refs[39:]
    me = Where(replicas, parts)
    span = me.span
    total, width = own.shape
    chunks = total // rows
    joint, apart = 5 * width // 8, 3 * width // 8
    side = me.side
    thin = width // 4
    z_cols = pl.ds(pl.multiple_of(side * thin, thin), width - thin)
    a_cols = pl.ds(pl.multiple_of(side * apart, 128), joint)
    thin_cols = pl.ds(pl.multiple_of((1 - side) * (width - thin), thin), thin)
    thin_out = pl.ds(pl.multiple_of(side * (width - thin), thin), thin)
    b_cols = pl.ds(pl.multiple_of((1 - side) * joint, 128), apart)
    b_out = pl.ds(pl.multiple_of(side * joint, 128), apart)

    table = Rows(parts, pixels.shape[1], width, text.shape[2], inner)
    table.pack(weights, own, own_sem)
    me.barrier()
    table.packed(own, own_sem)
    local = pltpu.make_async_copy(own, full.at[me.place // 2, me.core], own_sem.at[0])
    local.start()

    def at(k):
        return pl.ds(pl.multiple_of(k * rows, 16), rows)

    def copy(src, dst, send, recv, device):
        return pltpu.make_async_remote_copy(src_ref=src, dst_ref=dst, send_sem=send, recv_sem=recv, device_id=device, device_id_type=MESH)

    def piece(k, z, y, cols, core=None):
        return full.at[z * span + y, me.core if core is None else core, at(k), cols]

    def z_copy(k, z, step, mine):
        src = own.at[at(k), z_cols] if mine else piece(k, z, me.y, z_cols)
        return copy(src, piece(k, z, me.y, z_cols), z_send.at[k, z, (step + 1) // 2], z_recv.at[k, z], me.device(z=me.z + step))

    def y_copy(k, z, turn, mine):
        src = own.at[at(k), a_cols] if mine else piece(k, z, me.y, a_cols)
        return copy(src, piece(k, z, me.y, a_cols), y_send.at[k, z, turn - 1], y_recv.at[k, z, turn - 1], me.device(y=lax.rem(me.y + turn, span)))

    def thin_copy(k, z):
        return copy(piece(k, z, me.y, thin_out), piece(k, z, me.y, thin_out), s_send.at[k, z], s_recv.at[k, z], me.device(flip=True))

    def x_copy(k, z, turn):
        y = lax.rem(me.y + turn, span)
        return copy(piece(k, z, y, b_out), piece(k, z, y, b_out), x_send.at[k, z, turn - 1], x_recv.at[k, z, turn - 1], me.device(flip=True))

    def core_copy(k, core):
        lane = full.at[:, core, at(k)]
        return copy(lane, lane, c_send.at[k], c_recv.at[k], me.device(core=1 - me.core))

    below = lambda s: (me.z - s >= 0, me.z - s)
    above = lambda s: (me.z + s < DEPTH, me.z + s)

    def start_own(k):
        @pl.when(me.z < DEPTH - 1)
        def _():
            z_copy(k, me.z, 1, True).start()
        @pl.when(me.z > 0)
        def _():
            z_copy(k, me.z, -1, True).start()
        for turn in range(1, span):
            y_copy(k, me.z, turn, True).start()

    def along_z(k, s):
        for (ok, z), step in ((below(s), 1), (above(s), -1)):
            @pl.when(ok)
            def _():
                z_copy(k, z, step, False).wait_recv()
                if s < DEPTH - 1:
                    more = me.z < DEPTH - 1 if step > 0 else me.z > 0
                    @pl.when(more)
                    def _():
                        z_copy(k, z, step, False).start()
                for turn in range(1, span):
                    y_copy(k, z, turn, False).start()
                thin_copy(k, z).start()

    def across(k, s):
        for ok, z in ((below(s), above(s)) if s else (below(0),)):
            @pl.when(ok)
            def _():
                for turn in range(1, span):
                    y_copy(k, z, turn, False).wait_recv()
                    x_copy(k, z, span - turn).start()

    def beside(k, s):
        for ok, z in ((below(s), above(s)) if s else (below(0),)):
            @pl.when(ok)
            def _():
                for turn in range(1, span):
                    x_copy(k, z, turn).wait_recv()

    def beside_thin(k, s):
        for ok, z in (below(s), above(s)):
            @pl.when(ok)
            def _():
                thin_copy(k, z).wait_recv()

    def lane_in(k):
        core_copy(k, 1 - me.core).wait_recv()

    def to_all(make):
        def one(i, carry):
            make(lax.rem(me.place + i, parts)).start()
            return carry
        lax.fori_loop(1, parts, one, 0)

    def wait_all(ref, send, recv):
        others = ref.at[pl.ds(0, parts - 1)]
        every = copy(others, others, send, recv, me.device(core=1 - me.core))
        every.wait_send()
        every.wait_recv()

    def modulate():
        wait_all(sums, m_send, m_recv)
        total = jnp.sum(sums[...], axis=0)
        blocks = emb.shape[1] // 128
        for j in range(blocks):
            for image in range(images):
                row = image * blocks + j
                mod[image : image + 1, j * 128 : (j + 1) * 128] = total[row : row + 1, :] + vec[V_EMB : V_EMB + 1, j * 128 : (j + 1) * 128]

    def unpack():
        wait_all(notes, n_send, n_recv)
        vec[...] = jnp.zeros_like(vec)
        for row in range(V_OUT + 1):
            size = {V_IN_GAIN: pixels.shape[1], V_IN_SHIFT: pixels.shape[1], V_EMB: emb.shape[1]}.get(row, width)
            each = 128 * parts // size
            for block in range(size // 128):
                value = notes[block * each, images + row : images + row + 1, :].astype(jnp.float32)
                for i in range(1, each):
                    value = value + notes[block * each + i, images + row : images + row + 1, :].astype(jnp.float32)
                vec[row : row + 1, block * 128 : (block + 1) * 128] = value
        rows_in = notes.shape[1]
        blocks = emb.shape[1] // 128
        for j in range(blocks):
            product = jnp.dot(notes[...].reshape(parts * rows_in, 128), emb[:, j * 128 : (j + 1) * 128], preferred_element_type=jnp.float32)
            product = product.reshape(parts, rows_in, 128)
            for image in range(images):
                part[:, image * blocks + j, :] = product[:, image, :]
        to_all(lambda far: copy(part.at[far], sums.at[me.place], m_send, m_recv, (me.group, far)))
        sums[me.place] = part[me.place]

    to_all(lambda far: copy(note.at[far], notes.at[me.place], n_send, n_recv, (me.group, far)))
    notes[me.place] = note[me.place]

    forward = Forward(table, full, pixels, text, cotangent, present, vec, mod, outs, scratch)
    ready = (DEPTH + 1) * lag
    have = lambda row: (row - 1) // rows + ready
    plan = []
    spent = {}

    def add(earliest, cost, work):
        slot = max([earliest] + [when for when, _ in plan[-1:]])
        while spent.get(slot, 0) and spent[slot] + cost > BUDGET:
            slot += 1
        spent[slot] = spent.get(slot, 0) + cost
        plan.append((slot, work))
        return slot

    add(0, 1, forward.zero)
    add(3, 5, unpack)
    for image in range(3):
        add(4, 2, functools.partial(forward.first_norm, image))
    convs = []

    def add_conv(which, pad, acc):
        steps = table.arrivals(which)
        slots, early = [], []
        for i, (_, end) in enumerate(steps):
            slot = add(have(which[0] + end), 3.4, None)
            early.append(i > 0 and have(which[0] + end) <= slots[-1])
            slots.append(slot)
        convs.append((which, pad, acc, steps, early, slots))

    add_conv(table.first, forward.a1, forward.acc0)
    add(0, 1, modulate)
    for image in range(3):
        add(0, 2.4, functools.partial(forward.mid_norm, image))
    add_conv(table.second, forward.a2, forward.acc1)
    add(have(sum(table.attend_more)), 0.5, forward.load_small)
    add(0, 2.2, forward.skip_product)
    for image in range(3):
        add(0, 2, functools.partial(forward.last_norm, image))
    add(0, 1.5, forward.attended_grad)
    for i in range(3):
        add(0, 1.4, functools.partial(forward.project, i))
    slots = max(chunks + ready, plan[-1][0] + 1)
    if SHOW: print(slots, [(s, getattr(getattr(w, "func", w), "__name__", "conv")) for s, w in plan])

    def steps(t):
        if not STEPS:
            pl.when(t == DEPTH * lag - 1)(local.wait)
            pl.when(t == 3)(unpack)
            return
        def conv(which, pad, acc, table_steps, early, when):
            low, high = jnp.int32(0), jnp.int32(0)
            for slot in when:
                low = low + jnp.where(t > slot, 1, 0)
                high = high + jnp.where(t >= slot, 1, 0)
            def one(q, carry):
                forward.conv_step(q, pad, acc, which, table_steps, early)
                return carry
            lax.fori_loop(low, high, one, 0)
        pending = list(convs)
        pl.when(t == DEPTH * lag - 1)(local.wait)
        for i, (slot, work) in enumerate(plan):
            if work is not None:
                pl.when(t == slot)(work)
            elif i == 0 or plan[i - 1][1] is not None:
                conv(*pending.pop(0))

    for k in range(min(lead, chunks)):
        start_own(k)

    last = 2 * (DEPTH - 1) + 3

    def slot(t, carry):
        def stage(delay, work):
            k = t - delay
            @pl.when(jnp.logical_and(k >= 0, k < chunks))
            def _():
                work(k)
        @pl.when(t + lead < chunks)
        def _():
            start_own(t + lead)
        for s in range(1, DEPTH):
            stage((s - 1) * lag, functools.partial(along_z, s=s))
        for s in range(DEPTH):
            stage(s * lag, functools.partial(across, s=s))
        for s in range(1, DEPTH):
            stage(s * lag, functools.partial(beside_thin, s=s))
        for s in range(DEPTH):
            stage((s + 1) * lag, functools.partial(beside, s=s))
        stage(DEPTH * lag, lambda k: core_copy(k, me.core).start())
        stage(ready, lane_in)
        steps(t)
        return carry

    lax.fori_loop(0, slots, slot, 0)
    if STEPS:
        forward.load_text(jnp.int32(0))
        for q in range(4):
            forward.text_step(q, text_total)
    else:
        modulate()

    def finish(k, carry):
        for step, edge in ((1, me.z < DEPTH - 1), (-1, me.z > 0)):
            for s in range(DEPTH - 1):
                ok, z = below(s) if step > 0 else above(s)
                @pl.when(jnp.logical_and(ok, edge))
                def _():
                    z_copy(k, z, step, False).wait_send()
        for z in range(DEPTH):
            for turn in range(1, span):
                y_copy(k, z, turn, False).wait_send()
                x_copy(k, z, turn).wait_send()
            @pl.when(z != me.z)
            def _():
                thin_copy(k, z).wait_send()
        core_copy(k, me.core).wait_send()
        return carry

    lax.fori_loop(0, chunks, finish, 0)
    if STEPS:
        forward.finish()


def forward_all(weights, note, emb, pixels, text, cotangent, present, images, inner, replicas, parts, rows=80, lead=3, lag=1):
    width = weights[0].shape[1]
    total = Rows(parts, pixels.shape[1], width, text.shape[2], inner).total
    chunks = total // rows
    span = parts // (2 * DEPTH)
    pix, pix_width = pixels.shape
    dma = lambda *shape: pltpu.SemaphoreType.DMA(shape)
    bf = lambda *shape: jax.ShapeDtypeStruct(shape, BF16)
    fl = lambda *shape: jax.ShapeDtypeStruct(shape, F32)
    hbm, vmem = pl.BlockSpec(memory_space=pl.ANY), pl.BlockSpec(memory_space=pltpu.VMEM)
    return pl.pallas_call(
        functools.partial(forward_kernel, replicas, parts, rows, lead, lag, inner, images),
        out_shape=[
            bf(parts // 2, 2, total, width), fl(8, emb.shape[1]), fl(16, emb.shape[1]), bf(*note.shape),
            bf(3, PADDED, pix_width), bf(3, PADDED, width), fl(pix, width), fl(pix, width), fl(pix, width), bf(pix, width),
            bf(pix, 3 * inner), bf(3 * TEXT_ROWS, 2 * inner), bf(pix, inner), fl(24, width), bf(3 * TEXT_ROWS, text.shape[2]),
        ],
        in_specs=[hbm] * 6 + [vmem] * 5 + [pl.BlockSpec(memory_space=pltpu.SMEM)],
        out_specs=[hbm, vmem, vmem, vmem] + [hbm] * 6 + [vmem] * 4 + [hbm],
        scratch_shapes=[
            pltpu.VMEM((total, width), BF16),
            pltpu.VMEM((parts, images * emb.shape[1] // 128, 128), F32),
            pltpu.VMEM((parts, images * emb.shape[1] // 128, 128), F32),
            pltpu.VMEM((3 * TEXT_ROWS, width), F32),
            pltpu.VMEM((3, PADDED, pix_width), BF16), pltpu.VMEM((3, PADDED, width), BF16),
            pltpu.VMEM((pix, BLOCK), BF16), pltpu.VMEM((2, BLOCK, width), BF16),
            pltpu.VMEM((pix, width), F32), pltpu.VMEM((pix, width), F32), pltpu.VMEM((pix, width), BF16),
            pltpu.VMEM((width, 3 * inner), BF16), pltpu.VMEM((pix_width, width), BF16), pltpu.VMEM((inner, width), BF16), pltpu.VMEM((3 * TEXT_ROWS, text.shape[2]), BF16),
            dma(2), dma(3), dma(7),
            dma(), dma(), dma(), dma(),
            dma(chunks, DEPTH, 2), dma(chunks, DEPTH),
            dma(chunks, DEPTH, span - 1), dma(chunks, DEPTH, span - 1),
            dma(chunks, DEPTH), dma(chunks, DEPTH),
            dma(chunks, DEPTH, span - 1), dma(chunks, DEPTH, span - 1),
            dma(chunks), dma(chunks), dma(8),
        ],
        compiler_params=pltpu.CompilerParams(collective_id=0, has_side_effects=True, vmem_limit_bytes=60 << 20),
        name="forward_all",
    )(*weights, note, emb, pixels, text, cotangent, present)


class Seat(Where):
    def bit(self, b):
        step = 1 << b
        group = self.group + step - 2 * step * lax.rem(self.group // step, 2)
        return (group, self.place)

    def meet(self):
        sem = pltpu.get_barrier_semaphore()
        count = self.replicas * self.parts
        def one(i, carry):
            far = lax.rem(self.group * self.parts + self.place + i, count)
            pl.semaphore_signal(sem, inc=1, device_id=(far // self.parts, lax.rem(far, self.parts)), device_id_type=MESH)
            return carry
        lax.fori_loop(1, count, one, 0)
        pl.semaphore_wait(sem, count - 1)


def norm_pull(image, factor, inverse, grad, hat, plain, crossed, put):
    count = SIZES[image]
    mean_plain = group_mean(plain * factor, count)[:1]
    mean_crossed = group_mean(crossed * factor, count)[:1]
    def one(i, rows, carry):
        value = inverse * (grad(rows) * factor - mean_plain - hat(rows) * mean_crossed)
        put(i, rows, value)
        return carry + (value[:8] + value[8:])
    total = over_rows(image, one, jnp.zeros(plain.shape, F32))
    return jnp.sum(total, axis=0, keepdims=True)


def two_sums(image, channels, pair):
    def add(i, rows, carry):
        a, b = pair(i, rows)
        return carry[0] + (a[:8] + a[8:]), carry[1] + (b[:8] + b[8:])
    zero = jnp.zeros((8, channels), F32)
    sums = over_rows(image, add, (zero, zero))
    return [jnp.broadcast_to(jnp.sum(part, axis=0, keepdims=True), (8, channels)) for part in sums]


def silu_pull(value):
    gate = jax.nn.sigmoid(value)
    return gate * (1.0 + value * (1.0 - gate))


G_IN_GAIN, G_IN_SHIFT, G_FIRST, G_MID_GAIN, G_MID_SHIFT, G_SECOND, G_ATTN_GAIN, G_ATTN_SHIFT, G_OUT = range(9)


class Backward:
    def __init__(self, rows, full, r_low, pixels, vec, mod, inverses, a1, a2, mid_hat, outs, scratch):
        self.rows, self.full, self.r_low, self.pixels, self.vec, self.mod, self.inverses = rows, full, r_low, pixels, vec, mod, inverses
        self.h_a1, self.h_a2, self.h_mid = a1, a2, mid_hat
        self.g_first, self.g_second, self.g_skip, self.grad_pixels = outs
        (self.a1, self.pad, self.hat, self.acc, self.acc1, self.c_low, self.patch, self.weight, self.stage, self.w_skip,
         self.vecs, self.mods, self.in_sem, self.w_sem, self.o_sem) = scratch

    def row(self, r, channels=1024):
        return self.vec[r : r + 1, :channels]

    def add_row(self, r, value):
        width = value.shape[1]
        self.vecs[r : r + 1, :width] = self.vecs[r : r + 1, :width] + value[:1]

    def fetch(self):
        for i, (src, dst) in enumerate(((self.h_a2, self.pad), (self.h_a1, self.a1), (self.h_mid, self.hat))):
            pltpu.make_async_copy(src, dst, self.in_sem.at[i]).start()
        start, size = self.rows.skip
        def one(f, carry):
            pltpu.make_async_copy(shard_of(self.full, f, pl.ds(start, size)), self.w_skip.at[pl.ds(pl.multiple_of(f * size, SUB), size)], self.in_sem.at[3]).start()
            return carry
        lax.fori_loop(0, self.rows.parts, one, 0)

    def arrived(self, i):
        waited((self.pad, self.a1, self.hat, self.w_skip)[i], self.in_sem.at[i])

    def put_out(self, dst, first, count):
        span, size = dst.shape[1], dst.shape[3]
        for i in range(count):
            f = first + i
            pltpu.make_async_copy(
                self.stage.at[pl.ds(i * size, size)],
                dst.at[f // (2 * span), lax.rem(f // 2, span), lax.rem(f, 2)],
                self.o_sem,
            ).start()

    def weight_grad(self, q, pad, count, grad, dst):
        for known in range(count):
            @pl.when(q == known)
            def _():
                gather_blocks(pad, range(known * BLOCK // 128, (known + 1) * BLOCK // 128), self.patch)
        @pl.when(q > 0)
        def _():
            self.stored()
        for col in range(0, 1024, 256):
            cols = slice(col, col + 256)
            self.stage[:, cols] = lax.dot_general(self.patch[...], grad[:, cols], TN, preferred_element_type=F32).astype(BF16)
        each = BLOCK // dst.shape[3]
        self.put_out(dst, q * each, each)

    def second_weight(self, q):
        self.weight_grad(q, self.pad, 9 * self.pad.shape[2] // BLOCK, self.r_low, self.g_second)

    def first_weight(self, q):
        self.weight_grad(q, self.a1, 9 * self.a1.shape[2] // BLOCK, self.c_low, self.g_first)

    def stored(self, size=BLOCK):
        waited(self.stage.at[pl.ds(0, size)], self.o_sem)

    def skip_weight(self):
        size = self.pixels.shape[1]
        for col in range(0, 1024, 512):
            cols = slice(col, col + 512)
            self.stage[:size, cols] = lax.dot_general(self.pixels[...], self.r_low[:, cols], TN, preferred_element_type=F32).astype(BF16)
        self.put_out(self.g_skip, jnp.int32(0), self.rows.parts)
        self.stored(size)

    def pad_residual(self):
        zero_edges(self.pad)
        for image in range(3):
            def one(i, rows, carry):
                store_padded(self.pad, image, i, self.r_low[rows, :].astype(F32))
                return carry
            over_rows(image, one, 0)

    def load_tap(self, which, height, tap):
        start, size = which
        for known in range(9):
            @pl.when(tap == known)
            def _():
                at = known * height
                while at < (known + 1) * height:
                    shard, inside = divmod(at, size)
                    count = min(size - inside, (known + 1) * height - at)
                    pltpu.make_async_copy(
                        shard_of(self.full, shard, pl.ds(start + inside, count)),
                        self.weight.at[known % 2, pl.ds(at - known * height, count)],
                        self.w_sem.at[known % 2],
                    ).start()
                    at += count

    def pull_step(self, tap, which, height, acc):
        @pl.when(tap + 1 < 9)
        def _():
            self.load_tap(which, height, tap + 1)
        @pl.when(tap == 0)
        def _():
            acc[...] = jnp.zeros_like(acc)
        for known in range(9):
            @pl.when(tap == known)
            def _():
                for image in range(3):
                    self.patch[STARTS[image] : STARTS[image] + SIZES[image], :1024] = shifted(self.pad, known, image, slice(0, 1024), True)
        par = lax.rem(tap, 2)
        waited(self.weight.at[par, pl.ds(0, height)], self.w_sem.at[par])
        for col in range(0, height, 512):
            cols = slice(col, col + 512)
            acc[:, cols] = acc[:, cols] + lax.dot_general(self.patch[:, :1024], self.weight[par, cols, :], NT, preferred_element_type=F32)

    def load_second(self):
        self.load_tap(self.rows.second, 1024, jnp.int32(0))

    def second_pull(self, tap):
        self.pull_step(tap, self.rows.second, 1024, self.acc)

    def load_first(self):
        self.load_tap(self.rows.first, self.pixels.shape[1], jnp.int32(0))

    def first_pull(self, tap):
        self.pull_step(tap, self.rows.first, self.pixels.shape[1], self.acc1)

    def mid_pull(self, image):
        acc, hat, channels = self.acc, self.hat, 1024
        if image == 0:
            self.vecs[...] = jnp.zeros_like(self.vecs)
            self.mods[...] = jnp.zeros_like(self.mods)
            zero_edges(self.pad)
        scale, shift = 1.0 + self.mod[image : image + 1, :channels], self.mod[image : image + 1, channels:]
        gain, bias = self.row(V_MID_GAIN), self.row(V_MID_SHIFT)
        factor, lift = gain * scale, bias * scale + shift
        def pair(i, rows):
            h = hat[rows, :]
            grad = acc[rows, :] * silu_pull(h * factor + lift)
            acc[rows, :] = grad
            return grad, grad * h
        plain, crossed = two_sums(image, channels, pair)
        def put(i, rows, value):
            store_padded(self.pad, image, i, value)
            self.c_low[rows, :] = value.astype(BF16)
        inverse = self.inverses[3 + image : 4 + image, :]
        total = norm_pull(image, factor, inverse, lambda rows: acc[rows, :], lambda rows: hat[rows, :], plain, crossed, put)
        self.add_row(G_FIRST, total)
        self.add_row(G_MID_GAIN, crossed * scale)
        self.add_row(G_MID_SHIFT, plain * scale)
        self.mods[image : image + 1, :channels] = (crossed * gain + plain * bias)[:1]
        self.mods[image : image + 1, channels:] = plain[:1]

    def first_norm_pull(self, image):
        acc, pixels = self.acc1, self.pixels
        channels = pixels.shape[1]
        inverse, center = self.inverses[image : image + 1, :channels], self.inverses[16 + image : 17 + image, :channels]
        gain, bias = self.row(V_IN_GAIN, channels), self.row(V_IN_SHIFT, channels)
        hat = lambda rows: (pixels[rows, :].astype(F32) - center) * inverse
        def pair(i, rows):
            h = hat(rows)
            grad = acc[rows, :] * silu_pull(h * gain + bias)
            acc[rows, :] = grad
            return grad, grad * h
        plain, crossed = two_sums(image, channels, pair)
        def put(i, rows, value):
            self.grad_pixels[rows, :] = self.grad_pixels[rows, :] + value
        norm_pull(image, gain, inverse, lambda rows: acc[rows, :], hat, plain, crossed, put)
        self.add_row(G_IN_GAIN, crossed)
        self.add_row(G_IN_SHIFT, plain)

    def skip_pull(self):
        self.grad_pixels[...] = lax.dot_general(self.r_low[...], self.w_skip[...], NT, preferred_element_type=F32)


def reduce_kernel(replicas, parts, rows, spans, lead, ring, nrc, rb, lag, inner, text_dim, images, known, *refs):
    early = refs[:known]
    full, r_low, pixels, vec, mod, inverses, a1, a2, mid_hat, emb_note, more = refs[known : known + 11]
    kinds = len(spans)
    refs = refs[known + 11 :]
    outs, refs = refs[:kinds], refs[kinds:]
    notes, g_first, g_second, g_skip, grad_pixels, g_narrow, g_wide = refs[:7]
    rest = refs[7:]
    (hold, rc, xr, yr, tr, zu, zd, fr, tb, shared, target, shared32, target32) = rest[:13]
    scratch = rest[13:28]
    (l_sem, c_send, c_recv, x_send, x_recv, y_send, y_recv,
     u_send, u_recv, d_send, d_recv, f_send, f_recv, n_send, n_recv, t_send, t_recv, free, x_free, y_free, u_free, d_free) = rest[28:]
    me = Seat(replicas, parts)
    span = me.span
    width = r_low.shape[1]
    chunks = spans[-1][1]
    side = me.side
    bits = replicas.bit_length() - 1
    apart, joint = 3 * width // 8, 5 * width // 8
    thin = 128
    main = width - thin
    z_cols = pl.ds(pl.multiple_of(side * thin, thin), main)
    thin_cols = pl.ds(pl.multiple_of((1 - side) * main, thin), thin)
    thin_in = pl.ds(pl.multiple_of(side * main, thin), thin)
    x_in = pl.ds(pl.multiple_of(side * joint, 128), apart)
    y_cols = pl.ds(pl.multiple_of(side * apart, 128), joint)
    table = Rows(parts, pixels.shape[1], width, text_dim, inner)
    back = Backward(table, full, r_low, pixels, vec, mod, inverses, a1, a2, mid_hat, (g_first, g_second, g_skip, grad_pixels), scratch)
    grads = list(early) + [g_second, g_skip, g_first]

    me.meet()
    back.fetch()

    def copy(src, dst, send, recv, device):
        return pltpu.make_async_remote_copy(src_ref=src, dst_ref=dst, send_sem=send, recv_sem=recv, device_id=device, device_id_type=MESH)

    def give(sem, device):
        pl.semaphore_signal(sem, inc=1, device_id=device, device_id_type=MESH)

    def take(sem, k, size):
        @pl.when(k >= size)
        def _():
            pl.semaphore_wait(sem, 1)

    def core_copy(k, src):
        return copy(src, rc.at[lax.rem(k, nrc)], c_send.at[k], c_recv.at[lax.rem(k, nrc)], me.device(core=1 - me.core))

    def begin(k):
        take(free, k, nrc)
        for grad, (lo, hi) in zip(grads, spans):
            @pl.when(jnp.logical_and(k >= lo, k < hi))
            def _():
                at = pl.ds(pl.multiple_of((k - lo) * rows, 16), rows)
                slot = lax.rem(k, ring)
                pltpu.make_async_copy(grad.at[:, :, me.core, at, :], hold.at[slot], l_sem.at[slot]).start()
                core_copy(k, grad.at[:, :, 1 - me.core, at, :]).start()

    def x_copy(k, turn):
        slot = lax.rem(k, ring)
        cols = pl.ds(pl.multiple_of((1 - side) * joint, 128), apart)
        return copy(hold.at[slot, :, lax.rem(me.y + turn, span), :, cols], xr.at[lax.rem(k, rb), turn - 1], x_send.at[k, turn - 1], x_recv.at[k, turn - 1], me.bit(0))

    def y_copy(k, turn):
        slot = lax.rem(k, ring)
        return copy(hold.at[slot, :, lax.rem(me.y + turn, span), :, y_cols], yr.at[lax.rem(k, rb), turn - 1], y_send.at[k, turn - 1], y_recv.at[k, turn - 1], me.device(y=lax.rem(me.y + turn, span)))

    def t_copy(k):
        slot = lax.rem(k, ring)
        return copy(hold.at[slot, :, me.y, :, thin_cols], tr.at[lax.rem(k, rb)], t_send.at[k], t_recv.at[k], me.bit(0))

    def up_copy(k, z):
        slot = lax.rem(k, ring)
        return copy(hold.at[slot, z + 1 : DEPTH, me.y, :, z_cols], zu.at[lax.rem(k, rb), 0 : DEPTH - 1 - z], u_send.at[k], u_recv.at[k], me.device(z=me.z + 1))

    def down_copy(k, z):
        slot = lax.rem(k, ring)
        return copy(hold.at[slot, 0:z, me.y, :, z_cols], zd.at[lax.rem(k, rb), 0:z], d_send.at[k], d_recv.at[k], me.device(z=me.z - 1))

    def f_copy(k, b):
        slot = lax.rem(k, ring)
        src = hold.at[slot, me.z, me.y, :, z_cols] if b == 0 else tb.at[b - 1, k]
        dst = fr.at[b, k, :, pl.ds(0, main)] if b == 0 else fr.at[b, k]
        return copy(src, dst, f_send.at[b, k], f_recv.at[b, k], me.bit(b))

    def fold_core(k):
        slot = lax.rem(k, ring)
        waited(hold.at[slot], l_sem.at[slot])
        core_copy(k, rc.at[lax.rem(k, nrc)]).wait_recv()
        hold[slot] = hold[slot] + rc[lax.rem(k, nrc)]
        @pl.when(k + nrc < chunks)
        def _():
            give(free, me.device(core=1 - me.core))
        for turn in range(1, span):
            take(x_free.at[turn - 1], k, rb)
            x_copy(k, turn).start()
        t_copy(k).start()

    def fold_x(k):
        slot = lax.rem(k, ring)
        t_copy(k).wait_recv()
        hold[slot, :, me.y, :, thin_in] = hold[slot, :, me.y, :, thin_in] + tr[lax.rem(k, rb)]
        for turn in range(1, span):
            x_copy(k, turn).wait_recv()
            y = lax.rem(me.y + turn, span)
            hold[slot, :, y, :, x_in] = hold[slot, :, y, :, x_in] + xr[lax.rem(k, rb), turn - 1]
            @pl.when(k + rb < chunks)
            def _():
                give(x_free.at[turn - 1], me.bit(0))
            take(y_free.at[turn - 1], k, rb)
            y_copy(k, turn).start()

    def fold_y(k):
        slot = lax.rem(k, ring)
        for turn in range(1, span):
            y_copy(k, turn).wait_recv()
            hold[slot, :, me.y, :, y_cols] = hold[slot, :, me.y, :, y_cols] + yr[lax.rem(k, rb), turn - 1]
            @pl.when(k + rb < chunks)
            def _():
                give(y_free.at[turn - 1], me.device(y=lax.rem(me.y + span - turn, span)))

    def hop(k, h):
        slot = lax.rem(k, ring)
        @pl.when(me.z == h)
        def _():
            if h > 0:
                up_copy(k, h - 1).wait_recv()
                hold[slot, h:, me.y, :, z_cols] = hold[slot, h:, me.y, :, z_cols] + zu[lax.rem(k, rb), 0 : DEPTH - h]
                @pl.when(k + rb < chunks)
                def _():
                    give(u_free, me.device(z=me.z - 1))
            if h < DEPTH - 1:
                take(u_free, k, rb)
                up_copy(k, h).start()
        z = DEPTH - 1 - h
        @pl.when(me.z == z)
        def _():
            if h > 0:
                down_copy(k, z + 1).wait_recv()
                hold[slot, : z + 1, me.y, :, z_cols] = hold[slot, : z + 1, me.y, :, z_cols] + zd[lax.rem(k, rb), 0 : z + 1]
                @pl.when(k + rb < chunks)
                def _():
                    give(d_free, me.device(z=me.z + 1))
            if h < DEPTH - 1:
                take(d_free, k, rb)
                down_copy(k, z).start()

    def finish(k, b):
        slot = lax.rem(k, ring)
        f_copy(k, b).wait_recv()
        if b == 0:
            came = jnp.concatenate([fr[b, k, :, :main].astype(F32), jnp.zeros((rows, thin), F32)], 1)
            before = hold[slot, me.z, me.y].astype(F32)
            column = lax.broadcasted_iota(jnp.int32, before.shape, 1)
            came = pltpu.roll(came, thin * (1 - side), 1)
            ours = jnp.logical_and(column >= thin * side, column < main + thin * side)
            theirs = jnp.logical_and(column >= thin * (1 - side), column < main + thin * (1 - side))
            total = jnp.where(ours, before, 0.0) + jnp.where(theirs, came, 0.0)
        else:
            total = tb[b - 1, k].astype(F32) + fr[b, k].astype(F32)
        if b == bits - 1:
            for out, (lo, hi) in zip(outs, spans):
                @pl.when(jnp.logical_and(k >= lo, k < hi))
                def _():
                    out[pl.ds(pl.multiple_of((k - lo) * rows, 16), rows), :] = total
        else:
            tb[b, k] = total.astype(BF16)
            f_copy(k, b + 1).start()

    def retire(k):
        core_copy(k, rc.at[0]).wait_send()
        t_copy(k).wait_send()
        for turn in range(1, span):
            x_copy(k, turn).wait_send()
            y_copy(k, turn).wait_send()
        for z in range(DEPTH):
            @pl.when(me.z == z)
            def _():
                if z < DEPTH - 1:
                    up_copy(k, z).wait_send()
                if z > 0:
                    down_copy(k, z).wait_send()
        for b in range(bits):
            f_copy(k, b).wait_send()

    count = replicas * parts
    mine = me.group * parts + me.place
    tall = shared.shape[0]

    def note_copies(far):
        device = (far // parts, lax.rem(far, parts))
        return (
            copy(shared, notes.at[mine, pl.ds(0, tall)], n_send, n_recv, device),
            copy(target.at[lax.rem(far, parts)], notes.at[mine, pl.ds(tall, 16)], n_send, n_recv, device),
        )

    def tell():
        back.vecs[:, :] = back.vecs[:, :] + more[...]
        target32[...] = emb_note[...].astype(F32)
        each = 2 * width // 128
        for image in range(images):
            for j in range(each):
                shared32[image * each + j : image * each + j + 1, :] = back.mods[image : image + 1, j * 128 : (j + 1) * 128]
        shared[...] = shared32[...].astype(BF16)
        for row in range(G_OUT + 1):
            size = (pixels.shape[1] if row in (G_IN_GAIN, G_IN_SHIFT) else width) // parts
            for f in range(parts):
                block = f * size // 128
                target32[f, images + row : images + row + 1, :] = back.vecs[row : row + 1, block * 128 : (block + 1) * 128]
        target[...] = target32[...].astype(BF16)
        def send(i, carry):
            for one in note_copies(lax.rem(mine + i, count)):
                one.start()
            return carry
        lax.fori_loop(1, count, send, 0)
        notes[mine, :tall, :] = shared[...]
        notes[mine, tall:, :] = target[me.place]
    lo_second, lo_skip, lo_first = (spans[known + i][0] - lead for i in range(3))
    n2, n1 = 9 * width // BLOCK, 9 * pixels.shape[1] // BLOCK
    s0 = n2 + 1
    s1 = s0 + 9
    s2 = s1 + 3
    s3 = s2 + n1 + 1
    s4 = s3 + 5
    assert s0 <= lo_second and s2 + n1 < lo_first
    last = max(chunks + (2 + DEPTH + bits) * lag + 1, s4 + 5)

    def steps(t):
        if not STEPS:
            return
        def once(when, *work):
            @pl.when(t == when)
            def _():
                for one in work:
                    one()
        def many(when, until, each, limit, work):
            @pl.when(jnp.logical_and(t >= when, t < until))
            def _():
                for i in range(each):
                    at = (t - when) * each + i
                    if limit % each:
                        pl.when(at < limit)(lambda: work(at))
                    else:
                        work(at)
        once(0, lambda: back.arrived(0))
        many(0, n2, 1, n2, back.second_weight)
        once(n2, back.stored, back.skip_weight, back.pad_residual, back.load_second)
        many(s0, s1, 1, 9, back.second_pull)
        once(s1, lambda: back.arrived(1), lambda: back.arrived(2), lambda: back.arrived(3))
        for image in range(3):
            once(s1 + image, functools.partial(back.mid_pull, image))
        many(s2, s2 + n1, 1, n1, back.first_weight)
        once(s2 + n1, back.stored, back.load_first)
        many(s3, s4, 2, 9, back.first_pull)
        once(s4, back.skip_pull)
        for image in range(3):
            once(s4 + 1 + image, functools.partial(back.first_norm_pull, image))
        once(s4 + 4, tell)

    for k in range(lead):
        begin(jnp.int32(k))

    first_f = (2 + DEPTH) * lag

    def slot_work(t, carry):
        def stage(delay, work):
            k = t - delay
            @pl.when(jnp.logical_and(k >= 0, k < chunks))
            def _():
                work(k)
        for h in range(DEPTH - 1, 0, -1):
            stage((2 + h) * lag, functools.partial(hop, h=h))
        stage((1 + DEPTH) * lag, lambda k: f_copy(k, 0).start())
        def pair(k):
            fold_y(k)
            hop(k, 0)
        stage(2 * lag, pair)
        stage(lag, fold_x)
        stage(0, fold_core)
        for b in range(bits):
            stage(first_f + b * lag, functools.partial(finish, b=b))
        stage(first_f + bits * lag, retire)
        @pl.when(t + lead < chunks)
        def _():
            begin(t + lead)
        steps(t)
        return carry

    lax.fori_loop(0, last, slot_work, 0)
    others = notes.at[pl.ds(0, count - 1)]
    every = copy(others, others, n_send, n_recv, me.device(core=1 - me.core))
    every.wait_send()
    every.wait_recv()
    total = jnp.sum(notes[:, tall:, :].astype(F32), axis=0)
    for dst, first, last in ((g_narrow, G_IN_GAIN, G_IN_SHIFT), (g_wide, G_FIRST, G_OUT)):
        size = dst.shape[2]
        turn = lax.rem(128 - lax.rem(me.place * size, 128), 128)
        mine_only = pltpu.roll(total, turn, 1)
        for row in range(first, last + 1):
            dst[row - first] = mine_only[images + row : images + row + 1, :size]


def reduce_all(early, full, r_low, pixels, vec, mod, inverses, a1, a2, mid_hat, emb_note, more, inner, text_dim, images, replicas, parts, rows, lead=2, nrc=3, lag=2, rb=8):
    span = parts // (2 * DEPTH)
    pix, width = r_low.shape
    pix_width = pixels.shape[1]
    spans, at = [], 0
    views = []
    for size in [grad.shape[0] // parts for grad in early] + [9 * width // parts, pix_width // parts, 9 * pix_width // parts]:
        spans.append((at // rows, (at + size) // rows))
        at += size
    for grad in early:
        views.append(grad.reshape(DEPTH, span, 2, grad.shape[0] // parts, width))
    total = at
    chunks = total // rows
    bits = replicas.bit_length() - 1
    ring = lead + (2 + DEPTH + bits) * lag + 2
    dma = lambda *shape: pltpu.SemaphoreType.DMA(shape)
    reg = lambda *shape: pltpu.SemaphoreType.REGULAR(shape)
    vm = lambda *shape: pltpu.VMEM(shape, BF16)
    vf = lambda *shape: pltpu.VMEM(shape, F32)
    bf = lambda *shape: jax.ShapeDtypeStruct(shape, BF16)
    fl = lambda *shape: jax.ShapeDtypeStruct(shape, F32)
    hbm, vmem = pl.BlockSpec(memory_space=pl.ANY), pl.BlockSpec(memory_space=pltpu.VMEM)
    tall = images * 2 * width // 128
    return pl.pallas_call(
        functools.partial(reduce_kernel, replicas, parts, rows, spans, lead, ring, nrc, rb, lag, inner, text_dim, images, len(early)),
        out_shape=[
            *(fl((hi - lo) * rows, width) for lo, hi in spans), bf(replicas * parts, tall + 16, 128),
            *(bf(DEPTH, span, 2, size // parts, width) for size in (9 * pix_width, 9 * width, pix_width)), fl(pix, pix_width),
            fl(2, 1, pix_width // parts), fl(7, 1, width // parts),
        ],
        in_specs=[hbm] * (len(early) + 1) + [vmem] * 5 + [hbm] * 3 + [vmem] * 2,
        out_specs=[vmem] * (len(spans) + 1) + [hbm] * 3 + [vmem] * 3,
        scratch_shapes=[
            vm(ring, DEPTH, span, rows, width),
            vm(nrc, DEPTH, span, rows, width),
            vm(rb, span - 1, DEPTH, rows, 3 * width // 8),
            vm(rb, span - 1, DEPTH, rows, 5 * width // 8),
            vm(rb, DEPTH, rows, 128),
            vm(rb, DEPTH - 1, rows, width - 128),
            vm(rb, DEPTH - 1, rows, width - 128),
            vm(bits, chunks, rows, width),
            vm(max(bits - 1, 1), chunks if bits > 1 else 1, rows, width),
            vm(tall, 128), vm(parts, 16, 128), vf(tall, 128), vf(parts, 16, 128),
            vm(3, PADDED, pix_width), vm(3, PADDED, width), vf(pix, width), vf(pix, width), vf(pix, pix_width), vm(pix, width),
            vm(pix, BLOCK), vm(2, 1024, width), vm(BLOCK, width), vm(pix_width, width), vf(16, width), vf(8, 2 * width),
            dma(4), dma(2), dma(),
            dma(ring),
            dma(chunks), dma(nrc),
            dma(chunks, span - 1), dma(chunks, span - 1),
            dma(chunks, span - 1), dma(chunks, span - 1),
            dma(chunks), dma(chunks), dma(chunks), dma(chunks),
            dma(bits, chunks), dma(bits, chunks),
            pltpu.SemaphoreType.DMA, pltpu.SemaphoreType.DMA, dma(chunks), dma(chunks),
            pltpu.SemaphoreType.REGULAR, reg(span - 1), reg(span - 1), pltpu.SemaphoreType.REGULAR, pltpu.SemaphoreType.REGULAR,
        ],
        compiler_params=pltpu.CompilerParams(collective_id=1, has_side_effects=True, vmem_limit_bytes=62 << 20),
        name="reduce_all",
    )(*views, full, r_low, pixels, vec, mod, inverses, a1, a2, mid_hat, emb_note, more)


def middle_kernel(parts, inner, text_dim, triple, text_pair, keep, grad_attended, cotangent, vec, inverses, present, full, h_normed, h_hats, h_residual, h_text,
                  r_low, more, h_block, h_out, h_attend, h_more, h_g_text, attended, grad_triple, grad_text, rows_grad, w_attend, w_out, stage,
                  g_low, queries, outs, keys, values, normed, hats, residual, text, block_output, g_out, g_attend, g_more, sems, i_sems, o_sems):
    width = cotangent.shape[1]
    table = Rows(parts, 512, width, text_dim, inner)
    start, size = table.out
    def one(f, carry):
        pltpu.make_async_copy(shard_of(full, f, pl.ds(start, size)), w_out.at[pl.ds(pl.multiple_of(f * size, SUB), size)], sems.at[0]).start()
        return carry
    lax.fori_loop(0, parts, one, 0)
    table.load_attend(full, w_attend, sems.at[1])

    late = [pltpu.make_async_copy(src, dst, i_sems.at[i]) for i, (src, dst) in enumerate(((h_text, text), (h_residual, residual), (h_normed, normed), (h_hats, hats)))]
    for copy in late:
        copy.start()
    done = [pltpu.make_async_copy(src, dst, o_sems.at[i]) for i, (src, dst) in enumerate(((block_output, h_block), (g_out, h_out), (g_attend, h_attend), (g_more, h_more)))]

    for image in range(3):
        g_low[pl.ds(STARTS[image], SIZES[image]), :] = outgoing(cotangent, present, image)

    lane = lax.broadcasted_iota(jnp.int32, (1, 2 * HEAD), 1)
    scale = HEAD ** -0.5
    room = min(SIZES) + TEXT_ROWS
    for buf in (keys, values):
        buf[room:, :] = jnp.zeros((KEYS - room, 2 * HEAD), BF16)

    def heads(pair, carry):
        at = lambda shift: pl.ds(pl.multiple_of(pair * 2 * HEAD + shift * inner, 128), 2 * HEAD)
        for image in range(3):
            size = SIZES[image]
            rows = pl.ds(STARTS[image], size)
            text_rows = pl.ds(image * TEXT_ROWS, TEXT_ROWS)
            for buf, part in ((queries, triple[rows, at(0)] * jnp.asarray(scale, BF16)), (outs, grad_attended[rows, at(0)])):
                buf[:size, :] = jnp.where(lane < HEAD, part, jnp.zeros_like(part))
                buf[size : 2 * size, :] = jnp.where(lane < HEAD, jnp.zeros_like(part), part)
            for i, buf in enumerate((keys, values)):
                buf[:size, :] = triple[rows, at(1 + i)]
                buf[size : size + TEXT_ROWS, :] = text_pair[text_rows, at(i)]
            q, go = queries[: 2 * size, :], outs[: 2 * size, :]
            seen = keep[image : image + 1, :]
            s = lax.dot_general(q, keys[...], NT, preferred_element_type=F32)
            s = jnp.where(seen == 1, s, jnp.where(seen == 0, -1000000000.0, -jnp.inf))
            e = jnp.exp(s - jnp.max(s, axis=1, keepdims=True))
            p = e * (1.0 / jnp.sum(e, axis=1, keepdims=True))
            low = p.astype(BF16)
            out = dot(low, values[...])
            dv = lax.dot_general(low, go, TN, preferred_element_type=F32)
            dp = lax.dot_general(go, values[...], NT, preferred_element_type=F32)
            ds = (p * (dp - jnp.sum(dp * p, axis=1, keepdims=True))).astype(BF16)
            dq = dot(ds, keys[...]) * scale
            dk = lax.dot_general(ds, q, TN, preferred_element_type=F32)
            merge = lambda part: jnp.where(lane < HEAD, part[:size], part[size:]).astype(BF16)
            attended[rows, at(0)] = merge(out)
            grad_triple[rows, at(0)] = merge(dq)
            grad_triple[rows, at(1)] = dk[:size].astype(BF16)
            grad_triple[rows, at(2)] = dv[:size].astype(BF16)
            grad_text[text_rows, at(0)] = dk[size : size + TEXT_ROWS].astype(BF16)
            grad_text[text_rows, at(1)] = dv[size : size + TEXT_ROWS].astype(BF16)
        return carry

    lax.fori_loop(0, inner // (2 * HEAD), heads, 0)

    late[0].wait()

    def text_block(q, carry):
        at = pl.ds(pl.multiple_of(q * 1024, 128), 1024)
        for col in range(0, width, 512):
            cols = slice(col, col + 512)
            stage[at, cols] = lax.dot_general(text[:, at], grad_text[:, cols], TN, preferred_element_type=F32).astype(BF16)
        pltpu.make_async_copy(stage.at[at], h_g_text.at[at], o_sems.at[4]).start()
        return carry

    lax.fori_loop(0, text_dim // 1024, text_block, 0)

    waited(w_out, sems.at[0])
    late[1].wait()
    bias = vec[V_OUT : V_OUT + 1, :width]
    for image in range(3):
        rows = pl.ds(STARTS[image], SIZES[image])
        block_output[rows, :] = (
            present[0, image].astype(F32) * (residual[rows, :] + (dot(attended[rows, :], w_out[...]) + bias))
        ).astype(BF16)
    done[0].start()
    late[2].wait()
    for col in range(0, width, 512):
        cols = slice(col, col + 512)
        g_out[:, cols] = lax.dot_general(attended[...], g_low[:, cols], TN, preferred_element_type=F32).astype(BF16)
        g_attend[:, cols] = lax.dot_general(normed[...], grad_triple[:, cols], TN, preferred_element_type=F32).astype(BF16)
    last = lax.dot_general(normed[...], grad_triple[:, width:], TN, preferred_element_type=F32).astype(BF16)
    half = width // parts // 2
    for f in range(parts):
        for i in range(2):
            g_more[f * half : (f + 1) * half, 512 * i : 512 * (i + 1)] = last[(2 * f + i) * half : (2 * f + i + 1) * half]
    for copy in done[1:]:
        copy.start()
    waited(w_attend, sems.at[1])
    for col in range(0, width, 512):
        cols = slice(col, col + 512)
        rows_grad[:, cols] = lax.dot_general(grad_triple[...], w_attend[cols, :], NT, preferred_element_type=F32)

    late[3].wait()
    more[...] = jnp.zeros_like(more)
    gain = vec[V_ATTN_GAIN : V_ATTN_GAIN + 1, :width]
    for image in range(3):
        def pair(i, rows):
            grad = rows_grad[rows, :]
            return grad, grad * hats[rows, :]
        plain, crossed = two_sums(image, width, pair)
        def put(i, rows, value):
            rows_grad[rows, :] = value + g_low[rows, :].astype(F32)
        norm_pull(image, gain, inverses[6 + image : 7 + image, :], lambda rows: rows_grad[rows, :], lambda rows: hats[rows, :], plain, crossed, put)
        def ends(i, rows):
            value = rows_grad[rows, :]
            r_low[rows, :] = value.astype(BF16)
            return value, g_low[rows, :].astype(F32)
        total, outer = two_sums(image, width, ends)
        for row, value in ((G_ATTN_GAIN, crossed), (G_ATTN_SHIFT, plain), (G_SECOND, total), (G_OUT, outer)):
            more[row : row + 1, :] = more[row : row + 1, :] + value[:1]
    for copy in done:
        copy.wait()
    waited(stage, o_sems.at[4])


def middle(triple, text_pair, keep, grad_attended, cotangent, normed, hats, residual, text, vec, inverses, present, full, parts, inner, text_dim):
    pix, width = cotangent.shape
    bf = lambda *shape: jax.ShapeDtypeStruct(shape, BF16)
    vm = lambda *shape: pltpu.VMEM(shape, BF16)
    hbm, vmem = pl.BlockSpec(memory_space=pl.ANY), pl.BlockSpec(memory_space=pltpu.VMEM)
    return pl.pallas_call(
        functools.partial(middle_kernel, parts, inner, text_dim),
        out_shape=[bf(pix, width), jax.ShapeDtypeStruct((16, width), F32), bf(pix, width), bf(inner, width), bf(width, width), bf(width // 2, width), bf(text_dim, width)],
        in_specs=[vmem] * 7 + [pl.BlockSpec(memory_space=pltpu.SMEM)] + [hbm] * 5,
        out_specs=[vmem] * 2 + [hbm] * 5,
        scratch_shapes=[
            vm(pix, inner), vm(pix, 3 * inner), vm(text.shape[0], 2 * inner), pltpu.VMEM((pix, width), F32),
            vm(width, 3 * inner), vm(inner, width), vm(text_dim, width), vm(pix, width),
            vm(2 * max(SIZES), 2 * HEAD), vm(2 * max(SIZES), 2 * HEAD), vm(KEYS, 2 * HEAD), vm(KEYS, 2 * HEAD),
            vm(pix, width), pltpu.VMEM((pix, width), F32), pltpu.VMEM((pix, width), F32), vm(*text.shape),
            vm(pix, width), vm(inner, width), vm(width, width), vm(width // 2, width),
            pltpu.SemaphoreType.DMA((2,)), pltpu.SemaphoreType.DMA((4,)), pltpu.SemaphoreType.DMA((5,)),
        ],
        compiler_params=pltpu.CompilerParams(vmem_limit_bytes=60 << 20),
        name="middle",
    )(triple, text_pair, keep, grad_attended, cotangent, vec, inverses, present, full, normed, hats, residual, text)


def last_kernel(images, depth, tall, count, *refs):
    big, (h_attend, h_more, h_notes, narrow, wide) = refs[:count], refs[count : count + 5]
    refs = refs[count + 5 :]
    big_out, (o_attend, emb_weight, emb_bias) = refs[:count], refs[count : count + 3]
    vectors, refs = refs[count + 3 : count + 12], refs[count + 12 :]
    bufs, (attend, more, notes, plain, bias, i_sems, o_sems) = refs[:count], refs[count:]
    sources = list(big) + [h_attend, h_more, h_notes]
    targets = list(bufs) + [attend, more, notes]
    ins = [pltpu.make_async_copy(src, dst, i_sems.at[i]) for i, (src, dst) in enumerate(zip(sources, targets))]
    for copy in ins:
        copy.start()
    high, across = more.shape[0], more.shape[1] // 2
    jobs = list(zip(bufs, big_out)) + [(attend, o_attend.at[:, pl.ds(0, 2 * across)])]
    jobs += [(more.at[:, pl.ds(i * across, across)], o_attend.at[pl.ds(i * high, high), pl.ds(2 * across, across)]) for i in range(2)]
    out = [pltpu.make_async_copy(src, dst, o_sems.at[i]) for i, (src, dst) in enumerate(jobs)]
    for i in range(count + 1):
        ins[i].wait()
        out[i].start()
    ins[count + 1].wait()
    out[count + 1].start()
    out[count + 2].start()
    ins[count + 2].wait()
    plain[...] = notes[...].astype(F32)
    per_image = tall // images
    for j in range(per_image):
        total, sums = jnp.zeros((128, 128), F32), jnp.zeros((1, 128), F32)
        for image in range(images):
            mods = plain[:, image * per_image + j, :]
            total = total + lax.dot_general(plain[:, tall + image, :].astype(BF16), mods.astype(BF16), TN, preferred_element_type=F32)
            sums = sums + jnp.sum(mods, axis=0, keepdims=True)
        emb_weight[:, j * 128 : (j + 1) * 128] = total[:depth]
        bias[j : j + 1, :] = sums
    at = lax.axis_index("fsdp") * depth
    emb_bias[...] = pltpu.roll(jnp.broadcast_to(bias[pl.ds(at // 128, 1), :], (8, 128)), lax.rem(128 - lax.rem(at, 128), 128), 1)[:1, :depth]
    for i, dst in enumerate(vectors):
        dst[...] = narrow[i] if i < narrow.shape[0] else wide[i - narrow.shape[0]]
    for copy in out:
        copy.wait()


def last(big, attend, more, notes, narrow, wide, images, depth):
    tall = notes.shape[1] - 16
    columns = tall // images * 128
    hbm, vmem = pl.BlockSpec(memory_space=pl.ANY), pl.BlockSpec(memory_space=pltpu.VMEM)
    fl = lambda *shape: jax.ShapeDtypeStruct(shape, F32)
    vf = lambda *shape: pltpu.VMEM(shape, F32)
    sizes = [narrow.shape[2]] * narrow.shape[0] + [wide.shape[2]] * wide.shape[0]
    dma = lambda count: pltpu.SemaphoreType.DMA((count,))
    return pl.pallas_call(
        functools.partial(last_kernel, images, depth, tall, len(big)),
        out_shape=[fl(*part.shape) for part in big] + [fl(attend.shape[0], attend.shape[1] + more.shape[1] // 2), fl(depth, columns), fl(1, depth)] + [fl(1, size) for size in sizes],
        in_specs=[hbm] * (len(big) + 3) + [vmem] * 2,
        out_specs=[hbm] * (len(big) + 1) + [vmem] * (2 + len(sizes)),
        scratch_shapes=[vf(*part.shape) for part in big] + [
            vf(*attend.shape), vf(*more.shape), pltpu.VMEM(notes.shape, BF16), vf(*notes.shape), vf(max(8, tall // images), 128),
            dma(len(big) + 3), dma(len(big) + 3),
        ],
        compiler_params=pltpu.CompilerParams(vmem_limit_bytes=60 << 20),
        name="last",
    )(*big, attend, more, notes, narrow, wide)


def body(
    pixels,
    embedding,
    text_states,
    text_mask,
    occupancy,
    cotangent,
    in_gain,
    in_shift,
    conv_first,
    first_bias,
    emb_weight,
    emb_bias,
    mid_gain,
    mid_shift,
    conv_second,
    second_bias,
    skip_weight,
    skip_bias,
    attn_gain,
    attn_shift,
    attend_weight,
    text_weight,
    out_weight,
    out_bias,
):
    place = lax.axis_index("fsdp")
    group = lax.axis_index("dp")
    parts = lax.axis_size("fsdp")
    replicas = lax.axis_size("dp")
    depth = emb_weight.shape[0]
    images_here = embedding.shape[0]
    emb_act = jax.nn.silu(embedding.astype(F32)).astype(BF16)
    emb_cut = emb_act.reshape(images_here, parts, depth).transpose(1, 0, 2)
    emb_cut = jnp.pad(emb_cut, ((0, 0), (0, 0), (0, 128 - depth)))

    lane = lax.broadcasted_iota(jnp.int32, (1, 128), 1)

    def placed(vectors):
        size = vectors[0].shape[0]
        wide = jnp.concatenate([jnp.stack(vectors)] * (128 // size), 1)
        return jnp.where(lane // size == lax.rem(place, 128 // size), wide, jnp.zeros_like(wide))

    lines = [placed((in_gain, in_shift)), placed((emb_bias,)), placed((first_bias, mid_gain, mid_shift, second_bias, skip_bias, attn_gain, attn_shift, out_bias))]
    room = 16 - images_here - sum(line.shape[0] for line in lines)
    flat = jnp.concatenate(lines + [jnp.zeros((room, 128), BF16)] if room else lines, 0)[None]
    note = jnp.concatenate([emb_cut, jnp.broadcast_to(flat, (parts,) + flat.shape[1:])], 1)
    channels = skip_weight.shape[1]
    inner = out_weight.shape[0] * parts
    text_len = text_states.shape[1]
    (full, modulation, vec, _, act1, act2, mid_hats, residual, hats, normed, triple, text_pair, grad_attended, inverses, text_rows) = forward_all(
        (conv_first, conv_second, skip_weight, out_weight, attend_weight, text_weight), note, jnp.pad(emb_weight, ((0, 128 - depth), (0, 0))), pixels, text_states, cotangent, occupancy, images_here, inner, replicas, parts)
    keep = (text_mask > 0).astype(jnp.int32)
    keep = jnp.stack([
        jnp.pad(jnp.pad(keep[i], (size, 0), constant_values=1), (0, KEYS - size - text_len), constant_values=2)
        for i, size in enumerate(SIZES)
    ])
    r_low, more, block_output, g_out, g_attend, g_more, g_text = middle(
        triple, text_pair, keep, grad_attended, cotangent, normed, hats, residual, text_rows, vec, inverses, occupancy, full, parts, inner, text_states.shape[2]
    )
    (grad_text_weight, grad_out_weight, attend, attend_more, grad_conv_second, grad_skip_weight, grad_conv_first,
     notes, _, _, _, grad_pixels, narrow, wide) = reduce_all(
        [g_text, g_out, g_attend, g_more], full, r_low, pixels, vec, modulation, inverses, act1, act2, mid_hats, note, more,
        inner, text_states.shape[2], images_here, replicas, parts, 512 // parts,
    )
    (grad_text_weight, grad_out_weight, grad_conv_second, grad_skip_weight, grad_conv_first, grad_pixels, grad_attend_weight,
     grad_emb_weight, grad_emb_bias, *vectors) = last(
        [grad_text_weight, grad_out_weight, grad_conv_second, grad_skip_weight, grad_conv_first, grad_pixels],
        attend, attend_more, notes, narrow, wide, images_here, depth,
    )
    grad_emb_bias = grad_emb_bias.reshape(-1)
    small = lambda row: vectors[row].reshape(-1)
    grad_second_bias = small(G_SECOND)
    return (
        block_output,
        grad_pixels,
        small(G_IN_GAIN),
        small(G_IN_SHIFT),
        grad_conv_first,
        small(G_FIRST),
        grad_emb_weight,
        grad_emb_bias,
        small(G_MID_GAIN),
        small(G_MID_SHIFT),
        grad_conv_second,
        grad_second_bias,
        grad_skip_weight,
        grad_second_bias,
        small(G_ATTN_GAIN),
        small(G_ATTN_SHIFT),
        grad_attend_weight,
        grad_text_weight,
        grad_out_weight,
        small(G_OUT),
    )


def solution(mesh):
    rows = P(("dp", "fsdp"), None)
    vector = P("fsdp")
    matrix = P("fsdp", None)
    weights = (vector, vector, matrix, vector, matrix, vector, vector, vector, matrix, vector, matrix, vector, vector, vector, matrix, matrix, matrix, vector)
    return jax.shard_map(
        body,
        mesh=mesh,
        in_specs=(rows, rows, P(("dp", "fsdp"), None, None), rows, rows, rows) + weights,
        out_specs=(rows, rows) + weights,
        check_vma=False,
    )
```

```python
import functools

import jax
import jax.numpy as jnp
from jax import lax
from jax.experimental import pallas as pl
from jax.experimental.pallas import tpu as pltpu
from jax.sharding import PartitionSpec as P

BF16 = jnp.bfloat16
F32 = jnp.float32
HEADS = 8
HEAD = 64
GROUPS = 32
UNIT = 4
SHAPES = ((4 * UNIT, 4 * UNIT), (3 * UNIT, 5 * UNIT), (5 * UNIT, 3 * UNIT))
SIZES = tuple(height * breadth for height, breadth in SHAPES)
STARTS = (0, SIZES[0], SIZES[0] + SIZES[1])
PIX = sum(SIZES)
EDGE = 32
BASES = tuple(EDGE + start + i * EDGE for i, start in enumerate(STARTS))
PADDED = PIX + 4 * EDGE
BLOCK = 1152
KEYS = 384
TEXT_ROWS = 80
SUB = 16
NT = (((1,), (1,)), ((), ()))
TN = (((0,), (0,)), ((), ()))
V_IN_GAIN, V_IN_SHIFT, V_EMB, V_FIRST, V_MID_GAIN, V_MID_SHIFT, V_SECOND, V_SKIP, V_ATTN_GAIN, V_ATTN_SHIFT, V_OUT = range(11)


def dot(left, right, dims=((1,), (0,))):
    return lax.dot_general(left, right, (dims, ((), ())), preferred_element_type=F32)


def group_mean(sums, count):
    channels = sums.shape[1]
    width = channels // GROUPS
    lane = lax.broadcasted_iota(jnp.int32, sums.shape, 1)
    step = 1
    while step < width:
        odd = lax.rem(lane // step, 2) == 1
        sums = sums + jnp.where(odd, pltpu.roll(sums, step, 1), pltpu.roll(sums, channels - step, 1))
        step *= 2
    return sums / (count * width)


def rows_of(image, i):
    return pl.ds(pl.multiple_of(STARTS[image] + i * SUB, SUB), SUB)


def over_rows(image, work, start):
    return lax.fori_loop(0, SIZES[image] // SUB, lambda i, carry: work(i, rows_of(image, i), carry), start)


def column_sum(image, channels, value):
    def add(i, rows, carry):
        v = value(rows)
        return carry + (v[:8] + v[8:])
    total = over_rows(image, add, jnp.zeros((8, channels), F32))
    return jnp.broadcast_to(jnp.sum(total, axis=0, keepdims=True), (8, channels))


def norm_figures(image, channels, value):
    count = SIZES[image]
    center = group_mean(column_sum(image, channels, value), count)[:1]
    spread = group_mean(column_sum(image, channels, lambda rows: jnp.square(value(rows) - center)), count)[:1]
    return center, lax.rsqrt(spread + 1e-05)


def store_padded(pad, image, i, act):
    breadth = SHAPES[image][1]
    at = pl.ds(pl.multiple_of(BASES[image] + i * SUB, SUB), SUB)
    column = lax.rem(i * SUB + lax.broadcasted_iota(jnp.int32, (SUB, 1), 0), breadth)
    pad[0, at, :] = jnp.where(column == breadth - 1, 0.0, act).astype(BF16)
    pad[1, at, :] = act.astype(BF16)
    pad[2, at, :] = jnp.where(column == 0, 0.0, act).astype(BF16)


def zero_edges(pad):
    zeros = jnp.zeros((EDGE, pad.shape[2]), BF16)
    for side in range(3):
        for at in [base - EDGE for base in BASES] + [PADDED - EDGE]:
            pad[side, at : at + EDGE, :] = zeros


def shifted(pad, tap, image, cols, flip=False):
    down, across = divmod(8 - tap if flip else tap, 3)
    start = BASES[image] + (down - 1) * SHAPES[image][1] + across - 1
    return pad[across, start : start + SIZES[image], cols]


def gather_blocks(pad, blocks, out):
    per_tap = pad.shape[2] // 128
    for i, block in enumerate(blocks):
        tap, col = divmod(block, per_tap)
        for image in range(3):
            out[STARTS[image] : STARTS[image] + SIZES[image], i * 128 : (i + 1) * 128] = shifted(
                pad, tap, image, slice(col * 128, (col + 1) * 128)
            )


def shard_of(full, f, *where):
    return full.at[(f // 2, f % 2 if isinstance(f, int) else lax.rem(f, 2)) + where]


class Rows:
    def __init__(self, parts, pix_channels, channels, text_dim, inner):
        self.parts = parts
        sizes = (9 * pix_channels // parts, 9 * channels // parts, pix_channels // parts, inner // parts, channels // parts, channels // parts // 2, text_dim // parts)
        starts = [0]
        for size in sizes:
            starts.append(starts[-1] + size)
        self.first, self.second, self.skip, self.out, self.attend, self.attend_more, self.text = zip(starts, sizes)
        self.total = starts[-1]

    def arrivals(self, which):
        size = which[1]
        blocks = []
        for block in range(size * self.parts // 128):
            pieces, at = [], block * 128
            while at < (block + 1) * 128:
                shard, inside = divmod(at, size)
                count = min(size - inside, (block + 1) * 128 - at)
                pieces.append((shard, inside, count))
                at += count
            blocks.append((max(inside + count for _, inside, count in pieces), block, pieces))
        blocks.sort()
        each = BLOCK // 128
        steps = [blocks[i : i + each] for i in range(0, len(blocks), each)]
        return [([(block, pieces) for _, block, pieces in step], step[-1][0]) for step in steps]

    def load_step(self, full, which, step, buf, sem):
        at = 0
        for _, pieces in step:
            for shard, inside, count in pieces:
                pltpu.make_async_copy(shard_of(full, shard, pl.ds(which[0] + inside, count)), buf.at[pl.ds(at, count)], sem).start()
                at += count

    def pack(self, weights, own, sems):
        first, second, skip, out, attend, text = weights
        half = self.attend_more[1]
        wide = own.shape[1]
        jobs = [(ref, which) for ref, which in ((first, self.first), (second, self.second), (skip, self.skip), (out, self.out), (text, self.text))]
        jobs.append((attend.at[:, pl.ds(0, wide)], self.attend))
        for i, (ref, (start, size)) in enumerate(jobs):
            pltpu.make_async_copy(ref, own.at[pl.ds(start, size)], sems.at[i]).start()
        for i in range(2):
            pltpu.make_async_copy(
                attend.at[pl.ds(i * half, half), pl.ds(wide, wide // 2)],
                own.at[pl.ds(self.attend_more[0], half), pl.ds(i * wide // 2, wide // 2)],
                sems.at[6 + i],
            ).start()

    def packed(self, own, sems):
        wide = own.shape[1]
        for i, (start, size) in enumerate((self.first, self.second, self.skip, self.out, self.text, self.attend)):
            waited(own.at[pl.ds(start, size)], sems.at[i])
        for i in range(2):
            waited(own.at[pl.ds(self.attend_more[0], self.attend_more[1]), pl.ds(i * wide // 2, wide // 2)], sems.at[6 + i])

    def load(self, full, which, q, rows, buf, sem):
        start, size = which
        each = rows // size
        for i in range(each):
            pltpu.make_async_copy(shard_of(full, q * each + i, pl.ds(start, size)), buf.at[pl.ds(i * size, size)], sem).start()

    def load_attend(self, full, buf, sem):
        start, size = self.attend
        more, half = self.attend_more
        def one(f, carry):
            at = pl.multiple_of(f * size, SUB)
            pltpu.make_async_copy(shard_of(full, f, pl.ds(start, size)), buf.at[pl.ds(at, size), pl.ds(0, 1024)], sem).start()
            for i in range(2):
                pltpu.make_async_copy(
                    shard_of(full, f, pl.ds(more, half), pl.ds(512 * i, 512)),
                    buf.at[pl.ds(pl.multiple_of(at + i * half, SUB), half), pl.ds(1024, 512)],
                    sem,
                ).start()
            return carry
        lax.fori_loop(0, self.parts, one, 0)


def outgoing(cotangent, present, image):
    rows = pl.ds(STARTS[image], SIZES[image])
    return (cotangent[rows, :].astype(F32) * present[0, image].astype(F32)).astype(BF16)


def choose(value, options):
    if len(options) == 1:
        first, end, work = options[0]
        pl.when(jnp.logical_and(value >= first, value < end))(work)
        return
    middle = len(options) // 2
    border = options[middle][0]
    pl.when(value < border)(lambda: choose(value, options[:middle]))
    pl.when(value >= border)(lambda: choose(value, options[middle:]))


def waited(ref, sem):
    pltpu.make_async_copy(ref, ref, sem).wait()


class Forward:
    def __init__(self, rows, full, pixels, text_in, cotangent, present, vec, mod, outs, scratch):
        self.rows, self.full, self.pixels, self.text_in, self.cotangent, self.present, self.vec, self.mod = rows, full, pixels, text_in, cotangent, present, vec, mod
        (self.o_a1, self.o_a2, self.o_mid_hat, self.o_residual, self.o_hat, self.o_normed, self.triple, self.text_pair, self.grad_attended, self.inverses, self.o_text) = outs
        (self.a1, self.a2, self.patch, self.weight, self.acc0, self.acc1, self.normed, self.w_attend, self.w_skip, self.w_out, self.text, self.w_sem, self.s_sem, self.o_sem) = scratch

    def out_copy(self, i, src, dst):
        return pltpu.make_async_copy(src, dst, self.o_sem.at[i])

    def row(self, r, channels=1024):
        return self.vec[r : r + 1, :channels]

    def zero(self):
        zero_edges(self.a1)
        zero_edges(self.a2)
        count = self.text_in.shape[1]
        for image in range(3):
            at = image * TEXT_ROWS
            self.text[at + TEXT_ROWS - SUB : at + TEXT_ROWS, :] = jnp.zeros((SUB, self.text.shape[1]), BF16)
            self.text[at : at + count, :] = self.text_in[image]
        self.out_copy(6, self.text, self.o_text).start()

    def first_norm(self, image):
        pixels, channels = self.pixels, self.pixels.shape[1]
        value = lambda rows: pixels[rows, :].astype(F32)
        center, inverse = norm_figures(image, channels, value)
        gain, shift = self.row(V_IN_GAIN, channels) * inverse, self.row(V_IN_SHIFT, channels)
        self.inverses[image : image + 1, :channels] = inverse
        self.inverses[16 + image : 17 + image, :channels] = center
        def act(i, rows, carry):
            store_padded(self.a1, image, i, jax.nn.silu((value(rows) - center) * gain + shift))
            return carry
        over_rows(image, act, 0)
        if image == 2:
            self.out_copy(0, self.a1, self.o_a1).start()

    def load_text(self, q):
        self.rows.load(self.full, self.rows.text, q, 1024, self.weight.at[lax.rem(q, 2)], self.w_sem.at[lax.rem(q, 2)])

    def conv_step(self, q, pad, acc, which, steps, early):
        def load(known):
            self.rows.load_step(self.full, which, steps[known][0], self.weight.at[known % 2], self.w_sem.at[known % 2])
        for known in range(len(steps)):
            ahead = known + 1 < len(steps) and early[known + 1]
            @pl.when(q == known)
            def _():
                if not early[known]:
                    load(known)
                if ahead:
                    load(known + 1)
                gather_blocks(pad, [block for block, _ in steps[known][0]], self.patch)
        par = lax.rem(q, 2)
        waited(self.weight.at[par], self.w_sem.at[par])
        @pl.when(q == 0)
        def _():
            acc[...] = jnp.zeros_like(acc)
        for col in (0, 512):
            cols = slice(col, col + 512)
            acc[:, cols] = acc[:, cols] + dot(self.patch[...], self.weight[par, :, cols])

    def mid_norm(self, image):
        acc, channels = self.acc0, self.acc0.shape[1]
        bias = self.row(V_FIRST)
        def shift_up(i, rows, carry):
            acc[rows, :] = acc[rows, :] + bias
            return carry
        over_rows(image, shift_up, 0)
        center, inverse = norm_figures(image, channels, lambda rows: acc[rows, :])
        self.inverses[3 + image : 4 + image, :] = inverse
        scale, shift = 1.0 + self.mod[image : image + 1, :channels], self.mod[image : image + 1, channels:]
        gain, lift = self.row(V_MID_GAIN) * scale, self.row(V_MID_SHIFT) * scale + shift
        def act(i, rows, carry):
            hat = (acc[rows, :] - center) * inverse
            acc[rows, :] = hat
            store_padded(self.a2, image, i, jax.nn.silu(hat * gain + lift))
            return carry
        over_rows(image, act, 0)
        if image == 2:
            self.out_copy(1, self.a2, self.o_a2).start()
            self.out_copy(2, self.acc0, self.o_mid_hat).start()

    def load_small(self):
        rows = self.rows
        def one(f, carry):
            for i, ((start, size), buf) in enumerate(((rows.skip, self.w_skip), (rows.out, self.w_out))):
                pltpu.make_async_copy(shard_of(self.full, f, pl.ds(start, size)), buf.at[pl.ds(pl.multiple_of(f * size, SUB), size)], self.s_sem.at[i]).start()
            return carry
        lax.fori_loop(0, rows.parts, one, 0)
        rows.load_attend(self.full, self.w_attend, self.s_sem.at[2])

    def skip_product(self):
        for i, buf in enumerate((self.w_skip, self.w_out, self.w_attend)):
            waited(buf, self.s_sem.at[i])
        self.acc1[...] = self.acc1[...] + dot(self.pixels[...], self.w_skip[...])

    def attended_grad(self):
        for image in range(3):
            rows = pl.ds(STARTS[image], SIZES[image])
            grad = outgoing(self.cotangent, self.present, image)
            self.grad_attended[rows, :] = lax.dot_general(grad, self.w_out[...], NT, preferred_element_type=F32).astype(BF16)

    def last_norm(self, image):
        acc, hats, channels = self.acc1, self.acc0, self.acc1.shape[1]
        if image == 0:
            self.out_copy(2, self.acc0, self.o_mid_hat).wait()
        bias = self.row(V_SECOND) + self.row(V_SKIP)
        def shift_up(i, rows, carry):
            acc[rows, :] = acc[rows, :] + bias
            return carry
        over_rows(image, shift_up, 0)
        center, inverse = norm_figures(image, channels, lambda rows: acc[rows, :])
        self.inverses[6 + image : 7 + image, :] = inverse
        gain, shift = self.row(V_ATTN_GAIN), self.row(V_ATTN_SHIFT)
        def act(i, rows, carry):
            hat = (acc[rows, :] - center) * inverse
            hats[rows, :] = hat
            self.normed[rows, :] = (hat * gain + shift).astype(BF16)
            return carry
        over_rows(image, act, 0)
        if image == 2:
            self.out_copy(3, self.acc1, self.o_residual).start()
            self.out_copy(4, self.acc0, self.o_hat).start()
            self.out_copy(5, self.normed, self.o_normed).start()

    def project(self, i):
        cols = slice(512 * i, 512 * (i + 1))
        self.triple[:, cols] = dot(self.normed[...], self.w_attend[:, cols]).astype(BF16)

    def text_step(self, q, total):
        if q + 1 < 4:
            self.load_text(q + 1)
        par = q % 2
        waited(self.weight.at[par, pl.ds(0, 1024)], self.w_sem.at[par])
        part = dot(self.text[:, 1024 * q : 1024 * (q + 1)], self.weight[par, :1024, :])
        if q:
            part = total[...] + part
        if q < 3:
            total[...] = part
        else:
            self.text_pair[...] = part.astype(BF16)

    def finish(self):
        self.out_copy(0, self.a1, self.o_a1).wait()
        self.out_copy(1, self.a2, self.o_a2).wait()
        self.out_copy(3, self.acc1, self.o_residual).wait()
        self.out_copy(4, self.acc0, self.o_hat).wait()
        self.out_copy(5, self.normed, self.o_normed).wait()
        self.out_copy(6, self.text, self.o_text).wait()


MESH = pl.DeviceIdType.MESH
DEPTH = 4


STEPS = True
UNP = 3
BUDGET = 7.5
SHOW = False


class Where:
    def __init__(self, replicas, parts):
        self.replicas, self.parts = replicas, parts
        self.span = parts // (2 * DEPTH)
        self.group = lax.axis_index("dp")
        self.place = lax.axis_index("fsdp")
        self.core = lax.rem(self.place, 2)
        self.y = lax.rem(self.place // 2, self.span)
        self.z = self.place // (2 * self.span)
        self.side = lax.rem(self.group, 2)

    def index(self, z, y, core):
        return (z * self.span + y) * 2 + core

    def device(self, z=None, y=None, core=None, flip=False):
        z = self.z if z is None else z
        y = self.y if y is None else y
        core = self.core if core is None else core
        group = self.group + 1 - 2 * self.side if flip else self.group
        return (group, self.index(z, y, core))

    def barrier(self):
        sem = pltpu.get_barrier_semaphore()
        greet = lambda device: pl.semaphore_signal(sem, inc=1, device_id=device, device_id_type=MESH)
        greet(self.device(flip=True))
        def one(i, carry):
            greet((self.group, lax.rem(self.place + i, self.parts)))
            return carry
        lax.fori_loop(1, self.parts, one, 0)
        pl.semaphore_wait(sem, self.parts)


def forward_kernel(replicas, parts, rows, lead, lag, inner, images, *refs):
    weights, refs = refs[:6], refs[6:]
    note, emb, pixels, text, cotangent, present = refs[:6]
    full, mod, vec, notes = refs[6:10]
    outs = refs[10:21]
    own, part, sums, text_total = refs[21:25]
    scratch = refs[25:39]
    (n_send, n_recv, m_send, m_recv, z_send, z_recv, y_send, y_recv, s_send, s_recv, x_send, x_recv, c_send, c_recv, own_sem) = refs[39:]
    me = Where(replicas, parts)
    span = me.span
    total, width = own.shape
    chunks = total // rows
    joint, apart = 5 * width // 8, 3 * width // 8
    side = me.side
    thin = width // 4
    z_cols = pl.ds(pl.multiple_of(side * thin, thin), width - thin)
    a_cols = pl.ds(pl.multiple_of(side * apart, 128), joint)
    thin_cols = pl.ds(pl.multiple_of((1 - side) * (width - thin), thin), thin)
    thin_out = pl.ds(pl.multiple_of(side * (width - thin), thin), thin)
    b_cols = pl.ds(pl.multiple_of((1 - side) * joint, 128), apart)
    b_out = pl.ds(pl.multiple_of(side * joint, 128), apart)

    table = Rows(parts, pixels.shape[1], width, text.shape[2], inner)
    table.pack(weights, own, own_sem)
    me.barrier()
    table.packed(own, own_sem)
    local = pltpu.make_async_copy(own, full.at[me.place // 2, me.core], own_sem.at[0])
    local.start()

    def at(k):
        return pl.ds(pl.multiple_of(k * rows, 16), rows)

    def copy(src, dst, send, recv, device):
        return pltpu.make_async_remote_copy(src_ref=src, dst_ref=dst, send_sem=send, recv_sem=recv, device_id=device, device_id_type=MESH)

    def piece(k, z, y, cols, core=None):
        return full.at[z * span + y, me.core if core is None else core, at(k), cols]

    def z_copy(k, z, step, mine):
        src = own.at[at(k), z_cols] if mine else piece(k, z, me.y, z_cols)
        return copy(src, piece(k, z, me.y, z_cols), z_send.at[k, z, (step + 1) // 2], z_recv.at[k, z], me.device(z=me.z + step))

    def y_copy(k, z, turn, mine):
        src = own.at[at(k), a_cols] if mine else piece(k, z, me.y, a_cols)
        return copy(src, piece(k, z, me.y, a_cols), y_send.at[k, z, turn - 1], y_recv.at[k, z, turn - 1], me.device(y=lax.rem(me.y + turn, span)))

    def thin_copy(k, z):
        return copy(piece(k, z, me.y, thin_out), piece(k, z, me.y, thin_out), s_send.at[k, z], s_recv.at[k, z], me.device(flip=True))

    def x_copy(k, z, turn):
        y = lax.rem(me.y + turn, span)
        return copy(piece(k, z, y, b_out), piece(k, z, y, b_out), x_send.at[k, z, turn - 1], x_recv.at[k, z, turn - 1], me.device(flip=True))

    def core_copy(k, core):
        lane = full.at[:, core, at(k)]
        return copy(lane, lane, c_send.at[k], c_recv.at[k], me.device(core=1 - me.core))

    below = lambda s: (me.z - s >= 0, me.z - s)
    above = lambda s: (me.z + s < DEPTH, me.z + s)

    def start_own(k):
        @pl.when(me.z < DEPTH - 1)
        def _():
            z_copy(k, me.z, 1, True).start()
        @pl.when(me.z > 0)
        def _():
            z_copy(k, me.z, -1, True).start()
        for turn in range(1, span):
            y_copy(k, me.z, turn, True).start()

    def along_z(k, s):
        for (ok, z), step in ((below(s), 1), (above(s), -1)):
            @pl.when(ok)
            def _():
                z_copy(k, z, step, False).wait_recv()
                if s < DEPTH - 1:
                    more = me.z < DEPTH - 1 if step > 0 else me.z > 0
                    @pl.when(more)
                    def _():
                        z_copy(k, z, step, False).start()
                for turn in range(1, span):
                    y_copy(k, z, turn, False).start()
                thin_copy(k, z).start()

    def across(k, s):
        for ok, z in ((below(s), above(s)) if s else (below(0),)):
            @pl.when(ok)
            def _():
                for turn in range(1, span):
                    y_copy(k, z, turn, False).wait_recv()
                    x_copy(k, z, span - turn).start()

    def beside(k, s):
        for ok, z in ((below(s), above(s)) if s else (below(0),)):
            @pl.when(ok)
            def _():
                for turn in range(1, span):
                    x_copy(k, z, turn).wait_recv()

    def beside_thin(k, s):
        for ok, z in (below(s), above(s)):
            @pl.when(ok)
            def _():
                thin_copy(k, z).wait_recv()

    def lane_in(k):
        core_copy(k, 1 - me.core).wait_recv()

    def to_all(make):
        def one(i, carry):
            make(lax.rem(me.place + i, parts)).start()
            return carry
        lax.fori_loop(1, parts, one, 0)

    def wait_all(ref, send, recv):
        others = ref.at[pl.ds(0, parts - 1)]
        every = copy(others, others, send, recv, me.device(core=1 - me.core))
        every.wait_send()
        every.wait_recv()

    def modulate():
        wait_all(sums, m_send, m_recv)
        total = jnp.sum(sums[...], axis=0)
        blocks = emb.shape[1] // 128
        for j in range(blocks):
            for image in range(images):
                row = image * blocks + j
                mod[image : image + 1, j * 128 : (j + 1) * 128] = total[row : row + 1, :] + vec[V_EMB : V_EMB + 1, j * 128 : (j + 1) * 128]

    def unpack():
        wait_all(notes, n_send, n_recv)
        vec[...] = jnp.zeros_like(vec)
        for row in range(V_OUT + 1):
            size = {V_IN_GAIN: pixels.shape[1], V_IN_SHIFT: pixels.shape[1], V_EMB: emb.shape[1]}.get(row, width)
            each = 128 * parts // size
            for block in range(size // 128):
                value = notes[block * each, images + row : images + row + 1, :].astype(jnp.float32)
                for i in range(1, each):
                    value = value + notes[block * each + i, images + row : images + row + 1, :].astype(jnp.float32)
                vec[row : row + 1, block * 128 : (block + 1) * 128] = value
        rows_in = notes.shape[1]
        blocks = emb.shape[1] // 128
        for j in range(blocks):
            product = jnp.dot(notes[...].reshape(parts * rows_in, 128), emb[:, j * 128 : (j + 1) * 128], preferred_element_type=jnp.float32)
            product = product.reshape(parts, rows_in, 128)
            for image in range(images):
                part[:, image * blocks + j, :] = product[:, image, :]
        to_all(lambda far: copy(part.at[far], sums.at[me.place], m_send, m_recv, (me.group, far)))
        sums[me.place] = part[me.place]

    to_all(lambda far: copy(note.at[far], notes.at[me.place], n_send, n_recv, (me.group, far)))
    notes[me.place] = note[me.place]

    forward = Forward(table, full, pixels, text, cotangent, present, vec, mod, outs, scratch)
    ready = (DEPTH + 1) * lag
    have = lambda row: (row - 1) // rows + ready
    plan = []
    spent = {}

    def add(earliest, cost, work):
        slot = max([earliest] + [when for when, _ in plan[-1:]])
        while spent.get(slot, 0) and spent[slot] + cost > BUDGET:
            slot += 1
        spent[slot] = spent.get(slot, 0) + cost
        plan.append((slot, work))
        return slot

    add(0, 1, forward.zero)
    add(3, 5, unpack)
    for image in range(3):
        add(4, 2, functools.partial(forward.first_norm, image))
    convs = []

    def add_conv(which, pad, acc):
        steps = table.arrivals(which)
        slots, early = [], []
        for i, (_, end) in enumerate(steps):
            slot = add(have(which[0] + end), 3.4, None)
            early.append(i > 0 and have(which[0] + end) <= slots[-1])
            slots.append(slot)
        convs.append((which, pad, acc, steps, early, slots))

    add_conv(table.first, forward.a1, forward.acc0)
    add(0, 1, modulate)
    for image in range(3):
        add(0, 2.4, functools.partial(forward.mid_norm, image))
    add_conv(table.second, forward.a2, forward.acc1)
    add(have(sum(table.attend_more)), 0.5, forward.load_small)
    add(0, 2.2, forward.skip_product)
    for image in range(3):
        add(0, 2, functools.partial(forward.last_norm, image))
    add(0, 1.5, forward.attended_grad)
    for i in range(3):
        add(0, 1.4, functools.partial(forward.project, i))
    slots = max(chunks + ready, plan[-1][0] + 1)
    if SHOW: print(slots, [(s, getattr(getattr(w, "func", w), "__name__", "conv")) for s, w in plan])

    def steps(t):
        if not STEPS:
            pl.when(t == DEPTH * lag - 1)(local.wait)
            pl.when(t == 3)(unpack)
            return
        def conv(which, pad, acc, table_steps, early, when):
            low, high = jnp.int32(0), jnp.int32(0)
            for slot in when:
                low = low + jnp.where(t > slot, 1, 0)
                high = high + jnp.where(t >= slot, 1, 0)
            def one(q, carry):
                forward.conv_step(q, pad, acc, which, table_steps, early)
                return carry
            lax.fori_loop(low, high, one, 0)
        pending = list(convs)
        pl.when(t == DEPTH * lag - 1)(local.wait)
        for i, (slot, work) in enumerate(plan):
            if work is not None:
                pl.when(t == slot)(work)
            elif i == 0 or plan[i - 1][1] is not None:
                conv(*pending.pop(0))

    for k in range(min(lead, chunks)):
        start_own(k)

    last = 2 * (DEPTH - 1) + 3

    def slot(t, carry):
        def stage(delay, work):
            k = t - delay
            @pl.when(jnp.logical_and(k >= 0, k < chunks))
            def _():
                work(k)
        @pl.when(t + lead < chunks)
        def _():
            start_own(t + lead)
        for s in range(1, DEPTH):
            stage((s - 1) * lag, functools.partial(along_z, s=s))
        for s in range(DEPTH):
            stage(s * lag, functools.partial(across, s=s))
        for s in range(1, DEPTH):
            stage(s * lag, functools.partial(beside_thin, s=s))
        for s in range(DEPTH):
            stage((s + 1) * lag, functools.partial(beside, s=s))
        stage(DEPTH * lag, lambda k: core_copy(k, me.core).start())
        stage(ready, lane_in)
        steps(t)
        return carry

    lax.fori_loop(0, slots, slot, 0)
    if STEPS:
        forward.load_text(jnp.int32(0))
        for q in range(4):
            forward.text_step(q, text_total)
    else:
        modulate()

    def finish(k, carry):
        for step, edge in ((1, me.z < DEPTH - 1), (-1, me.z > 0)):
            for s in range(DEPTH - 1):
                ok, z = below(s) if step > 0 else above(s)
                @pl.when(jnp.logical_and(ok, edge))
                def _():
                    z_copy(k, z, step, False).wait_send()
        for z in range(DEPTH):
            for turn in range(1, span):
                y_copy(k, z, turn, False).wait_send()
                x_copy(k, z, turn).wait_send()
            @pl.when(z != me.z)
            def _():
                thin_copy(k, z).wait_send()
        core_copy(k, me.core).wait_send()
        return carry

    lax.fori_loop(0, chunks, finish, 0)
    if STEPS:
        forward.finish()


def forward_all(weights, note, emb, pixels, text, cotangent, present, images, inner, replicas, parts, rows=80, lead=3, lag=1):
    width = weights[0].shape[1]
    total = Rows(parts, pixels.shape[1], width, text.shape[2], inner).total
    chunks = total // rows
    span = parts // (2 * DEPTH)
    pix, pix_width = pixels.shape
    dma = lambda *shape: pltpu.SemaphoreType.DMA(shape)
    bf = lambda *shape: jax.ShapeDtypeStruct(shape, BF16)
    fl = lambda *shape: jax.ShapeDtypeStruct(shape, F32)
    hbm, vmem = pl.BlockSpec(memory_space=pl.ANY), pl.BlockSpec(memory_space=pltpu.VMEM)
    return pl.pallas_call(
        functools.partial(forward_kernel, replicas, parts, rows, lead, lag, inner, images),
        out_shape=[
            bf(parts // 2, 2, total, width), fl(8, emb.shape[1]), fl(16, emb.shape[1]), bf(*note.shape),
            bf(3, PADDED, pix_width), bf(3, PADDED, width), fl(pix, width), fl(pix, width), fl(pix, width), bf(pix, width),
            bf(pix, 3 * inner), bf(3 * TEXT_ROWS, 2 * inner), bf(pix, inner), fl(24, width), bf(3 * TEXT_ROWS, text.shape[2]),
        ],
        in_specs=[hbm] * 6 + [vmem] * 5 + [pl.BlockSpec(memory_space=pltpu.SMEM)],
        out_specs=[hbm, vmem, vmem, vmem] + [hbm] * 6 + [vmem] * 4 + [hbm],
        scratch_shapes=[
            pltpu.VMEM((total, width), BF16),
            pltpu.VMEM((parts, images * emb.shape[1] // 128, 128), F32),
            pltpu.VMEM((parts, images * emb.shape[1] // 128, 128), F32),
            pltpu.VMEM((3 * TEXT_ROWS, width), F32),
            pltpu.VMEM((3, PADDED, pix_width), BF16), pltpu.VMEM((3, PADDED, width), BF16),
            pltpu.VMEM((pix, BLOCK), BF16), pltpu.VMEM((2, BLOCK, width), BF16),
            pltpu.VMEM((pix, width), F32), pltpu.VMEM((pix, width), F32), pltpu.VMEM((pix, width), BF16),
            pltpu.VMEM((width, 3 * inner), BF16), pltpu.VMEM((pix_width, width), BF16), pltpu.VMEM((inner, width), BF16), pltpu.VMEM((3 * TEXT_ROWS, text.shape[2]), BF16),
            dma(2), dma(3), dma(7),
            dma(), dma(), dma(), dma(),
            dma(chunks, DEPTH, 2), dma(chunks, DEPTH),
            dma(chunks, DEPTH, span - 1), dma(chunks, DEPTH, span - 1),
            dma(chunks, DEPTH), dma(chunks, DEPTH),
            dma(chunks, DEPTH, span - 1), dma(chunks, DEPTH, span - 1),
            dma(chunks), dma(chunks), dma(8),
        ],
        compiler_params=pltpu.CompilerParams(collective_id=0, has_side_effects=True, vmem_limit_bytes=60 << 20),
        name="forward_all",
    )(*weights, note, emb, pixels, text, cotangent, present)


FILL = 3


class Seat(Where):
    def bit(self, b):
        step = 1 << b
        group = self.group + step - 2 * step * lax.rem(self.group // step, 2)
        return (group, self.place)

    def meet(self):
        sem = pltpu.get_barrier_semaphore()
        count = self.replicas * self.parts
        def one(i, carry):
            far = lax.rem(self.group * self.parts + self.place + i, count)
            pl.semaphore_signal(sem, inc=1, device_id=(far // self.parts, lax.rem(far, self.parts)), device_id_type=MESH)
            return carry
        lax.fori_loop(1, count, one, 0)
        pl.semaphore_wait(sem, count - 1)


def norm_pull(image, factor, inverse, grad, hat, plain, crossed, put):
    count = SIZES[image]
    mean_plain = group_mean(plain * factor, count)[:1]
    mean_crossed = group_mean(crossed * factor, count)[:1]
    def one(i, rows, carry):
        value = inverse * (grad(rows) * factor - mean_plain - hat(rows) * mean_crossed)
        put(i, rows, value)
        return carry + (value[:8] + value[8:])
    total = over_rows(image, one, jnp.zeros(plain.shape, F32))
    return jnp.sum(total, axis=0, keepdims=True)


def two_sums(image, channels, pair):
    def add(i, rows, carry):
        a, b = pair(i, rows)
        return carry[0] + (a[:8] + a[8:]), carry[1] + (b[:8] + b[8:])
    zero = jnp.zeros((8, channels), F32)
    sums = over_rows(image, add, (zero, zero))
    return [jnp.broadcast_to(jnp.sum(part, axis=0, keepdims=True), (8, channels)) for part in sums]


def silu_pull(value):
    gate = jax.nn.sigmoid(value)
    return gate * (1.0 + value * (1.0 - gate))


G_IN_GAIN, G_IN_SHIFT, G_FIRST, G_MID_GAIN, G_MID_SHIFT, G_SECOND, G_ATTN_GAIN, G_ATTN_SHIFT, G_OUT = range(9)


class Backward:
    def __init__(self, rows, full, r_low, pixels, vec, mod, inverses, a1, a2, mid_hat, outs, scratch):
        self.rows, self.full, self.r_low, self.pixels, self.vec, self.mod, self.inverses = rows, full, r_low, pixels, vec, mod, inverses
        self.h_a1, self.h_a2, self.h_mid = a1, a2, mid_hat
        self.g_first, self.g_second, self.g_skip, self.grad_pixels = outs
        (self.a1, self.pad, self.hat, self.acc, self.acc1, self.c_low, self.patch, self.weight, self.stage, self.w_skip,
         self.vecs, self.mods, self.in_sem, self.w_sem, self.o_sem) = scratch

    def row(self, r, channels=1024):
        return self.vec[r : r + 1, :channels]

    def add_row(self, r, value):
        width = value.shape[1]
        self.vecs[r : r + 1, :width] = self.vecs[r : r + 1, :width] + value[:1]

    def fetch(self):
        for i, (src, dst) in enumerate(((self.h_a2, self.pad), (self.h_a1, self.a1), (self.h_mid, self.hat))):
            pltpu.make_async_copy(src, dst, self.in_sem.at[i]).start()
        start, size = self.rows.skip
        def one(f, carry):
            pltpu.make_async_copy(shard_of(self.full, f, pl.ds(start, size)), self.w_skip.at[pl.ds(pl.multiple_of(f * size, SUB), size)], self.in_sem.at[3]).start()
            return carry
        lax.fori_loop(0, self.rows.parts, one, 0)

    def arrived(self, i):
        waited((self.pad, self.a1, self.hat, self.w_skip)[i], self.in_sem.at[i])

    def put_out(self, dst, first, count):
        span, size = dst.shape[1], dst.shape[3]
        for i in range(count):
            f = first + i
            pltpu.make_async_copy(
                self.stage.at[pl.ds(i * size, size)],
                dst.at[f // (2 * span), lax.rem(f // 2, span), lax.rem(f, 2)],
                self.o_sem,
            ).start()

    def weight_grad(self, q, pad, count, grad, dst):
        def prepare(known):
            gather_blocks(pad, range(known * BLOCK // 128, (known + 1) * BLOCK // 128), self.patch)
        choose(q, [(known, known + 1, functools.partial(prepare, known)) for known in range(count)])
        @pl.when(q > 0)
        def _():
            self.stored()
        for col in range(0, 1024, 256):
            cols = slice(col, col + 256)
            self.stage[:, cols] = lax.dot_general(self.patch[...], grad[:, cols], TN, preferred_element_type=F32).astype(BF16)
        each = BLOCK // dst.shape[3]
        self.put_out(dst, q * each, each)

    def second_weight(self, q):
        self.weight_grad(q, self.pad, 9 * self.pad.shape[2] // BLOCK, self.r_low, self.g_second)

    def first_weight(self, q):
        self.weight_grad(q, self.a1, 9 * self.a1.shape[2] // BLOCK, self.c_low, self.g_first)

    def stored(self, size=BLOCK):
        waited(self.stage.at[pl.ds(0, size)], self.o_sem)

    def skip_weight(self):
        size = self.pixels.shape[1]
        for col in range(0, 1024, 512):
            cols = slice(col, col + 512)
            self.stage[:size, cols] = lax.dot_general(self.pixels[...], self.r_low[:, cols], TN, preferred_element_type=F32).astype(BF16)
        self.put_out(self.g_skip, jnp.int32(0), self.rows.parts)
        self.stored(size)

    def pad_residual(self):
        zero_edges(self.pad)
        for image in range(3):
            def one(i, rows, carry):
                store_padded(self.pad, image, i, self.r_low[rows, :].astype(F32))
                return carry
            over_rows(image, one, 0)

    def load_tap(self, which, height, tap):
        start, size = which
        def one(known):
            at = known * height
            while at < (known + 1) * height:
                shard, inside = divmod(at, size)
                count = min(size - inside, (known + 1) * height - at)
                pltpu.make_async_copy(
                    shard_of(self.full, shard, pl.ds(start + inside, count)),
                    self.weight.at[known % 2, pl.ds(at - known * height, count)],
                    self.w_sem.at[known % 2],
                ).start()
                at += count
        if isinstance(tap, int):
            one(tap)
        else:
            choose(tap, [(known, known + 1, functools.partial(one, known)) for known in range(9)])

    def pull_step(self, tap, which, height, acc):
        @pl.when(tap + 1 < 9)
        def _():
            self.load_tap(which, height, tap + 1)
        @pl.when(tap == 0)
        def _():
            acc[...] = jnp.zeros_like(acc)
        def prepare(known):
            for image in range(3):
                self.patch[STARTS[image] : STARTS[image] + SIZES[image], :1024] = shifted(self.pad, known, image, slice(0, 1024), True)
        choose(tap, [(known, known + 1, functools.partial(prepare, known)) for known in range(9)])
        par = lax.rem(tap, 2)
        waited(self.weight.at[par, pl.ds(0, height)], self.w_sem.at[par])
        for col in range(0, height, 512):
            cols = slice(col, col + 512)
            acc[:, cols] = acc[:, cols] + lax.dot_general(self.patch[:, :1024], self.weight[par, cols, :], NT, preferred_element_type=F32)

    def load_second(self):
        self.load_tap(self.rows.second, 1024, 0)

    def second_pull(self, tap):
        self.pull_step(tap, self.rows.second, 1024, self.acc)

    def load_first(self):
        self.load_tap(self.rows.first, self.pixels.shape[1], 0)

    def first_pull(self, tap):
        self.pull_step(tap, self.rows.first, self.pixels.shape[1], self.acc1)

    def mid_pull(self, image):
        acc, hat, channels = self.acc, self.hat, 1024
        if image == 0:
            self.vecs[...] = jnp.zeros_like(self.vecs)
            self.mods[...] = jnp.zeros_like(self.mods)
            zero_edges(self.pad)
        scale, shift = 1.0 + self.mod[image : image + 1, :channels], self.mod[image : image + 1, channels:]
        gain, bias = self.row(V_MID_GAIN), self.row(V_MID_SHIFT)
        factor, lift = gain * scale, bias * scale + shift
        def pair(i, rows):
            h = hat[rows, :]
            grad = acc[rows, :] * silu_pull(h * factor + lift)
            acc[rows, :] = grad
            return grad, grad * h
        plain, crossed = two_sums(image, channels, pair)
        def put(i, rows, value):
            store_padded(self.pad, image, i, value)
            self.c_low[rows, :] = value.astype(BF16)
        inverse = self.inverses[3 + image : 4 + image, :]
        total = norm_pull(image, factor, inverse, lambda rows: acc[rows, :], lambda rows: hat[rows, :], plain, crossed, put)
        self.add_row(G_FIRST, total)
        self.add_row(G_MID_GAIN, crossed * scale)
        self.add_row(G_MID_SHIFT, plain * scale)
        self.mods[image : image + 1, :channels] = (crossed * gain + plain * bias)[:1]
        self.mods[image : image + 1, channels:] = plain[:1]

    def first_norm_pull(self, image):
        acc, pixels = self.acc1, self.pixels
        channels = pixels.shape[1]
        inverse, center = self.inverses[image : image + 1, :channels], self.inverses[16 + image : 17 + image, :channels]
        gain, bias = self.row(V_IN_GAIN, channels), self.row(V_IN_SHIFT, channels)
        hat = lambda rows: (pixels[rows, :].astype(F32) - center) * inverse
        def pair(i, rows):
            h = hat(rows)
            grad = acc[rows, :] * silu_pull(h * gain + bias)
            acc[rows, :] = grad
            return grad, grad * h
        plain, crossed = two_sums(image, channels, pair)
        def put(i, rows, value):
            self.grad_pixels[rows, :] = self.grad_pixels[rows, :] + value
        norm_pull(image, gain, inverse, lambda rows: acc[rows, :], hat, plain, crossed, put)
        self.add_row(G_IN_GAIN, crossed)
        self.add_row(G_IN_SHIFT, plain)

    def skip_pull(self):
        self.grad_pixels[...] = lax.dot_general(self.r_low[...], self.w_skip[...], NT, preferred_element_type=F32)


def reduce_kernel(replicas, parts, rows, spans, lead, ring, nrc, rb, lag, inner, text_dim, images, known, *refs):
    early = refs[:known]
    full, r_low, pixels, vec, mod, inverses, a1, a2, mid_hat, emb_note, more = refs[known : known + 11]
    kinds = len(spans)
    refs = refs[known + 11 :]
    outs, refs = refs[:kinds], refs[kinds:]
    notes, g_first, g_second, g_skip, grad_pixels, g_narrow, g_wide = refs[:7]
    rest = refs[7:]
    (hold, rc, xr, yr, tr, zu, zd, fr, tb, shared, target, shared32, target32) = rest[:13]
    scratch = rest[13:28]
    (l_sem, c_send, c_recv, x_send, x_recv, y_send, y_recv,
     u_send, u_recv, d_send, d_recv, f_send, f_recv, n_send, n_recv, t_send, t_recv, free, x_free, y_free, u_free, d_free) = rest[28:]
    me = Seat(replicas, parts)
    span = me.span
    width = r_low.shape[1]
    chunks = spans[-1][1]
    side = me.side
    bits = replicas.bit_length() - 1
    apart, joint = 3 * width // 8, 5 * width // 8
    thin = 128
    main = width - thin
    z_cols = pl.ds(pl.multiple_of(side * thin, thin), main)
    thin_cols = pl.ds(pl.multiple_of((1 - side) * main, thin), thin)
    thin_in = pl.ds(pl.multiple_of(side * main, thin), thin)
    x_in = pl.ds(pl.multiple_of(side * joint, 128), apart)
    y_cols = pl.ds(pl.multiple_of(side * apart, 128), joint)
    table = Rows(parts, pixels.shape[1], width, text_dim, inner)
    back = Backward(table, full, r_low, pixels, vec, mod, inverses, a1, a2, mid_hat, (g_first, g_second, g_skip, grad_pixels), scratch)
    grads = list(early) + [g_skip, g_second, g_first]

    me.meet()
    back.fetch()

    def copy(src, dst, send, recv, device):
        return pltpu.make_async_remote_copy(src_ref=src, dst_ref=dst, send_sem=send, recv_sem=recv, device_id=device, device_id_type=MESH)

    def give(sem, device):
        pl.semaphore_signal(sem, inc=1, device_id=device, device_id_type=MESH)

    def take(sem, k, size):
        @pl.when(k >= size)
        def _():
            pl.semaphore_wait(sem, 1)

    def core_copy(k, src):
        return copy(src, rc.at[lax.rem(k, nrc)], c_send.at[k], c_recv.at[lax.rem(k, nrc)], me.device(core=1 - me.core))

    def begin(k):
        take(free, k, nrc)
        for grad, (lo, hi) in zip(grads, spans):
            @pl.when(jnp.logical_and(k >= lo, k < hi))
            def _():
                at = pl.ds(pl.multiple_of((k - lo) * rows, 16), rows)
                slot = lax.rem(k, ring)
                pltpu.make_async_copy(grad.at[:, :, me.core, at, :], hold.at[slot], l_sem.at[slot]).start()
                core_copy(k, grad.at[:, :, 1 - me.core, at, :]).start()

    def x_copy(k, turn):
        slot = lax.rem(k, ring)
        cols = pl.ds(pl.multiple_of((1 - side) * joint, 128), apart)
        return copy(hold.at[slot, :, lax.rem(me.y + turn, span), :, cols], xr.at[lax.rem(k, rb), turn - 1], x_send.at[k, turn - 1], x_recv.at[k, turn - 1], me.bit(0))

    def y_copy(k, turn):
        slot = lax.rem(k, ring)
        return copy(hold.at[slot, :, lax.rem(me.y + turn, span), :, y_cols], yr.at[lax.rem(k, rb), turn - 1], y_send.at[k, turn - 1], y_recv.at[k, turn - 1], me.device(y=lax.rem(me.y + turn, span)))

    def t_copy(k):
        slot = lax.rem(k, ring)
        return copy(hold.at[slot, :, me.y, :, thin_cols], tr.at[lax.rem(k, rb)], t_send.at[k], t_recv.at[k], me.bit(0))

    def up_copy(k, z):
        slot = lax.rem(k, ring)
        return copy(hold.at[slot, z + 1 : DEPTH, me.y, :, z_cols], zu.at[lax.rem(k, rb), 0 : DEPTH - 1 - z], u_send.at[k], u_recv.at[k], me.device(z=me.z + 1))

    def down_copy(k, z):
        slot = lax.rem(k, ring)
        return copy(hold.at[slot, 0:z, me.y, :, z_cols], zd.at[lax.rem(k, rb), 0:z], d_send.at[k], d_recv.at[k], me.device(z=me.z - 1))

    def f_copy(k, b):
        slot = lax.rem(k, ring)
        src = hold.at[slot, me.z, me.y, :, z_cols] if b == 0 else tb.at[b - 1, k]
        dst = fr.at[b, k, :, pl.ds(0, main)] if b == 0 else fr.at[b, k]
        return copy(src, dst, f_send.at[b, k], f_recv.at[b, k], me.bit(b))

    def fold_core(k):
        slot = lax.rem(k, ring)
        waited(hold.at[slot], l_sem.at[slot])
        core_copy(k, rc.at[lax.rem(k, nrc)]).wait_recv()
        hold[slot] = hold[slot] + rc[lax.rem(k, nrc)]
        @pl.when(k + nrc < chunks)
        def _():
            give(free, me.device(core=1 - me.core))
        for turn in range(1, span):
            take(x_free.at[turn - 1], k, rb)
            x_copy(k, turn).start()
        t_copy(k).start()

    def fold_x(k):
        slot = lax.rem(k, ring)
        t_copy(k).wait_recv()
        hold[slot, :, me.y, :, thin_in] = hold[slot, :, me.y, :, thin_in] + tr[lax.rem(k, rb)]
        for turn in range(1, span):
            x_copy(k, turn).wait_recv()
            y = lax.rem(me.y + turn, span)
            hold[slot, :, y, :, x_in] = hold[slot, :, y, :, x_in] + xr[lax.rem(k, rb), turn - 1]
            @pl.when(k + rb < chunks)
            def _():
                give(x_free.at[turn - 1], me.bit(0))
            take(y_free.at[turn - 1], k, rb)
            y_copy(k, turn).start()

    def fold_y(k):
        slot = lax.rem(k, ring)
        for turn in range(1, span):
            y_copy(k, turn).wait_recv()
            hold[slot, :, me.y, :, y_cols] = hold[slot, :, me.y, :, y_cols] + yr[lax.rem(k, rb), turn - 1]
            @pl.when(k + rb < chunks)
            def _():
                give(y_free.at[turn - 1], me.device(y=lax.rem(me.y + span - turn, span)))

    def hop(k, h):
        slot = lax.rem(k, ring)
        @pl.when(me.z == h)
        def _():
            if h > 0:
                up_copy(k, h - 1).wait_recv()
                hold[slot, h:, me.y, :, z_cols] = hold[slot, h:, me.y, :, z_cols] + zu[lax.rem(k, rb), 0 : DEPTH - h]
                @pl.when(k + rb < chunks)
                def _():
                    give(u_free, me.device(z=me.z - 1))
            if h < DEPTH - 1:
                take(u_free, k, rb)
                up_copy(k, h).start()
        z = DEPTH - 1 - h
        @pl.when(me.z == z)
        def _():
            if h > 0:
                down_copy(k, z + 1).wait_recv()
                hold[slot, : z + 1, me.y, :, z_cols] = hold[slot, : z + 1, me.y, :, z_cols] + zd[lax.rem(k, rb), 0 : z + 1]
                @pl.when(k + rb < chunks)
                def _():
                    give(d_free, me.device(z=me.z + 1))
            if h < DEPTH - 1:
                take(d_free, k, rb)
                down_copy(k, z).start()

    def finish(k, b):
        slot = lax.rem(k, ring)
        f_copy(k, b).wait_recv()
        if b == 0:
            came = jnp.concatenate([fr[b, k, :, :main].astype(F32), jnp.zeros((rows, thin), F32)], 1)
            before = hold[slot, me.z, me.y].astype(F32)
            column = lax.broadcasted_iota(jnp.int32, before.shape, 1)
            came = pltpu.roll(came, thin * (1 - side), 1)
            ours = jnp.logical_and(column >= thin * side, column < main + thin * side)
            theirs = jnp.logical_and(column >= thin * (1 - side), column < main + thin * (1 - side))
            total = jnp.where(ours, before, 0.0) + jnp.where(theirs, came, 0.0)
        else:
            total = tb[b - 1, k].astype(F32) + fr[b, k].astype(F32)
        if b == bits - 1:
            for out, (lo, hi) in zip(outs, spans):
                @pl.when(jnp.logical_and(k >= lo, k < hi))
                def _():
                    out[pl.ds(pl.multiple_of((k - lo) * rows, 16), rows), :] = total
        else:
            tb[b, k] = total.astype(BF16)
            f_copy(k, b + 1).start()

    def retire(k):
        core_copy(k, rc.at[0]).wait_send()
        t_copy(k).wait_send()
        for turn in range(1, span):
            x_copy(k, turn).wait_send()
            y_copy(k, turn).wait_send()
        for z in range(DEPTH):
            @pl.when(me.z == z)
            def _():
                if z < DEPTH - 1:
                    up_copy(k, z).wait_send()
                if z > 0:
                    down_copy(k, z).wait_send()
        for b in range(bits):
            f_copy(k, b).wait_send()

    count = replicas * parts
    mine = me.group * parts + me.place
    tall = shared.shape[0]

    def note_copies(far):
        device = (far // parts, lax.rem(far, parts))
        return (
            copy(shared, notes.at[mine, pl.ds(0, tall)], n_send, n_recv, device),
            copy(target.at[lax.rem(far, parts)], notes.at[mine, pl.ds(tall, 16)], n_send, n_recv, device),
        )

    def tell():
        back.vecs[:, :] = back.vecs[:, :] + more[...]
        target32[...] = emb_note[...].astype(F32)
        each = 2 * width // 128
        for image in range(images):
            for j in range(each):
                shared32[image * each + j : image * each + j + 1, :] = back.mods[image : image + 1, j * 128 : (j + 1) * 128]
        shared[...] = shared32[...].astype(BF16)
        for row in range(G_OUT + 1):
            size = (pixels.shape[1] if row in (G_IN_GAIN, G_IN_SHIFT) else width) // parts
            for f in range(parts):
                block = f * size // 128
                target32[f, images + row : images + row + 1, :] = back.vecs[row : row + 1, block * 128 : (block + 1) * 128]
        target[...] = target32[...].astype(BF16)
        def send(i, carry):
            for one in note_copies(lax.rem(mine + i, count)):
                one.start()
            return carry
        lax.fori_loop(1, count, send, 0)
        notes[mine, :tall, :] = shared[...]
        notes[mine, tall:, :] = target[me.place]
    lo_skip, lo_second, lo_first = (spans[known + i][0] - lead for i in range(3))
    n2, n1 = 9 * width // BLOCK, 9 * pixels.shape[1] // BLOCK
    begun = min(FILL, lo_second - n2)
    s0 = begun + n2
    s1 = s0 + 10
    s2 = s1 + 3
    s3 = s2 + n1
    s4 = s3 + 6
    assert 1 <= lo_skip and begun >= 2 and s0 <= lo_second and s3 <= lo_first
    last = max(chunks + (2 + DEPTH + bits) * lag + 1, s4 + 5)

    def steps(t):
        options = []
        def once(when, *work):
            def run():
                for one in work:
                    one()
            options.append((when, when + 1, run))
        def many(when, until, each, limit, work):
            def run():
                for i in range(each):
                    at = (t - when) * each + i
                    if limit % each:
                        pl.when(at < limit)(lambda: work(at))
                    else:
                        work(at)
            options.append((when, until, run))
        def last_of(work):
            def run(i, end):
                work(i)
                pl.when(i == end - 1)(back.stored)
            return run
        second, first = last_of(back.second_weight), last_of(back.first_weight)
        once(0, back.skip_weight)
        once(begun - 1, lambda: back.arrived(0))
        many(begun, s0, 1, n2, lambda i: second(i, n2))
        once(s0, back.pad_residual, back.load_second)
        many(s0 + 1, s1, 1, 9, back.second_pull)
        for image in range(3):
            once(s1 + image, *([lambda: back.arrived(1), lambda: back.arrived(2), lambda: back.arrived(3)] if image == 0 else []), functools.partial(back.mid_pull, image))
        many(s2, s3, 1, n1, lambda i: first(i, n1))
        once(s3, back.load_first)
        many(s3 + 1, s4, 2, 9, back.first_pull)
        once(s4, back.skip_pull)
        for image in range(3):
            once(s4 + 1 + image, functools.partial(back.first_norm_pull, image))
        once(s4 + 4, tell)
        choose(t, options)

    for k in range(lead):
        begin(jnp.int32(k))

    first_f = (2 + DEPTH) * lag

    def slot_work(t, carry):
        def stage(delay, work):
            k = t - delay
            @pl.when(jnp.logical_and(k >= 0, k < chunks))
            def _():
                work(k)
        for h in range(DEPTH - 1, 0, -1):
            stage((2 + h) * lag, functools.partial(hop, h=h))
        stage((1 + DEPTH) * lag, lambda k: f_copy(k, 0).start())
        def pair(k):
            fold_y(k)
            hop(k, 0)
        stage(2 * lag, pair)
        stage(lag, fold_x)
        stage(0, fold_core)
        for b in range(bits):
            stage(first_f + b * lag, functools.partial(finish, b=b))
        stage(first_f + bits * lag, retire)
        @pl.when(t + lead < chunks)
        def _():
            begin(t + lead)
        steps(t)
        return carry

    lax.fori_loop(0, last, slot_work, 0)
    others = notes.at[pl.ds(0, count - 1)]
    every = copy(others, others, n_send, n_recv, me.device(core=1 - me.core))
    every.wait_send()
    every.wait_recv()
    total = jnp.sum(notes[:, tall:, :].astype(F32), axis=0)
    for dst, first, last in ((g_narrow, G_IN_GAIN, G_IN_SHIFT), (g_wide, G_FIRST, G_OUT)):
        size = dst.shape[2]
        turn = lax.rem(128 - lax.rem(me.place * size, 128), 128)
        mine_only = pltpu.roll(total, turn, 1)
        for row in range(first, last + 1):
            dst[row - first] = mine_only[images + row : images + row + 1, :size]


def reduce_all(early, full, r_low, pixels, vec, mod, inverses, a1, a2, mid_hat, emb_note, more, inner, text_dim, images, replicas, parts, rows, lead=2, nrc=3, lag=2, rb=8):
    span = parts // (2 * DEPTH)
    pix, width = r_low.shape
    pix_width = pixels.shape[1]
    spans, at = [], 0
    views = []
    for size in [grad.shape[0] // parts for grad in early] + [pix_width // parts, 9 * width // parts, 9 * pix_width // parts]:
        spans.append((at // rows, (at + size) // rows))
        at += size
    for grad in early:
        views.append(grad.reshape(DEPTH, span, 2, grad.shape[0] // parts, width))
    total = at
    chunks = total // rows
    bits = replicas.bit_length() - 1
    ring = lead + (2 + DEPTH + bits) * lag + 2
    dma = lambda *shape: pltpu.SemaphoreType.DMA(shape)
    reg = lambda *shape: pltpu.SemaphoreType.REGULAR(shape)
    vm = lambda *shape: pltpu.VMEM(shape, BF16)
    vf = lambda *shape: pltpu.VMEM(shape, F32)
    bf = lambda *shape: jax.ShapeDtypeStruct(shape, BF16)
    fl = lambda *shape: jax.ShapeDtypeStruct(shape, F32)
    hbm, vmem = pl.BlockSpec(memory_space=pl.ANY), pl.BlockSpec(memory_space=pltpu.VMEM)
    tall = images * 2 * width // 128
    return pl.pallas_call(
        functools.partial(reduce_kernel, replicas, parts, rows, spans, lead, ring, nrc, rb, lag, inner, text_dim, images, len(early)),
        out_shape=[
            *(fl((hi - lo) * rows, width) for lo, hi in spans), bf(replicas * parts, tall + 16, 128),
            *(bf(DEPTH, span, 2, size // parts, width) for size in (9 * pix_width, 9 * width, pix_width)), fl(pix, pix_width),
            fl(2, 1, pix_width // parts), fl(7, 1, width // parts),
        ],
        in_specs=[hbm] * (len(early) + 1) + [vmem] * 5 + [hbm] * 3 + [vmem] * 2,
        out_specs=[vmem] * (len(spans) + 1) + [hbm] * 3 + [vmem] * 3,
        scratch_shapes=[
            vm(ring, DEPTH, span, rows, width),
            vm(nrc, DEPTH, span, rows, width),
            vm(rb, span - 1, DEPTH, rows, 3 * width // 8),
            vm(rb, span - 1, DEPTH, rows, 5 * width // 8),
            vm(rb, DEPTH, rows, 128),
            vm(rb, DEPTH - 1, rows, width - 128),
            vm(rb, DEPTH - 1, rows, width - 128),
            vm(bits, chunks, rows, width),
            vm(max(bits - 1, 1), chunks if bits > 1 else 1, rows, width),
            vm(tall, 128), vm(parts, 16, 128), vf(tall, 128), vf(parts, 16, 128),
            vm(3, PADDED, pix_width), vm(3, PADDED, width), vf(pix, width), vf(pix, width), vf(pix, pix_width), vm(pix, width),
            vm(pix, BLOCK), vm(2, 1024, width), vm(BLOCK, width), vm(pix_width, width), vf(16, width), vf(8, 2 * width),
            dma(4), dma(2), dma(),
            dma(ring),
            dma(chunks), dma(nrc),
            dma(chunks, span - 1), dma(chunks, span - 1),
            dma(chunks, span - 1), dma(chunks, span - 1),
            dma(chunks), dma(chunks), dma(chunks), dma(chunks),
            dma(bits, chunks), dma(bits, chunks),
            pltpu.SemaphoreType.DMA, pltpu.SemaphoreType.DMA, dma(chunks), dma(chunks),
            pltpu.SemaphoreType.REGULAR, reg(span - 1), reg(span - 1), pltpu.SemaphoreType.REGULAR, pltpu.SemaphoreType.REGULAR,
        ],
        compiler_params=pltpu.CompilerParams(collective_id=1, has_side_effects=True, vmem_limit_bytes=62 << 20),
        name="reduce_all",
    )(*views, full, r_low, pixels, vec, mod, inverses, a1, a2, mid_hat, emb_note, more)


def middle_kernel(parts, inner, text_dim, triple, text_pair, keep, grad_attended, cotangent, vec, inverses, present, full, h_normed, h_hats, h_residual, h_text,
                  r_low, more, h_block, h_out, h_attend, h_more, h_g_text, attended, grad_triple, grad_text, rows_grad, w_attend, w_out, stage,
                  g_low, queries, outs, keys, values, normed, hats, residual, text, block_output, g_out, g_attend, g_more, sems, i_sems, o_sems):
    width = cotangent.shape[1]
    table = Rows(parts, 512, width, text_dim, inner)
    start, size = table.out
    def one(f, carry):
        pltpu.make_async_copy(shard_of(full, f, pl.ds(start, size)), w_out.at[pl.ds(pl.multiple_of(f * size, SUB), size)], sems.at[0]).start()
        return carry
    lax.fori_loop(0, parts, one, 0)
    table.load_attend(full, w_attend, sems.at[1])

    late = [pltpu.make_async_copy(src, dst, i_sems.at[i]) for i, (src, dst) in enumerate(((h_text, text), (h_residual, residual), (h_normed, normed), (h_hats, hats)))]
    for copy in late:
        copy.start()
    done = [pltpu.make_async_copy(src, dst, o_sems.at[i]) for i, (src, dst) in enumerate(((block_output, h_block), (g_out, h_out), (g_attend, h_attend), (g_more, h_more)))]

    for image in range(3):
        g_low[pl.ds(STARTS[image], SIZES[image]), :] = outgoing(cotangent, present, image)

    lane = lax.broadcasted_iota(jnp.int32, (1, 2 * HEAD), 1)
    scale = HEAD ** -0.5
    room = min(SIZES) + TEXT_ROWS
    for buf in (keys, values):
        buf[room:, :] = jnp.zeros((KEYS - room, 2 * HEAD), BF16)

    def heads(pair, carry):
        at = lambda shift: pl.ds(pl.multiple_of(pair * 2 * HEAD + shift * inner, 128), 2 * HEAD)
        for image in range(3):
            size = SIZES[image]
            rows = pl.ds(STARTS[image], size)
            text_rows = pl.ds(image * TEXT_ROWS, TEXT_ROWS)
            for buf, part in ((queries, triple[rows, at(0)] * jnp.asarray(scale, BF16)), (outs, grad_attended[rows, at(0)])):
                buf[:size, :] = jnp.where(lane < HEAD, part, jnp.zeros_like(part))
                buf[size : 2 * size, :] = jnp.where(lane < HEAD, jnp.zeros_like(part), part)
            for i, buf in enumerate((keys, values)):
                buf[:size, :] = triple[rows, at(1 + i)]
                buf[size : size + TEXT_ROWS, :] = text_pair[text_rows, at(i)]
            q, go = queries[: 2 * size, :], outs[: 2 * size, :]
            seen = keep[image : image + 1, :]
            s = lax.dot_general(q, keys[...], NT, preferred_element_type=F32)
            s = jnp.where(seen == 1, s, jnp.where(seen == 0, -1000000000.0, -jnp.inf))
            e = jnp.exp(s - jnp.max(s, axis=1, keepdims=True))
            p = e * (1.0 / jnp.sum(e, axis=1, keepdims=True))
            low = p.astype(BF16)
            out = dot(low, values[...])
            dv = lax.dot_general(low, go, TN, preferred_element_type=F32)
            dp = lax.dot_general(go, values[...], NT, preferred_element_type=F32)
            ds = (p * (dp - jnp.sum(dp * p, axis=1, keepdims=True))).astype(BF16)
            dq = dot(ds, keys[...]) * scale
            dk = lax.dot_general(ds, q, TN, preferred_element_type=F32)
            merge = lambda part: jnp.where(lane < HEAD, part[:size], part[size:]).astype(BF16)
            attended[rows, at(0)] = merge(out)
            grad_triple[rows, at(0)] = merge(dq)
            grad_triple[rows, at(1)] = dk[:size].astype(BF16)
            grad_triple[rows, at(2)] = dv[:size].astype(BF16)
            grad_text[text_rows, at(0)] = dk[size : size + TEXT_ROWS].astype(BF16)
            grad_text[text_rows, at(1)] = dv[size : size + TEXT_ROWS].astype(BF16)
        return carry

    lax.fori_loop(0, inner // (2 * HEAD), heads, 0)

    late[0].wait()

    def text_block(q, carry):
        at = pl.ds(pl.multiple_of(q * 1024, 128), 1024)
        for col in range(0, width, 512):
            cols = slice(col, col + 512)
            stage[at, cols] = lax.dot_general(text[:, at], grad_text[:, cols], TN, preferred_element_type=F32).astype(BF16)
        pltpu.make_async_copy(stage.at[at], h_g_text.at[at], o_sems.at[4]).start()
        return carry

    lax.fori_loop(0, text_dim // 1024, text_block, 0)

    waited(w_out, sems.at[0])
    late[1].wait()
    bias = vec[V_OUT : V_OUT + 1, :width]
    for image in range(3):
        rows = pl.ds(STARTS[image], SIZES[image])
        block_output[rows, :] = (
            present[0, image].astype(F32) * (residual[rows, :] + (dot(attended[rows, :], w_out[...]) + bias))
        ).astype(BF16)
    done[0].start()
    late[2].wait()
    for col in range(0, width, 512):
        cols = slice(col, col + 512)
        g_out[:, cols] = lax.dot_general(attended[...], g_low[:, cols], TN, preferred_element_type=F32).astype(BF16)
        g_attend[:, cols] = lax.dot_general(normed[...], grad_triple[:, cols], TN, preferred_element_type=F32).astype(BF16)
    last = lax.dot_general(normed[...], grad_triple[:, width:], TN, preferred_element_type=F32).astype(BF16)
    half = width // parts // 2
    for f in range(parts):
        for i in range(2):
            g_more[f * half : (f + 1) * half, 512 * i : 512 * (i + 1)] = last[(2 * f + i) * half : (2 * f + i + 1) * half]
    for copy in done[1:]:
        copy.start()
    waited(w_attend, sems.at[1])
    for col in range(0, width, 512):
        cols = slice(col, col + 512)
        rows_grad[:, cols] = lax.dot_general(grad_triple[...], w_attend[cols, :], NT, preferred_element_type=F32)

    late[3].wait()
    more[...] = jnp.zeros_like(more)
    gain = vec[V_ATTN_GAIN : V_ATTN_GAIN + 1, :width]
    for image in range(3):
        def pair(i, rows):
            grad = rows_grad[rows, :]
            return grad, grad * hats[rows, :]
        plain, crossed = two_sums(image, width, pair)
        def put(i, rows, value):
            rows_grad[rows, :] = value + g_low[rows, :].astype(F32)
        norm_pull(image, gain, inverses[6 + image : 7 + image, :], lambda rows: rows_grad[rows, :], lambda rows: hats[rows, :], plain, crossed, put)
        def ends(i, rows):
            value = rows_grad[rows, :]
            r_low[rows, :] = value.astype(BF16)
            return value, g_low[rows, :].astype(F32)
        total, outer = two_sums(image, width, ends)
        for row, value in ((G_ATTN_GAIN, crossed), (G_ATTN_SHIFT, plain), (G_SECOND, total), (G_OUT, outer)):
            more[row : row + 1, :] = more[row : row + 1, :] + value[:1]
    for copy in done:
        copy.wait()
    waited(stage, o_sems.at[4])


def middle(triple, text_pair, keep, grad_attended, cotangent, normed, hats, residual, text, vec, inverses, present, full, parts, inner, text_dim):
    pix, width = cotangent.shape
    bf = lambda *shape: jax.ShapeDtypeStruct(shape, BF16)
    vm = lambda *shape: pltpu.VMEM(shape, BF16)
    hbm, vmem = pl.BlockSpec(memory_space=pl.ANY), pl.BlockSpec(memory_space=pltpu.VMEM)
    return pl.pallas_call(
        functools.partial(middle_kernel, parts, inner, text_dim),
        out_shape=[bf(pix, width), jax.ShapeDtypeStruct((16, width), F32), bf(pix, width), bf(inner, width), bf(width, width), bf(width // 2, width), bf(text_dim, width)],
        in_specs=[vmem] * 7 + [pl.BlockSpec(memory_space=pltpu.SMEM)] + [hbm] * 5,
        out_specs=[vmem] * 2 + [hbm] * 5,
        scratch_shapes=[
            vm(pix, inner), vm(pix, 3 * inner), vm(text.shape[0], 2 * inner), pltpu.VMEM((pix, width), F32),
            vm(width, 3 * inner), vm(inner, width), vm(text_dim, width), vm(pix, width),
            vm(2 * max(SIZES), 2 * HEAD), vm(2 * max(SIZES), 2 * HEAD), vm(KEYS, 2 * HEAD), vm(KEYS, 2 * HEAD),
            vm(pix, width), pltpu.VMEM((pix, width), F32), pltpu.VMEM((pix, width), F32), vm(*text.shape),
            vm(pix, width), vm(inner, width), vm(width, width), vm(width // 2, width),
            pltpu.SemaphoreType.DMA((2,)), pltpu.SemaphoreType.DMA((4,)), pltpu.SemaphoreType.DMA((5,)),
        ],
        compiler_params=pltpu.CompilerParams(vmem_limit_bytes=60 << 20),
        name="middle",
    )(triple, text_pair, keep, grad_attended, cotangent, vec, inverses, present, full, normed, hats, residual, text)


def last_kernel(images, depth, tall, count, *refs):
    big, (h_attend, h_more, h_notes, narrow, wide) = refs[:count], refs[count : count + 5]
    refs = refs[count + 5 :]
    big_out, (o_attend, emb_weight, emb_bias) = refs[:count], refs[count : count + 3]
    vectors, refs = refs[count + 3 : count + 13], refs[count + 13 :]
    bufs, (attend, more, notes, plain, bias, i_sems, o_sems) = refs[:count], refs[count:]
    sources = [h_notes] + list(big) + [h_attend, h_more]
    targets = [notes] + list(bufs) + [attend, more]
    ins = [pltpu.make_async_copy(src, dst, i_sems.at[i]) for i, (src, dst) in enumerate(zip(sources, targets))]
    for copy in ins:
        copy.start()
    high, across = more.shape[0], more.shape[1] // 2
    jobs = [[job] for job in zip(bufs, big_out)] + [[(attend, o_attend.at[:, pl.ds(0, 2 * across)])]]
    jobs += [[(more.at[:, pl.ds(i * across, across)], o_attend.at[pl.ds(i * high, high), pl.ds(2 * across, across)]) for i in range(2)]]
    out = []

    def pass_on(i):
        ins[i + 1].wait()
        for src, dst in jobs[i]:
            out.append(pltpu.make_async_copy(src, dst, o_sems.at[len(out)]))
            out[-1].start()

    ins[0].wait()
    plain[...] = notes[...].astype(F32)
    per_image = tall // images
    for j in range(per_image):
        total, sums = jnp.zeros((128, 128), F32), jnp.zeros((1, 128), F32)
        for image in range(images):
            mods = plain[:, image * per_image + j, :]
            total = total + lax.dot_general(plain[:, tall + image, :].astype(BF16), mods.astype(BF16), TN, preferred_element_type=F32)
            sums = sums + jnp.sum(mods, axis=0, keepdims=True)
        emb_weight[:, j * 128 : (j + 1) * 128] = total[:depth]
        bias[j : j + 1, :] = sums
        if j >= 2 and j - 2 < len(jobs):
            pass_on(j - 2)
    for i in range(max(0, per_image - 2), len(jobs)):
        pass_on(i)
    at = lax.axis_index("fsdp") * depth
    emb_bias[...] = pltpu.roll(jnp.broadcast_to(bias[pl.ds(at // 128, 1), :], (8, 128)), lax.rem(128 - lax.rem(at, 128), 128), 1)[:1, :depth]
    for i, dst in enumerate(vectors):
        row = i if i < 9 else G_SECOND
        dst[...] = narrow[row] if row < narrow.shape[0] else wide[row - narrow.shape[0]]
    for copy in out:
        copy.wait()


def last(big, attend, more, notes, narrow, wide, images, depth):
    tall = notes.shape[1] - 16
    columns = tall // images * 128
    hbm, vmem = pl.BlockSpec(memory_space=pl.ANY), pl.BlockSpec(memory_space=pltpu.VMEM)
    fl = lambda *shape: jax.ShapeDtypeStruct(shape, F32)
    vf = lambda *shape: pltpu.VMEM(shape, F32)
    sizes = [narrow.shape[2]] * narrow.shape[0] + [wide.shape[2]] * (wide.shape[0] + 1)
    dma = lambda count: pltpu.SemaphoreType.DMA((count,))
    return pl.pallas_call(
        functools.partial(last_kernel, images, depth, tall, len(big)),
        out_shape=[fl(*part.shape) for part in big] + [fl(attend.shape[0], attend.shape[1] + more.shape[1] // 2), fl(depth, columns), fl(1, depth)] + [fl(1, size) for size in sizes],
        in_specs=[hbm] * (len(big) + 3) + [vmem] * 2,
        out_specs=[hbm] * (len(big) + 1) + [vmem] * (2 + len(sizes)),
        scratch_shapes=[vf(*part.shape) for part in big] + [
            vf(*attend.shape), vf(*more.shape), pltpu.VMEM(notes.shape, BF16), vf(*notes.shape), vf(max(8, tall // images), 128),
            dma(len(big) + 3), dma(len(big) + 3),
        ],
        compiler_params=pltpu.CompilerParams(vmem_limit_bytes=60 << 20),
        name="last",
    )(*big, attend, more, notes, narrow, wide)


def body(
    pixels,
    embedding,
    text_states,
    text_mask,
    occupancy,
    cotangent,
    in_gain,
    in_shift,
    conv_first,
    first_bias,
    emb_weight,
    emb_bias,
    mid_gain,
    mid_shift,
    conv_second,
    second_bias,
    skip_weight,
    skip_bias,
    attn_gain,
    attn_shift,
    attend_weight,
    text_weight,
    out_weight,
    out_bias,
):
    place = lax.axis_index("fsdp")
    group = lax.axis_index("dp")
    parts = lax.axis_size("fsdp")
    replicas = lax.axis_size("dp")
    depth = emb_weight.shape[0]
    images_here = embedding.shape[0]
    emb_act = jax.nn.silu(embedding.astype(F32)).astype(BF16)
    emb_cut = emb_act.reshape(images_here, parts, depth).transpose(1, 0, 2)
    emb_cut = jnp.pad(emb_cut, ((0, 0), (0, 0), (0, 128 - depth)))

    lane = lax.broadcasted_iota(jnp.int32, (1, 128), 1)

    def placed(vectors):
        size = vectors[0].shape[0]
        wide = jnp.concatenate([jnp.stack(vectors)] * (128 // size), 1)
        return jnp.where(lane // size == lax.rem(place, 128 // size), wide, jnp.zeros_like(wide))

    lines = [placed((in_gain, in_shift)), placed((emb_bias,)), placed((first_bias, mid_gain, mid_shift, second_bias, skip_bias, attn_gain, attn_shift, out_bias))]
    room = 16 - images_here - sum(line.shape[0] for line in lines)
    flat = jnp.concatenate(lines + [jnp.zeros((room, 128), BF16)] if room else lines, 0)[None]
    note = jnp.concatenate([emb_cut, jnp.broadcast_to(flat, (parts,) + flat.shape[1:])], 1)
    channels = skip_weight.shape[1]
    inner = out_weight.shape[0] * parts
    text_len = text_states.shape[1]
    (full, modulation, vec, _, act1, act2, mid_hats, residual, hats, normed, triple, text_pair, grad_attended, inverses, text_rows) = forward_all(
        (conv_first, conv_second, skip_weight, out_weight, attend_weight, text_weight), note, jnp.pad(emb_weight, ((0, 128 - depth), (0, 0))), pixels, text_states, cotangent, occupancy, images_here, inner, replicas, parts)
    keep = (text_mask > 0).astype(jnp.int32)
    keep = jnp.stack([
        jnp.pad(jnp.pad(keep[i], (size, 0), constant_values=1), (0, KEYS - size - text_len), constant_values=2)
        for i, size in enumerate(SIZES)
    ])
    r_low, more, block_output, g_out, g_attend, g_more, g_text = middle(
        triple, text_pair, keep, grad_attended, cotangent, normed, hats, residual, text_rows, vec, inverses, occupancy, full, parts, inner, text_states.shape[2]
    )
    (grad_out_weight, attend, attend_more, grad_text_weight, grad_skip_weight, grad_conv_second, grad_conv_first,
     notes, _, _, _, grad_pixels, narrow, wide) = reduce_all(
        [g_out, g_attend, g_more, g_text], full, r_low, pixels, vec, modulation, inverses, act1, act2, mid_hats, note, more,
        inner, text_states.shape[2], images_here, replicas, parts, 512 // parts,
    )
    (grad_text_weight, grad_out_weight, grad_conv_second, grad_skip_weight, grad_conv_first, grad_pixels, grad_attend_weight,
     grad_emb_weight, grad_emb_bias, *vectors) = last(
        [grad_text_weight, grad_out_weight, grad_conv_second, grad_skip_weight, grad_conv_first, grad_pixels],
        attend, attend_more, notes, narrow, wide, images_here, depth,
    )
    grad_emb_bias = grad_emb_bias.reshape(-1)
    small = lambda row: vectors[row].reshape(-1)
    return (
        block_output,
        grad_pixels,
        small(G_IN_GAIN),
        small(G_IN_SHIFT),
        grad_conv_first,
        small(G_FIRST),
        grad_emb_weight,
        grad_emb_bias,
        small(G_MID_GAIN),
        small(G_MID_SHIFT),
        grad_conv_second,
        small(G_SECOND),
        grad_skip_weight,
        vectors[-1].reshape(-1),
        small(G_ATTN_GAIN),
        small(G_ATTN_SHIFT),
        grad_attend_weight,
        grad_text_weight,
        grad_out_weight,
        small(G_OUT),
    )


def solution(mesh):
    rows = P(("dp", "fsdp"), None)
    vector = P("fsdp")
    matrix = P("fsdp", None)
    weights = (vector, vector, matrix, vector, matrix, vector, vector, vector, matrix, vector, matrix, vector, vector, vector, matrix, matrix, matrix, vector)
    return jax.shard_map(
        body,
        mesh=mesh,
        in_specs=(rows, rows, P(("dp", "fsdp"), None, None), rows, rows, rows) + weights,
        out_specs=(rows, rows) + weights,
        check_vma=False,
    )
```

```python
import functools

import jax
import jax.numpy as jnp
from jax import lax
from jax.experimental import pallas as pl
from jax.experimental.pallas import tpu as pltpu
from jax.sharding import PartitionSpec as P

BF16 = jnp.bfloat16
F32 = jnp.float32
HEADS = 8
HEAD = 64
GROUPS = 32
UNIT = 4
SHAPES = ((4 * UNIT, 4 * UNIT), (3 * UNIT, 5 * UNIT), (5 * UNIT, 3 * UNIT))
SIZES = tuple(height * breadth for height, breadth in SHAPES)
STARTS = (0, SIZES[0], SIZES[0] + SIZES[1])
PIX = sum(SIZES)
EDGE = 32
BASES = tuple(EDGE + start + i * EDGE for i, start in enumerate(STARTS))
PADDED = PIX + 4 * EDGE
BLOCK = 1152
KEYS = 384
TEXT_ROWS = 80
SUB = 16
NT = (((1,), (1,)), ((), ()))
TN = (((0,), (0,)), ((), ()))
V_IN_GAIN, V_IN_SHIFT, V_EMB, V_FIRST, V_MID_GAIN, V_MID_SHIFT, V_SECOND, V_SKIP, V_ATTN_GAIN, V_ATTN_SHIFT, V_OUT = range(11)


def dot(left, right, dims=((1,), (0,))):
    return lax.dot_general(left, right, (dims, ((), ())), preferred_element_type=F32)


def group_mean(sums, count):
    channels = sums.shape[1]
    width = channels // GROUPS
    lane = lax.broadcasted_iota(jnp.int32, sums.shape, 1)
    step = 1
    while step < width:
        odd = lax.rem(lane // step, 2) == 1
        sums = sums + jnp.where(odd, pltpu.roll(sums, step, 1), pltpu.roll(sums, channels - step, 1))
        step *= 2
    return sums / (count * width)


def rows_of(image, i):
    return pl.ds(pl.multiple_of(STARTS[image] + i * SUB, SUB), SUB)


def over_rows(image, work, start):
    return lax.fori_loop(0, SIZES[image] // SUB, lambda i, carry: work(i, rows_of(image, i), carry), start)


def column_sum(image, channels, value):
    def add(i, rows, carry):
        v = value(rows)
        return carry + (v[:8] + v[8:])
    total = over_rows(image, add, jnp.zeros((8, channels), F32))
    return jnp.broadcast_to(jnp.sum(total, axis=0, keepdims=True), (8, channels))


def norm_figures(image, channels, value):
    count = SIZES[image]
    center = group_mean(column_sum(image, channels, value), count)[:1]
    spread = group_mean(column_sum(image, channels, lambda rows: jnp.square(value(rows) - center)), count)[:1]
    return center, lax.rsqrt(spread + 1e-05)


def store_padded(pad, image, i, act):
    breadth = SHAPES[image][1]
    at = pl.ds(pl.multiple_of(BASES[image] + i * SUB, SUB), SUB)
    column = lax.rem(i * SUB + lax.broadcasted_iota(jnp.int32, (SUB, 1), 0), breadth)
    pad[0, at, :] = jnp.where(column == breadth - 1, 0.0, act).astype(BF16)
    pad[1, at, :] = act.astype(BF16)
    pad[2, at, :] = jnp.where(column == 0, 0.0, act).astype(BF16)


def zero_edges(pad):
    zeros = jnp.zeros((EDGE, pad.shape[2]), BF16)
    for side in range(3):
        for at in [base - EDGE for base in BASES] + [PADDED - EDGE]:
            pad[side, at : at + EDGE, :] = zeros


def shifted(pad, tap, image, cols, flip=False):
    down, across = divmod(8 - tap if flip else tap, 3)
    start = BASES[image] + (down - 1) * SHAPES[image][1] + across - 1
    return pad[across, start : start + SIZES[image], cols]


def gather_blocks(pad, blocks, out):
    per_tap = pad.shape[2] // 128
    for i, block in enumerate(blocks):
        tap, col = divmod(block, per_tap)
        for image in range(3):
            out[STARTS[image] : STARTS[image] + SIZES[image], i * 128 : (i + 1) * 128] = shifted(
                pad, tap, image, slice(col * 128, (col + 1) * 128)
            )


def shard_of(full, f, *where):
    return full.at[(f // 2, f % 2 if isinstance(f, int) else lax.rem(f, 2)) + where]


class Rows:
    def __init__(self, parts, pix_channels, channels, text_dim, inner):
        self.parts = parts
        sizes = (9 * pix_channels // parts, 9 * channels // parts, pix_channels // parts, inner // parts, channels // parts, channels // parts // 2, text_dim // parts)
        starts = [0]
        for size in sizes:
            starts.append(starts[-1] + size)
        self.first, self.second, self.skip, self.out, self.attend, self.attend_more, self.text = zip(starts, sizes)
        self.total = starts[-1]

    def arrivals(self, which):
        size = which[1]
        blocks = []
        for block in range(size * self.parts // 128):
            pieces, at = [], block * 128
            while at < (block + 1) * 128:
                shard, inside = divmod(at, size)
                count = min(size - inside, (block + 1) * 128 - at)
                pieces.append((shard, inside, count))
                at += count
            blocks.append((max(inside + count for _, inside, count in pieces), block, pieces))
        blocks.sort()
        each = BLOCK // 128
        steps = [blocks[i : i + each] for i in range(0, len(blocks), each)]
        return [([(block, pieces) for _, block, pieces in step], step[-1][0]) for step in steps]

    def load_step(self, full, which, step, buf, sem):
        at = 0
        for _, pieces in step:
            for shard, inside, count in pieces:
                pltpu.make_async_copy(shard_of(full, shard, pl.ds(which[0] + inside, count)), buf.at[pl.ds(at, count)], sem).start()
                at += count

    def pack(self, weights, own, sems):
        first, second, skip, out, attend, text = weights
        half = self.attend_more[1]
        wide = own.shape[1]
        jobs = [(ref, which) for ref, which in ((first, self.first), (second, self.second), (skip, self.skip), (out, self.out), (text, self.text))]
        jobs.append((attend.at[:, pl.ds(0, wide)], self.attend))
        for i, (ref, (start, size)) in enumerate(jobs):
            pltpu.make_async_copy(ref, own.at[pl.ds(start, size)], sems.at[i]).start()
        for i in range(2):
            pltpu.make_async_copy(
                attend.at[pl.ds(i * half, half), pl.ds(wide, wide // 2)],
                own.at[pl.ds(self.attend_more[0], half), pl.ds(i * wide // 2, wide // 2)],
                sems.at[6 + i],
            ).start()

    def packed(self, own, sems):
        wide = own.shape[1]
        for i, (start, size) in enumerate((self.first, self.second, self.skip, self.out, self.text, self.attend)):
            waited(own.at[pl.ds(start, size)], sems.at[i])
        for i in range(2):
            waited(own.at[pl.ds(self.attend_more[0], self.attend_more[1]), pl.ds(i * wide // 2, wide // 2)], sems.at[6 + i])

    def load(self, full, which, q, rows, buf, sem):
        start, size = which
        each = rows // size
        for i in range(each):
            pltpu.make_async_copy(shard_of(full, q * each + i, pl.ds(start, size)), buf.at[pl.ds(i * size, size)], sem).start()

    def load_attend(self, full, buf, sem):
        start, size = self.attend
        more, half = self.attend_more
        def one(f, carry):
            at = pl.multiple_of(f * size, SUB)
            pltpu.make_async_copy(shard_of(full, f, pl.ds(start, size)), buf.at[pl.ds(at, size), pl.ds(0, 1024)], sem).start()
            for i in range(2):
                pltpu.make_async_copy(
                    shard_of(full, f, pl.ds(more, half), pl.ds(512 * i, 512)),
                    buf.at[pl.ds(pl.multiple_of(at + i * half, SUB), half), pl.ds(1024, 512)],
                    sem,
                ).start()
            return carry
        lax.fori_loop(0, self.parts, one, 0)


def outgoing(cotangent, present, image):
    rows = pl.ds(STARTS[image], SIZES[image])
    return (cotangent[rows, :].astype(F32) * present[0, image].astype(F32)).astype(BF16)


def choose(value, options):
    if len(options) == 1:
        first, end, work = options[0]
        pl.when(jnp.logical_and(value >= first, value < end))(work)
        return
    middle = len(options) // 2
    border = options[middle][0]
    pl.when(value < border)(lambda: choose(value, options[:middle]))
    pl.when(value >= border)(lambda: choose(value, options[middle:]))


def waited(ref, sem):
    pltpu.make_async_copy(ref, ref, sem).wait()


class Forward:
    def __init__(self, rows, full, pixels, text_in, cotangent, present, vec, mod, outs, scratch):
        self.rows, self.full, self.pixels, self.text_in, self.cotangent, self.present, self.vec, self.mod = rows, full, pixels, text_in, cotangent, present, vec, mod
        (self.o_a1, self.o_a2, self.o_mid_hat, self.o_residual, self.o_hat, self.o_normed, self.triple, self.text_pair, self.grad_attended, self.inverses, self.o_text) = outs
        (self.a1, self.a2, self.patch, self.weight, self.acc0, self.acc1, self.normed, self.w_attend, self.w_skip, self.w_out, self.text, self.w_sem, self.s_sem, self.o_sem) = scratch

    def out_copy(self, i, src, dst):
        return pltpu.make_async_copy(src, dst, self.o_sem.at[i])

    def row(self, r, channels=1024):
        return self.vec[r : r + 1, :channels]

    def zero(self):
        zero_edges(self.a1)
        zero_edges(self.a2)
        count = self.text_in.shape[1]
        for image in range(3):
            at = image * TEXT_ROWS
            self.text[at + TEXT_ROWS - SUB : at + TEXT_ROWS, :] = jnp.zeros((SUB, self.text.shape[1]), BF16)
            self.text[at : at + count, :] = self.text_in[image]
        self.out_copy(6, self.text, self.o_text).start()

    def first_norm(self, image):
        pixels, channels = self.pixels, self.pixels.shape[1]
        value = lambda rows: pixels[rows, :].astype(F32)
        center, inverse = norm_figures(image, channels, value)
        gain, shift = self.row(V_IN_GAIN, channels) * inverse, self.row(V_IN_SHIFT, channels)
        self.inverses[image : image + 1, :channels] = inverse
        self.inverses[16 + image : 17 + image, :channels] = center
        def act(i, rows, carry):
            store_padded(self.a1, image, i, jax.nn.silu((value(rows) - center) * gain + shift))
            return carry
        over_rows(image, act, 0)
        if image == 2:
            self.out_copy(0, self.a1, self.o_a1).start()

    def load_text(self, q):
        self.rows.load(self.full, self.rows.text, q, 1024, self.weight.at[lax.rem(q, 2)], self.w_sem.at[lax.rem(q, 2)])

    def conv_step(self, q, pad, acc, which, steps, early):
        def load(known):
            self.rows.load_step(self.full, which, steps[known][0], self.weight.at[known % 2], self.w_sem.at[known % 2])
        for known in range(len(steps)):
            ahead = known + 1 < len(steps) and early[known + 1]
            @pl.when(q == known)
            def _():
                if not early[known]:
                    load(known)
                if ahead:
                    load(known + 1)
                gather_blocks(pad, [block for block, _ in steps[known][0]], self.patch)
        par = lax.rem(q, 2)
        waited(self.weight.at[par], self.w_sem.at[par])
        @pl.when(q == 0)
        def _():
            acc[...] = jnp.zeros_like(acc)
        for col in (0, 512):
            cols = slice(col, col + 512)
            acc[:, cols] = acc[:, cols] + dot(self.patch[...], self.weight[par, :, cols])

    def mid_norm(self, image):
        acc, channels = self.acc0, self.acc0.shape[1]
        bias = self.row(V_FIRST)
        def shift_up(i, rows, carry):
            acc[rows, :] = acc[rows, :] + bias
            return carry
        over_rows(image, shift_up, 0)
        center, inverse = norm_figures(image, channels, lambda rows: acc[rows, :])
        self.inverses[3 + image : 4 + image, :] = inverse
        scale, shift = 1.0 + self.mod[image : image + 1, :channels], self.mod[image : image + 1, channels:]
        gain, lift = self.row(V_MID_GAIN) * scale, self.row(V_MID_SHIFT) * scale + shift
        def act(i, rows, carry):
            hat = (acc[rows, :] - center) * inverse
            acc[rows, :] = hat
            store_padded(self.a2, image, i, jax.nn.silu(hat * gain + lift))
            return carry
        over_rows(image, act, 0)
        if image == 2:
            self.out_copy(1, self.a2, self.o_a2).start()
            self.out_copy(2, self.acc0, self.o_mid_hat).start()

    def load_small(self):
        rows = self.rows
        def one(f, carry):
            for i, ((start, size), buf) in enumerate(((rows.skip, self.w_skip), (rows.out, self.w_out))):
                pltpu.make_async_copy(shard_of(self.full, f, pl.ds(start, size)), buf.at[pl.ds(pl.multiple_of(f * size, SUB), size)], self.s_sem.at[i]).start()
            return carry
        lax.fori_loop(0, rows.parts, one, 0)
        rows.load_attend(self.full, self.w_attend, self.s_sem.at[2])

    def skip_product(self):
        for i, buf in enumerate((self.w_skip, self.w_out, self.w_attend)):
            waited(buf, self.s_sem.at[i])
        self.acc1[...] = self.acc1[...] + dot(self.pixels[...], self.w_skip[...])

    def attended_grad(self):
        for image in range(3):
            rows = pl.ds(STARTS[image], SIZES[image])
            grad = outgoing(self.cotangent, self.present, image)
            self.grad_attended[rows, :] = lax.dot_general(grad, self.w_out[...], NT, preferred_element_type=F32).astype(BF16)

    def last_norm(self, image):
        acc, hats, channels = self.acc1, self.acc0, self.acc1.shape[1]
        if image == 0:
            self.out_copy(2, self.acc0, self.o_mid_hat).wait()
        bias = self.row(V_SECOND) + self.row(V_SKIP)
        def shift_up(i, rows, carry):
            acc[rows, :] = acc[rows, :] + bias
            return carry
        over_rows(image, shift_up, 0)
        center, inverse = norm_figures(image, channels, lambda rows: acc[rows, :])
        self.inverses[6 + image : 7 + image, :] = inverse
        gain, shift = self.row(V_ATTN_GAIN), self.row(V_ATTN_SHIFT)
        def act(i, rows, carry):
            hat = (acc[rows, :] - center) * inverse
            hats[rows, :] = hat
            self.normed[rows, :] = (hat * gain + shift).astype(BF16)
            return carry
        over_rows(image, act, 0)
        if image == 2:
            self.out_copy(3, self.acc1, self.o_residual).start()
            self.out_copy(4, self.acc0, self.o_hat).start()
            self.out_copy(5, self.normed, self.o_normed).start()

    def project(self, i):
        cols = slice(512 * i, 512 * (i + 1))
        self.triple[:, cols] = dot(self.normed[...], self.w_attend[:, cols]).astype(BF16)

    def text_step(self, q, total):
        if q + 1 < 4:
            self.load_text(q + 1)
        par = q % 2
        waited(self.weight.at[par, pl.ds(0, 1024)], self.w_sem.at[par])
        part = dot(self.text[:, 1024 * q : 1024 * (q + 1)], self.weight[par, :1024, :])
        if q:
            part = total[...] + part
        if q < 3:
            total[...] = part
        else:
            self.text_pair[...] = part.astype(BF16)

    def finish(self):
        self.out_copy(0, self.a1, self.o_a1).wait()
        self.out_copy(1, self.a2, self.o_a2).wait()
        self.out_copy(3, self.acc1, self.o_residual).wait()
        self.out_copy(4, self.acc0, self.o_hat).wait()
        self.out_copy(5, self.normed, self.o_normed).wait()
        self.out_copy(6, self.text, self.o_text).wait()


MESH = pl.DeviceIdType.MESH
DEPTH = 4


BUDGET = 7.5


class Where:
    def __init__(self, replicas, parts):
        self.replicas, self.parts = replicas, parts
        self.span = parts // (2 * DEPTH)
        self.group = lax.axis_index("dp")
        self.place = lax.axis_index("fsdp")
        self.core = lax.rem(self.place, 2)
        self.y = lax.rem(self.place // 2, self.span)
        self.z = self.place // (2 * self.span)
        self.side = lax.rem(self.group, 2)

    def index(self, z, y, core):
        return (z * self.span + y) * 2 + core

    def device(self, z=None, y=None, core=None, flip=False):
        z = self.z if z is None else jnp.clip(z, 0, DEPTH - 1)
        y = self.y if y is None else y
        core = self.core if core is None else core
        group = self.group + 1 - 2 * self.side if flip else self.group
        return (group, self.index(z, y, core))

    def barrier(self):
        sem = pltpu.get_barrier_semaphore()
        greet = lambda device: pl.semaphore_signal(sem, inc=1, device_id=device, device_id_type=MESH)
        greet(self.device(flip=True))
        def one(i, carry):
            greet((self.group, lax.rem(self.place + i, self.parts)))
            return carry
        lax.fori_loop(1, self.parts, one, 0)
        pl.semaphore_wait(sem, self.parts)


def forward_kernel(replicas, parts, rows, lead, lag, inner, images, *refs):
    weights, refs = refs[:6], refs[6:]
    note, emb, pixels, text, cotangent, present = refs[:6]
    full, mod, vec, notes = refs[6:10]
    outs = refs[10:21]
    own, part, sums, text_total = refs[21:25]
    scratch = refs[25:39]
    (n_send, n_recv, m_send, m_recv, z_send, z_recv, y_send, y_recv, s_send, s_recv, x_send, x_recv, c_send, c_recv, own_sem) = refs[39:]
    me = Where(replicas, parts)
    span = me.span
    total, width = own.shape
    chunks = total // rows
    joint, apart = 5 * width // 8, 3 * width // 8
    side = me.side
    thin = width // 4
    z_cols = pl.ds(pl.multiple_of(side * thin, thin), width - thin)
    a_cols = pl.ds(pl.multiple_of(side * apart, 128), joint)
    thin_cols = pl.ds(pl.multiple_of((1 - side) * (width - thin), thin), thin)
    thin_out = pl.ds(pl.multiple_of(side * (width - thin), thin), thin)
    b_cols = pl.ds(pl.multiple_of((1 - side) * joint, 128), apart)
    b_out = pl.ds(pl.multiple_of(side * joint, 128), apart)

    table = Rows(parts, pixels.shape[1], width, text.shape[2], inner)
    table.pack(weights, own, own_sem)
    me.barrier()
    table.packed(own, own_sem)
    local = pltpu.make_async_copy(own, full.at[me.place // 2, me.core], own_sem.at[0])
    local.start()

    def at(k):
        return pl.ds(pl.multiple_of(k * rows, 16), rows)

    def copy(src, dst, send, recv, device):
        return pltpu.make_async_remote_copy(src_ref=src, dst_ref=dst, send_sem=send, recv_sem=recv, device_id=device, device_id_type=MESH)

    def piece(k, z, y, cols, core=None):
        return full.at[z * span + y, me.core if core is None else core, at(k), cols]

    def z_copy(k, z, step, mine):
        src = own.at[at(k), z_cols] if mine else piece(k, z, me.y, z_cols)
        return copy(src, piece(k, z, me.y, z_cols), z_send.at[k, z, (step + 1) // 2], z_recv.at[k, z], me.device(z=me.z + step))

    def y_copy(k, z, turn, mine):
        src = own.at[at(k), a_cols] if mine else piece(k, z, me.y, a_cols)
        return copy(src, piece(k, z, me.y, a_cols), y_send.at[k, z, turn - 1], y_recv.at[k, z, turn - 1], me.device(y=lax.rem(me.y + turn, span)))

    def thin_copy(k, z):
        return copy(piece(k, z, me.y, thin_out), piece(k, z, me.y, thin_out), s_send.at[k, z], s_recv.at[k, z], me.device(flip=True))

    def x_copy(k, z, turn):
        y = lax.rem(me.y + turn, span)
        return copy(piece(k, z, y, b_out), piece(k, z, y, b_out), x_send.at[k, z, turn - 1], x_recv.at[k, z, turn - 1], me.device(flip=True))

    def core_copy(k, core):
        lane = full.at[:, core, at(k)]
        return copy(lane, lane, c_send.at[k], c_recv.at[k], me.device(core=1 - me.core))

    below = lambda s: (me.z - s >= 0, me.z - s)
    above = lambda s: (me.z + s < DEPTH, me.z + s)

    def start_own(k):
        @pl.when(me.z < DEPTH - 1)
        def _():
            z_copy(k, me.z, 1, True).start()
        @pl.when(me.z > 0)
        def _():
            z_copy(k, me.z, -1, True).start()
        for turn in range(1, span):
            y_copy(k, me.z, turn, True).start()

    def along_z(k, s):
        for (ok, z), step in ((below(s), 1), (above(s), -1)):
            @pl.when(ok)
            def _():
                z_copy(k, z, step, False).wait_recv()
                if s < DEPTH - 1:
                    more = me.z < DEPTH - 1 if step > 0 else me.z > 0
                    @pl.when(more)
                    def _():
                        z_copy(k, z, step, False).start()
                for turn in range(1, span):
                    y_copy(k, z, turn, False).start()
                thin_copy(k, z).start()

    def across(k, s):
        for ok, z in ((below(s), above(s)) if s else (below(0),)):
            @pl.when(ok)
            def _():
                for turn in range(1, span):
                    y_copy(k, z, turn, False).wait_recv()
                    x_copy(k, z, span - turn).start()

    def beside(k, s):
        for ok, z in ((below(s), above(s)) if s else (below(0),)):
            @pl.when(ok)
            def _():
                for turn in range(1, span):
                    x_copy(k, z, turn).wait_recv()

    def beside_thin(k, s):
        for ok, z in (below(s), above(s)):
            @pl.when(ok)
            def _():
                thin_copy(k, z).wait_recv()

    def lane_in(k):
        core_copy(k, 1 - me.core).wait_recv()

    def to_all(make):
        def one(i, carry):
            make(lax.rem(me.place + i, parts)).start()
            return carry
        lax.fori_loop(1, parts, one, 0)

    def wait_all(ref, send, recv):
        others = ref.at[pl.ds(0, parts - 1)]
        every = copy(others, others, send, recv, me.device(core=1 - me.core))
        every.wait_send()
        every.wait_recv()

    def modulate():
        wait_all(sums, m_send, m_recv)
        total = jnp.sum(sums[...], axis=0)
        blocks = emb.shape[1] // 128
        for j in range(blocks):
            for image in range(images):
                row = image * blocks + j
                mod[image : image + 1, j * 128 : (j + 1) * 128] = total[row : row + 1, :] + vec[V_EMB : V_EMB + 1, j * 128 : (j + 1) * 128]

    def unpack():
        wait_all(notes, n_send, n_recv)
        vec[...] = jnp.zeros_like(vec)
        for row in range(V_OUT + 1):
            size = {V_IN_GAIN: pixels.shape[1], V_IN_SHIFT: pixels.shape[1], V_EMB: emb.shape[1]}.get(row, width)
            each = 128 * parts // size
            for block in range(size // 128):
                value = notes[block * each, images + row : images + row + 1, :].astype(jnp.float32)
                for i in range(1, each):
                    value = value + notes[block * each + i, images + row : images + row + 1, :].astype(jnp.float32)
                vec[row : row + 1, block * 128 : (block + 1) * 128] = value
        rows_in = notes.shape[1]
        blocks = emb.shape[1] // 128
        for j in range(blocks):
            product = jnp.dot(notes[...].reshape(parts * rows_in, 128), emb[:, j * 128 : (j + 1) * 128], preferred_element_type=jnp.float32)
            product = product.reshape(parts, rows_in, 128)
            for image in range(images):
                part[:, image * blocks + j, :] = product[:, image, :]
        to_all(lambda far: copy(part.at[far], sums.at[me.place], m_send, m_recv, (me.group, far)))
        sums[me.place] = part[me.place]

    to_all(lambda far: copy(note.at[far], notes.at[me.place], n_send, n_recv, (me.group, far)))
    notes[me.place] = note[me.place]

    forward = Forward(table, full, pixels, text, cotangent, present, vec, mod, outs, scratch)
    ready = (DEPTH + 1) * lag
    have = lambda row: (row - 1) // rows + ready
    plan = []
    spent = {}

    def add(earliest, cost, work):
        slot = max([earliest] + [when for when, _ in plan[-1:]])
        while spent.get(slot, 0) and spent[slot] + cost > BUDGET:
            slot += 1
        spent[slot] = spent.get(slot, 0) + cost
        plan.append((slot, work))
        return slot

    add(0, 1, forward.zero)
    add(3, 5, unpack)
    for image in range(3):
        add(4, 2, functools.partial(forward.first_norm, image))
    convs = []

    def add_conv(which, pad, acc):
        steps = table.arrivals(which)
        slots, early = [], []
        for i, (_, end) in enumerate(steps):
            slot = add(have(which[0] + end), 3.4, None)
            early.append(i > 0 and have(which[0] + end) <= slots[-1])
            slots.append(slot)
        convs.append((which, pad, acc, steps, early, slots))

    add_conv(table.first, forward.a1, forward.acc0)
    add(0, 1, modulate)
    for image in range(3):
        add(0, 2.4, functools.partial(forward.mid_norm, image))
    add_conv(table.second, forward.a2, forward.acc1)
    add(have(sum(table.attend_more)), 0.5, forward.load_small)
    add(0, 2.2, forward.skip_product)
    for image in range(3):
        add(0, 2, functools.partial(forward.last_norm, image))
    add(0, 1.5, forward.attended_grad)
    for i in range(3):
        add(0, 1.4, functools.partial(forward.project, i))
    slots = max(chunks + ready, plan[-1][0] + 1)

    def steps(t):
        def conv(which, pad, acc, table_steps, early, when):
            low, high = jnp.int32(0), jnp.int32(0)
            for slot in when:
                low = low + jnp.where(t > slot, 1, 0)
                high = high + jnp.where(t >= slot, 1, 0)
            def one(q, carry):
                forward.conv_step(q, pad, acc, which, table_steps, early)
                return carry
            lax.fori_loop(low, high, one, 0)
        pending = list(convs)
        pl.when(t == DEPTH * lag - 1)(local.wait)
        for i, (slot, work) in enumerate(plan):
            if work is not None:
                pl.when(t == slot)(work)
            elif i == 0 or plan[i - 1][1] is not None:
                conv(*pending.pop(0))

    for k in range(min(lead, chunks)):
        start_own(k)

    last = 2 * (DEPTH - 1) + 3

    def slot(t, carry):
        def stage(delay, work):
            k = t - delay
            @pl.when(jnp.logical_and(k >= 0, k < chunks))
            def _():
                work(k)
        @pl.when(t + lead < chunks)
        def _():
            start_own(t + lead)
        for s in range(1, DEPTH):
            stage((s - 1) * lag, functools.partial(along_z, s=s))
        for s in range(DEPTH):
            stage(s * lag, functools.partial(across, s=s))
        for s in range(1, DEPTH):
            stage(s * lag, functools.partial(beside_thin, s=s))
        for s in range(DEPTH):
            stage((s + 1) * lag, functools.partial(beside, s=s))
        stage(DEPTH * lag, lambda k: core_copy(k, me.core).start())
        stage(ready, lane_in)
        steps(t)
        return carry

    lax.fori_loop(0, slots, slot, 0)
    forward.load_text(jnp.int32(0))
    for q in range(4):
        forward.text_step(q, text_total)

    def finish(k, carry):
        for step, edge in ((1, me.z < DEPTH - 1), (-1, me.z > 0)):
            for s in range(DEPTH - 1):
                ok, z = below(s) if step > 0 else above(s)
                @pl.when(jnp.logical_and(ok, edge))
                def _():
                    z_copy(k, z, step, False).wait_send()
        for z in range(DEPTH):
            for turn in range(1, span):
                y_copy(k, z, turn, False).wait_send()
                x_copy(k, z, turn).wait_send()
            @pl.when(z != me.z)
            def _():
                thin_copy(k, z).wait_send()
        core_copy(k, me.core).wait_send()
        return carry

    lax.fori_loop(0, chunks, finish, 0)
    forward.finish()


def forward_all(weights, note, emb, pixels, text, cotangent, present, images, inner, replicas, parts, rows=80, lead=3, lag=1):
    width = weights[0].shape[1]
    total = Rows(parts, pixels.shape[1], width, text.shape[2], inner).total
    chunks = total // rows
    span = parts // (2 * DEPTH)
    pix, pix_width = pixels.shape
    dma = lambda *shape: pltpu.SemaphoreType.DMA(shape)
    bf = lambda *shape: jax.ShapeDtypeStruct(shape, BF16)
    fl = lambda *shape: jax.ShapeDtypeStruct(shape, F32)
    hbm, vmem = pl.BlockSpec(memory_space=pl.ANY), pl.BlockSpec(memory_space=pltpu.VMEM)
    return pl.pallas_call(
        functools.partial(forward_kernel, replicas, parts, rows, lead, lag, inner, images),
        out_shape=[
            bf(parts // 2, 2, total, width), fl(8, emb.shape[1]), fl(16, emb.shape[1]), bf(*note.shape),
            bf(3, PADDED, pix_width), bf(3, PADDED, width), fl(pix, width), fl(pix, width), fl(pix, width), bf(pix, width),
            bf(pix, 3 * inner), bf(3 * TEXT_ROWS, 2 * inner), bf(pix, inner), fl(24, width), bf(3 * TEXT_ROWS, text.shape[2]),
        ],
        in_specs=[hbm] * 6 + [vmem] * 5 + [pl.BlockSpec(memory_space=pltpu.SMEM)],
        out_specs=[hbm, vmem, vmem, vmem] + [hbm] * 6 + [vmem] * 4 + [hbm],
        scratch_shapes=[
            pltpu.VMEM((total, width), BF16),
            pltpu.VMEM((parts, images * emb.shape[1] // 128, 128), F32),
            pltpu.VMEM((parts, images * emb.shape[1] // 128, 128), F32),
            pltpu.VMEM((3 * TEXT_ROWS, width), F32),
            pltpu.VMEM((3, PADDED, pix_width), BF16), pltpu.VMEM((3, PADDED, width), BF16),
            pltpu.VMEM((pix, BLOCK), BF16), pltpu.VMEM((2, BLOCK, width), BF16),
            pltpu.VMEM((pix, width), F32), pltpu.VMEM((pix, width), F32), pltpu.VMEM((pix, width), BF16),
            pltpu.VMEM((width, 3 * inner), BF16), pltpu.VMEM((pix_width, width), BF16), pltpu.VMEM((inner, width), BF16), pltpu.VMEM((3 * TEXT_ROWS, text.shape[2]), BF16),
            dma(2), dma(3), dma(7),
            dma(), dma(), dma(), dma(),
            dma(chunks, DEPTH, 2), dma(chunks, DEPTH),
            dma(chunks, DEPTH, span - 1), dma(chunks, DEPTH, span - 1),
            dma(chunks, DEPTH), dma(chunks, DEPTH),
            dma(chunks, DEPTH, span - 1), dma(chunks, DEPTH, span - 1),
            dma(chunks), dma(chunks), dma(8),
        ],
        compiler_params=pltpu.CompilerParams(collective_id=0, has_side_effects=True, vmem_limit_bytes=60 << 20),
        name="forward_all",
    )(*weights, note, emb, pixels, text, cotangent, present)


FILL = 3


class Seat(Where):
    def bit(self, b):
        step = 1 << b
        group = self.group + step - 2 * step * lax.rem(self.group // step, 2)
        return (group, self.place)

    def meet(self):
        sem = pltpu.get_barrier_semaphore()
        count = self.replicas * self.parts
        def one(i, carry):
            far = lax.rem(self.group * self.parts + self.place + i, count)
            pl.semaphore_signal(sem, inc=1, device_id=(far // self.parts, lax.rem(far, self.parts)), device_id_type=MESH)
            return carry
        lax.fori_loop(1, count, one, 0)
        pl.semaphore_wait(sem, count - 1)


def norm_pull(image, factor, inverse, grad, hat, plain, crossed, put):
    count = SIZES[image]
    mean_plain = group_mean(plain * factor, count)[:1]
    mean_crossed = group_mean(crossed * factor, count)[:1]
    def one(i, rows, carry):
        value = inverse * (grad(rows) * factor - mean_plain - hat(rows) * mean_crossed)
        put(i, rows, value)
        return carry + (value[:8] + value[8:])
    total = over_rows(image, one, jnp.zeros(plain.shape, F32))
    return jnp.sum(total, axis=0, keepdims=True)


def two_sums(image, channels, pair):
    def add(i, rows, carry):
        a, b = pair(i, rows)
        return carry[0] + (a[:8] + a[8:]), carry[1] + (b[:8] + b[8:])
    zero = jnp.zeros((8, channels), F32)
    sums = over_rows(image, add, (zero, zero))
    return [jnp.broadcast_to(jnp.sum(part, axis=0, keepdims=True), (8, channels)) for part in sums]


def silu_pull(value):
    gate = jax.nn.sigmoid(value)
    return gate * (1.0 + value * (1.0 - gate))


G_IN_GAIN, G_IN_SHIFT, G_FIRST, G_MID_GAIN, G_MID_SHIFT, G_SECOND, G_ATTN_GAIN, G_ATTN_SHIFT, G_OUT = range(9)


class Backward:
    def __init__(self, rows, full, r_low, pixels, vec, mod, inverses, a1, a2, mid_hat, outs, scratch):
        self.rows, self.full, self.r_low, self.pixels, self.vec, self.mod, self.inverses = rows, full, r_low, pixels, vec, mod, inverses
        self.h_a1, self.h_a2, self.h_mid = a1, a2, mid_hat
        self.g_first, self.g_second, self.g_skip, self.grad_pixels = outs
        (self.a1, self.pad, self.hat, self.acc, self.acc1, self.c_low, self.patch, self.weight, self.stage, self.w_skip,
         self.vecs, self.mods, self.in_sem, self.w_sem, self.o_sem) = scratch

    def row(self, r, channels=1024):
        return self.vec[r : r + 1, :channels]

    def add_row(self, r, value):
        width = value.shape[1]
        self.vecs[r : r + 1, :width] = self.vecs[r : r + 1, :width] + value[:1]

    def fetch(self):
        for i, (src, dst) in enumerate(((self.h_a2, self.pad), (self.h_a1, self.a1), (self.h_mid, self.hat))):
            pltpu.make_async_copy(src, dst, self.in_sem.at[i]).start()
        start, size = self.rows.skip
        def one(f, carry):
            pltpu.make_async_copy(shard_of(self.full, f, pl.ds(start, size)), self.w_skip.at[pl.ds(pl.multiple_of(f * size, SUB), size)], self.in_sem.at[3]).start()
            return carry
        lax.fori_loop(0, self.rows.parts, one, 0)

    def arrived(self, i):
        waited((self.pad, self.a1, self.hat, self.w_skip)[i], self.in_sem.at[i])

    def put_out(self, dst, first, count):
        span, size = dst.shape[1], dst.shape[3]
        for i in range(count):
            f = first + i
            pltpu.make_async_copy(
                self.stage.at[pl.ds(i * size, size)],
                dst.at[f // (2 * span), lax.rem(f // 2, span), lax.rem(f, 2)],
                self.o_sem,
            ).start()

    def weight_grad(self, q, pad, count, grad, dst):
        def prepare(known):
            gather_blocks(pad, range(known * BLOCK // 128, (known + 1) * BLOCK // 128), self.patch)
        choose(q, [(known, known + 1, functools.partial(prepare, known)) for known in range(count)])
        @pl.when(q > 0)
        def _():
            self.stored()
        for col in range(0, 1024, 256):
            cols = slice(col, col + 256)
            self.stage[:, cols] = lax.dot_general(self.patch[...], grad[:, cols], TN, preferred_element_type=F32).astype(BF16)
        each = BLOCK // dst.shape[3]
        self.put_out(dst, q * each, each)

    def second_weight(self, q):
        self.weight_grad(q, self.pad, 9 * self.pad.shape[2] // BLOCK, self.r_low, self.g_second)

    def first_weight(self, q):
        self.weight_grad(q, self.a1, 9 * self.a1.shape[2] // BLOCK, self.c_low, self.g_first)

    def stored(self, size=BLOCK):
        waited(self.stage.at[pl.ds(0, size)], self.o_sem)

    def skip_weight(self):
        size = self.pixels.shape[1]
        for col in range(0, 1024, 512):
            cols = slice(col, col + 512)
            self.stage[:size, cols] = lax.dot_general(self.pixels[...], self.r_low[:, cols], TN, preferred_element_type=F32).astype(BF16)
        self.put_out(self.g_skip, jnp.int32(0), self.rows.parts)
        self.stored(size)

    def pad_residual(self):
        zero_edges(self.pad)
        for image in range(3):
            def one(i, rows, carry):
                store_padded(self.pad, image, i, self.r_low[rows, :].astype(F32))
                return carry
            over_rows(image, one, 0)

    def load_tap(self, which, height, tap):
        start, size = which
        def one(known):
            at = known * height
            while at < (known + 1) * height:
                shard, inside = divmod(at, size)
                count = min(size - inside, (known + 1) * height - at)
                pltpu.make_async_copy(
                    shard_of(self.full, shard, pl.ds(start + inside, count)),
                    self.weight.at[known % 2, pl.ds(at - known * height, count)],
                    self.w_sem.at[known % 2],
                ).start()
                at += count
        if isinstance(tap, int):
            one(tap)
        else:
            choose(tap, [(known, known + 1, functools.partial(one, known)) for known in range(9)])

    def pull_step(self, tap, which, height, acc):
        @pl.when(tap + 1 < 9)
        def _():
            self.load_tap(which, height, tap + 1)
        @pl.when(tap == 0)
        def _():
            acc[...] = jnp.zeros_like(acc)
        def prepare(known):
            for image in range(3):
                self.patch[STARTS[image] : STARTS[image] + SIZES[image], :1024] = shifted(self.pad, known, image, slice(0, 1024), True)
        choose(tap, [(known, known + 1, functools.partial(prepare, known)) for known in range(9)])
        par = lax.rem(tap, 2)
        waited(self.weight.at[par, pl.ds(0, height)], self.w_sem.at[par])
        for col in range(0, height, 512):
            cols = slice(col, col + 512)
            acc[:, cols] = acc[:, cols] + lax.dot_general(self.patch[:, :1024], self.weight[par, cols, :], NT, preferred_element_type=F32)

    def load_second(self):
        self.load_tap(self.rows.second, 1024, 0)

    def second_pull(self, tap):
        self.pull_step(tap, self.rows.second, 1024, self.acc)

    def load_first(self):
        self.load_tap(self.rows.first, self.pixels.shape[1], 0)

    def first_pull(self, tap):
        self.pull_step(tap, self.rows.first, self.pixels.shape[1], self.acc1)

    def mid_pull(self, image):
        acc, hat, channels = self.acc, self.hat, 1024
        if image == 0:
            self.vecs[...] = jnp.zeros_like(self.vecs)
            self.mods[...] = jnp.zeros_like(self.mods)
            zero_edges(self.pad)
        scale, shift = 1.0 + self.mod[image : image + 1, :channels], self.mod[image : image + 1, channels:]
        gain, bias = self.row(V_MID_GAIN), self.row(V_MID_SHIFT)
        factor, lift = gain * scale, bias * scale + shift
        def pair(i, rows):
            h = hat[rows, :]
            grad = acc[rows, :] * silu_pull(h * factor + lift)
            acc[rows, :] = grad
            return grad, grad * h
        plain, crossed = two_sums(image, channels, pair)
        def put(i, rows, value):
            store_padded(self.pad, image, i, value)
            self.c_low[rows, :] = value.astype(BF16)
        inverse = self.inverses[3 + image : 4 + image, :]
        total = norm_pull(image, factor, inverse, lambda rows: acc[rows, :], lambda rows: hat[rows, :], plain, crossed, put)
        self.add_row(G_FIRST, total)
        self.add_row(G_MID_GAIN, crossed * scale)
        self.add_row(G_MID_SHIFT, plain * scale)
        self.mods[image : image + 1, :channels] = (crossed * gain + plain * bias)[:1]
        self.mods[image : image + 1, channels:] = plain[:1]

    def first_norm_pull(self, image):
        acc, pixels = self.acc1, self.pixels
        channels = pixels.shape[1]
        inverse, center = self.inverses[image : image + 1, :channels], self.inverses[16 + image : 17 + image, :channels]
        gain, bias = self.row(V_IN_GAIN, channels), self.row(V_IN_SHIFT, channels)
        hat = lambda rows: (pixels[rows, :].astype(F32) - center) * inverse
        def pair(i, rows):
            h = hat(rows)
            grad = acc[rows, :] * silu_pull(h * gain + bias)
            acc[rows, :] = grad
            return grad, grad * h
        plain, crossed = two_sums(image, channels, pair)
        def put(i, rows, value):
            self.grad_pixels[rows, :] = self.grad_pixels[rows, :] + value
        norm_pull(image, gain, inverse, lambda rows: acc[rows, :], hat, plain, crossed, put)
        self.add_row(G_IN_GAIN, crossed)
        self.add_row(G_IN_SHIFT, plain)

    def skip_pull(self):
        self.grad_pixels[...] = lax.dot_general(self.r_low[...], self.w_skip[...], NT, preferred_element_type=F32)


def reduce_kernel(replicas, parts, rows, spans, lead, ring, nrc, rb, lag, inner, text_dim, images, known, *refs):
    early = refs[:known]
    full, r_low, pixels, vec, mod, inverses, a1, a2, mid_hat, emb_note, more = refs[known : known + 11]
    kinds = len(spans)
    refs = refs[known + 11 :]
    outs, refs = refs[:kinds], refs[kinds:]
    notes, g_first, g_second, g_skip, grad_pixels, g_narrow, g_wide = refs[:7]
    rest = refs[7:]
    (hold, rc, xr, yr, tr, zu, zd, fr, tb, shared, target, shared32, target32) = rest[:13]
    scratch = rest[13:28]
    (l_sem, c_send, c_recv, x_send, x_recv, y_send, y_recv,
     u_send, u_recv, d_send, d_recv, f_send, f_recv, n_send, n_recv, t_send, t_recv, free, x_free, y_free, u_free, d_free) = rest[28:]
    me = Seat(replicas, parts)
    span = me.span
    width = r_low.shape[1]
    chunks = spans[-1][1]
    side = me.side
    bits = replicas.bit_length() - 1
    apart, joint = 3 * width // 8, 5 * width // 8
    thin = 128
    main = width - thin
    z_cols = pl.ds(pl.multiple_of(side * thin, thin), main)
    thin_cols = pl.ds(pl.multiple_of((1 - side) * main, thin), thin)
    thin_in = pl.ds(pl.multiple_of(side * main, thin), thin)
    x_in = pl.ds(pl.multiple_of(side * joint, 128), apart)
    y_cols = pl.ds(pl.multiple_of(side * apart, 128), joint)
    table = Rows(parts, pixels.shape[1], width, text_dim, inner)
    back = Backward(table, full, r_low, pixels, vec, mod, inverses, a1, a2, mid_hat, (g_first, g_second, g_skip, grad_pixels), scratch)
    grads = list(early) + [g_skip, g_second, g_first]

    me.meet()
    back.fetch()

    def copy(src, dst, send, recv, device):
        return pltpu.make_async_remote_copy(src_ref=src, dst_ref=dst, send_sem=send, recv_sem=recv, device_id=device, device_id_type=MESH)

    def give(sem, device):
        pl.semaphore_signal(sem, inc=1, device_id=device, device_id_type=MESH)

    def take(sem, k, size):
        @pl.when(k >= size)
        def _():
            pl.semaphore_wait(sem, 1)

    def core_copy(k, src):
        return copy(src, rc.at[lax.rem(k, nrc)], c_send.at[k], c_recv.at[lax.rem(k, nrc)], me.device(core=1 - me.core))

    def begin(k):
        take(free, k, nrc)
        for grad, (lo, hi) in zip(grads, spans):
            @pl.when(jnp.logical_and(k >= lo, k < hi))
            def _():
                at = pl.ds(pl.multiple_of((k - lo) * rows, 16), rows)
                slot = lax.rem(k, ring)
                pltpu.make_async_copy(grad.at[:, :, me.core, at, :], hold.at[slot], l_sem.at[slot]).start()
                core_copy(k, grad.at[:, :, 1 - me.core, at, :]).start()

    def x_copy(k, turn):
        slot = lax.rem(k, ring)
        cols = pl.ds(pl.multiple_of((1 - side) * joint, 128), apart)
        return copy(hold.at[slot, :, lax.rem(me.y + turn, span), :, cols], xr.at[lax.rem(k, rb), turn - 1], x_send.at[k, turn - 1], x_recv.at[k, turn - 1], me.bit(0))

    def y_copy(k, turn):
        slot = lax.rem(k, ring)
        return copy(hold.at[slot, :, lax.rem(me.y + turn, span), :, y_cols], yr.at[lax.rem(k, rb), turn - 1], y_send.at[k, turn - 1], y_recv.at[k, turn - 1], me.device(y=lax.rem(me.y + turn, span)))

    def t_copy(k):
        slot = lax.rem(k, ring)
        return copy(hold.at[slot, :, me.y, :, thin_cols], tr.at[lax.rem(k, rb)], t_send.at[k], t_recv.at[k], me.bit(0))

    def up_copy(k, z):
        slot = lax.rem(k, ring)
        return copy(hold.at[slot, z + 1 : DEPTH, me.y, :, z_cols], zu.at[lax.rem(k, rb), 0 : DEPTH - 1 - z], u_send.at[k], u_recv.at[k], me.device(z=me.z + 1))

    def down_copy(k, z):
        slot = lax.rem(k, ring)
        return copy(hold.at[slot, 0:z, me.y, :, z_cols], zd.at[lax.rem(k, rb), 0:z], d_send.at[k], d_recv.at[k], me.device(z=me.z - 1))

    def f_copy(k, b):
        slot = lax.rem(k, ring)
        src = hold.at[slot, me.z, me.y, :, z_cols] if b == 0 else tb.at[b - 1, k]
        dst = fr.at[b, k, :, pl.ds(0, main)] if b == 0 else fr.at[b, k]
        return copy(src, dst, f_send.at[b, k], f_recv.at[b, k], me.bit(b))

    def fold_core(k):
        slot = lax.rem(k, ring)
        waited(hold.at[slot], l_sem.at[slot])
        core_copy(k, rc.at[lax.rem(k, nrc)]).wait_recv()
        hold[slot] = hold[slot] + rc[lax.rem(k, nrc)]
        @pl.when(k + nrc < chunks)
        def _():
            give(free, me.device(core=1 - me.core))
        for turn in range(1, span):
            take(x_free.at[turn - 1], k, rb)
            x_copy(k, turn).start()
        t_copy(k).start()

    def fold_x(k):
        slot = lax.rem(k, ring)
        t_copy(k).wait_recv()
        hold[slot, :, me.y, :, thin_in] = hold[slot, :, me.y, :, thin_in] + tr[lax.rem(k, rb)]
        for turn in range(1, span):
            x_copy(k, turn).wait_recv()
            y = lax.rem(me.y + turn, span)
            hold[slot, :, y, :, x_in] = hold[slot, :, y, :, x_in] + xr[lax.rem(k, rb), turn - 1]
            @pl.when(k + rb < chunks)
            def _():
                give(x_free.at[turn - 1], me.bit(0))
            take(y_free.at[turn - 1], k, rb)
            y_copy(k, turn).start()

    def fold_y(k):
        slot = lax.rem(k, ring)
        for turn in range(1, span):
            y_copy(k, turn).wait_recv()
            hold[slot, :, me.y, :, y_cols] = hold[slot, :, me.y, :, y_cols] + yr[lax.rem(k, rb), turn - 1]
            @pl.when(k + rb < chunks)
            def _():
                give(y_free.at[turn - 1], me.device(y=lax.rem(me.y + span - turn, span)))

    def hop(k, h):
        slot = lax.rem(k, ring)
        @pl.when(me.z == h)
        def _():
            if h > 0:
                up_copy(k, h - 1).wait_recv()
                hold[slot, h:, me.y, :, z_cols] = hold[slot, h:, me.y, :, z_cols] + zu[lax.rem(k, rb), 0 : DEPTH - h]
                @pl.when(k + rb < chunks)
                def _():
                    give(u_free, me.device(z=me.z - 1))
            if h < DEPTH - 1:
                take(u_free, k, rb)
                up_copy(k, h).start()
        z = DEPTH - 1 - h
        @pl.when(me.z == z)
        def _():
            if h > 0:
                down_copy(k, z + 1).wait_recv()
                hold[slot, : z + 1, me.y, :, z_cols] = hold[slot, : z + 1, me.y, :, z_cols] + zd[lax.rem(k, rb), 0 : z + 1]
                @pl.when(k + rb < chunks)
                def _():
                    give(d_free, me.device(z=me.z + 1))
            if h < DEPTH - 1:
                take(d_free, k, rb)
                down_copy(k, z).start()

    def finish(k, b):
        slot = lax.rem(k, ring)
        f_copy(k, b).wait_recv()
        if b == 0:
            came = jnp.concatenate([fr[b, k, :, :main].astype(F32), jnp.zeros((rows, thin), F32)], 1)
            before = hold[slot, me.z, me.y].astype(F32)
            column = lax.broadcasted_iota(jnp.int32, before.shape, 1)
            came = pltpu.roll(came, thin * (1 - side), 1)
            ours = jnp.logical_and(column >= thin * side, column < main + thin * side)
            theirs = jnp.logical_and(column >= thin * (1 - side), column < main + thin * (1 - side))
            total = jnp.where(ours, before, 0.0) + jnp.where(theirs, came, 0.0)
        else:
            total = tb[b - 1, k].astype(F32) + fr[b, k].astype(F32)
        if b == bits - 1:
            for out, (lo, hi) in zip(outs, spans):
                @pl.when(jnp.logical_and(k >= lo, k < hi))
                def _():
                    out[pl.ds(pl.multiple_of((k - lo) * rows, 16), rows), :] = total
        else:
            tb[b, k] = total.astype(BF16)
            f_copy(k, b + 1).start()

    def retire(k):
        core_copy(k, rc.at[0]).wait_send()
        t_copy(k).wait_send()
        for turn in range(1, span):
            x_copy(k, turn).wait_send()
            y_copy(k, turn).wait_send()
        for z in range(DEPTH):
            @pl.when(me.z == z)
            def _():
                if z < DEPTH - 1:
                    up_copy(k, z).wait_send()
                if z > 0:
                    down_copy(k, z).wait_send()
        for b in range(bits):
            f_copy(k, b).wait_send()

    count = replicas * parts
    mine = me.group * parts + me.place
    tall = shared.shape[0]

    def note_copies(far):
        device = (far // parts, lax.rem(far, parts))
        return (
            copy(shared, notes.at[mine, pl.ds(0, tall)], n_send, n_recv, device),
            copy(target.at[lax.rem(far, parts)], notes.at[mine, pl.ds(tall, 16)], n_send, n_recv, device),
        )

    def tell():
        back.vecs[:, :] = back.vecs[:, :] + more[...]
        target32[...] = emb_note[...].astype(F32)
        each = 2 * width // 128
        for image in range(images):
            for j in range(each):
                shared32[image * each + j : image * each + j + 1, :] = back.mods[image : image + 1, j * 128 : (j + 1) * 128]
        shared[...] = shared32[...].astype(BF16)
        for row in range(G_OUT + 1):
            size = (pixels.shape[1] if row in (G_IN_GAIN, G_IN_SHIFT) else width) // parts
            for f in range(parts):
                block = f * size // 128
                target32[f, images + row : images + row + 1, :] = back.vecs[row : row + 1, block * 128 : (block + 1) * 128]
        target[...] = target32[...].astype(BF16)
        def send(i, carry):
            for one in note_copies(lax.rem(mine + i, count)):
                one.start()
            return carry
        lax.fori_loop(1, count, send, 0)
        notes[mine, :tall, :] = shared[...]
        notes[mine, tall:, :] = target[me.place]
    lo_skip, lo_second, lo_first = (spans[known + i][0] - lead for i in range(3))
    n2, n1 = 9 * width // BLOCK, 9 * pixels.shape[1] // BLOCK
    begun = min(FILL, lo_second - n2)
    s0 = begun + n2
    s1 = s0 + 10
    s2 = s1 + 3
    s3 = s2 + n1
    s4 = s3 + 6
    assert 1 <= lo_skip and begun >= 2 and s0 <= lo_second and s3 <= lo_first
    last = max(chunks + (2 + DEPTH + bits) * lag + 1, s4 + 5)

    def steps(t):
        options = []
        def once(when, *work):
            def run():
                for one in work:
                    one()
            options.append((when, when + 1, run))
        def many(when, until, each, limit, work):
            def run():
                for i in range(each):
                    at = (t - when) * each + i
                    if limit % each:
                        pl.when(at < limit)(lambda: work(at))
                    else:
                        work(at)
            options.append((when, until, run))
        def last_of(work):
            def run(i, end):
                work(i)
                pl.when(i == end - 1)(back.stored)
            return run
        second, first = last_of(back.second_weight), last_of(back.first_weight)
        once(0, back.skip_weight)
        once(begun - 1, lambda: back.arrived(0))
        many(begun, s0, 1, n2, lambda i: second(i, n2))
        once(s0, back.pad_residual, back.load_second)
        many(s0 + 1, s1, 1, 9, back.second_pull)
        for image in range(3):
            once(s1 + image, *([lambda: back.arrived(1), lambda: back.arrived(2), lambda: back.arrived(3)] if image == 0 else []), functools.partial(back.mid_pull, image))
        many(s2, s3, 1, n1, lambda i: first(i, n1))
        once(s3, back.load_first)
        many(s3 + 1, s4, 2, 9, back.first_pull)
        once(s4, back.skip_pull)
        for image in range(3):
            once(s4 + 1 + image, functools.partial(back.first_norm_pull, image))
        once(s4 + 4, tell)
        choose(t, options)

    for k in range(lead):
        begin(jnp.int32(k))

    first_f = (2 + DEPTH) * lag

    def slot_work(t, carry):
        def stage(delay, work):
            k = t - delay
            @pl.when(jnp.logical_and(k >= 0, k < chunks))
            def _():
                work(k)
        for h in range(DEPTH - 1, 0, -1):
            stage((2 + h) * lag, functools.partial(hop, h=h))
        stage((1 + DEPTH) * lag, lambda k: f_copy(k, 0).start())
        def pair(k):
            fold_y(k)
            hop(k, 0)
        stage(2 * lag, pair)
        stage(lag, fold_x)
        stage(0, fold_core)
        for b in range(bits):
            stage(first_f + b * lag, functools.partial(finish, b=b))
        stage(first_f + bits * lag, retire)
        @pl.when(t + lead < chunks)
        def _():
            begin(t + lead)
        steps(t)
        return carry

    lax.fori_loop(0, last, slot_work, 0)
    others = notes.at[pl.ds(0, count - 1)]
    every = copy(others, others, n_send, n_recv, me.device(core=1 - me.core))
    every.wait_send()
    every.wait_recv()
    total = jnp.sum(notes[:, tall:, :].astype(F32), axis=0)
    for dst, first, last in ((g_narrow, G_IN_GAIN, G_IN_SHIFT), (g_wide, G_FIRST, G_OUT)):
        size = dst.shape[2]
        turn = lax.rem(128 - lax.rem(me.place * size, 128), 128)
        mine_only = pltpu.roll(total, turn, 1)
        for row in range(first, last + 1):
            dst[row - first] = mine_only[images + row : images + row + 1, :size]


def reduce_all(early, full, r_low, pixels, vec, mod, inverses, a1, a2, mid_hat, emb_note, more, inner, text_dim, images, replicas, parts, rows, lead=2, nrc=3, lag=2, rb=8):
    span = parts // (2 * DEPTH)
    pix, width = r_low.shape
    pix_width = pixels.shape[1]
    spans, at = [], 0
    views = []
    for size in [grad.shape[0] // parts for grad in early] + [pix_width // parts, 9 * width // parts, 9 * pix_width // parts]:
        spans.append((at // rows, (at + size) // rows))
        at += size
    for grad in early:
        views.append(grad.reshape(DEPTH, span, 2, grad.shape[0] // parts, width))
    total = at
    chunks = total // rows
    bits = replicas.bit_length() - 1
    ring = lead + (2 + DEPTH + bits) * lag + 2
    dma = lambda *shape: pltpu.SemaphoreType.DMA(shape)
    reg = lambda *shape: pltpu.SemaphoreType.REGULAR(shape)
    vm = lambda *shape: pltpu.VMEM(shape, BF16)
    vf = lambda *shape: pltpu.VMEM(shape, F32)
    bf = lambda *shape: jax.ShapeDtypeStruct(shape, BF16)
    fl = lambda *shape: jax.ShapeDtypeStruct(shape, F32)
    hbm, vmem = pl.BlockSpec(memory_space=pl.ANY), pl.BlockSpec(memory_space=pltpu.VMEM)
    tall = images * 2 * width // 128
    return pl.pallas_call(
        functools.partial(reduce_kernel, replicas, parts, rows, spans, lead, ring, nrc, rb, lag, inner, text_dim, images, len(early)),
        out_shape=[
            *(fl((hi - lo) * rows, width) for lo, hi in spans), bf(replicas * parts, tall + 16, 128),
            *(bf(DEPTH, span, 2, size // parts, width) for size in (9 * pix_width, 9 * width, pix_width)), fl(pix, pix_width),
            fl(2, 1, pix_width // parts), fl(7, 1, width // parts),
        ],
        in_specs=[hbm] * (len(early) + 1) + [vmem] * 5 + [hbm] * 3 + [vmem] * 2,
        out_specs=[vmem] * (len(spans) + 1) + [hbm] * 3 + [vmem] * 3,
        scratch_shapes=[
            vm(ring, DEPTH, span, rows, width),
            vm(nrc, DEPTH, span, rows, width),
            vm(rb, span - 1, DEPTH, rows, 3 * width // 8),
            vm(rb, span - 1, DEPTH, rows, 5 * width // 8),
            vm(rb, DEPTH, rows, 128),
            vm(rb, DEPTH - 1, rows, width - 128),
            vm(rb, DEPTH - 1, rows, width - 128),
            vm(bits, chunks, rows, width),
            vm(max(bits - 1, 1), chunks if bits > 1 else 1, rows, width),
            vm(tall, 128), vm(parts, 16, 128), vf(tall, 128), vf(parts, 16, 128),
            vm(3, PADDED, pix_width), vm(3, PADDED, width), vf(pix, width), vf(pix, width), vf(pix, pix_width), vm(pix, width),
            vm(pix, BLOCK), vm(2, 1024, width), vm(BLOCK, width), vm(pix_width, width), vf(16, width), vf(8, 2 * width),
            dma(4), dma(2), dma(),
            dma(ring),
            dma(chunks), dma(nrc),
            dma(chunks, span - 1), dma(chunks, span - 1),
            dma(chunks, span - 1), dma(chunks, span - 1),
            dma(chunks), dma(chunks), dma(chunks), dma(chunks),
            dma(bits, chunks), dma(bits, chunks),
            pltpu.SemaphoreType.DMA, pltpu.SemaphoreType.DMA, dma(chunks), dma(chunks),
            pltpu.SemaphoreType.REGULAR, reg(span - 1), reg(span - 1), pltpu.SemaphoreType.REGULAR, pltpu.SemaphoreType.REGULAR,
        ],
        compiler_params=pltpu.CompilerParams(collective_id=1, has_side_effects=True, vmem_limit_bytes=62 << 20),
        name="reduce_all",
    )(*views, full, r_low, pixels, vec, mod, inverses, a1, a2, mid_hat, emb_note, more)


def middle_kernel(parts, inner, text_dim, triple, text_pair, keep, grad_attended, cotangent, vec, inverses, present, full, h_normed, h_hats, h_residual, h_text,
                  r_low, more, h_block, h_out, h_attend, h_more, h_g_text, attended, grad_triple, grad_text, rows_grad, w_attend, w_out, stage,
                  g_low, queries, outs, keys, values, normed, hats, residual, text, block_output, g_out, g_attend, g_more, sems, i_sems, o_sems):
    width = cotangent.shape[1]
    table = Rows(parts, 512, width, text_dim, inner)
    start, size = table.out
    def one(f, carry):
        pltpu.make_async_copy(shard_of(full, f, pl.ds(start, size)), w_out.at[pl.ds(pl.multiple_of(f * size, SUB), size)], sems.at[0]).start()
        return carry
    lax.fori_loop(0, parts, one, 0)
    table.load_attend(full, w_attend, sems.at[1])

    late = [pltpu.make_async_copy(src, dst, i_sems.at[i]) for i, (src, dst) in enumerate(((h_text, text), (h_residual, residual), (h_normed, normed), (h_hats, hats)))]
    for copy in late:
        copy.start()
    done = [pltpu.make_async_copy(src, dst, o_sems.at[i]) for i, (src, dst) in enumerate(((block_output, h_block), (g_out, h_out), (g_attend, h_attend), (g_more, h_more)))]

    for image in range(3):
        g_low[pl.ds(STARTS[image], SIZES[image]), :] = outgoing(cotangent, present, image)

    lane = lax.broadcasted_iota(jnp.int32, (1, 2 * HEAD), 1)
    scale = HEAD ** -0.5
    room = min(SIZES) + TEXT_ROWS
    for buf in (keys, values):
        buf[room:, :] = jnp.zeros((KEYS - room, 2 * HEAD), BF16)

    def heads(pair, carry):
        at = lambda shift: pl.ds(pl.multiple_of(pair * 2 * HEAD + shift * inner, 128), 2 * HEAD)
        for image in range(3):
            size = SIZES[image]
            rows = pl.ds(STARTS[image], size)
            text_rows = pl.ds(image * TEXT_ROWS, TEXT_ROWS)
            for buf, part in ((queries, triple[rows, at(0)] * jnp.asarray(scale, BF16)), (outs, grad_attended[rows, at(0)])):
                buf[:size, :] = jnp.where(lane < HEAD, part, jnp.zeros_like(part))
                buf[size : 2 * size, :] = jnp.where(lane < HEAD, jnp.zeros_like(part), part)
            for i, buf in enumerate((keys, values)):
                buf[:size, :] = triple[rows, at(1 + i)]
                buf[size : size + TEXT_ROWS, :] = text_pair[text_rows, at(i)]
            q, go = queries[: 2 * size, :], outs[: 2 * size, :]
            seen = keep[image : image + 1, :]
            s = lax.dot_general(q, keys[...], NT, preferred_element_type=F32)
            s = jnp.where(seen == 1, s, jnp.where(seen == 0, -1000000000.0, -jnp.inf))
            e = jnp.exp(s - jnp.max(s, axis=1, keepdims=True))
            p = e * (1.0 / jnp.sum(e, axis=1, keepdims=True))
            low = p.astype(BF16)
            out = dot(low, values[...])
            dv = lax.dot_general(low, go, TN, preferred_element_type=F32)
            dp = lax.dot_general(go, values[...], NT, preferred_element_type=F32)
            ds = (p * (dp - jnp.sum(dp * p, axis=1, keepdims=True))).astype(BF16)
            dq = dot(ds, keys[...]) * scale
            dk = lax.dot_general(ds, q, TN, preferred_element_type=F32)
            merge = lambda part: jnp.where(lane < HEAD, part[:size], part[size:]).astype(BF16)
            attended[rows, at(0)] = merge(out)
            grad_triple[rows, at(0)] = merge(dq)
            grad_triple[rows, at(1)] = dk[:size].astype(BF16)
            grad_triple[rows, at(2)] = dv[:size].astype(BF16)
            grad_text[text_rows, at(0)] = dk[size : size + TEXT_ROWS].astype(BF16)
            grad_text[text_rows, at(1)] = dv[size : size + TEXT_ROWS].astype(BF16)
        return carry

    lax.fori_loop(0, inner // (2 * HEAD), heads, 0)

    late[0].wait()

    def text_block(q, carry):
        at = pl.ds(pl.multiple_of(q * 1024, 128), 1024)
        for col in range(0, width, 512):
            cols = slice(col, col + 512)
            stage[at, cols] = lax.dot_general(text[:, at], grad_text[:, cols], TN, preferred_element_type=F32).astype(BF16)
        pltpu.make_async_copy(stage.at[at], h_g_text.at[at], o_sems.at[4]).start()
        return carry

    lax.fori_loop(0, text_dim // 1024, text_block, 0)

    waited(w_out, sems.at[0])
    late[1].wait()
    bias = vec[V_OUT : V_OUT + 1, :width]
    for image in range(3):
        rows = pl.ds(STARTS[image], SIZES[image])
        block_output[rows, :] = (
            present[0, image].astype(F32) * (residual[rows, :] + (dot(attended[rows, :], w_out[...]) + bias))
        ).astype(BF16)
    done[0].start()
    late[2].wait()
    for col in range(0, width, 512):
        cols = slice(col, col + 512)
        g_out[:, cols] = lax.dot_general(attended[...], g_low[:, cols], TN, preferred_element_type=F32).astype(BF16)
        g_attend[:, cols] = lax.dot_general(normed[...], grad_triple[:, cols], TN, preferred_element_type=F32).astype(BF16)
    last = lax.dot_general(normed[...], grad_triple[:, width:], TN, preferred_element_type=F32).astype(BF16)
    half = width // parts // 2
    for f in range(parts):
        for i in range(2):
            g_more[f * half : (f + 1) * half, 512 * i : 512 * (i + 1)] = last[(2 * f + i) * half : (2 * f + i + 1) * half]
    for copy in done[1:]:
        copy.start()
    waited(w_attend, sems.at[1])
    for col in range(0, width, 512):
        cols = slice(col, col + 512)
        rows_grad[:, cols] = lax.dot_general(grad_triple[...], w_attend[cols, :], NT, preferred_element_type=F32)

    late[3].wait()
    more[...] = jnp.zeros_like(more)
    gain = vec[V_ATTN_GAIN : V_ATTN_GAIN + 1, :width]
    for image in range(3):
        def pair(i, rows):
            grad = rows_grad[rows, :]
            return grad, grad * hats[rows, :]
        plain, crossed = two_sums(image, width, pair)
        def put(i, rows, value):
            rows_grad[rows, :] = value + g_low[rows, :].astype(F32)
        norm_pull(image, gain, inverses[6 + image : 7 + image, :], lambda rows: rows_grad[rows, :], lambda rows: hats[rows, :], plain, crossed, put)
        def ends(i, rows):
            value = rows_grad[rows, :]
            r_low[rows, :] = value.astype(BF16)
            return value, g_low[rows, :].astype(F32)
        total, outer = two_sums(image, width, ends)
        for row, value in ((G_ATTN_GAIN, crossed), (G_ATTN_SHIFT, plain), (G_SECOND, total), (G_OUT, outer)):
            more[row : row + 1, :] = more[row : row + 1, :] + value[:1]
    for copy in done:
        copy.wait()
    waited(stage, o_sems.at[4])


def middle(triple, text_pair, keep, grad_attended, cotangent, normed, hats, residual, text, vec, inverses, present, full, parts, inner, text_dim):
    pix, width = cotangent.shape
    bf = lambda *shape: jax.ShapeDtypeStruct(shape, BF16)
    vm = lambda *shape: pltpu.VMEM(shape, BF16)
    hbm, vmem = pl.BlockSpec(memory_space=pl.ANY), pl.BlockSpec(memory_space=pltpu.VMEM)
    return pl.pallas_call(
        functools.partial(middle_kernel, parts, inner, text_dim),
        out_shape=[bf(pix, width), jax.ShapeDtypeStruct((16, width), F32), bf(pix, width), bf(inner, width), bf(width, width), bf(width // 2, width), bf(text_dim, width)],
        in_specs=[vmem] * 7 + [pl.BlockSpec(memory_space=pltpu.SMEM)] + [hbm] * 5,
        out_specs=[vmem] * 2 + [hbm] * 5,
        scratch_shapes=[
            vm(pix, inner), vm(pix, 3 * inner), vm(text.shape[0], 2 * inner), pltpu.VMEM((pix, width), F32),
            vm(width, 3 * inner), vm(inner, width), vm(text_dim, width), vm(pix, width),
            vm(2 * max(SIZES), 2 * HEAD), vm(2 * max(SIZES), 2 * HEAD), vm(KEYS, 2 * HEAD), vm(KEYS, 2 * HEAD),
            vm(pix, width), pltpu.VMEM((pix, width), F32), pltpu.VMEM((pix, width), F32), vm(*text.shape),
            vm(pix, width), vm(inner, width), vm(width, width), vm(width // 2, width),
            pltpu.SemaphoreType.DMA((2,)), pltpu.SemaphoreType.DMA((4,)), pltpu.SemaphoreType.DMA((5,)),
        ],
        compiler_params=pltpu.CompilerParams(vmem_limit_bytes=60 << 20),
        name="middle",
    )(triple, text_pair, keep, grad_attended, cotangent, vec, inverses, present, full, normed, hats, residual, text)


def last_kernel(images, depth, tall, count, *refs):
    big, (h_attend, h_more, h_notes, narrow, wide) = refs[:count], refs[count : count + 5]
    refs = refs[count + 5 :]
    big_out, (o_attend, emb_weight, emb_bias) = refs[:count], refs[count : count + 3]
    vectors, refs = refs[count + 3 : count + 13], refs[count + 13 :]
    bufs, (attend, more, notes, plain, bias, i_sems, o_sems) = refs[:count], refs[count:]
    sources = [h_notes] + list(big) + [h_attend, h_more]
    targets = [notes] + list(bufs) + [attend, more]
    ins = [pltpu.make_async_copy(src, dst, i_sems.at[i]) for i, (src, dst) in enumerate(zip(sources, targets))]
    for copy in ins:
        copy.start()
    high, across = more.shape[0], more.shape[1] // 2
    jobs = [[job] for job in zip(bufs, big_out)] + [[(attend, o_attend.at[:, pl.ds(0, 2 * across)])]]
    jobs += [[(more.at[:, pl.ds(i * across, across)], o_attend.at[pl.ds(i * high, high), pl.ds(2 * across, across)]) for i in range(2)]]
    out = []

    def pass_on(i):
        ins[i + 1].wait()
        for src, dst in jobs[i]:
            out.append(pltpu.make_async_copy(src, dst, o_sems.at[len(out)]))
            out[-1].start()

    ins[0].wait()
    plain[...] = notes[...].astype(F32)
    per_image = tall // images
    for j in range(per_image):
        total, sums = jnp.zeros((128, 128), F32), jnp.zeros((1, 128), F32)
        for image in range(images):
            mods = plain[:, image * per_image + j, :]
            total = total + lax.dot_general(plain[:, tall + image, :].astype(BF16), mods.astype(BF16), TN, preferred_element_type=F32)
            sums = sums + jnp.sum(mods, axis=0, keepdims=True)
        emb_weight[:, j * 128 : (j + 1) * 128] = total[:depth]
        bias[j : j + 1, :] = sums
        if j >= 2 and j - 2 < len(jobs):
            pass_on(j - 2)
    for i in range(max(0, per_image - 2), len(jobs)):
        pass_on(i)
    at = lax.axis_index("fsdp") * depth
    emb_bias[...] = pltpu.roll(jnp.broadcast_to(bias[pl.ds(at // 128, 1), :], (8, 128)), lax.rem(128 - lax.rem(at, 128), 128), 1)[:1, :depth]
    for i, dst in enumerate(vectors):
        row = i if i < 9 else G_SECOND
        dst[...] = narrow[row] if row < narrow.shape[0] else wide[row - narrow.shape[0]]
    for copy in out:
        copy.wait()


def last(big, attend, more, notes, narrow, wide, images, depth):
    tall = notes.shape[1] - 16
    columns = tall // images * 128
    hbm, vmem = pl.BlockSpec(memory_space=pl.ANY), pl.BlockSpec(memory_space=pltpu.VMEM)
    fl = lambda *shape: jax.ShapeDtypeStruct(shape, F32)
    vf = lambda *shape: pltpu.VMEM(shape, F32)
    sizes = [narrow.shape[2]] * narrow.shape[0] + [wide.shape[2]] * (wide.shape[0] + 1)
    dma = lambda count: pltpu.SemaphoreType.DMA((count,))
    return pl.pallas_call(
        functools.partial(last_kernel, images, depth, tall, len(big)),
        out_shape=[fl(*part.shape) for part in big] + [fl(attend.shape[0], attend.shape[1] + more.shape[1] // 2), fl(depth, columns), fl(1, depth)] + [fl(1, size) for size in sizes],
        in_specs=[hbm] * (len(big) + 3) + [vmem] * 2,
        out_specs=[hbm] * (len(big) + 1) + [vmem] * (2 + len(sizes)),
        scratch_shapes=[vf(*part.shape) for part in big] + [
            vf(*attend.shape), vf(*more.shape), pltpu.VMEM(notes.shape, BF16), vf(*notes.shape), vf(max(8, tall // images), 128),
            dma(len(big) + 3), dma(len(big) + 3),
        ],
        compiler_params=pltpu.CompilerParams(vmem_limit_bytes=60 << 20),
        name="last",
    )(*big, attend, more, notes, narrow, wide)


def body(
    pixels,
    embedding,
    text_states,
    text_mask,
    occupancy,
    cotangent,
    in_gain,
    in_shift,
    conv_first,
    first_bias,
    emb_weight,
    emb_bias,
    mid_gain,
    mid_shift,
    conv_second,
    second_bias,
    skip_weight,
    skip_bias,
    attn_gain,
    attn_shift,
    attend_weight,
    text_weight,
    out_weight,
    out_bias,
):
    place = lax.axis_index("fsdp")
    group = lax.axis_index("dp")
    parts = lax.axis_size("fsdp")
    replicas = lax.axis_size("dp")
    depth = emb_weight.shape[0]
    images_here = embedding.shape[0]
    emb_act = jax.nn.silu(embedding.astype(F32)).astype(BF16)
    emb_cut = emb_act.reshape(images_here, parts, depth).transpose(1, 0, 2)
    emb_cut = jnp.pad(emb_cut, ((0, 0), (0, 0), (0, 128 - depth)))

    lane = lax.broadcasted_iota(jnp.int32, (1, 128), 1)

    def placed(vectors):
        size = vectors[0].shape[0]
        wide = jnp.concatenate([jnp.stack(vectors)] * (128 // size), 1)
        return jnp.where(lane // size == lax.rem(place, 128 // size), wide, jnp.zeros_like(wide))

    lines = [placed((in_gain, in_shift)), placed((emb_bias,)), placed((first_bias, mid_gain, mid_shift, second_bias, skip_bias, attn_gain, attn_shift, out_bias))]
    room = 16 - images_here - sum(line.shape[0] for line in lines)
    flat = jnp.concatenate(lines + [jnp.zeros((room, 128), BF16)] if room else lines, 0)[None]
    note = jnp.concatenate([emb_cut, jnp.broadcast_to(flat, (parts,) + flat.shape[1:])], 1)
    channels = skip_weight.shape[1]
    inner = out_weight.shape[0] * parts
    text_len = text_states.shape[1]
    (full, modulation, vec, _, act1, act2, mid_hats, residual, hats, normed, triple, text_pair, grad_attended, inverses, text_rows) = forward_all(
        (conv_first, conv_second, skip_weight, out_weight, attend_weight, text_weight), note, jnp.pad(emb_weight, ((0, 128 - depth), (0, 0))), pixels, text_states, cotangent, occupancy, images_here, inner, replicas, parts)
    keep = (text_mask > 0).astype(jnp.int32)
    keep = jnp.stack([
        jnp.pad(jnp.pad(keep[i], (size, 0), constant_values=1), (0, KEYS - size - text_len), constant_values=2)
        for i, size in enumerate(SIZES)
    ])
    r_low, more, block_output, g_out, g_attend, g_more, g_text = middle(
        triple, text_pair, keep, grad_attended, cotangent, normed, hats, residual, text_rows, vec, inverses, occupancy, full, parts, inner, text_states.shape[2]
    )
    (grad_out_weight, attend, attend_more, grad_text_weight, grad_skip_weight, grad_conv_second, grad_conv_first,
     notes, _, _, _, grad_pixels, narrow, wide) = reduce_all(
        [g_out, g_attend, g_more, g_text], full, r_low, pixels, vec, modulation, inverses, act1, act2, mid_hats, note, more,
        inner, text_states.shape[2], images_here, replicas, parts, 512 // parts,
    )
    (grad_text_weight, grad_out_weight, grad_conv_second, grad_skip_weight, grad_conv_first, grad_pixels, grad_attend_weight,
     grad_emb_weight, grad_emb_bias, *vectors) = last(
        [grad_text_weight, grad_out_weight, grad_conv_second, grad_skip_weight, grad_conv_first, grad_pixels],
        attend, attend_more, notes, narrow, wide, images_here, depth,
    )
    grad_emb_bias = grad_emb_bias.reshape(-1)
    small = lambda row: vectors[row].reshape(-1)
    return (
        block_output,
        grad_pixels,
        small(G_IN_GAIN),
        small(G_IN_SHIFT),
        grad_conv_first,
        small(G_FIRST),
        grad_emb_weight,
        grad_emb_bias,
        small(G_MID_GAIN),
        small(G_MID_SHIFT),
        grad_conv_second,
        small(G_SECOND),
        grad_skip_weight,
        vectors[-1].reshape(-1),
        small(G_ATTN_GAIN),
        small(G_ATTN_SHIFT),
        grad_attend_weight,
        grad_text_weight,
        grad_out_weight,
        small(G_OUT),
    )


def solution(mesh):
    rows = P(("dp", "fsdp"), None)
    vector = P("fsdp")
    matrix = P("fsdp", None)
    weights = (vector, vector, matrix, vector, matrix, vector, vector, vector, matrix, vector, matrix, vector, vector, vector, matrix, matrix, matrix, vector)
    return jax.shard_map(
        body,
        mesh=mesh,
        in_specs=(rows, rows, P(("dp", "fsdp"), None, None), rows, rows, rows) + weights,
        out_specs=(rows, rows) + weights,
        check_vma=False,
    )
```
